32 devices in a mesh: tiles: 2 (over y), cols: 4 (over z), lines: 2 (over x), view: 2 (over core).
Axes of the slice: x: 2, y: 2, z: 4, core: 2. Of those that a mesh axis runs over, the one named last changes fastest.
Arguments:
- features: bfloat16 [2, 64, 64, 1024], P('view', ('tiles', 'lines'), None, 'cols'), parts along dimension 1, as said below
- valid_cols: int32 [2, 2048], P(None, ('tiles', 'cols')), parts along dimension 1, may hold values 0 or 1
- offsets: int32 [64], P(('tiles', 'lines')), parts along dimension 0, may hold values from 0 to 32
- guide_weight: bfloat16 [64, 108], replicated, may hold values from -0.75 to 0.75
Outputs:
- disparity: float32 [4, 16, 1024], P(('tiles', 'lines'), 'cols'), parts along dimension 0
The draws below stay inside these ranges and needn't reach their ends.
There are 2 independent parts, one for each index of `tiles`. The reference program is written for one: setup_inputs(seed, part) draws one part's arguments, and reference() takes and returns one part's arrays. A program takes and returns all parts, laid end to end along the dimension named above; an argument that names none is the same for every part. Nothing has to cross between parts.
Inputs may be any that keep to these rules, and one draw needn't show every extreme that they name: `features`: features of one tile's two views.
All inputs are finite; a program needn't handle non-finite values. No bound on the sum of `valid_cols` on one device may be relied on, other than what follows from the above.
Results may differ from the reference program's by a relative error of at most 0.0066.
Values may be sent and summed in bfloat16 or wider, within the bound.
No kernel may reach another device: no remote copies, remote signals or barrier semaphores. Data moves between devices by JAX's collectives and lax.ppermute only.
A program may use at most 64 MiB of HBM per device.

```python
import math
import jax
import jax.numpy as jnp
from jax import lax

C = 64
DISP = 192
OFFMAX = 32
DGROUP = 16
LAYERS = 3
LINE_ROWS = 16
HEIGHT = 32
WIDTH = 1024
RIM = 224
GROUPS = 12
N_LINES = 2


def draw_features(key, part):
    keys = jax.random.split(key, 3)
    base_feats = jnp.clip(jax.random.normal(keys[0], (HEIGHT, C, WIDTH), jnp.float32), -4.0, 4.0)
    shifts = jax.random.randint(keys[1], (HEIGHT, WIDTH // 64), 0, RIM)
    shift_cols = jnp.repeat(shifts, 64, axis=1)
    source_col = jnp.arange(WIDTH)[None, :] + shift_cols
    inside = source_col < WIDTH
    source_col = jnp.minimum(source_col, WIDTH - 1)
    matched = jax.vmap(lambda feats_row, cols_row: feats_row[:, cols_row])(base_feats, source_col)
    noise_part = jnp.clip(jax.random.normal(keys[2], (HEIGHT, C, WIDTH), jnp.float32), -4.0, 4.0)
    sec_feats = jnp.where(inside[:, None, :], jnp.clip(0.8 * matched + 0.6 * noise_part, -4.0, 4.0), noise_part)
    return jnp.stack([base_feats, sec_feats]).astype(jnp.bfloat16)


def touch_ends(array, stream_key, smallest, top_value):
    dims = array.shape
    spot = [jax.random.randint(jax.random.fold_in(stream_key, axis), (), 0, dims[axis]) for axis in range(len(dims))]
    array = array.at[tuple(spot)].set(smallest)
    longest = dims.index(max(dims))
    spot[longest] = (spot[longest] + 1) % dims[longest]
    return array.at[tuple(spot)].set(top_value)


def normal_values(rng, shape, scale, limit, held_as=jnp.bfloat16):
    array = scale * jax.random.normal(rng, shape, jnp.float32)
    return jnp.clip(array, min=-limit, max=limit).astype(held_as)


def setup_inputs(seed: int = 0, part: int = 0) -> dict:
    splits = jax.random.split(jax.random.key(seed), 5)
    part_keys = jax.random.split(jax.random.fold_in(splits[4], part), 5)
    return {
        "features": draw_features(jax.random.fold_in(jax.random.fold_in(splits[4], part), 71), part),
        "valid_cols": touch_ends((jax.random.randint(part_keys[1], (2, WIDTH), 0, 8) < 7).astype(jnp.int32), jax.random.fold_in(part_keys[1], 1), 0, 1),
        "offsets": touch_ends(jax.random.randint(part_keys[2], (HEIGHT,), 0, OFFMAX + 1), jax.random.fold_in(part_keys[2], 1), 0, OFFMAX).astype(jnp.int32),
        "guide_weight": normal_values(splits[3], (C, LAYERS * 3 * GROUPS), C ** -0.5, 0.75),
    }


SHARPNESS = 2.0

def reference(features, valid_cols, offsets, guide_weight):
    channels = features.shape[2]
    line_width = features.shape[3]
    corr_scale = 1.0 / math.sqrt(channels)
    sec_view = features[1] * valid_cols[1].astype(jnp.bfloat16)[None, None, :]
    padded_sec = jnp.pad(sec_view.astype(jnp.float32), ((0, 0), (0, 0), (RIM, 0)))
    mask_ref = valid_cols[0].astype(jnp.float32)
    disp_values = jnp.arange(DISP).astype(jnp.float32)

    def one_line(packed):
        ref_row, sec_row, line_offset = packed
        ref_float = ref_row.astype(jnp.float32)

        def per_disp(shift_value):
            start_col = (RIM - shift_value - line_offset).astype(jnp.int32)
            window = lax.dynamic_slice_in_dim(sec_row, start_col, line_width, 1)
            return (lax.optimization_barrier(jnp.sum(ref_float * window, axis=0)) * corr_scale * mask_ref).astype(jnp.bfloat16)
        cost = lax.map(per_disp, jnp.arange(DISP).astype(jnp.int32))
        gate_maps = (0.1 + 0.9 * jax.nn.sigmoid(jnp.dot(guide_weight.T, ref_row, preferred_element_type=jnp.float32))).astype(jnp.bfloat16)
        weights = gate_maps.astype(jnp.float32).reshape(LAYERS, 3, GROUPS, 1, line_width)
        volume = cost.astype(jnp.float32).reshape(GROUPS, DGROUP, line_width)
        for layer_index in range(LAYERS):
            dilation = 3 ** layer_index
            padded = jnp.pad(volume, ((0, 0), (0, 0), (dilation, dilation)))
            left_part = padded[:, :, :line_width]
            right_part = padded[:, :, 2 * dilation:]
            first = weights[layer_index, 0]
            middle = weights[layer_index, 1]
            last = weights[layer_index, 2]
            volume = (first * left_part + middle * volume + last * right_part) / (first + middle + last)
        logits = SHARPNESS * volume.reshape(DISP, line_width)
        prob = jax.nn.softmax(logits, axis=0)
        return lax.optimization_barrier(jnp.sum(prob * disp_values[:, None], axis=0)) / DISP + line_offset.astype(jnp.float32) / DISP
    disparity = lax.map(one_line, (features[0], padded_sec, offsets))
    return disparity.reshape(N_LINES, LINE_ROWS, line_width)
```

```python
import functools
import math

import jax
import jax.numpy as jnp
from jax import lax
from jax.experimental import pallas as pl
from jax.experimental.pallas import tpu as pltpu
from jax.sharding import PartitionSpec as P

DISP = 192
DGROUP = 16
GROUPS = DISP // DGROUP
LAYERS = 3
SHARPNESS = 2.0
HALO = 32
CUT = 16
STEP = 3
LANES = 128
LINES = 8
CHANNELS = 64
BLOCK = 256
SPAN = BLOCK + HALO
USED = SPAN // STEP
KEYS = 112
PACK = LANES // HALO
OUT = BLOCK + LANES

BF = jnp.bfloat16
F32 = jnp.float32


def iota(shape, dim):
    return lax.broadcasted_iota(jnp.int32, shape, dim)


def dot_t(a, b, precision=None):
    return lax.dot_general(
        a, b, (((1,), (1,)), ((), ())), preferred_element_type=F32, precision=precision
    )


def column_of(n_shape, lane_dim):
    lane = iota(n_shape, lane_dim)
    return SPAN - 1 - STEP * (lane & (LANES - 1)) - (lane >> 7), (lane & (LANES - 1)) < USED


def kernel(
    scal, kept, swapped, sec_a, sec_b, halo_a, halo_b, mask_own, mask_left, guide, out, vol, gate, ref_rows
):
    first_view = scal[0] == 0
    first_block = scal[1] == 0

    def pick(a, b):
        return jnp.where(first_view, a, b)

    for line in range(LINES):
        lo = line * CHANNELS
        ref_rows[lo : lo + CHANNELS, LANES:] = pick(kept[line], swapped[line])
        packed = pick(halo_a[line // PACK], halo_b[line // PACK]).astype(F32)
        turn = (LANES - HALO) - HALO * (line % PACK)
        if turn:
            packed = pltpu.roll(packed, turn, 1)
        ref_rows[lo : lo + CHANNELS, :LANES] = packed.astype(BF)

    wide = STEP * LANES
    col, real = column_of((wide, wide), 0)
    place = iota((wide, wide), 1)
    perm = jnp.where(real & (place == col + (LANES - HALO)), 1.0, 0.0).astype(BF)
    ref_mask = jnp.concatenate([mask_left[0:1, BLOCK - LANES :], mask_own[0:1, :]], axis=1).astype(F32)
    ref_mask = ref_mask * (1.0 / math.sqrt(CHANNELS))
    mask_cols = dot_t(perm, jnp.broadcast_to(ref_mask, (BLOCK, wide)).astype(BF))
    sec_mask = jnp.concatenate([mask_left[1:2, :], mask_own[1:2, :]], axis=1).astype(F32)

    eye = jnp.where(iota((KEYS, KEYS), 0) == iota((KEYS, KEYS), 1), 1.0, 0.0).astype(BF)
    keys = LAYERS * 3 * GROUPS
    guide_t = dot_t(eye[:, :keys], guide[...]).astype(BF)
    zero_guide = jnp.zeros((KEYS, CHANNELS), BF)

    disp_row = iota((DISP, 2 * LANES), 0)
    flip = jnp.where(iota((DISP, 2 * LANES), 1) == 2 * LANES - 1 - disp_row, 1.0, 0.0).astype(BF)

    lane = iota((8, LANES), 1)
    skewed = lane - STEP * iota((8, LANES), 0)

    for quad in range(LINES // 4):
        rows = ref_rows[quad * 4 * CHANNELS : (quad + 1) * 4 * CHANNELS, :]
        ref_t = dot_t(perm, rows)
        guides = jnp.concatenate(
            [
                jnp.concatenate([guide_t if a == b else zero_guide for a in range(4)], axis=1)
                for b in range(4)
            ],
            axis=0,
        )
        logits = dot_t(guides, ref_t.astype(BF))
        ref_t = (ref_t * mask_cols).astype(BF)
        for q in range(4):
            line = quad * 4 + q
            for t in range(STEP):
                gate[t, pl.ds(line, KEYS, stride=8), :] = logits[
                    q * KEYS : (q + 1) * KEYS, t * LANES : (t + 1) * LANES
                ]
            off = scal[2 + line]
            left = pick(sec_b[line], sec_a[line]).astype(F32) * sec_mask[:, :BLOCK]
            own = pick(swapped[line], kept[line]).astype(F32) * sec_mask[:, BLOCK:]
            tiles = [left[:, :LANES], left[:, LANES:], own[:, :LANES], own[:, LANES:]]
            tiles = [pltpu.roll(tile, off, 1) for tile in tiles]
            ch_lane = iota((CHANNELS, LANES), 1)
            shifted = [
                jnp.where(ch_lane < off, tiles[max(i - 1, 0)], tiles[i]).astype(BF) for i in range(4)
            ]
            shifted = jnp.concatenate(shifted, axis=1)
            lhs = ref_t[:, q * CHANNELS : (q + 1) * CHANNELS]
            blocks = []
            for t in range(STEP):
                products = jnp.dot(
                    lhs[t * LANES : t * LANES + USED], shifted, preferred_element_type=F32
                )
                parts = []
                for j in range(USED // 8):
                    base = 8 * STEP * j + t
                    rolled = {}

                    def turned(i):
                        if i not in rolled:
                            tile = products[8 * j : 8 * j + 8, i * LANES : (i + 1) * LANES]
                            turn = base % LANES
                            if turn + 7 * STEP >= LANES:
                                tile = pltpu.roll(tile, turn, 1)
                                turn = 0
                            rolled[i] = pltpu.roll(tile, turn, 1, stride=STEP, stride_axis=0)
                        return rolled[i]

                    pair = []
                    for v in (2, 3):
                        lowest = max(v + (-7 * STEP - base) // LANES, 0)
                        highest = v + (LANES - 1 - base) // LANES
                        value = turned(lowest)
                        for i in range(lowest + 1, highest + 1):
                            value = jnp.where(skewed >= base + LANES * (i - v), turned(i), value)
                        pair.append(value)
                    parts.append(jnp.concatenate(pair, axis=1))
                parts.append(jnp.zeros((LANES - USED, 2 * LANES), F32))
                blocks.append(jnp.concatenate(parts, axis=0).astype(BF))
            costs = dot_t(flip, jnp.concatenate(blocks, axis=0))
            for t in range(STEP):
                vol[t, pl.ds(line, DISP, stride=8), :] = costs[:, t * LANES : (t + 1) * LANES]

    inside = []
    for t in range(STEP):
        col_t = SPAN - 1 - t - STEP * lane
        keep = (lane < USED) & ((col_t >= HALO) | jnp.logical_not(first_block))
        inside.append(jnp.where(keep, 1.0, 0.0))

    def aggregate(group, largest):
        weights = []
        for layer in range(LAYERS):
            per_tile = []
            for t in range(STEP):
                taps = []
                for tap in range(3):
                    at = pl.multiple_of(((3 * layer + tap) * GROUPS + group) * 8, 8)
                    z = gate[t, pl.ds(at, 8), :]
                    taps.append((0.55 + 0.45 * jnp.tanh(0.5 * z)).astype(BF).astype(F32))
                scale = inside[t] / (taps[0] + taps[1] + taps[2])
                per_tile.append([tap * scale for tap in taps])
            weights.append(per_tile)
        largest = list(largest)
        for d in range(DGROUP):
            at = pl.multiple_of((group * DGROUP + d) * 8, 8)
            v = [vol[t, pl.ds(at, 8), :] for t in range(STEP)]
            before = [v[1], v[2], pltpu.roll(v[0], LANES - 1, 1)]
            after = [pltpu.roll(v[2], 1, 1), v[0], v[1]]
            for layer in range(LAYERS):
                if layer:
                    turn = 3 ** (layer - 1)
                    before = [pltpu.roll(a, LANES - turn, 1) for a in v]
                    after = [pltpu.roll(a, turn, 1) for a in v]
                w = weights[layer]
                v = [
                    w[t][0] * before[t] + w[t][1] * v[t] + w[t][2] * after[t] for t in range(STEP)
                ]
            for t in range(STEP):
                vol[t, pl.ds(at, 8), :] = v[t]
                largest[t] = jnp.maximum(largest[t], v[t])
        return tuple(largest)

    lowest = jnp.full((8, LANES), -jnp.inf, F32)
    largest = lax.fori_loop(0, GROUPS, aggregate, (lowest,) * STEP)

    def accumulate(group, state):
        totals, moments = list(state[:STEP]), list(state[STEP:])
        base = (group * DGROUP).astype(F32)
        for t in range(STEP):
            part = jnp.zeros((8, LANES), F32)
            first = jnp.zeros((8, LANES), F32)
            for d in range(DGROUP):
                at = pl.multiple_of((group * DGROUP + d) * 8, 8)
                e = jnp.exp(SHARPNESS * (vol[t, pl.ds(at, 8), :] - largest[t]))
                part = part + e
                if d:
                    first = first + e * float(d)
            totals[t] = totals[t] + part
            moments[t] = moments[t] + (first + base * part)
        return tuple(totals + moments)

    zero = jnp.zeros((8, LANES), F32)
    state = lax.fori_loop(0, GROUPS, accumulate, (zero,) * (2 * STEP))
    offs = zero
    for line in range(LINES):
        offs = jnp.where(iota((8, LANES), 0) == line, scal[2 + line].astype(F32), offs)
    flat = jnp.concatenate(
        [(state[STEP + t] / state[t] + offs) * (1.0 / DISP) for t in range(STEP)], axis=1
    )
    col, real = column_of((wide, OUT), 0)
    place = iota((wide, OUT), 1)
    want = jnp.where(
        place < BLOCK - CUT,
        place + HALO,
        jnp.where(place < BLOCK, place - (BLOCK - CUT) + CUT, place + (SPAN - CUT - BLOCK)),
    )
    spread = jnp.where(real & (want == col), 1.0, 0.0)
    out[...] = jnp.dot(flat, spread, preferred_element_type=F32, precision=lax.Precision.HIGHEST)


def disparities(scal, *arrays):
    specs = [pl.BlockSpec(memory_space=pltpu.SMEM)] + [pl.BlockSpec(memory_space=pltpu.VMEM)] * 9
    return pl.pallas_call(
        kernel,
        out_shape=jax.ShapeDtypeStruct((LINES, OUT), F32),
        in_specs=specs,
        out_specs=pl.BlockSpec(memory_space=pltpu.VMEM),
        scratch_shapes=[
            pltpu.VMEM((STEP, DISP * 8, LANES), F32),
            pltpu.VMEM((STEP, KEYS * 8, LANES), F32),
            pltpu.VMEM((LINES * CHANNELS, STEP * LANES), BF),
        ],
        compiler_params=pltpu.CompilerParams(vmem_limit_bytes=32 * 1024 * 1024),
        cost_estimate=pl.CostEstimate(flops=4_000_000_000, bytes_accessed=2_000_000, transcendentals=1_000_000),
    )(scal, *arrays)


def pack_halo(block):
    tail = block[:, :, BLOCK - HALO :].reshape(LINES // PACK, PACK, CHANNELS, HALO)
    return jnp.concatenate([tail[:, p] for p in range(PACK)], axis=2)


def on_device(features, valid_cols, offsets, guide_weight):
    own = features[0]
    n = lax.axis_size("cols")
    view = lax.axis_index("view")
    block = lax.axis_index("cols")
    both = ("cols", "view")

    def send(x, moves):
        return lax.ppermute(x, both, [(2 * a + b, 2 * c + d) for a, b, c, d in moves])

    kept = lax.dynamic_slice_in_dim(own, view * LINES, LINES, 0)
    given = lax.dynamic_slice_in_dim(own, (1 - view) * LINES, LINES, 0)
    steps = range(n - 1)
    sec_a = send(kept, [(c, 1, c + 1, 1) for c in steps])
    sec_b = send(given, [(c, 1, c + 1, 0) for c in steps])
    swapped = send(given, [(c, v, c, 1 - v) for c in range(n) for v in range(2)])
    halo_a = send(pack_halo(kept), [(c, 0, c + 1, 0) for c in steps])
    halo_b = send(pack_halo(given), [(c, 0, c + 1, 1) for c in steps])
    mask_left = send(valid_cols, [(c, v, c + 1, v) for c in steps for v in range(2)])
    my_offsets = lax.dynamic_slice_in_dim(offsets, view * LINES, LINES, 0)
    scal = jnp.concatenate([jnp.stack([view, block]).astype(jnp.int32), my_offsets])
    result = disparities(
        scal, kept, swapped, sec_a, sec_b, halo_a, halo_b, valid_cols, mask_left, guide_weight
    )

    sub = own.shape[0] // n
    pieces = []
    for k in range(n):
        target = lax.rem(block + k, n) // 2
        piece = lax.dynamic_slice_in_dim(result, target * sub, sub, 0)
        moves = []
        for c in range(n):
            for v in range(2):
                a, b = divmod((c + k) % n, 2)
                moves.append((c, v, n // 2 * v + a, b))
        pieces.append(send(piece, moves))
    mine = 2 * lax.rem(block, n // 2) + view
    ring = jnp.stack(pieces[::-1])
    ring = jnp.concatenate([ring, ring], axis=0)
    ordered = lax.dynamic_slice_in_dim(ring, lax.rem(2 * n - 1 - mine, n), n, 0)
    main = ordered[:, :, :BLOCK]
    tail = ordered[n - 1 :, :, BLOCK:]
    tail = jnp.concatenate([tail[:, :, CUT:], tail[:, :, :CUT]], axis=2)
    tail = jnp.concatenate([jnp.zeros_like(tail), tail], axis=2)
    following = jnp.concatenate([main[1:], tail], axis=0)
    columns = jnp.arange(BLOCK)
    joined = jnp.where(columns[None, None, :] < BLOCK - CUT, main, following)
    return jnp.transpose(joined, (1, 0, 2)).reshape(1, sub, n * BLOCK)


def solution(mesh):
    return jax.shard_map(
        on_device,
        mesh=mesh,
        in_specs=(
            P("view", ("tiles", "lines"), None, "cols"),
            P(None, ("tiles", "cols")),
            P(("tiles", "lines")),
            P(),
        ),
        out_specs=P(("tiles", "lines"), "cols", None),
        check_vma=False,
    )
```

```python
import math

import jax
import jax.numpy as jnp
from jax import lax
from jax.experimental import pallas as pl
from jax.experimental.pallas import tpu as pltpu
from jax.sharding import PartitionSpec as P

DISP = 192
DGROUP = 16
GROUPS = DISP // DGROUP
LAYERS = 3
SHARPNESS = 2.0
HALO = 32
LANES = 128
LINES = 8
CHANNELS = 64
BLOCK = 256
SPAN = BLOCK + HALO
PARTS = LANES // LINES
RUN = SPAN // PARTS
KEYS = 40
WIDE = BLOCK + LANES
SEC_ROWS = LINES * CHANNELS
PAYLOAD = SEC_ROWS + CHANNELS + 16
PACK = LANES // HALO
CUT = 16

BF = jnp.bfloat16
F32 = jnp.float32


def iota(shape, dim):
    return lax.broadcasted_iota(jnp.int32, shape, dim)


def dot_t(a, b):
    return lax.dot_general(a, b, (((1,), (1,)), ((), ())), preferred_element_type=F32)


def payload_kernel(own, other, valid, out):
    view = lax.axis_index("view")
    first_view = view == 0
    sec_mask = valid[1:2, :].astype(F32).astype(BF)
    lane = iota((CHANNELS, LANES), 1)
    tails = []
    for line in range(LINES):
        at = view * LINES + line
        mine, theirs = own[at], other[at]
        out[line * CHANNELS : (line + 1) * CHANNELS, :] = jnp.where(first_view, theirs, mine) * sec_mask
        tail = jnp.where(first_view, mine[:, BLOCK - LANES :], theirs[:, BLOCK - LANES :]).astype(F32)
        slot = line % PACK
        turn = (HALO * (slot + 1)) % LANES
        if turn:
            tail = pltpu.roll(tail, turn, 1)
        if slot:
            tail = jnp.where(lane >= HALO * slot, tail, tails[-1])
            tails[-1] = tail
        else:
            tails.append(tail)
    for i, tail in enumerate(tails):
        out[SEC_ROWS : SEC_ROWS + CHANNELS, i * LANES : (i + 1) * LANES] = tail.astype(BF)
    ref_mask = jnp.broadcast_to(valid[0:1, :].astype(F32), (16, BLOCK))
    out[SEC_ROWS + CHANNELS :, :] = ref_mask.astype(BF)


def payload(own, other, valid):
    return pl.pallas_call(
        payload_kernel,
        out_shape=jax.ShapeDtypeStruct((PAYLOAD, BLOCK), BF),
        in_specs=[pl.BlockSpec(memory_space=pltpu.VMEM)] * 3,
        out_specs=pl.BlockSpec(memory_space=pltpu.VMEM),
        compiler_params=pltpu.CompilerParams(vmem_limit_bytes=16 * 1024 * 1024),
    )(own, other, valid)


def main_kernel(
    offsets, own, other, mine, left, valid, guide, out,
    ref_rows, ref_cols, skew, cost_rows, gate_rows, vol, wts, vals, turned
):
    view = lax.axis_index("view")
    first_view = view == 0
    low = jnp.where(lax.axis_index("cols") == 0, HALO, 0)
    base = view * LINES

    for line in range(LINES):
        lo = line * CHANNELS
        ref_rows[lo : lo + CHANNELS, LANES:] = jnp.where(first_view, own[base + line], other[base + line])
        half = line // PACK
        packed = left[SEC_ROWS : SEC_ROWS + CHANNELS, half * LANES : (half + 1) * LANES].astype(F32)
        turn = (LANES - HALO) - HALO * (line % PACK)
        if turn:
            packed = pltpu.roll(packed, turn, 1)
        ref_rows[lo : lo + CHANNELS, :LANES] = packed.astype(BF)

    perm = jnp.where(iota((SPAN, WIDE), 1) == WIDE - 1 - iota((SPAN, WIDE), 0), 1.0, 0.0).astype(BF)
    mask_left = left[SEC_ROWS + CHANNELS : SEC_ROWS + CHANNELS + 1, BLOCK - LANES :].astype(F32)
    ref_mask = jnp.concatenate([mask_left, valid[0:1, :].astype(F32)], axis=1)
    ref_mask = jnp.broadcast_to(ref_mask * (1.0 / math.sqrt(CHANNELS)), (LANES, WIDE))
    mask_cols = dot_t(perm, ref_mask.astype(BF))

    keys = LAYERS * 3 * GROUPS
    row = iota((3 * KEYS, keys), 0)
    tap = jnp.where(row >= KEYS, 1, 0) + jnp.where(row >= 2 * KEYS, 1, 0)
    row = row - KEYS * tap
    layer = jnp.where(row >= GROUPS, 1, 0) + jnp.where(row >= 2 * GROUPS, 1, 0)
    key = 2 * GROUPS * layer + GROUPS * tap + row
    chosen = jnp.where((iota((3 * KEYS, keys), 1) == key) & (row < 3 * GROUPS), 1.0, 0.0).astype(BF)
    guide_t = dot_t(chosen, guide[...]).astype(BF)
    guide_t = jnp.concatenate([guide_t, guide_t], axis=1)

    flip = 2 * LANES - 1 - iota((DISP, 2 * LANES), 0)
    flip = jnp.where(iota((DISP, 2 * LANES), 1) == flip, 1.0, 0.0).astype(BF)

    ch_lane = iota((CHANNELS, LANES), 1)
    diagonal = iota((8, LANES), 1) - iota((8, LANES), 0)
    half_lane = iota((PARTS, LANES), 1) < CHANNELS
    span_lane = iota((SPAN, LANES), 1) < CHANNELS

    def shifted(line):
        off = offsets[base + line]
        lo = line * CHANNELS
        tiles = [
            src[lo : lo + CHANNELS, i * LANES : (i + 1) * LANES].astype(F32)
            for src in (left, mine)
            for i in range(2)
        ]
        tiles = [pltpu.roll(tile, off, 1) for tile in tiles]
        tiles = [jnp.where(ch_lane < off, tiles[max(i - 1, 0)], tiles[i]).astype(BF) for i in range(4)]
        return jnp.concatenate(tiles, axis=1)

    for quad in range(LINES // 4):
        ref_t = dot_t(perm, ref_rows[quad * 4 * CHANNELS : (quad + 1) * 4 * CHANNELS, :])
        for pair in range(2):
            cols = ref_t[:, pair * LANES : (pair + 1) * LANES]
            slot = quad * 2 + pair
            ref_cols[slot] = cols
            masked = cols * mask_cols
            rhs = jnp.concatenate([shifted(2 * slot), shifted(2 * slot + 1)], axis=0)
            for side in range(2):
                line = 2 * slot + side
                for t in range(RUN):
                    picked = ref_cols[slot, pl.ds(t, PARTS, stride=RUN), :]
                    picked = jnp.where(half_lane if side == 0 else ~half_lane, picked, 0.0)
                    at = t * LANES + line * PARTS
                    gate_rows[at : at + PARTS, :] = picked.astype(BF)
                lhs = jnp.where(span_lane if side == 0 else ~span_lane, masked, 0.0).astype(BF)
                for chunk in range(3):
                    rows = min(LANES, SPAN - chunk * LANES)
                    first = max(1 - chunk, 0)
                    last = 3 - chunk
                    products = jnp.dot(
                        lhs[chunk * LANES : chunk * LANES + rows],
                        rhs[:, first * LANES : (last + 1) * LANES],
                        preferred_element_type=F32,
                    )
                    for j in range(rows // 8):
                        tiles = [
                            pltpu.roll(
                                products[8 * j : 8 * j + 8, i * LANES : (i + 1) * LANES],
                                8 * j, 1, stride=1, stride_axis=0,
                            )
                            for i in range(last + 1 - first)
                        ]
                        if len(tiles) < 3:
                            tiles = [tiles[0]] + tiles
                        beyond = diagonal >= 8 * j
                        at = chunk * LANES + 8 * j
                        skew[line, 0, at : at + 8, :] = jnp.where(beyond, tiles[1], tiles[0])
                        skew[line, 1, at : at + 8, :] = jnp.where(beyond, tiles[2], tiles[1])
                for t in range(RUN):
                    at = t * LANES + line * PARTS
                    for v in range(2):
                        cost_rows[at : at + PARTS, v * LANES : (v + 1) * LANES] = skew[
                            line, v, pl.ds(t, PARTS, stride=RUN), :
                        ].astype(BF)

    place = iota((KEYS, LANES), 1)
    x_base = SPAN - 1 - RUN * (place & (PARTS - 1))
    row = iota((KEYS, LANES), 0)
    reach = jnp.where(row >= 2 * GROUPS, 9, jnp.where(row >= GROUPS, 3, 1))
    room_left = x_base - reach - low
    room_right = x_base + reach - SPAN

    for two in range(RUN // 2):
        at = 2 * two * LANES
        costs = dot_t(flip, cost_rows[at : at + 2 * LANES, :])
        logits = dot_t(guide_t, gate_rows[at : at + 2 * LANES, :])
        for i in range(2):
            t = 2 * two + i
            vol[t] = costs[:, i * LANES : (i + 1) * LANES]
            z = logits[:, i * LANES : (i + 1) * LANES]
            z = (0.55 + 0.45 * jnp.tanh(0.5 * z)).astype(BF).astype(F32)
            taps = [z[k * KEYS : (k + 1) * KEYS] for k in range(3)]
            scale = 1.0 / (taps[0] + taps[1] + taps[2])
            wts[t, 0:KEYS, :] = jnp.where(room_left >= t, taps[0] * scale, 0.0)
            wts[t, KEYS : 2 * KEYS, :] = taps[1] * scale
            wts[t, 2 * KEYS : 3 * KEYS, :] = jnp.where(room_right < t, taps[2] * scale, 0.0)

    def aggregate(group, carry):
        for half in range(2):
            at = pl.multiple_of(group * DGROUP + half * 8, 8)
            v = [vol[t, pl.ds(at, 8), :] for t in range(RUN)]
            for layer in range(LAYERS):
                s = 3**layer
                before = [v[t + s] if t + s < RUN else pltpu.roll(v[t + s - RUN], LANES - 1, 1) for t in range(RUN)]
                after = [v[t - s] if t >= s else pltpu.roll(v[t - s + RUN], 1, 1) for t in range(RUN)]
                fresh = []
                for t in range(RUN):
                    w = [wts[t, pl.ds(k * KEYS + layer * GROUPS + group, 1), :] for k in range(3)]
                    fresh.append(w[0] * before[t] + w[1] * v[t] + w[2] * after[t])
                v = fresh
            for t in range(RUN):
                vol[t, pl.ds(at, 8), :] = v[t]
        return carry

    lax.fori_loop(0, GROUPS, aggregate, 0)

    vals[...] = jnp.zeros((LANES, LANES), F32)
    sub = iota((8, LANES), 0).astype(F32)
    line_of = iota((1, LANES), 1) >> 4
    offs = jnp.zeros((1, LANES), F32)
    for line in range(LINES):
        offs = jnp.where(line_of == line, offsets[base + line].astype(F32), offs)

    def softmax(t, carry):
        v = [vol[t, 8 * i : 8 * i + 8, :] for i in range(DISP // 8)]
        top = v
        while len(top) > 1:
            top = [jnp.maximum(a, b) for a, b in zip(top[::2], top[1::2])] + top[len(top) & ~1 :]
        top = jnp.max(top[0], axis=0, keepdims=True)
        e = [jnp.exp(SHARPNESS * (a - top)) for a in v]
        total = e[0]
        moment = jnp.zeros((8, LANES), F32)
        for i in range(1, DISP // 8):
            total = total + e[i]
            moment = moment + float(8 * i) * e[i]
        moment = jnp.sum(moment + sub * total, axis=0, keepdims=True)
        total = jnp.sum(total, axis=0, keepdims=True)
        vals[pl.ds(RUN - 1 - t, 1), :] = (moment / total + offs) * (1.0 / DISP)
        return carry

    lax.fori_loop(0, RUN, softmax, 0)

    turned[...] = jnp.transpose(vals[...])
    lane = iota((8, LANES), 1)
    result = [jnp.zeros((8, LANES), F32) for _ in range(WIDE // LANES)]
    for part in range(PARTS):
        piece = turned[pl.ds(part, LINES, stride=PARTS), :]
        start = (RUN * (PARTS - 1 - part) - HALO) % WIDE
        tile, turn = divmod(start, LANES)
        if turn:
            piece = pltpu.roll(piece, turn, 1)
        if turn + RUN > LANES:
            after = (tile + 1) % len(result)
            result[after] = result[after] + jnp.where(lane < turn, piece, 0.0)
            piece = jnp.where(lane >= turn, piece, 0.0)
        result[tile] = result[tile] + piece
    for i in range(out.shape[0]):
        for tile, value in enumerate(result):
            out[i, :, tile * LANES : (tile + 1) * LANES] = value


def disparities(copies, offsets, *arrays):
    specs = [pl.BlockSpec(memory_space=pltpu.SMEM)] + [pl.BlockSpec(memory_space=pltpu.VMEM)] * 6
    return pl.pallas_call(
        main_kernel,
        out_shape=jax.ShapeDtypeStruct((copies, LINES, WIDE), F32),
        in_specs=specs,
        out_specs=pl.BlockSpec(memory_space=pltpu.VMEM),
        scratch_shapes=[
            pltpu.VMEM((SEC_ROWS, WIDE), BF),
            pltpu.VMEM((LINES // 2, SPAN, LANES), F32),
            pltpu.VMEM((LINES, 2, SPAN, LANES), F32),
            pltpu.VMEM((RUN * LANES, 2 * LANES), BF),
            pltpu.VMEM((RUN * LANES, LANES), BF),
            pltpu.VMEM((RUN, DISP, LANES), F32),
            pltpu.VMEM((RUN, 3 * KEYS, LANES), F32),
            pltpu.VMEM((LANES, LANES), F32),
            pltpu.VMEM((LANES, LANES), F32),
        ],
        compiler_params=pltpu.CompilerParams(vmem_limit_bytes=40 * 1024 * 1024),
    )(offsets, *arrays)


def join_kernel(pieces, out):
    n = out.shape[2] // BLOCK
    sub = out.shape[1]
    block = lax.axis_index("cols")
    view = block // (n // 2)
    at = (block % (n // 2)) * sub
    keep = iota((sub, LANES), 1) < LANES - CUT

    def rows(b, lo):
        whole = pieces[2 * b + view, :, lo : lo + LANES]
        picked = whole[:sub]
        for start in range(sub, LINES, sub):
            picked = jnp.where(at == start, whole[start : start + sub], picked)
        return picked

    for b in range(n):
        lo = b * BLOCK
        out[0, :, lo : lo + LANES] = rows(b, 0)
        second = rows(b, LANES)
        if b + 1 < n:
            second = jnp.where(keep, second, rows(b + 1, BLOCK))
        out[0, :, lo + LANES : lo + BLOCK] = second


def join(pieces, sub, n):
    return pl.pallas_call(
        join_kernel,
        out_shape=jax.ShapeDtypeStruct((1, sub, n * BLOCK), F32),
        in_specs=[pl.BlockSpec(memory_space=pltpu.VMEM)],
        out_specs=pl.BlockSpec(memory_space=pltpu.VMEM),
    )(pieces)


def on_device(features, valid_cols, offsets, guide_weight):
    own = features[0]
    n = lax.axis_size("cols")
    other = lax.ppermute(own, "view", [(0, 1), (1, 0)])
    mine = payload(own, other, valid_cols)
    left = lax.ppermute(mine, "cols", [(c, c + 1) for c in range(n - 1)])
    result = disparities(2 * n, offsets, own, other, mine, left, valid_cols, guide_weight)
    pieces = lax.all_to_all(result, ("cols", "view"), split_axis=0, concat_axis=0, tiled=True)
    return join(pieces, own.shape[0] // n, n)


def solution(mesh):
    return jax.shard_map(
        on_device,
        mesh=mesh,
        in_specs=(
            P("view", ("tiles", "lines"), None, "cols"),
            P(None, ("tiles", "cols")),
            P(("tiles", "lines")),
            P(),
        ),
        out_specs=P(("tiles", "lines"), "cols", None),
        check_vma=False,
    )
```

```python
import math

import jax
import jax.numpy as jnp
from jax import lax
from jax.experimental import pallas as pl
from jax.experimental.pallas import tpu as pltpu
from jax.sharding import PartitionSpec as P

DISP = 192
DGROUP = 16
GROUPS = DISP // DGROUP
LAYERS = 3
SHARPNESS = 2.0
HALO = 32
LANES = 128
LINES = 8
CHANNELS = 64
BLOCK = 256
SPAN = BLOCK + HALO
PARTS = LANES // LINES
RUN = SPAN // PARTS
KEYS = 40
WIDE = BLOCK + LANES
SEC_ROWS = LINES * CHANNELS
QUAD_ROWS = SEC_ROWS // 2
MASK_AT = QUAD_ROWS + CHANNELS
PAYLOAD = MASK_AT + 16
QUAD = LINES // 2
QUAD_LANES = LANES // 2
PACK = LANES // HALO
CUT = 16

BF = jnp.bfloat16
F32 = jnp.float32


def iota(shape, dim):
    return lax.broadcasted_iota(jnp.int32, shape, dim)


def dot_t(a, b):
    return lax.dot_general(a, b, (((1,), (1,)), ((), ())), preferred_element_type=F32)


def call(kernel, outs, scratch, smem, args, flops=0, space=pltpu.VMEM):
    specs = [pl.BlockSpec(memory_space=pltpu.SMEM)] * smem
    specs += [pl.BlockSpec(memory_space=space)] * (len(args) - smem)
    return pl.pallas_call(
        kernel,
        out_shape=[jax.ShapeDtypeStruct(shape, dtype) for shape, dtype in outs],
        in_specs=specs,
        out_specs=[pl.BlockSpec(memory_space=pltpu.VMEM)] * len(outs),
        scratch_shapes=scratch,
        compiler_params=pltpu.CompilerParams(vmem_limit_bytes=24 * 1024 * 1024),
        cost_estimate=pl.CostEstimate(flops=flops, bytes_accessed=1_000_000, transcendentals=0),
    )(*args)


def prefetch_kernel(own, valid, guide, own_out, masks, perm, flip, guide_out, valid_in, guide_in, sems):
    copies = [
        pltpu.make_async_copy(src, dst, sems.at[i])
        for i, (src, dst) in enumerate([(own, own_out), (guide, guide_in), (valid, valid_in)])
    ]
    for copy in copies:
        copy.start()
    perm[...] = jnp.where(
        iota((SPAN, WIDE), 1) == WIDE - 1 - iota((SPAN, WIDE), 0), 1.0, 0.0
    ).astype(BF)
    back = 2 * LANES - 1 - iota((DISP, 2 * LANES), 0)
    flip[...] = jnp.where(iota((DISP, 2 * LANES), 1) == back, 1.0, 0.0).astype(BF)

    keys = LAYERS * 3 * GROUPS
    row = iota((3 * KEYS, keys), 0)
    tap = jnp.where(row >= KEYS, 1, 0) + jnp.where(row >= 2 * KEYS, 1, 0)
    row = row - KEYS * tap
    layer = jnp.where(row >= GROUPS, 1, 0) + jnp.where(row >= 2 * GROUPS, 1, 0)
    key = 2 * GROUPS * layer + GROUPS * tap + row
    chosen = jnp.where((iota((3 * KEYS, keys), 1) == key) & (row < 3 * GROUPS), 1.0, 0.0).astype(BF)
    copies[1].wait()
    guide_t = dot_t(chosen, guide_in[...]).astype(BF)
    guide_out[...] = jnp.concatenate([guide_t, guide_t], axis=1)
    copies[2].wait()
    masks[...] = valid_in[...].astype(F32)
    copies[0].wait()


def payload_kernel(own, other, masks, first, second, ref_own):
    view = lax.axis_index("view")
    first_view = view == 0
    sec_mask = masks[1:2, :].astype(BF)
    lane = iota((CHANNELS, LANES), 1)
    tails = []
    for line in range(LINES):
        at = view * LINES + line
        mine, theirs = own[at], other[at]
        lo = line * CHANNELS
        dest, start = (first, lo) if line < QUAD else (second, lo - QUAD_ROWS)
        dest[start : start + CHANNELS, :] = jnp.where(first_view, theirs, mine) * sec_mask
        ref = jnp.where(first_view, mine, theirs)
        ref_own[lo : lo + CHANNELS, :] = ref
        tail = ref[:, BLOCK - LANES :].astype(F32)
        slot = line % PACK
        turn = (HALO * (slot + 1)) % LANES
        if turn:
            tail = pltpu.roll(tail, turn, 1)
        if slot:
            tails[-1] = jnp.where(lane >= HALO * slot, tail, tails[-1])
        else:
            tails.append(tail)
    for i, tail in enumerate(tails):
        first[QUAD_ROWS:MASK_AT, i * LANES : (i + 1) * LANES] = tail.astype(BF)
    first[MASK_AT:, :] = jnp.broadcast_to(masks[0:1, :], (16, BLOCK)).astype(BF)


def shifted(left, mine, lo, off):
    ch_lane = iota((CHANNELS, LANES), 1)
    tiles = [
        src[lo : lo + CHANNELS, i * LANES : (i + 1) * LANES].astype(F32)
        for src in (left, mine)
        for i in range(2)
    ]
    tiles = [pltpu.roll(tile, off, 1) for tile in tiles]
    tiles = [jnp.where(ch_lane < off, tiles[max(i - 1, 0)], tiles[i]).astype(BF) for i in range(4)]
    return jnp.concatenate(tiles, axis=1)


def line_costs(lhs, rhs, slot, skew, cost_rows):
    diagonal = iota((8, LANES), 1) - iota((8, LANES), 0)
    for chunk in range(3):
        rows = min(LANES, SPAN - chunk * LANES)
        first = max(1 - chunk, 0)
        last = 3 - chunk
        products = jnp.dot(
            lhs[chunk * LANES : chunk * LANES + rows],
            rhs[:, first * LANES : (last + 1) * LANES],
            preferred_element_type=F32,
        )
        for j in range(rows // 8):
            tiles = [
                pltpu.roll(
                    products[8 * j : 8 * j + 8, i * LANES : (i + 1) * LANES],
                    8 * j, 1, stride=1, stride_axis=0,
                )
                for i in range(last + 1 - first)
            ]
            if len(tiles) < 3:
                tiles = [tiles[0]] + tiles
            beyond = diagonal >= 8 * j
            at = chunk * LANES + 8 * j
            skew[slot, 0, at : at + 8, :] = jnp.where(beyond, tiles[1], tiles[0])
            skew[slot, 1, at : at + 8, :] = jnp.where(beyond, tiles[2], tiles[1])
    for t in range(RUN):
        at = t * QUAD_LANES + slot * PARTS
        for v in range(2):
            cost_rows[at : at + PARTS, v * LANES : (v + 1) * LANES] = skew[
                slot, v, pl.ds(t, PARTS, stride=RUN), :
            ].astype(BF)


def early_kernel(
    offsets, ref_own, mine, left, masks, perm, guide, wts, cost_rows, lhs_out,
    ref_rows, ref_cols, gate_rows, skew
):
    base = lax.axis_index("view") * LINES
    low = jnp.where(lax.axis_index("cols") == 0, HALO, 0)
    for line in range(LINES):
        lo = line * CHANNELS
        ref_rows[lo : lo + CHANNELS, LANES:] = ref_own[lo : lo + CHANNELS, :]
        half = line // PACK
        packed = left[QUAD_ROWS:MASK_AT, half * LANES : (half + 1) * LANES].astype(F32)
        turn = (LANES - HALO) - HALO * (line % PACK)
        if turn:
            packed = pltpu.roll(packed, turn, 1)
        ref_rows[lo : lo + CHANNELS, :LANES] = packed.astype(BF)

    mask_left = left[MASK_AT : MASK_AT + 1, BLOCK - LANES :].astype(F32)
    ref_mask = jnp.concatenate([mask_left, masks[0:1, :]], axis=1)
    ref_mask = jnp.broadcast_to(ref_mask * (1.0 / math.sqrt(CHANNELS)), (LANES, WIDE))
    mask_cols = dot_t(perm[...], ref_mask.astype(BF))
    half_lane = iota((PARTS, LANES), 1) < CHANNELS
    span_lane = iota((SPAN, LANES), 1) < CHANNELS

    for quad in range(LINES // QUAD):
        ref_t = dot_t(perm[...], ref_rows[quad * QUAD_ROWS : (quad + 1) * QUAD_ROWS, :])
        for pair in range(QUAD // 2):
            cols = ref_t[:, pair * LANES : (pair + 1) * LANES]
            slot = quad * 2 + pair
            ref_cols[slot] = cols
            masked = cols * mask_cols
            if quad == 0:
                rhs = jnp.concatenate(
                    [
                        shifted(left, mine, line * CHANNELS, offsets[base + line])
                        for line in (2 * slot, 2 * slot + 1)
                    ],
                    axis=0,
                )
            for side in range(2):
                line = 2 * slot + side
                for t in range(RUN):
                    picked = ref_cols[slot, pl.ds(t, PARTS, stride=RUN), :]
                    picked = jnp.where(half_lane if side == 0 else ~half_lane, picked, 0.0)
                    at = t * LANES + line * PARTS
                    gate_rows[at : at + PARTS, :] = picked.astype(BF)
                lhs = jnp.where(span_lane if side == 0 else ~span_lane, masked, 0.0).astype(BF)
                if quad == 0:
                    line_costs(lhs, rhs, line, skew, cost_rows)
                else:
                    lhs_out[line - QUAD] = lhs

    place = iota((KEYS, LANES), 1)
    x_base = SPAN - 1 - RUN * (place & (PARTS - 1))
    row = iota((KEYS, LANES), 0)
    reach = jnp.where(row >= 2 * GROUPS, 9, jnp.where(row >= GROUPS, 3, 1))
    room_left = x_base - reach - low
    room_right = x_base + reach - SPAN
    for two in range(RUN // 2):
        at = 2 * two * LANES
        logits = dot_t(guide[...], gate_rows[at : at + 2 * LANES, :])
        for i in range(2):
            t = 2 * two + i
            z = logits[:, i * LANES : (i + 1) * LANES]
            z = (0.55 + 0.45 * jnp.tanh(0.5 * z)).astype(BF).astype(F32)
            taps = [z[k * KEYS : (k + 1) * KEYS] for k in range(3)]
            scale = 1.0 / (taps[0] + taps[1] + taps[2])
            wts[t, 0:KEYS, :] = jnp.where(room_left >= t, taps[0] * scale, 0.0)
            wts[t, KEYS : 2 * KEYS, :] = taps[1] * scale
            wts[t, 2 * KEYS : 3 * KEYS, :] = jnp.where(room_right < t, taps[2] * scale, 0.0)


def late_kernel(
    offsets, mine, left, lhs, early_rows, wts, flip, out, skew, cost_rows, vol, vals, turned
):
    base = lax.axis_index("view") * LINES
    for pair in range(QUAD // 2):
        rhs = jnp.concatenate(
            [
                shifted(left, mine, line * CHANNELS, offsets[base + QUAD + line])
                for line in (2 * pair, 2 * pair + 1)
            ],
            axis=0,
        )
        for line in (2 * pair, 2 * pair + 1):
            line_costs(lhs[line], rhs, line, skew, cost_rows)

    for two in range(RUN // 2):
        rows = []
        for t in (2 * two, 2 * two + 1):
            for part in (early_rows, cost_rows):
                rows.append(part[t * QUAD_LANES : (t + 1) * QUAD_LANES, :])
        costs = dot_t(flip[...], jnp.concatenate(rows, axis=0))
        vol[2 * two] = costs[:, :LANES]
        vol[2 * two + 1] = costs[:, LANES:]

    def aggregate(group, carry):
        for half in range(2):
            at = pl.multiple_of(group * DGROUP + half * 8, 8)
            v = [vol[t, pl.ds(at, 8), :] for t in range(RUN)]
            for layer in range(LAYERS):
                s = 3**layer
                before = [v[t + s] if t + s < RUN else pltpu.roll(v[t + s - RUN], LANES - 1, 1) for t in range(RUN)]
                after = [v[t - s] if t >= s else pltpu.roll(v[t - s + RUN], 1, 1) for t in range(RUN)]
                fresh = []
                for t in range(RUN):
                    w = [wts[t, pl.ds(k * KEYS + layer * GROUPS + group, 1), :] for k in range(3)]
                    fresh.append(w[0] * before[t] + w[1] * v[t] + w[2] * after[t])
                v = fresh
            for t in range(RUN):
                vol[t, pl.ds(at, 8), :] = v[t]
        return carry

    lax.fori_loop(0, GROUPS, aggregate, 0)

    vals[...] = jnp.zeros((LANES, LANES), F32)
    sub = iota((8, LANES), 0).astype(F32)
    line_of = iota((1, LANES), 1) >> 4
    offs = jnp.zeros((1, LANES), F32)
    for line in range(LINES):
        offs = jnp.where(line_of == line, offsets[base + line].astype(F32), offs)

    def softmax(t, carry):
        v = [vol[t, 8 * i : 8 * i + 8, :] for i in range(DISP // 8)]
        top = v
        while len(top) > 1:
            top = [jnp.maximum(a, b) for a, b in zip(top[::2], top[1::2])] + top[len(top) & ~1 :]
        top = jnp.max(top[0], axis=0, keepdims=True)
        e = [jnp.exp(SHARPNESS * (a - top)) for a in v]
        total = e[0]
        moment = jnp.zeros((8, LANES), F32)
        for i in range(1, DISP // 8):
            total = total + e[i]
            moment = moment + float(8 * i) * e[i]
        moment = jnp.sum(moment + sub * total, axis=0, keepdims=True)
        total = jnp.sum(total, axis=0, keepdims=True)
        vals[pl.ds(RUN - 1 - t, 1), :] = (moment / total + offs) * (1.0 / DISP)
        return carry

    lax.fori_loop(0, RUN, softmax, 0)

    turned[...] = jnp.transpose(vals[...])
    lane = iota((8, LANES), 1)
    result = [jnp.zeros((8, LANES), F32) for _ in range(WIDE // LANES)]
    for part in range(PARTS):
        piece = turned[pl.ds(part, LINES, stride=PARTS), :]
        start = (RUN * (PARTS - 1 - part) - HALO) % WIDE
        tile, turn = divmod(start, LANES)
        if turn:
            piece = pltpu.roll(piece, turn, 1)
        if turn + RUN > LANES:
            after = (tile + 1) % len(result)
            result[after] = result[after] + jnp.where(lane < turn, piece, 0.0)
            piece = jnp.where(lane >= turn, piece, 0.0)
        result[tile] = result[tile] + piece
    for tile, value in enumerate(result):
        out[:, tile * LANES : (tile + 1) * LANES] = value


def join(pieces, sub, n):
    block = lax.axis_index("cols")
    pieces = pieces.reshape(n, 2, LINES, WIDE)
    start = (0, block // (n // 2), (block % (n // 2)) * sub, 0)
    pieces = lax.dynamic_slice(pieces, start, (n, 1, sub, WIDE))[:, 0]
    main = pieces[:, :, :BLOCK]
    tail = jnp.pad(pieces[1:, :, BLOCK:], ((0, 1), (0, 0), (LANES, 0)))
    place = (n, sub, BLOCK)
    keep = (iota(place, 2) < BLOCK - CUT) | (iota(place, 0) == n - 1)
    joined = jnp.where(keep, main, tail)
    return jnp.transpose(joined, (1, 0, 2)).reshape(1, sub, n * BLOCK)


def on_device(features, valid_cols, offsets, guide_weight):
    own = features[0]
    n = lax.axis_size("cols")
    right = [(c, c + 1) for c in range(n - 1)]
    other = lax.ppermute(own, "view", [(0, 1), (1, 0)])
    near, masks, perm, flip, guide = call(
        prefetch_kernel,
        [(own.shape, BF), (valid_cols.shape, F32), ((SPAN, WIDE), BF), ((DISP, 2 * LANES), BF), ((3 * KEYS, LANES), BF)],
        [pltpu.VMEM(valid_cols.shape, jnp.int32), pltpu.VMEM(guide_weight.shape, BF), pltpu.SemaphoreType.DMA((3,))],
        0, (own, valid_cols, guide_weight), 100_000_000, pl.ANY,
    )
    first, second, ref_own = call(
        payload_kernel,
        [((PAYLOAD, BLOCK), BF), ((QUAD_ROWS, BLOCK), BF), ((SEC_ROWS, BLOCK), BF)],
        [], 0, (near, other, masks),
    )
    left_first = lax.ppermute(first, "cols", right)
    left_second = lax.ppermute(second, "cols", right)
    quad_rows = (RUN * QUAD_LANES, 2 * LANES)
    skew = pltpu.VMEM((QUAD, 2, SPAN, LANES), F32)
    square = pltpu.VMEM((LANES, LANES), F32)
    wts, early_rows, lhs = call(
        early_kernel,
        [((RUN, 3 * KEYS, LANES), F32), (quad_rows, BF), ((QUAD, SPAN, LANES), BF)],
        [pltpu.VMEM((SEC_ROWS, WIDE), BF), pltpu.VMEM((QUAD, SPAN, LANES), F32), pltpu.VMEM((RUN * LANES, LANES), BF), skew],
        1, (offsets, ref_own, first, left_first, masks, perm, guide), 1_000_000_000,
    )
    (result,) = call(
        late_kernel,
        [((LINES, WIDE), F32)],
        [skew, pltpu.VMEM(quad_rows, BF), pltpu.VMEM((RUN, DISP, LANES), F32), square, square],
        1, (offsets, second, left_second, lhs, early_rows, wts, flip), 1_000_000_000,
    )
    pieces = lax.all_gather(result, ("cols", "view"), axis=0)
    return join(pieces, own.shape[0] // n, n)


def solution(mesh):
    return jax.shard_map(
        on_device,
        mesh=mesh,
        in_specs=(
            P("view", ("tiles", "lines"), None, "cols"),
            P(None, ("tiles", "cols")),
            P(("tiles", "lines")),
            P(),
        ),
        out_specs=P(("tiles", "lines"), "cols", None),
        check_vma=False,
    )
```

```python
import functools
import math

import jax
import jax.numpy as jnp
from jax import lax
from jax.experimental import pallas as pl
from jax.experimental.pallas import tpu as pltpu
from jax.sharding import PartitionSpec as P

DISP = 192
DGROUP = 16
GROUPS = DISP // DGROUP
LAYERS = 3
SHARPNESS = 2.0
HALO = 32
LANES = 128
LINES = 8
CHANNELS = 64
BLOCK = 256
SPAN = BLOCK + HALO
PARTS = LANES // LINES
RUN = SPAN // PARTS
KEYS = 40
WIDE = BLOCK + LANES
SEC_ROWS = LINES * CHANNELS
QUAD_ROWS = SEC_ROWS // 2
MASK_AT = QUAD_ROWS + CHANNELS
PAYLOAD = MASK_AT + 16
QUAD = LINES // 2
QUAD_LANES = LANES // 2
PACK = LANES // HALO
CUT = 16

BF = jnp.bfloat16
F32 = jnp.float32


def iota(shape, dim):
    return lax.broadcasted_iota(jnp.int32, shape, dim)


def dot_t(a, b):
    return lax.dot_general(a, b, (((1,), (1,)), ((), ())), preferred_element_type=F32)


def call(kernel, outs, scratch, smem, args, flops=0, space=pltpu.VMEM):
    specs = [pl.BlockSpec(memory_space=pltpu.SMEM)] * smem
    specs += [pl.BlockSpec(memory_space=space)] * (len(args) - smem)
    return pl.pallas_call(
        kernel,
        out_shape=[jax.ShapeDtypeStruct(shape, dtype) for shape, dtype in outs],
        in_specs=specs,
        out_specs=[pl.BlockSpec(memory_space=pltpu.VMEM)] * len(outs),
        scratch_shapes=scratch,
        compiler_params=pltpu.CompilerParams(vmem_limit_bytes=24 * 1024 * 1024),
        cost_estimate=pl.CostEstimate(flops=flops, bytes_accessed=1_000_000, transcendentals=0),
    )(*args)


def spread_guide(guide):
    keys = LAYERS * 3 * GROUPS
    row = iota((3 * KEYS, keys), 0)
    tap = jnp.where(row >= KEYS, 1, 0) + jnp.where(row >= 2 * KEYS, 1, 0)
    row = row - KEYS * tap
    layer = jnp.where(row >= GROUPS, 1, 0) + jnp.where(row >= 2 * GROUPS, 1, 0)
    key = 2 * GROUPS * layer + GROUPS * tap + row
    chosen = jnp.where((iota((3 * KEYS, keys), 1) == key) & (row < 3 * GROUPS), 1.0, 0.0).astype(BF)
    guide_t = dot_t(chosen, guide).astype(BF)
    return jnp.concatenate([guide_t, guide_t], axis=1)


def normalise(z, wts, t, room_left, room_right):
    z = (0.55 + 0.45 * jnp.tanh(0.5 * z)).astype(BF).astype(F32)
    taps = [z[k * KEYS : (k + 1) * KEYS] for k in range(3)]
    scale = 1.0 / (taps[0] + taps[1] + taps[2])
    wts[t, 0:KEYS, :] = jnp.where(room_left >= t, taps[0] * scale, 0.0)
    wts[t, KEYS : 2 * KEYS, :] = taps[1] * scale
    wts[t, 2 * KEYS : 3 * KEYS, :] = jnp.where(room_right < t, taps[2] * scale, 0.0)


def prefetch_kernel(own, valid, guide, own_out, masks, perm, flip, guide_out, valid_in, guide_in, sems):
    copies = [
        pltpu.make_async_copy(src, dst, sems.at[i])
        for i, (src, dst) in enumerate([(own, own_out), (guide, guide_in), (valid, valid_in)])
    ]
    for copy in copies:
        copy.start()
    perm[...] = jnp.where(
        iota((SPAN, WIDE), 1) == WIDE - 1 - iota((SPAN, WIDE), 0), 1.0, 0.0
    ).astype(BF)
    back = 2 * LANES - 1 - iota((DISP, 2 * LANES), 0)
    flip[...] = jnp.where(iota((DISP, 2 * LANES), 1) == back, 1.0, 0.0).astype(BF)

    copies[1].wait()
    guide_out[...] = spread_guide(guide_in[...])
    copies[2].wait()
    masks[...] = valid_in[...].astype(F32)
    copies[0].wait()


def payload_kernel(own, other, masks, first, second, ref_own):
    view = lax.axis_index("view")
    first_view = view == 0
    sec_mask = masks[1:2, :].astype(BF)
    lane = iota((CHANNELS, LANES), 1)
    tails = []
    for line in range(LINES):
        at = view * LINES + line
        mine, theirs = own[at], other[at]
        lo = line * CHANNELS
        dest, start = (first, lo) if line < QUAD else (second, lo - QUAD_ROWS)
        dest[start : start + CHANNELS, :] = jnp.where(first_view, theirs, mine) * sec_mask
        ref = jnp.where(first_view, mine, theirs)
        ref_own[lo : lo + CHANNELS, :] = ref
        tail = ref[:, BLOCK - LANES :].astype(F32)
        slot = line % PACK
        turn = (HALO * (slot + 1)) % LANES
        if turn:
            tail = pltpu.roll(tail, turn, 1)
        if slot:
            tails[-1] = jnp.where(lane >= HALO * slot, tail, tails[-1])
        else:
            tails.append(tail)
    for i, tail in enumerate(tails):
        first[QUAD_ROWS:MASK_AT, i * LANES : (i + 1) * LANES] = tail.astype(BF)
    first[MASK_AT:, :] = jnp.broadcast_to(masks[0:1, :], (16, BLOCK)).astype(BF)


def shifted(left, mine, lo, off):
    ch_lane = iota((CHANNELS, LANES), 1)
    tiles = [
        src[lo : lo + CHANNELS, i * LANES : (i + 1) * LANES].astype(F32)
        for src in (left, mine)
        for i in range(2)
    ]
    tiles = [pltpu.roll(tile, off, 1) for tile in tiles]
    tiles = [jnp.where(ch_lane < off, tiles[max(i - 1, 0)], tiles[i]).astype(BF) for i in range(4)]
    return jnp.concatenate(tiles, axis=1)


def line_costs(lhs, rhs, slot, skew, cost_rows):
    diagonal = iota((8, LANES), 1) - iota((8, LANES), 0)
    for chunk in range(3):
        rows = min(LANES, SPAN - chunk * LANES)
        first = max(1 - chunk, 0)
        last = 3 - chunk
        products = jnp.dot(
            lhs[chunk * LANES : chunk * LANES + rows],
            rhs[:, first * LANES : (last + 1) * LANES],
            preferred_element_type=F32,
        )
        for j in range(rows // 8):
            tiles = [
                pltpu.roll(
                    products[8 * j : 8 * j + 8, i * LANES : (i + 1) * LANES],
                    8 * j, 1, stride=1, stride_axis=0,
                )
                for i in range(last + 1 - first)
            ]
            if len(tiles) < 3:
                tiles = [tiles[0]] + tiles
            beyond = diagonal >= 8 * j
            at = chunk * LANES + 8 * j
            skew[slot, 0, at : at + 8, :] = jnp.where(beyond, tiles[1], tiles[0])
            skew[slot, 1, at : at + 8, :] = jnp.where(beyond, tiles[2], tiles[1])
    for t in range(RUN):
        at = t * QUAD_LANES + slot * PARTS
        for v in range(2):
            cost_rows[at : at + PARTS, v * LANES : (v + 1) * LANES] = skew[
                slot, v, pl.ds(t, PARTS, stride=RUN), :
            ].astype(BF)


def early_kernel(
    offsets, ref_own, mine, left, masks, perm, guide, wts, cost_rows, lhs_out,
    ref_rows, ref_cols, gate_rows, skew
):
    base = lax.axis_index("view") * LINES
    low = jnp.where(lax.axis_index("cols") == 0, HALO, 0)
    for line in range(LINES):
        lo = line * CHANNELS
        ref_rows[lo : lo + CHANNELS, LANES:] = ref_own[lo : lo + CHANNELS, :]
        half = line // PACK
        packed = left[QUAD_ROWS:MASK_AT, half * LANES : (half + 1) * LANES].astype(F32)
        turn = (LANES - HALO) - HALO * (line % PACK)
        if turn:
            packed = pltpu.roll(packed, turn, 1)
        ref_rows[lo : lo + CHANNELS, :LANES] = packed.astype(BF)

    mask_left = left[MASK_AT : MASK_AT + 1, BLOCK - LANES :].astype(F32)
    ref_mask = jnp.concatenate([mask_left, masks[0:1, :]], axis=1)
    ref_mask = jnp.broadcast_to(ref_mask * (1.0 / math.sqrt(CHANNELS)), (LANES, WIDE))
    mask_cols = dot_t(perm[...], ref_mask.astype(BF))
    half_lane = iota((PARTS, LANES), 1) < CHANNELS
    span_lane = iota((SPAN, LANES), 1) < CHANNELS

    for quad in range(LINES // QUAD):
        ref_t = dot_t(perm[...], ref_rows[quad * QUAD_ROWS : (quad + 1) * QUAD_ROWS, :])
        for pair in range(QUAD // 2):
            cols = ref_t[:, pair * LANES : (pair + 1) * LANES]
            slot = quad * 2 + pair
            ref_cols[slot] = cols
            masked = cols * mask_cols
            if quad == 0:
                rhs = jnp.concatenate(
                    [
                        shifted(left, mine, line * CHANNELS, offsets[base + line])
                        for line in (2 * slot, 2 * slot + 1)
                    ],
                    axis=0,
                )
            for side in range(2):
                line = 2 * slot + side
                for t in range(RUN):
                    picked = ref_cols[slot, pl.ds(t, PARTS, stride=RUN), :]
                    picked = jnp.where(half_lane if side == 0 else ~half_lane, picked, 0.0)
                    at = t * LANES + line * PARTS
                    gate_rows[at : at + PARTS, :] = picked.astype(BF)
                lhs = jnp.where(span_lane if side == 0 else ~span_lane, masked, 0.0).astype(BF)
                if quad == 0:
                    line_costs(lhs, rhs, line, skew, cost_rows)
                else:
                    lhs_out[line - QUAD] = lhs

    place = iota((KEYS, LANES), 1)
    x_base = SPAN - 1 - RUN * (place & (PARTS - 1))
    row = iota((KEYS, LANES), 0)
    reach = jnp.where(row >= 2 * GROUPS, 9, jnp.where(row >= GROUPS, 3, 1))
    room_left = x_base - reach - low
    room_right = x_base + reach - SPAN
    for two in range(RUN // 2):
        at = 2 * two * LANES
        logits = dot_t(guide[...], gate_rows[at : at + 2 * LANES, :])
        for i in range(2):
            t = 2 * two + i
            normalise(logits[:, i * LANES : (i + 1) * LANES], wts, t, room_left, room_right)


def late_kernel(
    offsets, mine, left, lhs, early_rows, wts, flip, out, skew, cost_rows, vol, vals, turned
):
    base = lax.axis_index("view") * LINES
    for pair in range(QUAD // 2):
        rhs = jnp.concatenate(
            [
                shifted(left, mine, line * CHANNELS, offsets[base + QUAD + line])
                for line in (2 * pair, 2 * pair + 1)
            ],
            axis=0,
        )
        for line in (2 * pair, 2 * pair + 1):
            line_costs(lhs[line], rhs, line, skew, cost_rows)

    for two in range(RUN // 2):
        rows = []
        for t in (2 * two, 2 * two + 1):
            for part in (early_rows, cost_rows):
                rows.append(part[t * QUAD_LANES : (t + 1) * QUAD_LANES, :])
        costs = dot_t(flip[...], jnp.concatenate(rows, axis=0))
        vol[2 * two] = costs[:, :LANES]
        vol[2 * two + 1] = costs[:, LANES:]

    def aggregate(group, carry):
        for half in range(2):
            at = pl.multiple_of(group * DGROUP + half * 8, 8)
            v = [vol[t, pl.ds(at, 8), :] for t in range(RUN)]
            for layer in range(LAYERS):
                s = 3**layer
                before = [v[t + s] if t + s < RUN else pltpu.roll(v[t + s - RUN], LANES - 1, 1) for t in range(RUN)]
                after = [v[t - s] if t >= s else pltpu.roll(v[t - s + RUN], 1, 1) for t in range(RUN)]
                fresh = []
                for t in range(RUN):
                    w = [wts[t, pl.ds(k * KEYS + layer * GROUPS + group, 1), :] for k in range(3)]
                    fresh.append(w[0] * before[t] + w[1] * v[t] + w[2] * after[t])
                v = fresh
            for t in range(RUN):
                vol[t, pl.ds(at, 8), :] = v[t]
        return carry

    lax.fori_loop(0, GROUPS, aggregate, 0)

    vals[...] = jnp.zeros((LANES, LANES), F32)
    sub = iota((8, LANES), 0).astype(F32)
    line_of = iota((1, LANES), 1) >> 4
    offs = jnp.zeros((1, LANES), F32)
    for line in range(LINES):
        offs = jnp.where(line_of == line, offsets[base + line].astype(F32), offs)

    def softmax(t, carry):
        v = [vol[t, 8 * i : 8 * i + 8, :] for i in range(DISP // 8)]
        top = v
        while len(top) > 1:
            top = [jnp.maximum(a, b) for a, b in zip(top[::2], top[1::2])] + top[len(top) & ~1 :]
        top = jnp.max(top[0], axis=0, keepdims=True)
        e = [jnp.exp(SHARPNESS * (a - top)) for a in v]
        total = e[0]
        moment = jnp.zeros((8, LANES), F32)
        for i in range(1, DISP // 8):
            total = total + e[i]
            moment = moment + float(8 * i) * e[i]
        moment = jnp.sum(moment + sub * total, axis=0, keepdims=True)
        total = jnp.sum(total, axis=0, keepdims=True)
        vals[pl.ds(RUN - 1 - t, 1), :] = (moment / total + offs) * (1.0 / DISP)
        return carry

    lax.fori_loop(0, RUN, softmax, 0)

    turned[...] = jnp.transpose(vals[...])
    lane = iota((8, LANES), 1)
    result = [jnp.zeros((8, LANES), F32) for _ in range(WIDE // LANES)]
    for part in range(PARTS):
        piece = turned[pl.ds(part, LINES, stride=PARTS), :]
        start = (RUN * (PARTS - 1 - part) - HALO) % WIDE
        tile, turn = divmod(start, LANES)
        if turn:
            piece = pltpu.roll(piece, turn, 1)
        if turn + RUN > LANES:
            after = (tile + 1) % len(result)
            result[after] = result[after] + jnp.where(lane < turn, piece, 0.0)
            piece = jnp.where(lane >= turn, piece, 0.0)
        result[tile] = result[tile] + piece
    for tile, value in enumerate(result):
        out[:, tile * LANES : (tile + 1) * LANES] = value


def join(pieces, sub, n):
    block = lax.axis_index("cols")
    pieces = pieces.reshape(n, 2, LINES, WIDE)
    start = (0, block // (n // 2), (block % (n // 2)) * sub, 0)
    pieces = lax.dynamic_slice(pieces, start, (n, 1, sub, WIDE))[:, 0]
    main = pieces[:, :, :BLOCK]
    tail = jnp.pad(pieces[1:, :, BLOCK:], ((0, 1), (0, 0), (LANES, 0)))
    place = (n, sub, BLOCK)
    keep = (iota(place, 2) < BLOCK - CUT) | (iota(place, 0) == n - 1)
    joined = jnp.where(keep, main, tail)
    return jnp.transpose(joined, (1, 0, 2)).reshape(1, sub, n * BLOCK)


def halo_plan(features, valid_cols, offsets, guide_weight):
    own = features[0]
    n = lax.axis_size("cols")
    right = [(c, c + 1) for c in range(n - 1)]
    other = lax.ppermute(own, "view", [(0, 1), (1, 0)])
    near, masks, perm, flip, guide = call(
        prefetch_kernel,
        [(own.shape, BF), (valid_cols.shape, F32), ((SPAN, WIDE), BF), ((DISP, 2 * LANES), BF), ((3 * KEYS, LANES), BF)],
        [pltpu.VMEM(valid_cols.shape, jnp.int32), pltpu.VMEM(guide_weight.shape, BF), pltpu.SemaphoreType.DMA((3,))],
        0, (own, valid_cols, guide_weight), 100_000_000, pl.ANY,
    )
    first, second, ref_own = call(
        payload_kernel,
        [((PAYLOAD, BLOCK), BF), ((QUAD_ROWS, BLOCK), BF), ((SEC_ROWS, BLOCK), BF)],
        [], 0, (near, other, masks),
    )
    left_first = lax.ppermute(first, "cols", right)
    left_second = lax.ppermute(second, "cols", right)
    quad_rows = (RUN * QUAD_LANES, 2 * LANES)
    skew = pltpu.VMEM((QUAD, 2, SPAN, LANES), F32)
    square = pltpu.VMEM((LANES, LANES), F32)
    wts, early_rows, lhs = call(
        early_kernel,
        [((RUN, 3 * KEYS, LANES), F32), (quad_rows, BF), ((QUAD, SPAN, LANES), BF)],
        [pltpu.VMEM((SEC_ROWS, WIDE), BF), pltpu.VMEM((QUAD, SPAN, LANES), F32), pltpu.VMEM((RUN * LANES, LANES), BF), skew],
        1, (offsets, ref_own, first, left_first, masks, perm, guide), 1_000_000_000,
    )
    (result,) = call(
        late_kernel,
        [((LINES, WIDE), F32)],
        [skew, pltpu.VMEM(quad_rows, BF), pltpu.VMEM((RUN, DISP, LANES), F32), square, square],
        1, (offsets, second, left_second, lhs, early_rows, wts, flip), 1_000_000_000,
    )
    copies = jnp.broadcast_to(result[None], (2 * n, LINES, WIDE))
    pieces = lax.all_to_all(copies, ("cols", "view"), split_axis=0, concat_axis=0, tiled=True)
    return join(pieces, own.shape[0] // n, n)


LINE_RUN = 8
MASK_ROWS = 16


def constants_kernel(guide, order, flip, guide_out, spread):
    row = iota((LANES, LANES), 0)
    from_lane = LANES - 1 - LINE_RUN * (row & (PARTS - 1)) - (row >> 4)
    order[...] = jnp.where(iota((LANES, LANES), 1) == from_lane, 1.0, 0.0).astype(BF)
    back = 2 * LANES - 1 - iota((DISP, 2 * LANES), 0)
    flip[...] = jnp.where(iota((DISP, 2 * LANES), 1) == back, 1.0, 0.0).astype(BF)
    guide_out[...] = spread_guide(guide[...])
    block_of = spread.shape[1] // LINE_RUN - 1 - (iota(spread.shape, 1) >> 3)
    spread[...] = jnp.where(iota(spread.shape, 0) == block_of, 1.0, 0.0).astype(BF)


def pack_kernel(first, own, valid, out, own_in, valid_in, sems):
    targets = out.shape[0]
    start = 0 if first else 1
    copies = [
        pltpu.make_async_copy(own.at[2 * i + start], own_in.at[i], sems.at[i]) for i in range(targets)
    ]
    copies.append(pltpu.make_async_copy(valid, valid_in, sems.at[targets]))
    for copy in copies:
        copy.start()
    copies[-1].wait()
    masks = valid_in[...].astype(F32)
    factor = jnp.where(lax.axis_index("view") == 1, masks[1:2, :], 1.0).astype(BF)
    ref_mask = jnp.broadcast_to(masks[0:1, :], (MASK_ROWS, BLOCK)).astype(BF)
    for i in range(targets):
        copies[i].wait()
        out[i, :CHANNELS, :] = own_in[i] * factor
        if first:
            out[i, CHANNELS:, :] = ref_mask


def line_kernel(
    which, offsets, blocks, masks, order, flip, guide, spread, *rest
):
    if which:
        earlier, out, gate_rows, cost_rows, vol, done, wts = rest
    else:
        out, gate_rows, cost_rows, vol, done, wts = rest
    tiles = blocks.shape[0]
    width = tiles * LANES
    at = lax.axis_index("cols") * (2 * offsets.shape[0] // tiles) + 2 * lax.axis_index("view") + which
    off = offsets[at]

    def tile_of(view, w):
        lo = (w % 2) * LANES
        return blocks[2 * (w // 2) + view, :CHANNELS, lo : lo + LANES]

    ch_lane = iota((CHANNELS, LANES), 1)
    rolled = [pltpu.roll(tile_of(1, w).astype(F32), off, 1) for w in range(tiles)]
    empty = jnp.zeros((CHANNELS, LANES), F32)
    shifted = [empty.astype(BF)] * 2
    for w in range(tiles):
        shifted.append(jnp.where(ch_lane < off, rolled[w - 1] if w else empty, rolled[w]).astype(BF))
    shifted = [jnp.concatenate([tile, tile], axis=0) for tile in shifted]

    diagonal = iota((8, LANES), 1) - LINE_RUN * iota((8, LANES), 0)
    low_half = iota((LANES, LANES), 1) < CHANNELS
    scale = 1.0 / math.sqrt(CHANNELS)
    for quad in range(tiles // 4):
        refs, masked = [], []
        for w in range(4 * quad, 4 * quad + 4):
            tile = tile_of(0, w)
            lo = (w % 2) * LANES
            mask = masks[2 * (w // 2), CHANNELS : CHANNELS + 1, lo : lo + LANES].astype(F32) * scale
            refs.append(tile)
            masked.append(tile * mask.astype(BF))
        cols = dot_t(order[...], jnp.concatenate(refs, axis=0))
        masked = dot_t(order[...], jnp.concatenate(masked, axis=0))
        for q in range(4):
            w = 4 * quad + q
            place = (tiles - 1 - w) * PARTS
            keep = low_half if q % 2 == 0 else ~low_half
            lo = (q // 2) * LANES
            gates = jnp.where(keep, cols[:, lo : lo + LANES], 0.0).astype(BF)
            lhs = jnp.where(keep, masked[:, lo : lo + LANES], 0.0).astype(BF)
            rhs = jnp.concatenate(shifted[w : w + 3], axis=1)
            products = jnp.dot(lhs, rhs, preferred_element_type=F32)
            for t in range(LINE_RUN):
                row = t * LANES + place
                gate_rows[row : row + PARTS, :] = gates[t * PARTS : (t + 1) * PARTS]
                halves = []
                for half in range(2):
                    base = half * LANES // 2 + t
                    r = t * PARTS + 8 * half
                    turned = [
                        pltpu.roll(
                            products[r : r + 8, i * LANES : (i + 1) * LANES],
                            base, 1, stride=LINE_RUN, stride_axis=0,
                        )
                        for i in range(3)
                    ]
                    beyond = diagonal >= base
                    halves.append(
                        jnp.concatenate(
                            [jnp.where(beyond, turned[1], turned[0]), jnp.where(beyond, turned[2], turned[1])],
                            axis=1,
                        )
                    )
                cost_rows[row : row + PARTS, :] = jnp.concatenate(halves, axis=0).astype(BF)

    x_base = width - 1 - LINE_RUN * iota((KEYS, LANES), 1)
    row = iota((KEYS, LANES), 0)
    reach = jnp.where(row >= 2 * GROUPS, 9, jnp.where(row >= GROUPS, 3, 1))
    room_left = x_base - reach
    room_right = x_base + reach - width
    for two in range(LINE_RUN // 2):
        lo = 2 * two * LANES
        costs = dot_t(flip[...], cost_rows[lo : lo + 2 * LANES, :])
        logits = dot_t(guide[...], gate_rows[lo : lo + 2 * LANES, :])
        for i in range(2):
            t = 2 * two + i
            vol[t] = costs[:, i * LANES : (i + 1) * LANES]
            normalise(logits[:, i * LANES : (i + 1) * LANES], wts, t, room_left, room_right)

    def aggregate(group, top):
        at = pl.multiple_of(group * DGROUP, DGROUP)
        v = [[vol[t, pl.ds(at + 8 * h, 8), :] for t in range(LINE_RUN)] for h in range(2)]
        for layer in range(LAYERS):
            s = 3**layer
            fresh = [[], []]
            for t in range(LINE_RUN):
                w = [wts[t, pl.ds(k * KEYS + layer * GROUPS + group, 1), :] for k in range(3)]
                w = [jnp.broadcast_to(a, (8, LANES)) for a in w]
                for h in range(2):
                    blk, r = divmod(t + s, LINE_RUN)
                    before = pltpu.roll(v[h][r], LANES - blk, 1) if blk else v[h][r]
                    blk, r = divmod(t - s, LINE_RUN)
                    after = pltpu.roll(v[h][r], -blk, 1) if blk else v[h][r]
                    fresh[h].append(w[0] * before + w[1] * v[h][t] + w[2] * after)
            v = fresh
        for h in range(2):
            for t in range(LINE_RUN):
                done[t, pl.ds(at + 8 * h, 8), :] = v[h][t]
        return tuple(jnp.maximum(top[t], jnp.maximum(v[0][t], v[1][t])) for t in range(LINE_RUN))

    top = lax.fori_loop(0, GROUPS, aggregate, (jnp.full((8, LANES), -jnp.inf, F32),) * LINE_RUN)
    top = [jnp.max(a, axis=0, keepdims=True) for a in top]
    sub = iota((8, LANES), 0)
    totals = jnp.zeros((8, LANES), F32)
    moments = totals
    for t in range(LINE_RUN):
        total = jnp.zeros((8, LANES), F32)
        moment = total
        for i in range(DISP // 8):
            e = jnp.exp(SHARPNESS * (done[t, 8 * i : 8 * i + 8, :] - top[t]))
            total = total + e
            if i:
                moment = moment + float(8 * i) * e
        moment = moment + sub.astype(F32) * total
        here = sub == LINE_RUN - 1 - t
        totals = jnp.where(here, jnp.sum(total, axis=0, keepdims=True), totals)
        moments = jnp.where(here, jnp.sum(moment, axis=0, keepdims=True), moments)
    vals = (moments / totals + off.astype(F32)) * (1.0 / DISP)
    high = vals.astype(BF)
    rest_of = vals - high.astype(F32)
    middle = rest_of.astype(BF)
    low = (rest_of - middle.astype(F32)).astype(BF)
    zero = jnp.zeros((8, LANES), BF)
    pieces = jnp.dot(
        jnp.concatenate([high, middle, low, zero], axis=0), spread[...], preferred_element_type=F32
    )
    pieces = pieces[0:8] + pieces[8:16] + pieces[16:24]
    wanted = iota((8, width), 0) == (iota((8, width), 1) & (LINE_RUN - 1))
    line = jnp.sum(jnp.where(wanted, pieces, 0.0), axis=0, keepdims=True)
    if which:
        out[0:1, :] = earlier[...]
        out[1:2, :] = line
    else:
        out[...] = line


def lines_plan(features, valid_cols, offsets, guide_weight):
    own = features[0]
    n = lax.axis_size("cols")
    devices = 2 * n
    width = n * BLOCK
    got = []
    for first in (True, False):
        rows = CHANNELS + (MASK_ROWS if first else 0)
        (packed,) = call(
            functools.partial(pack_kernel, first),
            [((devices, rows, BLOCK), BF)],
            [
                pltpu.VMEM((devices, CHANNELS, BLOCK), BF),
                pltpu.VMEM(valid_cols.shape, jnp.int32),
                pltpu.SemaphoreType.DMA((devices + 1,)),
            ],
            0, (own, valid_cols), 1_000_000, pl.ANY,
        )
        got.append(lax.all_to_all(packed, ("cols", "view"), split_axis=0, concat_axis=0, tiled=True))
    consts = call(
        constants_kernel,
        [((LANES, LANES), BF), ((DISP, 2 * LANES), BF), ((3 * KEYS, LANES), BF), ((LANES, width), BF)],
        [], 0, (guide_weight,), 1_000_000,
    )
    line = ()
    for which in range(2):
        line = call(
            functools.partial(line_kernel, which),
            [((1 + which, width), F32)],
            [
                pltpu.VMEM((LINE_RUN * LANES, LANES), BF),
                pltpu.VMEM((LINE_RUN * LANES, 2 * LANES), BF),
                pltpu.VMEM((LINE_RUN, DISP, LANES), F32),
                pltpu.VMEM((LINE_RUN, DISP, LANES), F32),
                pltpu.VMEM((LINE_RUN, 3 * KEYS, LANES), F32),
            ],
            1, (offsets, got[which], got[0], *consts, *line), 1_000_000_000,
        )
    return lax.all_gather(line[0], "view", axis=0, tiled=True)[None]


def on_device(features, valid_cols, offsets, guide_weight):
    n = lax.axis_size("cols")
    lines = features.shape[1]
    if lines == 4 * n and n * BLOCK == LINE_RUN * LANES:
        return lines_plan(features, valid_cols, offsets, guide_weight)
    return halo_plan(features, valid_cols, offsets, guide_weight)


def solution(mesh):
    return jax.shard_map(
        on_device,
        mesh=mesh,
        in_specs=(
            P("view", ("tiles", "lines"), None, "cols"),
            P(None, ("tiles", "cols")),
            P(("tiles", "lines")),
            P(),
        ),
        out_specs=P(("tiles", "lines"), "cols", None),
        check_vma=False,
    )
```

```python
import functools
import math

import jax
import jax.numpy as jnp
from jax import lax
from jax.experimental import pallas as pl
from jax.experimental.pallas import tpu as pltpu
from jax.sharding import PartitionSpec as P

DISP = 192
DGROUP = 16
GROUPS = DISP // DGROUP
LAYERS = 3
SHARPNESS = 2.0
HALO = 32
LANES = 128
LINES = 8
CHANNELS = 64
BLOCK = 256
SPAN = BLOCK + HALO
PARTS = LANES // LINES
RUN = SPAN // PARTS
KEYS = 40
WIDE = BLOCK + LANES
SEC_ROWS = LINES * CHANNELS
QUAD_ROWS = SEC_ROWS // 2
MASK_AT = QUAD_ROWS + CHANNELS
PAYLOAD = MASK_AT + 16
QUAD = LINES // 2
QUAD_LANES = LANES // 2
PACK = LANES // HALO
CUT = 16

BF = jnp.bfloat16
F32 = jnp.float32


def iota(shape, dim):
    return lax.broadcasted_iota(jnp.int32, shape, dim)


def dot_t(a, b):
    return lax.dot_general(a, b, (((1,), (1,)), ((), ())), preferred_element_type=F32)


def call(kernel, outs, scratch, smem, args, flops=0, space=pltpu.VMEM):
    specs = [pl.BlockSpec(memory_space=pltpu.SMEM)] * smem
    specs += [pl.BlockSpec(memory_space=space)] * (len(args) - smem)
    return pl.pallas_call(
        kernel,
        out_shape=[jax.ShapeDtypeStruct(shape, dtype) for shape, dtype in outs],
        in_specs=specs,
        out_specs=[pl.BlockSpec(memory_space=pltpu.VMEM)] * len(outs),
        scratch_shapes=scratch,
        compiler_params=pltpu.CompilerParams(vmem_limit_bytes=24 * 1024 * 1024),
        cost_estimate=pl.CostEstimate(flops=flops, bytes_accessed=1_000_000, transcendentals=0),
    )(*args)


def spread_guide(guide):
    keys = LAYERS * 3 * GROUPS
    row = iota((3 * KEYS, keys), 0)
    tap = jnp.where(row >= KEYS, 1, 0) + jnp.where(row >= 2 * KEYS, 1, 0)
    row = row - KEYS * tap
    layer = jnp.where(row >= GROUPS, 1, 0) + jnp.where(row >= 2 * GROUPS, 1, 0)
    key = 2 * GROUPS * layer + GROUPS * tap + row
    chosen = jnp.where((iota((3 * KEYS, keys), 1) == key) & (row < 3 * GROUPS), 1.0, 0.0).astype(BF)
    guide_t = dot_t(chosen, guide).astype(BF)
    return jnp.concatenate([guide_t, guide_t], axis=1)


def normalise(z, wts, t, room_left, room_right):
    z = (0.55 + 0.45 * jnp.tanh(0.5 * z)).astype(BF).astype(F32)
    taps = [z[k * KEYS : (k + 1) * KEYS] for k in range(3)]
    scale = 1.0 / (taps[0] + taps[1] + taps[2])
    wts[t, 0:KEYS, :] = jnp.where(room_left >= t, taps[0] * scale, 0.0)
    wts[t, KEYS : 2 * KEYS, :] = taps[1] * scale
    wts[t, 2 * KEYS : 3 * KEYS, :] = jnp.where(room_right < t, taps[2] * scale, 0.0)


def prefetch_kernel(own, valid, guide, own_out, masks, perm, flip, guide_out, valid_in, guide_in, sems):
    copies = [
        pltpu.make_async_copy(src, dst, sems.at[i])
        for i, (src, dst) in enumerate([(own, own_out), (guide, guide_in), (valid, valid_in)])
    ]
    for copy in copies:
        copy.start()
    perm[...] = jnp.where(
        iota((SPAN, WIDE), 1) == WIDE - 1 - iota((SPAN, WIDE), 0), 1.0, 0.0
    ).astype(BF)
    back = 2 * LANES - 1 - iota((DISP, 2 * LANES), 0)
    flip[...] = jnp.where(iota((DISP, 2 * LANES), 1) == back, 1.0, 0.0).astype(BF)

    copies[1].wait()
    guide_out[...] = spread_guide(guide_in[...])
    copies[2].wait()
    masks[...] = valid_in[...].astype(F32)
    copies[0].wait()


def payload_kernel(own, other, masks, first, second, ref_own):
    view = lax.axis_index("view")
    first_view = view == 0
    sec_mask = masks[1:2, :].astype(BF)
    lane = iota((CHANNELS, LANES), 1)
    tails = []
    for line in range(LINES):
        at = view * LINES + line
        mine, theirs = own[at], other[at]
        lo = line * CHANNELS
        dest, start = (first, lo) if line < QUAD else (second, lo - QUAD_ROWS)
        dest[start : start + CHANNELS, :] = jnp.where(first_view, theirs, mine) * sec_mask
        ref = jnp.where(first_view, mine, theirs)
        ref_own[lo : lo + CHANNELS, :] = ref
        tail = ref[:, BLOCK - LANES :].astype(F32)
        slot = line % PACK
        turn = (HALO * (slot + 1)) % LANES
        if turn:
            tail = pltpu.roll(tail, turn, 1)
        if slot:
            tails[-1] = jnp.where(lane >= HALO * slot, tail, tails[-1])
        else:
            tails.append(tail)
    for i, tail in enumerate(tails):
        first[QUAD_ROWS:MASK_AT, i * LANES : (i + 1) * LANES] = tail.astype(BF)
    first[MASK_AT:, :] = jnp.broadcast_to(masks[0:1, :], (16, BLOCK)).astype(BF)


def shifted(left, mine, lo, off):
    ch_lane = iota((CHANNELS, LANES), 1)
    tiles = [
        src[lo : lo + CHANNELS, i * LANES : (i + 1) * LANES].astype(F32)
        for src in (left, mine)
        for i in range(2)
    ]
    tiles = [pltpu.roll(tile, off, 1) for tile in tiles]
    tiles = [jnp.where(ch_lane < off, tiles[max(i - 1, 0)], tiles[i]).astype(BF) for i in range(4)]
    return jnp.concatenate(tiles, axis=1)


def line_costs(lhs, rhs, slot, skew, cost_rows):
    diagonal = iota((8, LANES), 1) - iota((8, LANES), 0)
    for chunk in range(3):
        rows = min(LANES, SPAN - chunk * LANES)
        first = max(1 - chunk, 0)
        last = 3 - chunk
        products = jnp.dot(
            lhs[chunk * LANES : chunk * LANES + rows],
            rhs[:, first * LANES : (last + 1) * LANES],
            preferred_element_type=F32,
        )
        for j in range(rows // 8):
            tiles = [
                pltpu.roll(
                    products[8 * j : 8 * j + 8, i * LANES : (i + 1) * LANES],
                    8 * j, 1, stride=1, stride_axis=0,
                )
                for i in range(last + 1 - first)
            ]
            if len(tiles) < 3:
                tiles = [tiles[0]] + tiles
            beyond = diagonal >= 8 * j
            at = chunk * LANES + 8 * j
            skew[slot, 0, at : at + 8, :] = jnp.where(beyond, tiles[1], tiles[0])
            skew[slot, 1, at : at + 8, :] = jnp.where(beyond, tiles[2], tiles[1])
    for t in range(RUN):
        at = t * QUAD_LANES + slot * PARTS
        for v in range(2):
            cost_rows[at : at + PARTS, v * LANES : (v + 1) * LANES] = skew[
                slot, v, pl.ds(t, PARTS, stride=RUN), :
            ].astype(BF)


def early_kernel(
    offsets, ref_own, mine, left, masks, perm, guide, wts, cost_rows, lhs_out,
    ref_rows, ref_cols, gate_rows, skew
):
    base = lax.axis_index("view") * LINES
    low = jnp.where(lax.axis_index("cols") == 0, HALO, 0)
    for line in range(LINES):
        lo = line * CHANNELS
        ref_rows[lo : lo + CHANNELS, LANES:] = ref_own[lo : lo + CHANNELS, :]
        half = line // PACK
        packed = left[QUAD_ROWS:MASK_AT, half * LANES : (half + 1) * LANES].astype(F32)
        turn = (LANES - HALO) - HALO * (line % PACK)
        if turn:
            packed = pltpu.roll(packed, turn, 1)
        ref_rows[lo : lo + CHANNELS, :LANES] = packed.astype(BF)

    mask_left = left[MASK_AT : MASK_AT + 1, BLOCK - LANES :].astype(F32)
    ref_mask = jnp.concatenate([mask_left, masks[0:1, :]], axis=1)
    ref_mask = jnp.broadcast_to(ref_mask * (1.0 / math.sqrt(CHANNELS)), (LANES, WIDE))
    mask_cols = dot_t(perm[...], ref_mask.astype(BF))
    half_lane = iota((PARTS, LANES), 1) < CHANNELS
    span_lane = iota((SPAN, LANES), 1) < CHANNELS

    for quad in range(LINES // QUAD):
        ref_t = dot_t(perm[...], ref_rows[quad * QUAD_ROWS : (quad + 1) * QUAD_ROWS, :])
        for pair in range(QUAD // 2):
            cols = ref_t[:, pair * LANES : (pair + 1) * LANES]
            slot = quad * 2 + pair
            ref_cols[slot] = cols
            masked = cols * mask_cols
            if quad == 0:
                rhs = jnp.concatenate(
                    [
                        shifted(left, mine, line * CHANNELS, offsets[base + line])
                        for line in (2 * slot, 2 * slot + 1)
                    ],
                    axis=0,
                )
            for side in range(2):
                line = 2 * slot + side
                for t in range(RUN):
                    picked = ref_cols[slot, pl.ds(t, PARTS, stride=RUN), :]
                    picked = jnp.where(half_lane if side == 0 else ~half_lane, picked, 0.0)
                    at = t * LANES + line * PARTS
                    gate_rows[at : at + PARTS, :] = picked.astype(BF)
                lhs = jnp.where(span_lane if side == 0 else ~span_lane, masked, 0.0).astype(BF)
                if quad == 0:
                    line_costs(lhs, rhs, line, skew, cost_rows)
                else:
                    lhs_out[line - QUAD] = lhs

    place = iota((KEYS, LANES), 1)
    x_base = SPAN - 1 - RUN * (place & (PARTS - 1))
    row = iota((KEYS, LANES), 0)
    reach = jnp.where(row >= 2 * GROUPS, 9, jnp.where(row >= GROUPS, 3, 1))
    room_left = x_base - reach - low
    room_right = x_base + reach - SPAN
    for two in range(RUN // 2):
        at = 2 * two * LANES
        logits = dot_t(guide[...], gate_rows[at : at + 2 * LANES, :])
        for i in range(2):
            t = 2 * two + i
            normalise(logits[:, i * LANES : (i + 1) * LANES], wts, t, room_left, room_right)


def late_kernel(
    offsets, mine, left, lhs, early_rows, wts, flip, out, skew, cost_rows, vol, vals, turned
):
    base = lax.axis_index("view") * LINES
    for pair in range(QUAD // 2):
        rhs = jnp.concatenate(
            [
                shifted(left, mine, line * CHANNELS, offsets[base + QUAD + line])
                for line in (2 * pair, 2 * pair + 1)
            ],
            axis=0,
        )
        for line in (2 * pair, 2 * pair + 1):
            line_costs(lhs[line], rhs, line, skew, cost_rows)

    for two in range(RUN // 2):
        rows = []
        for t in (2 * two, 2 * two + 1):
            for part in (early_rows, cost_rows):
                rows.append(part[t * QUAD_LANES : (t + 1) * QUAD_LANES, :])
        costs = dot_t(flip[...], jnp.concatenate(rows, axis=0))
        vol[2 * two] = costs[:, :LANES]
        vol[2 * two + 1] = costs[:, LANES:]

    def aggregate(group, carry):
        for half in range(2):
            at = pl.multiple_of(group * DGROUP + half * 8, 8)
            v = [vol[t, pl.ds(at, 8), :] for t in range(RUN)]
            for layer in range(LAYERS):
                s = 3**layer
                before = [v[t + s] if t + s < RUN else pltpu.roll(v[t + s - RUN], LANES - 1, 1) for t in range(RUN)]
                after = [v[t - s] if t >= s else pltpu.roll(v[t - s + RUN], 1, 1) for t in range(RUN)]
                fresh = []
                for t in range(RUN):
                    w = [wts[t, pl.ds(k * KEYS + layer * GROUPS + group, 1), :] for k in range(3)]
                    fresh.append(w[0] * before[t] + w[1] * v[t] + w[2] * after[t])
                v = fresh
            for t in range(RUN):
                vol[t, pl.ds(at, 8), :] = v[t]
        return carry

    lax.fori_loop(0, GROUPS, aggregate, 0)

    vals[...] = jnp.zeros((LANES, LANES), F32)
    sub = iota((8, LANES), 0).astype(F32)
    line_of = iota((1, LANES), 1) >> 4
    offs = jnp.zeros((1, LANES), F32)
    for line in range(LINES):
        offs = jnp.where(line_of == line, offsets[base + line].astype(F32), offs)

    def softmax(t, carry):
        v = [vol[t, 8 * i : 8 * i + 8, :] for i in range(DISP // 8)]
        top = v
        while len(top) > 1:
            top = [jnp.maximum(a, b) for a, b in zip(top[::2], top[1::2])] + top[len(top) & ~1 :]
        top = jnp.max(top[0], axis=0, keepdims=True)
        e = [jnp.exp(SHARPNESS * (a - top)) for a in v]
        total = e[0]
        moment = jnp.zeros((8, LANES), F32)
        for i in range(1, DISP // 8):
            total = total + e[i]
            moment = moment + float(8 * i) * e[i]
        moment = jnp.sum(moment + sub * total, axis=0, keepdims=True)
        total = jnp.sum(total, axis=0, keepdims=True)
        vals[pl.ds(RUN - 1 - t, 1), :] = (moment / total + offs) * (1.0 / DISP)
        return carry

    lax.fori_loop(0, RUN, softmax, 0)

    turned[...] = jnp.transpose(vals[...])
    lane = iota((8, LANES), 1)
    result = [jnp.zeros((8, LANES), F32) for _ in range(WIDE // LANES)]
    for part in range(PARTS):
        piece = turned[pl.ds(part, LINES, stride=PARTS), :]
        start = (RUN * (PARTS - 1 - part) - HALO) % WIDE
        tile, turn = divmod(start, LANES)
        if turn:
            piece = pltpu.roll(piece, turn, 1)
        if turn + RUN > LANES:
            after = (tile + 1) % len(result)
            result[after] = result[after] + jnp.where(lane < turn, piece, 0.0)
            piece = jnp.where(lane >= turn, piece, 0.0)
        result[tile] = result[tile] + piece
    for tile, value in enumerate(result):
        out[:, tile * LANES : (tile + 1) * LANES] = value


def join(pieces, sub, n):
    block = lax.axis_index("cols")
    pieces = pieces.reshape(n, 2, LINES, WIDE)
    start = (0, block // (n // 2), (block % (n // 2)) * sub, 0)
    pieces = lax.dynamic_slice(pieces, start, (n, 1, sub, WIDE))[:, 0]
    main = pieces[:, :, :BLOCK]
    tail = jnp.pad(pieces[1:, :, BLOCK:], ((0, 1), (0, 0), (LANES, 0)))
    place = (n, sub, BLOCK)
    keep = (iota(place, 2) < BLOCK - CUT) | (iota(place, 0) == n - 1)
    joined = jnp.where(keep, main, tail)
    return jnp.transpose(joined, (1, 0, 2)).reshape(1, sub, n * BLOCK)


def halo_plan(features, valid_cols, offsets, guide_weight):
    own = features[0]
    n = lax.axis_size("cols")
    right = [(c, c + 1) for c in range(n - 1)]
    other = lax.ppermute(own, "view", [(0, 1), (1, 0)])
    near, masks, perm, flip, guide = call(
        prefetch_kernel,
        [(own.shape, BF), (valid_cols.shape, F32), ((SPAN, WIDE), BF), ((DISP, 2 * LANES), BF), ((3 * KEYS, LANES), BF)],
        [pltpu.VMEM(valid_cols.shape, jnp.int32), pltpu.VMEM(guide_weight.shape, BF), pltpu.SemaphoreType.DMA((3,))],
        0, (own, valid_cols, guide_weight), 100_000_000, pl.ANY,
    )
    first, second, ref_own = call(
        payload_kernel,
        [((PAYLOAD, BLOCK), BF), ((QUAD_ROWS, BLOCK), BF), ((SEC_ROWS, BLOCK), BF)],
        [], 0, (near, other, masks),
    )
    left_first = lax.ppermute(first, "cols", right)
    left_second = lax.ppermute(second, "cols", right)
    quad_rows = (RUN * QUAD_LANES, 2 * LANES)
    skew = pltpu.VMEM((QUAD, 2, SPAN, LANES), F32)
    square = pltpu.VMEM((LANES, LANES), F32)
    wts, early_rows, lhs = call(
        early_kernel,
        [((RUN, 3 * KEYS, LANES), F32), (quad_rows, BF), ((QUAD, SPAN, LANES), BF)],
        [pltpu.VMEM((SEC_ROWS, WIDE), BF), pltpu.VMEM((QUAD, SPAN, LANES), F32), pltpu.VMEM((RUN * LANES, LANES), BF), skew],
        1, (offsets, ref_own, first, left_first, masks, perm, guide), 1_000_000_000,
    )
    (result,) = call(
        late_kernel,
        [((LINES, WIDE), F32)],
        [skew, pltpu.VMEM(quad_rows, BF), pltpu.VMEM((RUN, DISP, LANES), F32), square, square],
        1, (offsets, second, left_second, lhs, early_rows, wts, flip), 1_000_000_000,
    )
    copies = jnp.broadcast_to(result[None], (2 * n, LINES, WIDE))
    pieces = lax.all_to_all(copies, ("cols", "view"), split_axis=0, concat_axis=0, tiled=True)
    return join(pieces, own.shape[0] // n, n)


LINE_RUN = 16
PAIR = 2
LINE_PARTS = LANES // PAIR


def constants_kernel(guide, order, flip, guide_out, spread):
    row = iota((LANES, LANES), 0)
    from_lane = LANES - 1 - LINE_RUN * (row & 7) - (row >> 3)
    order[...] = jnp.where(iota((LANES, LANES), 1) == from_lane, 1.0, 0.0).astype(BF)
    back = 2 * LANES - 1 - iota((DISP, 2 * LANES), 0)
    flip[...] = jnp.where(iota((DISP, 2 * LANES), 1) == back, 1.0, 0.0).astype(BF)
    guide_out[...] = spread_guide(guide[...])
    block_of = LINE_PARTS - 1 - (iota(spread.shape, 1) >> 4)
    here = (iota(spread.shape, 0) & (LINE_PARTS - 1)) == block_of
    spread[...] = jnp.where(here, 1.0, 0.0).astype(BF)


def lines_kernel(
    offsets, blocks, valid, order, flip, guide, spread, out, gate_rows, cost_rows, vol, done, wts
):
    tiles = blocks.shape[0]
    width = tiles * LANES
    at = lax.axis_index("cols") * (PAIR * offsets.shape[0] // tiles) + PAIR * lax.axis_index("view")
    offs = [offsets[at + i] for i in range(PAIR)]
    ch_lane = iota((CHANNELS, LANES), 1)
    diagonal = iota((8, LANES), 1) - LINE_RUN * iota((8, LANES), 0)
    low_half = iota((LANES, LANES), 1) < CHANNELS
    scale = 1.0 / math.sqrt(CHANNELS)
    empty = jnp.zeros((CHANNELS, LANES), F32)

    def mask_of(view, w):
        lo = (w % 2) * LANES
        return valid[w // 2, view : view + 1, lo : lo + LANES].astype(F32)

    for i in range(PAIR):

        def tile_of(view, w):
            lo = (w % 2) * LANES
            return blocks[2 * (w // 2) + view, i, :, lo : lo + LANES]

        off = offs[i]
        rolled = [pltpu.roll(tile_of(1, w).astype(F32) * mask_of(1, w), off, 1) for w in range(tiles)]
        shifted = [empty.astype(BF)] * 2
        for w in range(tiles):
            shifted.append(jnp.where(ch_lane < off, rolled[w - 1] if w else empty, rolled[w]).astype(BF))
        shifted = [jnp.concatenate([tile, tile], axis=0) for tile in shifted]
        for quad in range(tiles // 4):
            refs = [tile_of(0, 4 * quad + q) for q in range(4)]
            masked = [refs[q] * (mask_of(0, 4 * quad + q) * scale).astype(BF) for q in range(4)]
            cols = dot_t(order[...], jnp.concatenate(refs, axis=0))
            masked = dot_t(order[...], jnp.concatenate(masked, axis=0))
            for two in range(2):
                lo = two * LANES
                gates, products = [], []
                for side in range(2):
                    w = 4 * quad + 2 * two + side
                    keep = low_half if side == 0 else ~low_half
                    gates.append(jnp.where(keep, cols[:, lo : lo + LANES], 0.0))
                    lhs = jnp.where(keep, masked[:, lo : lo + LANES], 0.0).astype(BF)
                    rhs = jnp.concatenate(shifted[w : w + 3], axis=1)
                    products.append(jnp.dot(lhs, rhs, preferred_element_type=F32))
                place = i * LINE_PARTS + 8 * (tiles - 2 - 4 * quad - 2 * two)
                for t in range(LINE_RUN):
                    row = t * LANES + place
                    r = 8 * t
                    gate_rows[row : row + 16, :] = jnp.concatenate(
                        [gates[1][r : r + 8], gates[0][r : r + 8]], axis=0
                    ).astype(BF)
                    beyond = diagonal >= t
                    both = []
                    for side in (1, 0):
                        turned = [
                            pltpu.roll(
                                products[side][r : r + 8, m * LANES : (m + 1) * LANES],
                                t, 1, stride=LINE_RUN, stride_axis=0,
                            )
                            for m in range(3)
                        ]
                        both.append(
                            jnp.concatenate(
                                [jnp.where(beyond, turned[1], turned[0]), jnp.where(beyond, turned[2], turned[1])],
                                axis=1,
                            )
                        )
                    cost_rows[row : row + 16, :] = jnp.concatenate(both, axis=0).astype(BF)

    x_base = width - 1 - LINE_RUN * (iota((KEYS, LANES), 1) & (LINE_PARTS - 1))
    row = iota((KEYS, LANES), 0)
    reach = jnp.where(row >= 2 * GROUPS, 9, jnp.where(row >= GROUPS, 3, 1))
    room_left = x_base - reach
    room_right = x_base + reach - width
    for two in range(LINE_RUN // 2):
        lo = 2 * two * LANES
        costs = dot_t(flip[...], cost_rows[lo : lo + 2 * LANES, :])
        logits = dot_t(guide[...], gate_rows[lo : lo + 2 * LANES, :])
        for i in range(2):
            t = 2 * two + i
            vol[t] = costs[:, i * LANES : (i + 1) * LANES]
            normalise(logits[:, i * LANES : (i + 1) * LANES], wts, t, room_left, room_right)

    for group in range(GROUPS):
        for at in (group * DGROUP, group * DGROUP + 8):
            v = [vol[t, at : at + 8, :] for t in range(LINE_RUN)]
            for layer in range(LAYERS):
                s = 3**layer
                fresh = []
                for t in range(LINE_RUN):
                    rows = [k * KEYS + layer * GROUPS + group for k in range(3)]
                    w = [wts[t, r : r + 1, :] for r in rows]
                    blk, r = divmod(t + s, LINE_RUN)
                    before = pltpu.roll(v[r], LANES - blk, 1) if blk else v[r]
                    blk, r = divmod(t - s, LINE_RUN)
                    after = pltpu.roll(v[r], -blk, 1) if blk else v[r]
                    fresh.append(w[0] * before + w[1] * v[t] + w[2] * after)
                v = fresh
            for t in range(LINE_RUN):
                done[t, at : at + 8, :] = v[t]

    sub = iota((8, LANES), 0)
    results = []
    for block in range(LINE_RUN // 8):
        totals = jnp.zeros((8, LANES), F32)
        moments = totals
        for s in range(8):
            t = LINE_RUN - 1 - (8 * block + s)
            v = [done[t, 8 * i : 8 * i + 8, :] for i in range(DISP // 8)]
            top = v
            while len(top) > 1:
                top = [jnp.maximum(a, b) for a, b in zip(top[::2], top[1::2])] + top[len(top) & ~1 :]
            top = jnp.max(top[0], axis=0, keepdims=True)
            total = jnp.zeros((8, LANES), F32)
            moment = total
            for i in range(DISP // 8):
                e = jnp.exp(SHARPNESS * (v[i] - top))
                total = total + e
                if i:
                    moment = moment + float(8 * i) * e
            moment = moment + sub.astype(F32) * total
            totals = jnp.where(sub == s, jnp.sum(total, axis=0, keepdims=True), totals)
            moments = jnp.where(sub == s, jnp.sum(moment, axis=0, keepdims=True), moments)
        lane_line = iota((8, LANES), 1) >> 6
        shift = jnp.zeros((8, LANES), F32)
        for i in range(PAIR):
            shift = jnp.where(lane_line == i, offs[i].astype(F32), shift)
        results.append((moments / totals + shift) * (1.0 / DISP))
    vals = jnp.concatenate(results, axis=0)
    lane_line = iota((LINE_RUN, LANES), 1) >> 6
    both = jnp.concatenate([jnp.where(lane_line == i, vals, 0.0) for i in range(PAIR)], axis=0)
    high = both.astype(BF)
    rest = both - high.astype(F32)
    middle = rest.astype(BF)
    low = (rest - middle.astype(F32)).astype(BF)
    pieces = jnp.dot(
        jnp.concatenate([high, middle, low], axis=0), spread[...], preferred_element_type=F32
    )
    size = PAIR * LINE_RUN
    pieces = pieces[:size] + pieces[size : 2 * size] + pieces[2 * size :]
    wanted = iota((LINE_RUN, width), 0) == (iota((LINE_RUN, width), 1) & (LINE_RUN - 1))
    for i in range(PAIR):
        piece = jnp.where(wanted, pieces[i * LINE_RUN : (i + 1) * LINE_RUN], 0.0)
        out[i : i + 1, :] = jnp.sum(piece, axis=0, keepdims=True)


def lines_plan(features, valid_cols, offsets, guide_weight):
    n = lax.axis_size("cols")
    devices = 2 * n
    width = n * BLOCK
    own = features.reshape(devices, PAIR, CHANNELS, BLOCK)
    blocks = lax.all_to_all(own, ("cols", "view"), split_axis=0, concat_axis=0, tiled=True)
    valid = lax.all_gather(valid_cols, "cols", axis=0)
    consts = call(
        constants_kernel,
        [((LANES, LANES), BF), ((DISP, 2 * LANES), BF), ((3 * KEYS, LANES), BF), ((LANES, width), BF)],
        [], 0, (guide_weight,), 1_000_000,
    )
    (rows,) = call(
        lines_kernel,
        [((PAIR, width), F32)],
        [
            pltpu.VMEM((LINE_RUN * LANES, LANES), BF),
            pltpu.VMEM((LINE_RUN * LANES, 2 * LANES), BF),
            pltpu.VMEM((LINE_RUN, DISP, LANES), F32),
            pltpu.VMEM((LINE_RUN, DISP, LANES), F32),
            pltpu.VMEM((LINE_RUN, 3 * KEYS, LANES), F32),
        ],
        1, (offsets, blocks, valid, *consts), 1_000_000_000,
    )
    return lax.all_gather(rows, "view", axis=0, tiled=True)[None]


def on_device(features, valid_cols, offsets, guide_weight):
    n = lax.axis_size("cols")
    lines = features.shape[1]
    if lines == 2 * PAIR * n and n * BLOCK == LINE_RUN * LINE_PARTS:
        return lines_plan(features, valid_cols, offsets, guide_weight)
    return halo_plan(features, valid_cols, offsets, guide_weight)


def solution(mesh):
    return jax.shard_map(
        on_device,
        mesh=mesh,
        in_specs=(
            P("view", ("tiles", "lines"), None, "cols"),
            P(None, ("tiles", "cols")),
            P(("tiles", "lines")),
            P(),
        ),
        out_specs=P(("tiles", "lines"), "cols", None),
        check_vma=False,
    )
```

```python
import functools
import math

import jax
import jax.numpy as jnp
from jax import lax
from jax.experimental import pallas as pl
from jax.experimental.pallas import tpu as pltpu
from jax.sharding import PartitionSpec as P

DISP = 192
DGROUP = 16
GROUPS = DISP // DGROUP
LAYERS = 3
SHARPNESS = 2.0
HALO = 32
LANES = 128
LINES = 8
CHANNELS = 64
BLOCK = 256
SPAN = BLOCK + HALO
PARTS = LANES // LINES
RUN = SPAN // PARTS
KEYS = 40
WIDE = BLOCK + LANES
SEC_ROWS = LINES * CHANNELS
QUAD_ROWS = SEC_ROWS // 2
MASK_AT = QUAD_ROWS + CHANNELS
PAYLOAD = MASK_AT + 16
QUAD = LINES // 2
QUAD_LANES = LANES // 2
PACK = LANES // HALO
CUT = 16

BF = jnp.bfloat16
F32 = jnp.float32


def iota(shape, dim):
    return lax.broadcasted_iota(jnp.int32, shape, dim)


def dot_t(a, b):
    return lax.dot_general(a, b, (((1,), (1,)), ((), ())), preferred_element_type=F32)


def call(kernel, outs, scratch, smem, args, flops=0, space=pltpu.VMEM):
    specs = [pl.BlockSpec(memory_space=pltpu.SMEM)] * smem
    specs += [pl.BlockSpec(memory_space=space)] * (len(args) - smem)
    return pl.pallas_call(
        kernel,
        out_shape=[jax.ShapeDtypeStruct(shape, dtype) for shape, dtype in outs],
        in_specs=specs,
        out_specs=[pl.BlockSpec(memory_space=pltpu.VMEM)] * len(outs),
        scratch_shapes=scratch,
        compiler_params=pltpu.CompilerParams(vmem_limit_bytes=24 * 1024 * 1024),
        cost_estimate=pl.CostEstimate(flops=flops, bytes_accessed=1_000_000, transcendentals=0),
    )(*args)


def spread_guide(guide):
    keys = LAYERS * 3 * GROUPS
    row = iota((3 * KEYS, keys), 0)
    tap = jnp.where(row >= KEYS, 1, 0) + jnp.where(row >= 2 * KEYS, 1, 0)
    row = row - KEYS * tap
    layer = jnp.where(row >= GROUPS, 1, 0) + jnp.where(row >= 2 * GROUPS, 1, 0)
    key = 2 * GROUPS * layer + GROUPS * tap + row
    chosen = jnp.where((iota((3 * KEYS, keys), 1) == key) & (row < 3 * GROUPS), 1.0, 0.0).astype(BF)
    guide_t = dot_t(chosen, guide).astype(BF)
    return jnp.concatenate([guide_t, guide_t], axis=1)


def normalise(z, wts, t, room_left, room_right):
    z = (0.55 + 0.45 * jnp.tanh(0.5 * z)).astype(BF).astype(F32)
    taps = [z[k * KEYS : (k + 1) * KEYS] for k in range(3)]
    scale = 1.0 / (taps[0] + taps[1] + taps[2])
    wts[t, 0:KEYS, :] = jnp.where(room_left >= t, taps[0] * scale, 0.0)
    wts[t, KEYS : 2 * KEYS, :] = taps[1] * scale
    wts[t, 2 * KEYS : 3 * KEYS, :] = jnp.where(room_right < t, taps[2] * scale, 0.0)


def prefetch_kernel(own, valid, guide, own_out, masks, perm, flip, guide_out, valid_in, guide_in, sems):
    copies = [
        pltpu.make_async_copy(src, dst, sems.at[i])
        for i, (src, dst) in enumerate([(own, own_out), (guide, guide_in), (valid, valid_in)])
    ]
    for copy in copies:
        copy.start()
    perm[...] = jnp.where(
        iota((SPAN, WIDE), 1) == WIDE - 1 - iota((SPAN, WIDE), 0), 1.0, 0.0
    ).astype(BF)
    back = 2 * LANES - 1 - iota((DISP, 2 * LANES), 0)
    flip[...] = jnp.where(iota((DISP, 2 * LANES), 1) == back, 1.0, 0.0).astype(BF)

    copies[1].wait()
    guide_out[...] = spread_guide(guide_in[...])
    copies[2].wait()
    masks[...] = valid_in[...].astype(F32)
    copies[0].wait()


def payload_kernel(own, other, masks, first, second, ref_own):
    view = lax.axis_index("view")
    first_view = view == 0
    sec_mask = masks[1:2, :].astype(BF)
    lane = iota((CHANNELS, LANES), 1)
    tails = []
    for line in range(LINES):
        at = view * LINES + line
        mine, theirs = own[at], other[at]
        lo = line * CHANNELS
        dest, start = (first, lo) if line < QUAD else (second, lo - QUAD_ROWS)
        dest[start : start + CHANNELS, :] = jnp.where(first_view, theirs, mine) * sec_mask
        ref = jnp.where(first_view, mine, theirs)
        ref_own[lo : lo + CHANNELS, :] = ref
        tail = ref[:, BLOCK - LANES :].astype(F32)
        slot = line % PACK
        turn = (HALO * (slot + 1)) % LANES
        if turn:
            tail = pltpu.roll(tail, turn, 1)
        if slot:
            tails[-1] = jnp.where(lane >= HALO * slot, tail, tails[-1])
        else:
            tails.append(tail)
    for i, tail in enumerate(tails):
        first[QUAD_ROWS:MASK_AT, i * LANES : (i + 1) * LANES] = tail.astype(BF)
    first[MASK_AT:, :] = jnp.broadcast_to(masks[0:1, :], (16, BLOCK)).astype(BF)


def shifted(left, mine, lo, off):
    ch_lane = iota((CHANNELS, LANES), 1)
    tiles = [
        src[lo : lo + CHANNELS, i * LANES : (i + 1) * LANES].astype(F32)
        for src in (left, mine)
        for i in range(2)
    ]
    tiles = [pltpu.roll(tile, off, 1) for tile in tiles]
    tiles = [jnp.where(ch_lane < off, tiles[max(i - 1, 0)], tiles[i]).astype(BF) for i in range(4)]
    return jnp.concatenate(tiles, axis=1)


def line_costs(lhs, rhs, slot, skew, cost_rows):
    diagonal = iota((8, LANES), 1) - iota((8, LANES), 0)
    for chunk in range(3):
        rows = min(LANES, SPAN - chunk * LANES)
        first = max(1 - chunk, 0)
        last = 3 - chunk
        products = jnp.dot(
            lhs[chunk * LANES : chunk * LANES + rows],
            rhs[:, first * LANES : (last + 1) * LANES],
            preferred_element_type=F32,
        )
        for j in range(rows // 8):
            tiles = [
                pltpu.roll(
                    products[8 * j : 8 * j + 8, i * LANES : (i + 1) * LANES],
                    8 * j, 1, stride=1, stride_axis=0,
                )
                for i in range(last + 1 - first)
            ]
            if len(tiles) < 3:
                tiles = [tiles[0]] + tiles
            beyond = diagonal >= 8 * j
            at = chunk * LANES + 8 * j
            skew[slot, 0, at : at + 8, :] = jnp.where(beyond, tiles[1], tiles[0])
            skew[slot, 1, at : at + 8, :] = jnp.where(beyond, tiles[2], tiles[1])
    for t in range(RUN):
        at = t * QUAD_LANES + slot * PARTS
        for v in range(2):
            cost_rows[at : at + PARTS, v * LANES : (v + 1) * LANES] = skew[
                slot, v, pl.ds(t, PARTS, stride=RUN), :
            ].astype(BF)


def early_kernel(
    offsets, ref_own, mine, left, masks, perm, guide, wts, cost_rows, lhs_out,
    ref_rows, ref_cols, gate_rows, skew
):
    base = lax.axis_index("view") * LINES
    low = jnp.where(lax.axis_index("cols") == 0, HALO, 0)
    for line in range(LINES):
        lo = line * CHANNELS
        ref_rows[lo : lo + CHANNELS, LANES:] = ref_own[lo : lo + CHANNELS, :]
        half = line // PACK
        packed = left[QUAD_ROWS:MASK_AT, half * LANES : (half + 1) * LANES].astype(F32)
        turn = (LANES - HALO) - HALO * (line % PACK)
        if turn:
            packed = pltpu.roll(packed, turn, 1)
        ref_rows[lo : lo + CHANNELS, :LANES] = packed.astype(BF)

    mask_left = left[MASK_AT : MASK_AT + 1, BLOCK - LANES :].astype(F32)
    ref_mask = jnp.concatenate([mask_left, masks[0:1, :]], axis=1)
    ref_mask = jnp.broadcast_to(ref_mask * (1.0 / math.sqrt(CHANNELS)), (LANES, WIDE))
    mask_cols = dot_t(perm[...], ref_mask.astype(BF))
    half_lane = iota((PARTS, LANES), 1) < CHANNELS
    span_lane = iota((SPAN, LANES), 1) < CHANNELS

    for quad in range(LINES // QUAD):
        ref_t = dot_t(perm[...], ref_rows[quad * QUAD_ROWS : (quad + 1) * QUAD_ROWS, :])
        for pair in range(QUAD // 2):
            cols = ref_t[:, pair * LANES : (pair + 1) * LANES]
            slot = quad * 2 + pair
            ref_cols[slot] = cols
            masked = cols * mask_cols
            if quad == 0:
                rhs = jnp.concatenate(
                    [
                        shifted(left, mine, line * CHANNELS, offsets[base + line])
                        for line in (2 * slot, 2 * slot + 1)
                    ],
                    axis=0,
                )
            for side in range(2):
                line = 2 * slot + side
                for t in range(RUN):
                    picked = ref_cols[slot, pl.ds(t, PARTS, stride=RUN), :]
                    picked = jnp.where(half_lane if side == 0 else ~half_lane, picked, 0.0)
                    at = t * LANES + line * PARTS
                    gate_rows[at : at + PARTS, :] = picked.astype(BF)
                lhs = jnp.where(span_lane if side == 0 else ~span_lane, masked, 0.0).astype(BF)
                if quad == 0:
                    line_costs(lhs, rhs, line, skew, cost_rows)
                else:
                    lhs_out[line - QUAD] = lhs

    place = iota((KEYS, LANES), 1)
    x_base = SPAN - 1 - RUN * (place & (PARTS - 1))
    row = iota((KEYS, LANES), 0)
    reach = jnp.where(row >= 2 * GROUPS, 9, jnp.where(row >= GROUPS, 3, 1))
    room_left = x_base - reach - low
    room_right = x_base + reach - SPAN
    for two in range(RUN // 2):
        at = 2 * two * LANES
        logits = dot_t(guide[...], gate_rows[at : at + 2 * LANES, :])
        for i in range(2):
            t = 2 * two + i
            normalise(logits[:, i * LANES : (i + 1) * LANES], wts, t, room_left, room_right)


def late_kernel(
    offsets, mine, left, lhs, early_rows, wts, flip, out, skew, cost_rows, vol, vals, turned
):
    base = lax.axis_index("view") * LINES
    for pair in range(QUAD // 2):
        rhs = jnp.concatenate(
            [
                shifted(left, mine, line * CHANNELS, offsets[base + QUAD + line])
                for line in (2 * pair, 2 * pair + 1)
            ],
            axis=0,
        )
        for line in (2 * pair, 2 * pair + 1):
            line_costs(lhs[line], rhs, line, skew, cost_rows)

    for two in range(RUN // 2):
        rows = []
        for t in (2 * two, 2 * two + 1):
            for part in (early_rows, cost_rows):
                rows.append(part[t * QUAD_LANES : (t + 1) * QUAD_LANES, :])
        costs = dot_t(flip[...], jnp.concatenate(rows, axis=0))
        vol[2 * two] = costs[:, :LANES]
        vol[2 * two + 1] = costs[:, LANES:]

    def aggregate(group, carry):
        for half in range(2):
            at = pl.multiple_of(group * DGROUP + half * 8, 8)
            v = [vol[t, pl.ds(at, 8), :] for t in range(RUN)]
            for layer in range(LAYERS):
                s = 3**layer
                before = [v[t + s] if t + s < RUN else pltpu.roll(v[t + s - RUN], LANES - 1, 1) for t in range(RUN)]
                after = [v[t - s] if t >= s else pltpu.roll(v[t - s + RUN], 1, 1) for t in range(RUN)]
                fresh = []
                for t in range(RUN):
                    w = [wts[t, pl.ds(k * KEYS + layer * GROUPS + group, 1), :] for k in range(3)]
                    fresh.append(w[0] * before[t] + w[1] * v[t] + w[2] * after[t])
                v = fresh
            for t in range(RUN):
                vol[t, pl.ds(at, 8), :] = v[t]
        return carry

    lax.fori_loop(0, GROUPS, aggregate, 0)

    vals[...] = jnp.zeros((LANES, LANES), F32)
    sub = iota((8, LANES), 0).astype(F32)
    line_of = iota((1, LANES), 1) >> 4
    offs = jnp.zeros((1, LANES), F32)
    for line in range(LINES):
        offs = jnp.where(line_of == line, offsets[base + line].astype(F32), offs)

    def softmax(t, carry):
        v = [vol[t, 8 * i : 8 * i + 8, :] for i in range(DISP // 8)]
        top = v
        while len(top) > 1:
            top = [jnp.maximum(a, b) for a, b in zip(top[::2], top[1::2])] + top[len(top) & ~1 :]
        top = jnp.max(top[0], axis=0, keepdims=True)
        e = [jnp.exp(SHARPNESS * (a - top)) for a in v]
        total = e[0]
        moment = jnp.zeros((8, LANES), F32)
        for i in range(1, DISP // 8):
            total = total + e[i]
            moment = moment + float(8 * i) * e[i]
        moment = jnp.sum(moment + sub * total, axis=0, keepdims=True)
        total = jnp.sum(total, axis=0, keepdims=True)
        vals[pl.ds(RUN - 1 - t, 1), :] = (moment / total + offs) * (1.0 / DISP)
        return carry

    lax.fori_loop(0, RUN, softmax, 0)

    turned[...] = jnp.transpose(vals[...])
    lane = iota((8, LANES), 1)
    result = [jnp.zeros((8, LANES), F32) for _ in range(WIDE // LANES)]
    for part in range(PARTS):
        piece = turned[pl.ds(part, LINES, stride=PARTS), :]
        start = (RUN * (PARTS - 1 - part) - HALO) % WIDE
        tile, turn = divmod(start, LANES)
        if turn:
            piece = pltpu.roll(piece, turn, 1)
        if turn + RUN > LANES:
            after = (tile + 1) % len(result)
            result[after] = result[after] + jnp.where(lane < turn, piece, 0.0)
            piece = jnp.where(lane >= turn, piece, 0.0)
        result[tile] = result[tile] + piece
    for tile, value in enumerate(result):
        out[:, tile * LANES : (tile + 1) * LANES] = value


def join(pieces, sub, n):
    block = lax.axis_index("cols")
    pieces = pieces.reshape(n, 2, LINES, WIDE)
    start = (0, block // (n // 2), (block % (n // 2)) * sub, 0)
    pieces = lax.dynamic_slice(pieces, start, (n, 1, sub, WIDE))[:, 0]
    main = pieces[:, :, :BLOCK]
    tail = jnp.pad(pieces[1:, :, BLOCK:], ((0, 1), (0, 0), (LANES, 0)))
    place = (n, sub, BLOCK)
    keep = (iota(place, 2) < BLOCK - CUT) | (iota(place, 0) == n - 1)
    joined = jnp.where(keep, main, tail)
    return jnp.transpose(joined, (1, 0, 2)).reshape(1, sub, n * BLOCK)


def halo_plan(features, valid_cols, offsets, guide_weight):
    own = features[0]
    n = lax.axis_size("cols")
    right = [(c, c + 1) for c in range(n - 1)]
    other = lax.ppermute(own, "view", [(0, 1), (1, 0)])
    near, masks, perm, flip, guide = call(
        prefetch_kernel,
        [(own.shape, BF), (valid_cols.shape, F32), ((SPAN, WIDE), BF), ((DISP, 2 * LANES), BF), ((3 * KEYS, LANES), BF)],
        [pltpu.VMEM(valid_cols.shape, jnp.int32), pltpu.VMEM(guide_weight.shape, BF), pltpu.SemaphoreType.DMA((3,))],
        0, (own, valid_cols, guide_weight), 100_000_000, pl.ANY,
    )
    first, second, ref_own = call(
        payload_kernel,
        [((PAYLOAD, BLOCK), BF), ((QUAD_ROWS, BLOCK), BF), ((SEC_ROWS, BLOCK), BF)],
        [], 0, (near, other, masks),
    )
    left_first = lax.ppermute(first, "cols", right)
    left_second = lax.ppermute(second, "cols", right)
    quad_rows = (RUN * QUAD_LANES, 2 * LANES)
    skew = pltpu.VMEM((QUAD, 2, SPAN, LANES), F32)
    square = pltpu.VMEM((LANES, LANES), F32)
    wts, early_rows, lhs = call(
        early_kernel,
        [((RUN, 3 * KEYS, LANES), F32), (quad_rows, BF), ((QUAD, SPAN, LANES), BF)],
        [pltpu.VMEM((SEC_ROWS, WIDE), BF), pltpu.VMEM((QUAD, SPAN, LANES), F32), pltpu.VMEM((RUN * LANES, LANES), BF), skew],
        1, (offsets, ref_own, first, left_first, masks, perm, guide), 1_000_000_000,
    )
    (result,) = call(
        late_kernel,
        [((LINES, WIDE), F32)],
        [skew, pltpu.VMEM(quad_rows, BF), pltpu.VMEM((RUN, DISP, LANES), F32), square, square],
        1, (offsets, second, left_second, lhs, early_rows, wts, flip), 1_000_000_000,
    )
    copies = jnp.broadcast_to(result[None], (2 * n, LINES, WIDE))
    pieces = lax.all_to_all(copies, ("cols", "view"), split_axis=0, concat_axis=0, tiled=True)
    return join(pieces, own.shape[0] // n, n)


LINE_RUN = 16
PAIR = 2
LINE_PARTS = LANES // PAIR


def constants_kernel(guide, order, flip, guide_out, spread):
    row = iota((LANES, LANES), 0)
    from_lane = LANES - 1 - LINE_RUN * (row & 7) - (row >> 3)
    order[...] = jnp.where(iota((LANES, LANES), 1) == from_lane, 1.0, 0.0).astype(BF)
    back = 2 * LANES - 1 - iota((DISP, 2 * LANES), 0)
    flip[...] = jnp.where(iota((DISP, 2 * LANES), 1) == back, 1.0, 0.0).astype(BF)
    guide_out[...] = spread_guide(guide[...])
    block_of = LINE_PARTS - 1 - (iota(spread.shape, 1) >> 4)
    here = (iota(spread.shape, 0) & (LINE_PARTS - 1)) == block_of
    spread[...] = jnp.where(here, 1.0, 0.0).astype(BF)


def lines_kernel(
    offsets, blocks, order, flip, guide, spread, *rest
):
    near, (out, valid, gate_rows, cost_rows, vol, done, wts) = rest[:-7], rest[-7:]
    tiles = blocks.shape[0]
    width = tiles * LANES
    for k, masks in enumerate(near):
        valid[lax.axis_index("cols") ^ k] = masks[...].astype(F32)
    at = lax.axis_index("cols") * (PAIR * offsets.shape[0] // tiles) + PAIR * lax.axis_index("view")
    offs = [offsets[at + i] for i in range(PAIR)]
    ch_lane = iota((CHANNELS, LANES), 1)
    diagonal = iota((8, LANES), 1) - LINE_RUN * iota((8, LANES), 0)
    low_half = iota((LANES, LANES), 1) < CHANNELS
    scale = 1.0 / math.sqrt(CHANNELS)
    empty = jnp.zeros((CHANNELS, LANES), F32)

    def mask_of(view, w):
        lo = (w % 2) * LANES
        return valid[w // 2, view : view + 1, lo : lo + LANES]

    for i in range(PAIR):

        def tile_of(view, w):
            lo = (w % 2) * LANES
            return blocks[2 * (w // 2) + view, i, :, lo : lo + LANES]

        off = offs[i]
        rolled = [pltpu.roll(tile_of(1, w).astype(F32) * mask_of(1, w), off, 1) for w in range(tiles)]
        shifted = [empty.astype(BF)] * 2
        for w in range(tiles):
            shifted.append(jnp.where(ch_lane < off, rolled[w - 1] if w else empty, rolled[w]).astype(BF))
        shifted = [jnp.concatenate([tile, tile], axis=0) for tile in shifted]
        for quad in range(tiles // 4):
            refs = [tile_of(0, 4 * quad + q) for q in range(4)]
            masked = [refs[q] * (mask_of(0, 4 * quad + q) * scale).astype(BF) for q in range(4)]
            cols = dot_t(order[...], jnp.concatenate(refs, axis=0))
            masked = dot_t(order[...], jnp.concatenate(masked, axis=0))
            for two in range(2):
                lo = two * LANES
                gates, products = [], []
                for side in range(2):
                    w = 4 * quad + 2 * two + side
                    keep = low_half if side == 0 else ~low_half
                    gates.append(jnp.where(keep, cols[:, lo : lo + LANES], 0.0))
                    lhs = jnp.where(keep, masked[:, lo : lo + LANES], 0.0).astype(BF)
                    rhs = jnp.concatenate(shifted[w : w + 3], axis=1)
                    products.append(jnp.dot(lhs, rhs, preferred_element_type=F32))
                place = i * LINE_PARTS + 8 * (tiles - 2 - 4 * quad - 2 * two)
                for t in range(LINE_RUN):
                    row = t * LANES + place
                    r = 8 * t
                    gate_rows[row : row + 16, :] = jnp.concatenate(
                        [gates[1][r : r + 8], gates[0][r : r + 8]], axis=0
                    ).astype(BF)
                    beyond = diagonal >= t
                    both = []
                    for side in (1, 0):
                        turned = [
                            pltpu.roll(
                                products[side][r : r + 8, m * LANES : (m + 1) * LANES],
                                t, 1, stride=LINE_RUN, stride_axis=0,
                            )
                            for m in range(3)
                        ]
                        both.append(
                            jnp.concatenate(
                                [jnp.where(beyond, turned[1], turned[0]), jnp.where(beyond, turned[2], turned[1])],
                                axis=1,
                            )
                        )
                    cost_rows[row : row + 16, :] = jnp.concatenate(both, axis=0).astype(BF)

    x_base = width - 1 - LINE_RUN * (iota((KEYS, LANES), 1) & (LINE_PARTS - 1))
    row = iota((KEYS, LANES), 0)
    reach = jnp.where(row >= 2 * GROUPS, 9, jnp.where(row >= GROUPS, 3, 1))
    room_left = x_base - reach
    room_right = x_base + reach - width
    for two in range(LINE_RUN // 2):
        lo = 2 * two * LANES
        costs = dot_t(flip[...], cost_rows[lo : lo + 2 * LANES, :])
        logits = dot_t(guide[...], gate_rows[lo : lo + 2 * LANES, :])
        for i in range(2):
            t = 2 * two + i
            vol[t] = costs[:, i * LANES : (i + 1) * LANES]
            normalise(logits[:, i * LANES : (i + 1) * LANES], wts, t, room_left, room_right)

    for group in range(GROUPS):
        for at in (group * DGROUP, group * DGROUP + 8):
            v = [vol[t, at : at + 8, :] for t in range(LINE_RUN)]
            for layer in range(LAYERS):
                s = 3**layer
                fresh = []
                for t in range(LINE_RUN):
                    rows = [k * KEYS + layer * GROUPS + group for k in range(3)]
                    w = [wts[t, r : r + 1, :] for r in rows]
                    blk, r = divmod(t + s, LINE_RUN)
                    before = pltpu.roll(v[r], LANES - blk, 1) if blk else v[r]
                    blk, r = divmod(t - s, LINE_RUN)
                    after = pltpu.roll(v[r], -blk, 1) if blk else v[r]
                    fresh.append(w[0] * before + w[1] * v[t] + w[2] * after)
                v = fresh
            for t in range(LINE_RUN):
                done[t, at : at + 8, :] = v[t]

    sub = iota((8, LANES), 0)
    results = []
    for block in range(LINE_RUN // 8):
        totals = jnp.zeros((8, LANES), F32)
        moments = totals
        for s in range(8):
            t = LINE_RUN - 1 - (8 * block + s)
            v = [done[t, 8 * i : 8 * i + 8, :] for i in range(DISP // 8)]
            top = v
            while len(top) > 1:
                top = [jnp.maximum(a, b) for a, b in zip(top[::2], top[1::2])] + top[len(top) & ~1 :]
            top = jnp.max(top[0], axis=0, keepdims=True)
            total = jnp.zeros((8, LANES), F32)
            moment = total
            for i in range(DISP // 8):
                e = jnp.exp(SHARPNESS * (v[i] - top))
                total = total + e
                if i:
                    moment = moment + float(8 * i) * e
            moment = moment + sub.astype(F32) * total
            totals = jnp.where(sub == s, jnp.sum(total, axis=0, keepdims=True), totals)
            moments = jnp.where(sub == s, jnp.sum(moment, axis=0, keepdims=True), moments)
        lane_line = iota((8, LANES), 1) >> 6
        shift = jnp.zeros((8, LANES), F32)
        for i in range(PAIR):
            shift = jnp.where(lane_line == i, offs[i].astype(F32), shift)
        results.append((moments / totals + shift) * (1.0 / DISP))
    vals = jnp.concatenate(results, axis=0)
    lane_line = iota((LINE_RUN, LANES), 1) >> 6
    both = jnp.concatenate([jnp.where(lane_line == i, vals, 0.0) for i in range(PAIR)], axis=0)
    high = both.astype(BF)
    rest = both - high.astype(F32)
    middle = rest.astype(BF)
    low = (rest - middle.astype(F32)).astype(BF)
    pieces = jnp.dot(
        jnp.concatenate([high, middle, low], axis=0), spread[...], preferred_element_type=F32
    )
    size = PAIR * LINE_RUN
    pieces = pieces[:size] + pieces[size : 2 * size] + pieces[2 * size :]
    wanted = iota((LINE_RUN, width), 0) == (iota((LINE_RUN, width), 1) & (LINE_RUN - 1))
    for i in range(PAIR):
        piece = jnp.where(wanted, pieces[i * LINE_RUN : (i + 1) * LINE_RUN], 0.0)
        out[i : i + 1, :] = jnp.sum(piece, axis=0, keepdims=True)


def lines_plan(features, valid_cols, offsets, guide_weight):
    n = lax.axis_size("cols")
    devices = 2 * n
    width = n * BLOCK
    own = features.reshape(devices, PAIR, CHANNELS, BLOCK)
    blocks = lax.all_to_all(own, ("cols", "view"), split_axis=0, concat_axis=0, tiled=True)
    near = [valid_cols]
    for k in range(1, n):
        near.append(lax.ppermute(valid_cols, "cols", [(c, c ^ k) for c in range(n)]))
    consts = call(
        constants_kernel,
        [((LANES, LANES), BF), ((DISP, 2 * LANES), BF), ((3 * KEYS, LANES), BF), ((LANES, width), BF)],
        [], 0, (guide_weight,), 1_000_000,
    )
    (rows,) = call(
        lines_kernel,
        [((PAIR, width), F32)],
        [
            pltpu.VMEM((n,) + valid_cols.shape, F32),
            pltpu.VMEM((LINE_RUN * LANES, LANES), BF),
            pltpu.VMEM((LINE_RUN * LANES, 2 * LANES), BF),
            pltpu.VMEM((LINE_RUN, DISP, LANES), F32),
            pltpu.VMEM((LINE_RUN, DISP, LANES), F32),
            pltpu.VMEM((LINE_RUN, 3 * KEYS, LANES), F32),
        ],
        1, (offsets, blocks, *consts, *near), 1_000_000_000,
    )
    return lax.all_gather(rows, "view", axis=0, tiled=True)[None]


def on_device(features, valid_cols, offsets, guide_weight):
    n = lax.axis_size("cols")
    lines = features.shape[1]
    if lines == 2 * PAIR * n and n * BLOCK == LINE_RUN * LINE_PARTS:
        return lines_plan(features, valid_cols, offsets, guide_weight)
    return halo_plan(features, valid_cols, offsets, guide_weight)


def solution(mesh):
    return jax.shard_map(
        on_device,
        mesh=mesh,
        in_specs=(
            P("view", ("tiles", "lines"), None, "cols"),
            P(None, ("tiles", "cols")),
            P(("tiles", "lines")),
            P(),
        ),
        out_specs=P(("tiles", "lines"), "cols", None),
        check_vma=False,
    )
```

```python
import functools
import math

import jax
import jax.numpy as jnp
from jax import lax
from jax.experimental import pallas as pl
from jax.experimental.pallas import tpu as pltpu
from jax.sharding import PartitionSpec as P

DISP = 192
DGROUP = 16
GROUPS = DISP // DGROUP
LAYERS = 3
SHARPNESS = 2.0
HALO = 32
LANES = 128
LINES = 8
CHANNELS = 64
BLOCK = 256
SPAN = BLOCK + HALO
PARTS = LANES // LINES
RUN = SPAN // PARTS
KEYS = 40
WIDE = BLOCK + LANES
SEC_ROWS = LINES * CHANNELS
QUAD_ROWS = SEC_ROWS // 2
MASK_AT = QUAD_ROWS + CHANNELS
PAYLOAD = MASK_AT + 16
QUAD = LINES // 2
QUAD_LANES = LANES // 2
PACK = LANES // HALO
CUT = 16

BF = jnp.bfloat16
F32 = jnp.float32


def iota(shape, dim):
    return lax.broadcasted_iota(jnp.int32, shape, dim)


def dot_t(a, b):
    return lax.dot_general(a, b, (((1,), (1,)), ((), ())), preferred_element_type=F32)


def call(kernel, outs, scratch, smem, args, flops=0, space=pltpu.VMEM, limit=24, to=None):
    specs = [pl.BlockSpec(memory_space=pltpu.SMEM)] * smem
    specs += [pl.BlockSpec(memory_space=space)] * (len(args) - smem)
    return pl.pallas_call(
        kernel,
        out_shape=[jax.ShapeDtypeStruct(shape, dtype) for shape, dtype in outs],
        in_specs=specs,
        out_specs=[pl.BlockSpec(memory_space=to or space)] * len(outs),
        scratch_shapes=scratch,
        compiler_params=pltpu.CompilerParams(vmem_limit_bytes=limit * 1024 * 1024),
        cost_estimate=pl.CostEstimate(flops=flops, bytes_accessed=1_000_000, transcendentals=0),
    )(*args)


def spread_guide(guide):
    keys = LAYERS * 3 * GROUPS
    row = iota((3 * KEYS, keys), 0)
    tap = jnp.where(row >= KEYS, 1, 0) + jnp.where(row >= 2 * KEYS, 1, 0)
    row = row - KEYS * tap
    layer = jnp.where(row >= GROUPS, 1, 0) + jnp.where(row >= 2 * GROUPS, 1, 0)
    key = 2 * GROUPS * layer + GROUPS * tap + row
    chosen = jnp.where((iota((3 * KEYS, keys), 1) == key) & (row < 3 * GROUPS), 1.0, 0.0).astype(BF)
    guide_t = dot_t(chosen, guide).astype(BF)
    return jnp.concatenate([guide_t, guide_t], axis=1)


def normalise(z, wts, t, room_left, room_right):
    z = (0.55 + 0.45 * jnp.tanh(0.5 * z)).astype(BF).astype(F32)
    taps = [z[k * KEYS : (k + 1) * KEYS] for k in range(3)]
    scale = 1.0 / (taps[0] + taps[1] + taps[2])
    wts[t, 0:KEYS, :] = jnp.where(room_left >= t, taps[0] * scale, 0.0)
    wts[t, KEYS : 2 * KEYS, :] = taps[1] * scale
    wts[t, 2 * KEYS : 3 * KEYS, :] = jnp.where(room_right < t, taps[2] * scale, 0.0)


def prefetch_kernel(own, valid, guide, own_out, masks, perm, flip, guide_out, valid_in, guide_in, sems):
    copies = [
        pltpu.make_async_copy(src, dst, sems.at[i])
        for i, (src, dst) in enumerate([(own, own_out), (guide, guide_in), (valid, valid_in)])
    ]
    for copy in copies:
        copy.start()
    perm[...] = jnp.where(
        iota((SPAN, WIDE), 1) == WIDE - 1 - iota((SPAN, WIDE), 0), 1.0, 0.0
    ).astype(BF)
    back = 2 * LANES - 1 - iota((DISP, 2 * LANES), 0)
    flip[...] = jnp.where(iota((DISP, 2 * LANES), 1) == back, 1.0, 0.0).astype(BF)

    copies[1].wait()
    guide_out[...] = spread_guide(guide_in[...])
    copies[2].wait()
    masks[...] = valid_in[...].astype(F32)
    copies[0].wait()


def payload_kernel(own, other, masks, first, second, ref_own):
    view = lax.axis_index("view")
    first_view = view == 0
    sec_mask = masks[1:2, :].astype(BF)
    lane = iota((CHANNELS, LANES), 1)
    tails = []
    for line in range(LINES):
        at = view * LINES + line
        mine, theirs = own[at], other[at]
        lo = line * CHANNELS
        dest, start = (first, lo) if line < QUAD else (second, lo - QUAD_ROWS)
        dest[start : start + CHANNELS, :] = jnp.where(first_view, theirs, mine) * sec_mask
        ref = jnp.where(first_view, mine, theirs)
        ref_own[lo : lo + CHANNELS, :] = ref
        tail = ref[:, BLOCK - LANES :].astype(F32)
        slot = line % PACK
        turn = (HALO * (slot + 1)) % LANES
        if turn:
            tail = pltpu.roll(tail, turn, 1)
        if slot:
            tails[-1] = jnp.where(lane >= HALO * slot, tail, tails[-1])
        else:
            tails.append(tail)
    for i, tail in enumerate(tails):
        first[QUAD_ROWS:MASK_AT, i * LANES : (i + 1) * LANES] = tail.astype(BF)
    first[MASK_AT:, :] = jnp.broadcast_to(masks[0:1, :], (16, BLOCK)).astype(BF)


def shifted(left, mine, lo, off):
    ch_lane = iota((CHANNELS, LANES), 1)
    tiles = [
        src[lo : lo + CHANNELS, i * LANES : (i + 1) * LANES].astype(F32)
        for src in (left, mine)
        for i in range(2)
    ]
    tiles = [pltpu.roll(tile, off, 1) for tile in tiles]
    tiles = [jnp.where(ch_lane < off, tiles[max(i - 1, 0)], tiles[i]).astype(BF) for i in range(4)]
    return jnp.concatenate(tiles, axis=1)


def line_costs(lhs, rhs, slot, skew, cost_rows):
    diagonal = iota((8, LANES), 1) - iota((8, LANES), 0)
    for chunk in range(3):
        rows = min(LANES, SPAN - chunk * LANES)
        first = max(1 - chunk, 0)
        last = 3 - chunk
        products = jnp.dot(
            lhs[chunk * LANES : chunk * LANES + rows],
            rhs[:, first * LANES : (last + 1) * LANES],
            preferred_element_type=F32,
        )
        for j in range(rows // 8):
            tiles = [
                pltpu.roll(
                    products[8 * j : 8 * j + 8, i * LANES : (i + 1) * LANES],
                    8 * j, 1, stride=1, stride_axis=0,
                )
                for i in range(last + 1 - first)
            ]
            if len(tiles) < 3:
                tiles = [tiles[0]] + tiles
            beyond = diagonal >= 8 * j
            at = chunk * LANES + 8 * j
            skew[slot, 0, at : at + 8, :] = jnp.where(beyond, tiles[1], tiles[0])
            skew[slot, 1, at : at + 8, :] = jnp.where(beyond, tiles[2], tiles[1])
    for t in range(RUN):
        at = t * QUAD_LANES + slot * PARTS
        for v in range(2):
            cost_rows[at : at + PARTS, v * LANES : (v + 1) * LANES] = skew[
                slot, v, pl.ds(t, PARTS, stride=RUN), :
            ].astype(BF)


def early_kernel(
    offsets, ref_own, mine, left, masks, perm, guide, wts, cost_rows, lhs_out,
    ref_rows, ref_cols, gate_rows, skew
):
    base = lax.axis_index("view") * LINES
    low = jnp.where(lax.axis_index("cols") == 0, HALO, 0)
    for line in range(LINES):
        lo = line * CHANNELS
        ref_rows[lo : lo + CHANNELS, LANES:] = ref_own[lo : lo + CHANNELS, :]
        half = line // PACK
        packed = left[QUAD_ROWS:MASK_AT, half * LANES : (half + 1) * LANES].astype(F32)
        turn = (LANES - HALO) - HALO * (line % PACK)
        if turn:
            packed = pltpu.roll(packed, turn, 1)
        ref_rows[lo : lo + CHANNELS, :LANES] = packed.astype(BF)

    mask_left = left[MASK_AT : MASK_AT + 1, BLOCK - LANES :].astype(F32)
    ref_mask = jnp.concatenate([mask_left, masks[0:1, :]], axis=1)
    ref_mask = jnp.broadcast_to(ref_mask * (1.0 / math.sqrt(CHANNELS)), (LANES, WIDE))
    mask_cols = dot_t(perm[...], ref_mask.astype(BF))
    half_lane = iota((PARTS, LANES), 1) < CHANNELS
    span_lane = iota((SPAN, LANES), 1) < CHANNELS

    for quad in range(LINES // QUAD):
        ref_t = dot_t(perm[...], ref_rows[quad * QUAD_ROWS : (quad + 1) * QUAD_ROWS, :])
        for pair in range(QUAD // 2):
            cols = ref_t[:, pair * LANES : (pair + 1) * LANES]
            slot = quad * 2 + pair
            ref_cols[slot] = cols
            masked = cols * mask_cols
            if quad == 0:
                rhs = jnp.concatenate(
                    [
                        shifted(left, mine, line * CHANNELS, offsets[base + line])
                        for line in (2 * slot, 2 * slot + 1)
                    ],
                    axis=0,
                )
            for side in range(2):
                line = 2 * slot + side
                for t in range(RUN):
                    picked = ref_cols[slot, pl.ds(t, PARTS, stride=RUN), :]
                    picked = jnp.where(half_lane if side == 0 else ~half_lane, picked, 0.0)
                    at = t * LANES + line * PARTS
                    gate_rows[at : at + PARTS, :] = picked.astype(BF)
                lhs = jnp.where(span_lane if side == 0 else ~span_lane, masked, 0.0).astype(BF)
                if quad == 0:
                    line_costs(lhs, rhs, line, skew, cost_rows)
                else:
                    lhs_out[line - QUAD] = lhs

    place = iota((KEYS, LANES), 1)
    x_base = SPAN - 1 - RUN * (place & (PARTS - 1))
    row = iota((KEYS, LANES), 0)
    reach = jnp.where(row >= 2 * GROUPS, 9, jnp.where(row >= GROUPS, 3, 1))
    room_left = x_base - reach - low
    room_right = x_base + reach - SPAN
    for two in range(RUN // 2):
        at = 2 * two * LANES
        logits = dot_t(guide[...], gate_rows[at : at + 2 * LANES, :])
        for i in range(2):
            t = 2 * two + i
            normalise(logits[:, i * LANES : (i + 1) * LANES], wts, t, room_left, room_right)


def late_kernel(
    offsets, mine, left, lhs, early_rows, wts, flip, out, skew, cost_rows, vol, vals, turned
):
    base = lax.axis_index("view") * LINES
    for pair in range(QUAD // 2):
        rhs = jnp.concatenate(
            [
                shifted(left, mine, line * CHANNELS, offsets[base + QUAD + line])
                for line in (2 * pair, 2 * pair + 1)
            ],
            axis=0,
        )
        for line in (2 * pair, 2 * pair + 1):
            line_costs(lhs[line], rhs, line, skew, cost_rows)

    for two in range(RUN // 2):
        rows = []
        for t in (2 * two, 2 * two + 1):
            for part in (early_rows, cost_rows):
                rows.append(part[t * QUAD_LANES : (t + 1) * QUAD_LANES, :])
        costs = dot_t(flip[...], jnp.concatenate(rows, axis=0))
        vol[2 * two] = costs[:, :LANES]
        vol[2 * two + 1] = costs[:, LANES:]

    def aggregate(group, carry):
        for half in range(2):
            at = pl.multiple_of(group * DGROUP + half * 8, 8)
            v = [vol[t, pl.ds(at, 8), :] for t in range(RUN)]
            for layer in range(LAYERS):
                s = 3**layer
                before = [v[t + s] if t + s < RUN else pltpu.roll(v[t + s - RUN], LANES - 1, 1) for t in range(RUN)]
                after = [v[t - s] if t >= s else pltpu.roll(v[t - s + RUN], 1, 1) for t in range(RUN)]
                fresh = []
                for t in range(RUN):
                    w = [wts[t, pl.ds(k * KEYS + layer * GROUPS + group, 1), :] for k in range(3)]
                    fresh.append(w[0] * before[t] + w[1] * v[t] + w[2] * after[t])
                v = fresh
            for t in range(RUN):
                vol[t, pl.ds(at, 8), :] = v[t]
        return carry

    lax.fori_loop(0, GROUPS, aggregate, 0)

    vals[...] = jnp.zeros((LANES, LANES), F32)
    sub = iota((8, LANES), 0).astype(F32)
    line_of = iota((1, LANES), 1) >> 4
    offs = jnp.zeros((1, LANES), F32)
    for line in range(LINES):
        offs = jnp.where(line_of == line, offsets[base + line].astype(F32), offs)

    def softmax(t, carry):
        v = [vol[t, 8 * i : 8 * i + 8, :] for i in range(DISP // 8)]
        top = v
        while len(top) > 1:
            top = [jnp.maximum(a, b) for a, b in zip(top[::2], top[1::2])] + top[len(top) & ~1 :]
        top = jnp.max(top[0], axis=0, keepdims=True)
        e = [jnp.exp(SHARPNESS * (a - top)) for a in v]
        total = e[0]
        moment = jnp.zeros((8, LANES), F32)
        for i in range(1, DISP // 8):
            total = total + e[i]
            moment = moment + float(8 * i) * e[i]
        moment = jnp.sum(moment + sub * total, axis=0, keepdims=True)
        total = jnp.sum(total, axis=0, keepdims=True)
        vals[pl.ds(RUN - 1 - t, 1), :] = (moment / total + offs) * (1.0 / DISP)
        return carry

    lax.fori_loop(0, RUN, softmax, 0)

    turned[...] = jnp.transpose(vals[...])
    lane = iota((8, LANES), 1)
    result = [jnp.zeros((8, LANES), F32) for _ in range(WIDE // LANES)]
    for part in range(PARTS):
        piece = turned[pl.ds(part, LINES, stride=PARTS), :]
        start = (RUN * (PARTS - 1 - part) - HALO) % WIDE
        tile, turn = divmod(start, LANES)
        if turn:
            piece = pltpu.roll(piece, turn, 1)
        if turn + RUN > LANES:
            after = (tile + 1) % len(result)
            result[after] = result[after] + jnp.where(lane < turn, piece, 0.0)
            piece = jnp.where(lane >= turn, piece, 0.0)
        result[tile] = result[tile] + piece
    for tile, value in enumerate(result):
        out[:, tile * LANES : (tile + 1) * LANES] = value


def join(pieces, sub, n):
    block = lax.axis_index("cols")
    pieces = pieces.reshape(n, 2, LINES, WIDE)
    start = (0, block // (n // 2), (block % (n // 2)) * sub, 0)
    pieces = lax.dynamic_slice(pieces, start, (n, 1, sub, WIDE))[:, 0]
    main = pieces[:, :, :BLOCK]
    tail = jnp.pad(pieces[1:, :, BLOCK:], ((0, 1), (0, 0), (LANES, 0)))
    place = (n, sub, BLOCK)
    keep = (iota(place, 2) < BLOCK - CUT) | (iota(place, 0) == n - 1)
    joined = jnp.where(keep, main, tail)
    return jnp.transpose(joined, (1, 0, 2)).reshape(1, sub, n * BLOCK)


def halo_plan(features, valid_cols, offsets, guide_weight):
    own = features[0]
    n = lax.axis_size("cols")
    right = [(c, c + 1) for c in range(n - 1)]
    other = lax.ppermute(own, "view", [(0, 1), (1, 0)])
    near, masks, perm, flip, guide = call(
        prefetch_kernel,
        [(own.shape, BF), (valid_cols.shape, F32), ((SPAN, WIDE), BF), ((DISP, 2 * LANES), BF), ((3 * KEYS, LANES), BF)],
        [pltpu.VMEM(valid_cols.shape, jnp.int32), pltpu.VMEM(guide_weight.shape, BF), pltpu.SemaphoreType.DMA((3,))],
        0, (own, valid_cols, guide_weight), 100_000_000, pl.ANY, 24, pltpu.VMEM,
    )
    first, second, ref_own = call(
        payload_kernel,
        [((PAYLOAD, BLOCK), BF), ((QUAD_ROWS, BLOCK), BF), ((SEC_ROWS, BLOCK), BF)],
        [], 0, (near, other, masks),
    )
    left_first = lax.ppermute(first, "cols", right)
    left_second = lax.ppermute(second, "cols", right)
    quad_rows = (RUN * QUAD_LANES, 2 * LANES)
    skew = pltpu.VMEM((QUAD, 2, SPAN, LANES), F32)
    square = pltpu.VMEM((LANES, LANES), F32)
    wts, early_rows, lhs = call(
        early_kernel,
        [((RUN, 3 * KEYS, LANES), F32), (quad_rows, BF), ((QUAD, SPAN, LANES), BF)],
        [pltpu.VMEM((SEC_ROWS, WIDE), BF), pltpu.VMEM((QUAD, SPAN, LANES), F32), pltpu.VMEM((RUN * LANES, LANES), BF), skew],
        1, (offsets, ref_own, first, left_first, masks, perm, guide), 1_000_000_000,
    )
    (result,) = call(
        late_kernel,
        [((LINES, WIDE), F32)],
        [skew, pltpu.VMEM(quad_rows, BF), pltpu.VMEM((RUN, DISP, LANES), F32), square, square],
        1, (offsets, second, left_second, lhs, early_rows, wts, flip), 1_000_000_000,
    )
    copies = jnp.broadcast_to(result[None], (2 * n, LINES, WIDE))
    pieces = lax.all_to_all(copies, ("cols", "view"), split_axis=0, concat_axis=0, tiled=True)
    return join(pieces, own.shape[0] // n, n)


LINE_RUN = 16
PAIR = 2
LINE_PARTS = LANES // PAIR


MASKS = 8


def pack_kernel(keys, own, valid, *rest):
    outs, (valid_in, masks_in, sems) = rest[-3 - len(keys) : -3], rest[-3:]
    me = 2 * lax.axis_index("cols") + lax.axis_index("view")
    rows = PAIR * CHANNELS
    masked = [out for out in outs if out.shape[0] > rows]
    copies = []
    if masked:
        masks = pltpu.make_async_copy(valid, valid_in, sems.at[len(keys)])
        masks.start()
    for i, (key, out) in enumerate(zip(keys, outs)):
        dest = out if out.shape[0] == rows else out.at[pl.ds(0, rows)]
        copies.append(pltpu.make_async_copy(own.at[me ^ key], dest, sems.at[i]))
        copies[-1].start()
    if masked:
        masks.wait()
        masks = valid_in[...].astype(F32)
        masks_in[...] = jnp.where(
            iota((MASKS, BLOCK), 0) < MASKS // 2, masks[0:1, :], masks[1:2, :]
        ).astype(BF)
        for i, out in enumerate(masked):
            sem = sems.at[len(keys) + 1 + i]
            copies.append(pltpu.make_async_copy(masks_in, out.at[pl.ds(rows, MASKS)], sem))
            copies[-1].start()
    for copy in copies:
        copy.wait()


def constants_kernel(offsets, guide, own, valid, order, flip, guide_out, spread, own_out, masks):
    own_out[...] = own[...]
    masks[...] = valid[...].astype(F32)
    row = iota((LANES, LANES), 0)
    from_lane = LANES - 1 - LINE_RUN * (row & 7) - (row >> 3)
    order[...] = jnp.where(iota((LANES, LANES), 1) == from_lane, 1.0, 0.0).astype(BF)
    back = 2 * LANES - 1 - iota((DISP, 2 * LANES), 0)
    flip[...] = jnp.where(iota((DISP, 2 * LANES), 1) == back, 1.0, 0.0).astype(BF)
    guide_out[...] = spread_guide(guide[...])
    block_of = LINE_PARTS - 1 - (iota(spread.shape, 1) >> 4)
    here = (iota(spread.shape, 0) & (LINE_PARTS - 1)) == block_of
    spread[...] = jnp.where(here, 1.0, 0.0).astype(BF)


def lines_kernel(
    offsets, order, flip, guide, spread, *rest
):
    pieces, (out, blocks, valid, gate_rows, cost_rows, vol, done, wts) = rest[:-8], rest[-8:]
    near, pieces = pieces[1], (pieces[0],) + pieces[2:]
    tiles = len(pieces)
    width = tiles * LANES
    me = 2 * lax.axis_index("cols") + lax.axis_index("view")
    rows = PAIR * CHANNELS
    for key, piece in enumerate(pieces):
        blocks[me ^ key] = piece[:rows, :]
        if piece.shape[0] > rows:
            masks = piece[rows:, :].astype(F32)
            valid[(me ^ key) // 2] = jnp.concatenate([masks[0:1], masks[MASKS // 2 : MASKS // 2 + 1]], axis=0)
    valid[me // 2] = near[...]
    at = PAIR * me
    offs = [offsets[at + i] for i in range(PAIR)]
    ch_lane = iota((CHANNELS, LANES), 1)
    diagonal = iota((8, LANES), 1) - LINE_RUN * iota((8, LANES), 0)
    low_half = iota((LANES, LANES), 1) < CHANNELS
    scale = 1.0 / math.sqrt(CHANNELS)
    empty = jnp.zeros((CHANNELS, LANES), F32)

    def mask_of(view, w):
        lo = (w % 2) * LANES
        return valid[w // 2, view : view + 1, lo : lo + LANES]

    for i in range(PAIR):

        def tile_of(view, w):
            lo = (w % 2) * LANES
            return blocks[2 * (w // 2) + view, i * CHANNELS : (i + 1) * CHANNELS, lo : lo + LANES]

        off = offs[i]
        rolled = [pltpu.roll(tile_of(1, w).astype(F32) * mask_of(1, w), off, 1) for w in range(tiles)]
        shifted = [empty.astype(BF)] * 2
        for w in range(tiles):
            shifted.append(jnp.where(ch_lane < off, rolled[w - 1] if w else empty, rolled[w]).astype(BF))
        shifted = [jnp.concatenate([tile, tile], axis=0) for tile in shifted]
        for quad in range(tiles // 4):
            refs = [tile_of(0, 4 * quad + q) for q in range(4)]
            masked = [refs[q] * (mask_of(0, 4 * quad + q) * scale).astype(BF) for q in range(4)]
            cols = dot_t(order[...], jnp.concatenate(refs, axis=0))
            masked = dot_t(order[...], jnp.concatenate(masked, axis=0))
            for two in range(2):
                lo = two * LANES
                gates, products = [], []
                for side in range(2):
                    w = 4 * quad + 2 * two + side
                    keep = low_half if side == 0 else ~low_half
                    gates.append(jnp.where(keep, cols[:, lo : lo + LANES], 0.0))
                    lhs = jnp.where(keep, masked[:, lo : lo + LANES], 0.0).astype(BF)
                    rhs = jnp.concatenate(shifted[w : w + 3], axis=1)
                    products.append(jnp.dot(lhs, rhs, preferred_element_type=F32))
                place = i * LINE_PARTS + 8 * (tiles - 2 - 4 * quad - 2 * two)
                for t in range(LINE_RUN):
                    row = t * LANES + place
                    r = 8 * t
                    gate_rows[row : row + 16, :] = jnp.concatenate(
                        [gates[1][r : r + 8], gates[0][r : r + 8]], axis=0
                    ).astype(BF)
                    beyond = diagonal >= t
                    both = []
                    for side in (1, 0):
                        turned = [
                            pltpu.roll(
                                products[side][r : r + 8, m * LANES : (m + 1) * LANES],
                                t, 1, stride=LINE_RUN, stride_axis=0,
                            )
                            for m in range(3)
                        ]
                        both.append(
                            jnp.concatenate(
                                [jnp.where(beyond, turned[1], turned[0]), jnp.where(beyond, turned[2], turned[1])],
                                axis=1,
                            )
                        )
                    cost_rows[row : row + 16, :] = jnp.concatenate(both, axis=0).astype(BF)

    x_base = width - 1 - LINE_RUN * (iota((KEYS, LANES), 1) & (LINE_PARTS - 1))
    row = iota((KEYS, LANES), 0)
    reach = jnp.where(row >= 2 * GROUPS, 9, jnp.where(row >= GROUPS, 3, 1))
    room_left = x_base - reach
    room_right = x_base + reach - width
    for two in range(LINE_RUN // 2):
        lo = 2 * two * LANES
        costs = dot_t(flip[...], cost_rows[lo : lo + 2 * LANES, :])
        logits = dot_t(guide[...], gate_rows[lo : lo + 2 * LANES, :])
        for i in range(2):
            t = 2 * two + i
            vol[t] = costs[:, i * LANES : (i + 1) * LANES]
            normalise(logits[:, i * LANES : (i + 1) * LANES], wts, t, room_left, room_right)

    for group in range(GROUPS):
        for at in (group * DGROUP, group * DGROUP + 8):
            v = [vol[t, at : at + 8, :] for t in range(LINE_RUN)]
            for layer in range(LAYERS):
                s = 3**layer
                fresh = []
                for t in range(LINE_RUN):
                    rows = [k * KEYS + layer * GROUPS + group for k in range(3)]
                    w = [wts[t, r : r + 1, :] for r in rows]
                    blk, r = divmod(t + s, LINE_RUN)
                    before = pltpu.roll(v[r], LANES - blk, 1) if blk else v[r]
                    blk, r = divmod(t - s, LINE_RUN)
                    after = pltpu.roll(v[r], -blk, 1) if blk else v[r]
                    fresh.append(w[0] * before + w[1] * v[t] + w[2] * after)
                v = fresh
            for t in range(LINE_RUN):
                done[t, at : at + 8, :] = v[t]

    sub = iota((8, LANES), 0)
    results = []
    for block in range(LINE_RUN // 8):
        totals = jnp.zeros((8, LANES), F32)
        moments = totals
        for s in range(8):
            t = LINE_RUN - 1 - (8 * block + s)
            v = [done[t, 8 * i : 8 * i + 8, :] for i in range(DISP // 8)]
            top = v
            while len(top) > 1:
                top = [jnp.maximum(a, b) for a, b in zip(top[::2], top[1::2])] + top[len(top) & ~1 :]
            top = jnp.max(top[0], axis=0, keepdims=True)
            total = jnp.zeros((8, LANES), F32)
            moment = total
            for i in range(DISP // 8):
                e = jnp.exp(SHARPNESS * (v[i] - top))
                total = total + e
                if i:
                    moment = moment + float(8 * i) * e
            moment = moment + sub.astype(F32) * total
            totals = jnp.where(sub == s, jnp.sum(total, axis=0, keepdims=True), totals)
            moments = jnp.where(sub == s, jnp.sum(moment, axis=0, keepdims=True), moments)
        lane_line = iota((8, LANES), 1) >> 6
        shift = jnp.zeros((8, LANES), F32)
        for i in range(PAIR):
            shift = jnp.where(lane_line == i, offs[i].astype(F32), shift)
        results.append((moments / totals + shift) * (1.0 / DISP))
    vals = jnp.concatenate(results, axis=0)
    lane_line = iota((LINE_RUN, LANES), 1) >> 6
    both = jnp.concatenate([jnp.where(lane_line == i, vals, 0.0) for i in range(PAIR)], axis=0)
    high = both.astype(BF)
    rest = both - high.astype(F32)
    middle = rest.astype(BF)
    low = (rest - middle.astype(F32)).astype(BF)
    pieces = jnp.dot(
        jnp.concatenate([high, middle, low], axis=0), spread[...], preferred_element_type=F32
    )
    size = PAIR * LINE_RUN
    pieces = pieces[:size] + pieces[size : 2 * size] + pieces[2 * size :]
    wanted = iota((LINE_RUN, width), 0) == (iota((LINE_RUN, width), 1) & (LINE_RUN - 1))
    for i in range(PAIR):
        piece = jnp.where(wanted, pieces[i * LINE_RUN : (i + 1) * LINE_RUN], 0.0)
        out[i : i + 1, :] = jnp.sum(piece, axis=0, keepdims=True)


def lines_plan(features, valid_cols, offsets, guide_weight):
    n = lax.axis_size("cols")
    devices = 2 * n
    width = n * BLOCK
    rows = PAIR * CHANNELS
    own = features.reshape(devices, rows, BLOCK)
    pieces = [None] * devices
    gone = ()
    same = tuple(range(n, devices, 2))
    for keys in (same, tuple(key for key in reversed(range(devices)) if key not in same)):
        gone = call(
            functools.partial(pack_kernel, keys),
            [((rows + (MASKS if key % 2 and key > 1 else 0), BLOCK), BF) for key in keys],
            [
                pltpu.VMEM(valid_cols.shape, jnp.int32),
                pltpu.VMEM((MASKS, BLOCK), BF),
                pltpu.SemaphoreType.DMA((2 * devices,)),
            ],
            0, (own, valid_cols, *gone[:1]), 1_000_000, pl.ANY, 60,
        )
        for key, piece in zip(keys, gone):
            moves = [(i, i ^ key) for i in range(devices)]
            pieces[key] = lax.ppermute(piece, ("cols", "view"), moves) if key else piece
    consts = call(
        constants_kernel,
        [
            ((LANES, LANES), BF), ((DISP, 2 * LANES), BF), ((3 * KEYS, LANES), BF), ((LANES, width), BF),
            ((rows, BLOCK), BF), (valid_cols.shape, F32),
        ],
        [], 1, (offsets, guide_weight, pieces[0], valid_cols), 1_000_000,
    )
    (rows,) = call(
        lines_kernel,
        [((PAIR, width), F32)],
        [
            pltpu.VMEM((devices, rows, BLOCK), BF),
            pltpu.VMEM((n,) + valid_cols.shape, F32),
            pltpu.VMEM((LINE_RUN * LANES, LANES), BF),
            pltpu.VMEM((LINE_RUN * LANES, 2 * LANES), BF),
            pltpu.VMEM((LINE_RUN, DISP, LANES), F32),
            pltpu.VMEM((LINE_RUN, DISP, LANES), F32),
            pltpu.VMEM((LINE_RUN, 3 * KEYS, LANES), F32),
        ],
        1, (offsets, *consts, *pieces[1:]), 1_000_000_000,
    )
    return lax.all_gather(rows, "view", axis=0, tiled=True)[None]


def on_device(features, valid_cols, offsets, guide_weight):
    n = lax.axis_size("cols")
    lines = features.shape[1]
    if lines == 2 * PAIR * n and n * BLOCK == LINE_RUN * LINE_PARTS:
        return lines_plan(features, valid_cols, offsets, guide_weight)
    return halo_plan(features, valid_cols, offsets, guide_weight)


def solution(mesh):
    return jax.shard_map(
        on_device,
        mesh=mesh,
        in_specs=(
            P("view", ("tiles", "lines"), None, "cols"),
            P(None, ("tiles", "cols")),
            P(("tiles", "lines")),
            P(),
        ),
        out_specs=P(("tiles", "lines"), "cols", None),
        check_vma=False,
    )
```

```python
import functools
import math

import jax
import jax.numpy as jnp
from jax import lax
from jax.experimental import pallas as pl
from jax.experimental.pallas import tpu as pltpu
from jax.sharding import PartitionSpec as P

DISP = 192
DGROUP = 16
GROUPS = DISP // DGROUP
LAYERS = 3
SHARPNESS = 2.0
HALO = 32
LANES = 128
LINES = 8
CHANNELS = 64
BLOCK = 256
SPAN = BLOCK + HALO
PARTS = LANES // LINES
RUN = SPAN // PARTS
KEYS = 40
WIDE = BLOCK + LANES
SEC_ROWS = LINES * CHANNELS
QUAD_ROWS = SEC_ROWS // 2
MASK_AT = QUAD_ROWS + CHANNELS
PAYLOAD = MASK_AT + 16
QUAD = LINES // 2
QUAD_LANES = LANES // 2
PACK = LANES // HALO
CUT = 16

BF = jnp.bfloat16
F32 = jnp.float32


def iota(shape, dim):
    return lax.broadcasted_iota(jnp.int32, shape, dim)


def dot_t(a, b):
    return lax.dot_general(a, b, (((1,), (1,)), ((), ())), preferred_element_type=F32)


def call(kernel, outs, scratch, smem, args, flops=0, space=pltpu.VMEM, limit=24, to=None):
    specs = [pl.BlockSpec(memory_space=pltpu.SMEM)] * smem
    specs += [pl.BlockSpec(memory_space=space)] * (len(args) - smem)
    return pl.pallas_call(
        kernel,
        out_shape=[jax.ShapeDtypeStruct(shape, dtype) for shape, dtype in outs],
        in_specs=specs,
        out_specs=[pl.BlockSpec(memory_space=to or space)] * len(outs),
        scratch_shapes=scratch,
        compiler_params=pltpu.CompilerParams(vmem_limit_bytes=limit * 1024 * 1024),
        cost_estimate=pl.CostEstimate(flops=flops, bytes_accessed=1_000_000, transcendentals=0),
    )(*args)


def spread_guide(guide):
    keys = LAYERS * 3 * GROUPS
    row = iota((3 * KEYS, keys), 0)
    tap = jnp.where(row >= KEYS, 1, 0) + jnp.where(row >= 2 * KEYS, 1, 0)
    row = row - KEYS * tap
    layer = jnp.where(row >= GROUPS, 1, 0) + jnp.where(row >= 2 * GROUPS, 1, 0)
    key = 2 * GROUPS * layer + GROUPS * tap + row
    chosen = jnp.where((iota((3 * KEYS, keys), 1) == key) & (row < 3 * GROUPS), 1.0, 0.0).astype(BF)
    guide_t = dot_t(chosen, guide).astype(BF)
    return jnp.concatenate([guide_t, guide_t], axis=1)


def normalise(z, wts, t, room_left, room_right):
    z = (0.55 + 0.45 * jnp.tanh(0.5 * z)).astype(BF).astype(F32)
    taps = [z[k * KEYS : (k + 1) * KEYS] for k in range(3)]
    scale = 1.0 / (taps[0] + taps[1] + taps[2])
    wts[t, 0:KEYS, :] = jnp.where(room_left >= t, taps[0] * scale, 0.0)
    wts[t, KEYS : 2 * KEYS, :] = taps[1] * scale
    wts[t, 2 * KEYS : 3 * KEYS, :] = jnp.where(room_right < t, taps[2] * scale, 0.0)


def prefetch_kernel(own, valid, guide, own_out, masks, perm, flip, guide_out, valid_in, guide_in, sems):
    copies = [
        pltpu.make_async_copy(src, dst, sems.at[i])
        for i, (src, dst) in enumerate([(own, own_out), (guide, guide_in), (valid, valid_in)])
    ]
    for copy in copies:
        copy.start()
    perm[...] = jnp.where(
        iota((SPAN, WIDE), 1) == WIDE - 1 - iota((SPAN, WIDE), 0), 1.0, 0.0
    ).astype(BF)
    back = 2 * LANES - 1 - iota((DISP, 2 * LANES), 0)
    flip[...] = jnp.where(iota((DISP, 2 * LANES), 1) == back, 1.0, 0.0).astype(BF)

    copies[1].wait()
    guide_out[...] = spread_guide(guide_in[...])
    copies[2].wait()
    masks[...] = valid_in[...].astype(F32)
    copies[0].wait()


def payload_kernel(own, other, masks, first, second, ref_own):
    view = lax.axis_index("view")
    first_view = view == 0
    sec_mask = masks[1:2, :].astype(BF)
    lane = iota((CHANNELS, LANES), 1)
    tails = []
    for line in range(LINES):
        at = view * LINES + line
        mine, theirs = own[at], other[at]
        lo = line * CHANNELS
        dest, start = (first, lo) if line < QUAD else (second, lo - QUAD_ROWS)
        dest[start : start + CHANNELS, :] = jnp.where(first_view, theirs, mine) * sec_mask
        ref = jnp.where(first_view, mine, theirs)
        ref_own[lo : lo + CHANNELS, :] = ref
        tail = ref[:, BLOCK - LANES :].astype(F32)
        slot = line % PACK
        turn = (HALO * (slot + 1)) % LANES
        if turn:
            tail = pltpu.roll(tail, turn, 1)
        if slot:
            tails[-1] = jnp.where(lane >= HALO * slot, tail, tails[-1])
        else:
            tails.append(tail)
    for i, tail in enumerate(tails):
        first[QUAD_ROWS:MASK_AT, i * LANES : (i + 1) * LANES] = tail.astype(BF)
    first[MASK_AT:, :] = jnp.broadcast_to(masks[0:1, :], (16, BLOCK)).astype(BF)


def shifted(left, mine, lo, off):
    ch_lane = iota((CHANNELS, LANES), 1)
    tiles = [
        src[lo : lo + CHANNELS, i * LANES : (i + 1) * LANES].astype(F32)
        for src in (left, mine)
        for i in range(2)
    ]
    tiles = [pltpu.roll(tile, off, 1) for tile in tiles]
    tiles = [jnp.where(ch_lane < off, tiles[max(i - 1, 0)], tiles[i]).astype(BF) for i in range(4)]
    return jnp.concatenate(tiles, axis=1)


def line_costs(lhs, rhs, slot, skew, cost_rows):
    diagonal = iota((8, LANES), 1) - iota((8, LANES), 0)
    for chunk in range(3):
        rows = min(LANES, SPAN - chunk * LANES)
        first = max(1 - chunk, 0)
        last = 3 - chunk
        products = jnp.dot(
            lhs[chunk * LANES : chunk * LANES + rows],
            rhs[:, first * LANES : (last + 1) * LANES],
            preferred_element_type=F32,
        )
        for j in range(rows // 8):
            tiles = [
                pltpu.roll(
                    products[8 * j : 8 * j + 8, i * LANES : (i + 1) * LANES],
                    8 * j, 1, stride=1, stride_axis=0,
                )
                for i in range(last + 1 - first)
            ]
            if len(tiles) < 3:
                tiles = [tiles[0]] + tiles
            beyond = diagonal >= 8 * j
            at = chunk * LANES + 8 * j
            skew[slot, 0, at : at + 8, :] = jnp.where(beyond, tiles[1], tiles[0])
            skew[slot, 1, at : at + 8, :] = jnp.where(beyond, tiles[2], tiles[1])
    for t in range(RUN):
        at = t * QUAD_LANES + slot * PARTS
        for v in range(2):
            cost_rows[at : at + PARTS, v * LANES : (v + 1) * LANES] = skew[
                slot, v, pl.ds(t, PARTS, stride=RUN), :
            ].astype(BF)


def early_kernel(
    offsets, ref_own, mine, left, masks, perm, guide, wts, cost_rows, lhs_out,
    ref_rows, ref_cols, gate_rows, skew
):
    base = lax.axis_index("view") * LINES
    low = jnp.where(lax.axis_index("cols") == 0, HALO, 0)
    for line in range(LINES):
        lo = line * CHANNELS
        ref_rows[lo : lo + CHANNELS, LANES:] = ref_own[lo : lo + CHANNELS, :]
        half = line // PACK
        packed = left[QUAD_ROWS:MASK_AT, half * LANES : (half + 1) * LANES].astype(F32)
        turn = (LANES - HALO) - HALO * (line % PACK)
        if turn:
            packed = pltpu.roll(packed, turn, 1)
        ref_rows[lo : lo + CHANNELS, :LANES] = packed.astype(BF)

    mask_left = left[MASK_AT : MASK_AT + 1, BLOCK - LANES :].astype(F32)
    ref_mask = jnp.concatenate([mask_left, masks[0:1, :]], axis=1)
    ref_mask = jnp.broadcast_to(ref_mask * (1.0 / math.sqrt(CHANNELS)), (LANES, WIDE))
    mask_cols = dot_t(perm[...], ref_mask.astype(BF))
    half_lane = iota((PARTS, LANES), 1) < CHANNELS
    span_lane = iota((SPAN, LANES), 1) < CHANNELS

    for quad in range(LINES // QUAD):
        ref_t = dot_t(perm[...], ref_rows[quad * QUAD_ROWS : (quad + 1) * QUAD_ROWS, :])
        for pair in range(QUAD // 2):
            cols = ref_t[:, pair * LANES : (pair + 1) * LANES]
            slot = quad * 2 + pair
            ref_cols[slot] = cols
            masked = cols * mask_cols
            if quad == 0:
                rhs = jnp.concatenate(
                    [
                        shifted(left, mine, line * CHANNELS, offsets[base + line])
                        for line in (2 * slot, 2 * slot + 1)
                    ],
                    axis=0,
                )
            for side in range(2):
                line = 2 * slot + side
                for t in range(RUN):
                    picked = ref_cols[slot, pl.ds(t, PARTS, stride=RUN), :]
                    picked = jnp.where(half_lane if side == 0 else ~half_lane, picked, 0.0)
                    at = t * LANES + line * PARTS
                    gate_rows[at : at + PARTS, :] = picked.astype(BF)
                lhs = jnp.where(span_lane if side == 0 else ~span_lane, masked, 0.0).astype(BF)
                if quad == 0:
                    line_costs(lhs, rhs, line, skew, cost_rows)
                else:
                    lhs_out[line - QUAD] = lhs

    place = iota((KEYS, LANES), 1)
    x_base = SPAN - 1 - RUN * (place & (PARTS - 1))
    row = iota((KEYS, LANES), 0)
    reach = jnp.where(row >= 2 * GROUPS, 9, jnp.where(row >= GROUPS, 3, 1))
    room_left = x_base - reach - low
    room_right = x_base + reach - SPAN
    for two in range(RUN // 2):
        at = 2 * two * LANES
        logits = dot_t(guide[...], gate_rows[at : at + 2 * LANES, :])
        for i in range(2):
            t = 2 * two + i
            normalise(logits[:, i * LANES : (i + 1) * LANES], wts, t, room_left, room_right)


def late_kernel(
    offsets, mine, left, lhs, early_rows, wts, flip, out, skew, cost_rows, vol, vals, turned
):
    base = lax.axis_index("view") * LINES
    for pair in range(QUAD // 2):
        rhs = jnp.concatenate(
            [
                shifted(left, mine, line * CHANNELS, offsets[base + QUAD + line])
                for line in (2 * pair, 2 * pair + 1)
            ],
            axis=0,
        )
        for line in (2 * pair, 2 * pair + 1):
            line_costs(lhs[line], rhs, line, skew, cost_rows)

    for two in range(RUN // 2):
        rows = []
        for t in (2 * two, 2 * two + 1):
            for part in (early_rows, cost_rows):
                rows.append(part[t * QUAD_LANES : (t + 1) * QUAD_LANES, :])
        costs = dot_t(flip[...], jnp.concatenate(rows, axis=0))
        vol[2 * two] = costs[:, :LANES]
        vol[2 * two + 1] = costs[:, LANES:]

    def aggregate(group, carry):
        for half in range(2):
            at = pl.multiple_of(group * DGROUP + half * 8, 8)
            v = [vol[t, pl.ds(at, 8), :] for t in range(RUN)]
            for layer in range(LAYERS):
                s = 3**layer
                before = [v[t + s] if t + s < RUN else pltpu.roll(v[t + s - RUN], LANES - 1, 1) for t in range(RUN)]
                after = [v[t - s] if t >= s else pltpu.roll(v[t - s + RUN], 1, 1) for t in range(RUN)]
                fresh = []
                for t in range(RUN):
                    w = [wts[t, pl.ds(k * KEYS + layer * GROUPS + group, 1), :] for k in range(3)]
                    fresh.append(w[0] * before[t] + w[1] * v[t] + w[2] * after[t])
                v = fresh
            for t in range(RUN):
                vol[t, pl.ds(at, 8), :] = v[t]
        return carry

    lax.fori_loop(0, GROUPS, aggregate, 0)

    vals[...] = jnp.zeros((LANES, LANES), F32)
    sub = iota((8, LANES), 0).astype(F32)
    line_of = iota((1, LANES), 1) >> 4
    offs = jnp.zeros((1, LANES), F32)
    for line in range(LINES):
        offs = jnp.where(line_of == line, offsets[base + line].astype(F32), offs)

    def softmax(t, carry):
        v = [vol[t, 8 * i : 8 * i + 8, :] for i in range(DISP // 8)]
        top = v
        while len(top) > 1:
            top = [jnp.maximum(a, b) for a, b in zip(top[::2], top[1::2])] + top[len(top) & ~1 :]
        top = jnp.max(top[0], axis=0, keepdims=True)
        e = [jnp.exp(SHARPNESS * (a - top)) for a in v]
        total = e[0]
        moment = jnp.zeros((8, LANES), F32)
        for i in range(1, DISP // 8):
            total = total + e[i]
            moment = moment + float(8 * i) * e[i]
        moment = jnp.sum(moment + sub * total, axis=0, keepdims=True)
        total = jnp.sum(total, axis=0, keepdims=True)
        vals[pl.ds(RUN - 1 - t, 1), :] = (moment / total + offs) * (1.0 / DISP)
        return carry

    lax.fori_loop(0, RUN, softmax, 0)

    turned[...] = jnp.transpose(vals[...])
    lane = iota((8, LANES), 1)
    result = [jnp.zeros((8, LANES), F32) for _ in range(WIDE // LANES)]
    for part in range(PARTS):
        piece = turned[pl.ds(part, LINES, stride=PARTS), :]
        start = (RUN * (PARTS - 1 - part) - HALO) % WIDE
        tile, turn = divmod(start, LANES)
        if turn:
            piece = pltpu.roll(piece, turn, 1)
        if turn + RUN > LANES:
            after = (tile + 1) % len(result)
            result[after] = result[after] + jnp.where(lane < turn, piece, 0.0)
            piece = jnp.where(lane >= turn, piece, 0.0)
        result[tile] = result[tile] + piece
    for tile, value in enumerate(result):
        out[:, tile * LANES : (tile + 1) * LANES] = value


def join(pieces, sub, n):
    block = lax.axis_index("cols")
    pieces = pieces.reshape(n, 2, LINES, WIDE)
    start = (0, block // (n // 2), (block % (n // 2)) * sub, 0)
    pieces = lax.dynamic_slice(pieces, start, (n, 1, sub, WIDE))[:, 0]
    main = pieces[:, :, :BLOCK]
    tail = jnp.pad(pieces[1:, :, BLOCK:], ((0, 1), (0, 0), (LANES, 0)))
    place = (n, sub, BLOCK)
    keep = (iota(place, 2) < BLOCK - CUT) | (iota(place, 0) == n - 1)
    joined = jnp.where(keep, main, tail)
    return jnp.transpose(joined, (1, 0, 2)).reshape(1, sub, n * BLOCK)


def halo_plan(features, valid_cols, offsets, guide_weight):
    own = features[0]
    n = lax.axis_size("cols")
    right = [(c, c + 1) for c in range(n - 1)]
    other = lax.ppermute(own, "view", [(0, 1), (1, 0)])
    near, masks, perm, flip, guide = call(
        prefetch_kernel,
        [(own.shape, BF), (valid_cols.shape, F32), ((SPAN, WIDE), BF), ((DISP, 2 * LANES), BF), ((3 * KEYS, LANES), BF)],
        [pltpu.VMEM(valid_cols.shape, jnp.int32), pltpu.VMEM(guide_weight.shape, BF), pltpu.SemaphoreType.DMA((3,))],
        0, (own, valid_cols, guide_weight), 100_000_000, pl.ANY, 24, pltpu.VMEM,
    )
    first, second, ref_own = call(
        payload_kernel,
        [((PAYLOAD, BLOCK), BF), ((QUAD_ROWS, BLOCK), BF), ((SEC_ROWS, BLOCK), BF)],
        [], 0, (near, other, masks),
    )
    left_first = lax.ppermute(first, "cols", right)
    left_second = lax.ppermute(second, "cols", right)
    quad_rows = (RUN * QUAD_LANES, 2 * LANES)
    skew = pltpu.VMEM((QUAD, 2, SPAN, LANES), F32)
    square = pltpu.VMEM((LANES, LANES), F32)
    wts, early_rows, lhs = call(
        early_kernel,
        [((RUN, 3 * KEYS, LANES), F32), (quad_rows, BF), ((QUAD, SPAN, LANES), BF)],
        [pltpu.VMEM((SEC_ROWS, WIDE), BF), pltpu.VMEM((QUAD, SPAN, LANES), F32), pltpu.VMEM((RUN * LANES, LANES), BF), skew],
        1, (offsets, ref_own, first, left_first, masks, perm, guide), 1_000_000_000,
    )
    (result,) = call(
        late_kernel,
        [((LINES, WIDE), F32)],
        [skew, pltpu.VMEM(quad_rows, BF), pltpu.VMEM((RUN, DISP, LANES), F32), square, square],
        1, (offsets, second, left_second, lhs, early_rows, wts, flip), 1_000_000_000,
    )
    copies = jnp.broadcast_to(result[None], (2 * n, LINES, WIDE))
    pieces = lax.all_to_all(copies, ("cols", "view"), split_axis=0, concat_axis=0, tiled=True)
    return join(pieces, own.shape[0] // n, n)


LINE_RUN = 16
PAIR = 2
LINE_PARTS = LANES // PAIR


MASKS = 8


def pack_kernel(keys, own, valid, *rest):
    outs = rest[-len(keys) :]
    me = 2 * lax.axis_index("cols") + lax.axis_index("view")
    rows = PAIR * CHANNELS
    for key, out in zip(keys, outs):
        out[:rows, :] = own[me ^ key]
        if out.shape[0] > rows:
            masks = valid[...].astype(F32)
            out[rows:, :] = jnp.where(
                iota((MASKS, BLOCK), 0) < MASKS // 2, masks[0:1, :], masks[1:2, :]
            ).astype(BF)


def constants_kernel(offsets, guide, valid, order, flip, guide_out, spread, masks):
    masks[...] = valid[...].astype(F32)
    row = iota((LANES, LANES), 0)
    from_lane = LANES - 1 - LINE_RUN * (row & 7) - (row >> 3)
    order[...] = jnp.where(iota((LANES, LANES), 1) == from_lane, 1.0, 0.0).astype(BF)
    back = 2 * LANES - 1 - iota((DISP, 2 * LANES), 0)
    flip[...] = jnp.where(iota((DISP, 2 * LANES), 1) == back, 1.0, 0.0).astype(BF)
    guide_out[...] = spread_guide(guide[...])
    block_of = LINE_PARTS - 1 - (iota(spread.shape, 1) >> 4)
    here = (iota(spread.shape, 0) & (LINE_PARTS - 1)) == block_of
    spread[...] = jnp.where(here, 1.0, 0.0).astype(BF)


def lines_kernel(
    offsets, order, flip, guide, spread, *rest
):
    pieces, (out, blocks, valid, gate_rows, cost_rows, vol, done, wts) = rest[:-8], rest[-8:]
    near, pieces = pieces[0], pieces[1:]
    tiles = len(pieces)
    width = tiles * LANES
    me = 2 * lax.axis_index("cols") + lax.axis_index("view")
    rows = PAIR * CHANNELS
    for key, piece in enumerate(pieces):
        blocks[me ^ key] = piece[:rows, :]
        if piece.shape[0] > rows:
            masks = piece[rows:, :].astype(F32)
            valid[(me ^ key) // 2] = jnp.concatenate([masks[0:1], masks[MASKS // 2 : MASKS // 2 + 1]], axis=0)
    valid[me // 2] = near[...]
    at = PAIR * me
    offs = [offsets[at + i] for i in range(PAIR)]
    ch_lane = iota((CHANNELS, LANES), 1)
    diagonal = iota((8, LANES), 1) - LINE_RUN * iota((8, LANES), 0)
    low_half = iota((LANES, LANES), 1) < CHANNELS
    scale = 1.0 / math.sqrt(CHANNELS)
    empty = jnp.zeros((CHANNELS, LANES), F32)

    def mask_of(view, w):
        lo = (w % 2) * LANES
        return valid[w // 2, view : view + 1, lo : lo + LANES]

    for i in range(PAIR):

        def tile_of(view, w):
            lo = (w % 2) * LANES
            return blocks[2 * (w // 2) + view, i * CHANNELS : (i + 1) * CHANNELS, lo : lo + LANES]

        off = offs[i]
        rolled = [pltpu.roll(tile_of(1, w).astype(F32) * mask_of(1, w), off, 1) for w in range(tiles)]
        shifted = [empty.astype(BF)] * 2
        for w in range(tiles):
            shifted.append(jnp.where(ch_lane < off, rolled[w - 1] if w else empty, rolled[w]).astype(BF))
        shifted = [jnp.concatenate([tile, tile], axis=0) for tile in shifted]
        for quad in range(tiles // 4):
            refs = [tile_of(0, 4 * quad + q) for q in range(4)]
            masked = [refs[q] * (mask_of(0, 4 * quad + q) * scale).astype(BF) for q in range(4)]
            cols = dot_t(order[...], jnp.concatenate(refs, axis=0))
            masked = dot_t(order[...], jnp.concatenate(masked, axis=0))
            for two in range(2):
                lo = two * LANES
                gates, products = [], []
                for side in range(2):
                    w = 4 * quad + 2 * two + side
                    keep = low_half if side == 0 else ~low_half
                    gates.append(jnp.where(keep, cols[:, lo : lo + LANES], 0.0))
                    lhs = jnp.where(keep, masked[:, lo : lo + LANES], 0.0).astype(BF)
                    rhs = jnp.concatenate(shifted[w : w + 3], axis=1)
                    products.append(jnp.dot(lhs, rhs, preferred_element_type=F32))
                place = i * LINE_PARTS + 8 * (tiles - 2 - 4 * quad - 2 * two)
                for t in range(LINE_RUN):
                    row = t * LANES + place
                    r = 8 * t
                    gate_rows[row : row + 16, :] = jnp.concatenate(
                        [gates[1][r : r + 8], gates[0][r : r + 8]], axis=0
                    ).astype(BF)
                    beyond = diagonal >= t
                    both = []
                    for side in (1, 0):
                        turned = [
                            pltpu.roll(
                                products[side][r : r + 8, m * LANES : (m + 1) * LANES],
                                t, 1, stride=LINE_RUN, stride_axis=0,
                            )
                            for m in range(3)
                        ]
                        both.append(
                            jnp.concatenate(
                                [jnp.where(beyond, turned[1], turned[0]), jnp.where(beyond, turned[2], turned[1])],
                                axis=1,
                            )
                        )
                    cost_rows[row : row + 16, :] = jnp.concatenate(both, axis=0).astype(BF)

    x_base = width - 1 - LINE_RUN * (iota((KEYS, LANES), 1) & (LINE_PARTS - 1))
    row = iota((KEYS, LANES), 0)
    reach = jnp.where(row >= 2 * GROUPS, 9, jnp.where(row >= GROUPS, 3, 1))
    room_left = x_base - reach
    room_right = x_base + reach - width
    for two in range(LINE_RUN // 2):
        lo = 2 * two * LANES
        costs = dot_t(flip[...], cost_rows[lo : lo + 2 * LANES, :])
        logits = dot_t(guide[...], gate_rows[lo : lo + 2 * LANES, :])
        for i in range(2):
            t = 2 * two + i
            vol[t] = costs[:, i * LANES : (i + 1) * LANES]
            normalise(logits[:, i * LANES : (i + 1) * LANES], wts, t, room_left, room_right)

    for group in range(GROUPS):
        for at in (group * DGROUP, group * DGROUP + 8):
            v = [vol[t, at : at + 8, :] for t in range(LINE_RUN)]
            for layer in range(LAYERS):
                s = 3**layer
                fresh = []
                for t in range(LINE_RUN):
                    rows = [k * KEYS + layer * GROUPS + group for k in range(3)]
                    w = [wts[t, r : r + 1, :] for r in rows]
                    blk, r = divmod(t + s, LINE_RUN)
                    before = pltpu.roll(v[r], LANES - blk, 1) if blk else v[r]
                    blk, r = divmod(t - s, LINE_RUN)
                    after = pltpu.roll(v[r], -blk, 1) if blk else v[r]
                    fresh.append(w[0] * before + w[1] * v[t] + w[2] * after)
                v = fresh
            for t in range(LINE_RUN):
                done[t, at : at + 8, :] = v[t]

    sub = iota((8, LANES), 0)
    results = []
    for block in range(LINE_RUN // 8):
        totals = jnp.zeros((8, LANES), F32)
        moments = totals
        for s in range(8):
            t = LINE_RUN - 1 - (8 * block + s)
            v = [done[t, 8 * i : 8 * i + 8, :] for i in range(DISP // 8)]
            top = v
            while len(top) > 1:
                top = [jnp.maximum(a, b) for a, b in zip(top[::2], top[1::2])] + top[len(top) & ~1 :]
            top = jnp.max(top[0], axis=0, keepdims=True)
            total = jnp.zeros((8, LANES), F32)
            moment = total
            for i in range(DISP // 8):
                e = jnp.exp(SHARPNESS * (v[i] - top))
                total = total + e
                if i:
                    moment = moment + float(8 * i) * e
            moment = moment + sub.astype(F32) * total
            totals = jnp.where(sub == s, jnp.sum(total, axis=0, keepdims=True), totals)
            moments = jnp.where(sub == s, jnp.sum(moment, axis=0, keepdims=True), moments)
        lane_line = iota((8, LANES), 1) >> 6
        shift = jnp.zeros((8, LANES), F32)
        for i in range(PAIR):
            shift = jnp.where(lane_line == i, offs[i].astype(F32), shift)
        results.append((moments / totals + shift) * (1.0 / DISP))
    vals = jnp.concatenate(results, axis=0)
    lane_line = iota((LINE_RUN, LANES), 1) >> 6
    both = jnp.concatenate([jnp.where(lane_line == i, vals, 0.0) for i in range(PAIR)], axis=0)
    high = both.astype(BF)
    rest = both - high.astype(F32)
    middle = rest.astype(BF)
    low = (rest - middle.astype(F32)).astype(BF)
    pieces = jnp.dot(
        jnp.concatenate([high, middle, low], axis=0), spread[...], preferred_element_type=F32
    )
    size = PAIR * LINE_RUN
    pieces = pieces[:size] + pieces[size : 2 * size] + pieces[2 * size :]
    wanted = iota((LINE_RUN, width), 0) == (iota((LINE_RUN, width), 1) & (LINE_RUN - 1))
    for i in range(PAIR):
        piece = jnp.where(wanted, pieces[i * LINE_RUN : (i + 1) * LINE_RUN], 0.0)
        out[i : i + 1, :] = jnp.sum(piece, axis=0, keepdims=True)


def lines_plan(features, valid_cols, offsets, guide_weight):
    n = lax.axis_size("cols")
    devices = 2 * n
    width = n * BLOCK
    rows = PAIR * CHANNELS
    own = features.reshape(devices, rows, BLOCK)
    pieces = [None] * devices
    gone = ()
    far = range(n, devices)
    batches = (
        tuple(key for key in far if key % 2 == 0),
        tuple(key for key in far if key % 2),
        tuple(reversed(range(n))),
    )
    for keys in batches:
        gone = call(
            functools.partial(pack_kernel, keys),
            [((rows + (MASKS if key % 2 and key > 1 else 0), BLOCK), BF) for key in keys],
            [], 0, (own, valid_cols, *gone[:1]), 1_000_000,
        )
        for key, piece in zip(keys, gone):
            moves = [(i, i ^ key) for i in range(devices)]
            pieces[key] = lax.ppermute(piece, ("cols", "view"), moves) if key else piece
    consts = call(
        constants_kernel,
        [
            ((LANES, LANES), BF), ((DISP, 2 * LANES), BF), ((3 * KEYS, LANES), BF), ((LANES, width), BF),
            (valid_cols.shape, F32),
        ],
        [], 1, (offsets, guide_weight, valid_cols), 1_000_000,
    )
    (rows,) = call(
        lines_kernel,
        [((PAIR, width), F32)],
        [
            pltpu.VMEM((devices, rows, BLOCK), BF),
            pltpu.VMEM((n,) + valid_cols.shape, F32),
            pltpu.VMEM((LINE_RUN * LANES, LANES), BF),
            pltpu.VMEM((LINE_RUN * LANES, 2 * LANES), BF),
            pltpu.VMEM((LINE_RUN, DISP, LANES), F32),
            pltpu.VMEM((LINE_RUN, DISP, LANES), F32),
            pltpu.VMEM((LINE_RUN, 3 * KEYS, LANES), F32),
        ],
        1, (offsets, *consts, *pieces), 1_000_000_000,
    )
    return lax.all_gather(rows, "view", axis=0, tiled=True)[None]


def on_device(features, valid_cols, offsets, guide_weight):
    n = lax.axis_size("cols")
    lines = features.shape[1]
    if lines == 2 * PAIR * n and n * BLOCK == LINE_RUN * LINE_PARTS:
        return lines_plan(features, valid_cols, offsets, guide_weight)
    return halo_plan(features, valid_cols, offsets, guide_weight)


def solution(mesh):
    return jax.shard_map(
        on_device,
        mesh=mesh,
        in_specs=(
            P("view", ("tiles", "lines"), None, "cols"),
            P(None, ("tiles", "cols")),
            P(("tiles", "lines")),
            P(),
        ),
        out_specs=P(("tiles", "lines"), "cols", None),
        check_vma=False,
    )
```

```python
import functools
import math

import jax
import jax.numpy as jnp
from jax import lax
from jax.experimental import pallas as pl
from jax.experimental.pallas import tpu as pltpu
from jax.sharding import PartitionSpec as P

DISP = 192
DGROUP = 16
GROUPS = DISP // DGROUP
LAYERS = 3
SHARPNESS = 2.0
HALO = 32
LANES = 128
LINES = 8
CHANNELS = 64
BLOCK = 256
SPAN = BLOCK + HALO
PARTS = LANES // LINES
RUN = SPAN // PARTS
KEYS = 40
WIDE = BLOCK + LANES
SEC_ROWS = LINES * CHANNELS
QUAD_ROWS = SEC_ROWS // 2
MASK_AT = QUAD_ROWS + CHANNELS
PAYLOAD = MASK_AT + 16
QUAD = LINES // 2
QUAD_LANES = LANES // 2
PACK = LANES // HALO
CUT = 16

BF = jnp.bfloat16
F32 = jnp.float32


def iota(shape, dim):
    return lax.broadcasted_iota(jnp.int32, shape, dim)


def dot_t(a, b):
    return lax.dot_general(a, b, (((1,), (1,)), ((), ())), preferred_element_type=F32)


def call(kernel, outs, scratch, smem, args, flops=0, space=pltpu.VMEM, limit=24, to=None):
    specs = [pl.BlockSpec(memory_space=pltpu.SMEM)] * smem
    specs += [pl.BlockSpec(memory_space=space)] * (len(args) - smem)
    return pl.pallas_call(
        kernel,
        out_shape=[jax.ShapeDtypeStruct(shape, dtype) for shape, dtype in outs],
        in_specs=specs,
        out_specs=[pl.BlockSpec(memory_space=to or space)] * len(outs),
        scratch_shapes=scratch,
        compiler_params=pltpu.CompilerParams(vmem_limit_bytes=limit * 1024 * 1024),
        cost_estimate=pl.CostEstimate(flops=flops, bytes_accessed=1_000_000, transcendentals=0),
    )(*args)


def spread_guide(guide):
    keys = LAYERS * 3 * GROUPS
    row = iota((3 * KEYS, keys), 0)
    tap = jnp.where(row >= KEYS, 1, 0) + jnp.where(row >= 2 * KEYS, 1, 0)
    row = row - KEYS * tap
    layer = jnp.where(row >= GROUPS, 1, 0) + jnp.where(row >= 2 * GROUPS, 1, 0)
    key = 2 * GROUPS * layer + GROUPS * tap + row
    chosen = jnp.where((iota((3 * KEYS, keys), 1) == key) & (row < 3 * GROUPS), 1.0, 0.0).astype(BF)
    guide_t = dot_t(chosen, guide).astype(BF)
    return jnp.concatenate([guide_t, guide_t], axis=1)


def normalise(z, wts, t, room_left, room_right):
    z = (0.55 + 0.45 * jnp.tanh(0.5 * z)).astype(BF).astype(F32)
    taps = [z[k * KEYS : (k + 1) * KEYS] for k in range(3)]
    scale = 1.0 / (taps[0] + taps[1] + taps[2])
    wts[t, 0:KEYS, :] = jnp.where(room_left >= t, taps[0] * scale, 0.0)
    wts[t, KEYS : 2 * KEYS, :] = taps[1] * scale
    wts[t, 2 * KEYS : 3 * KEYS, :] = jnp.where(room_right < t, taps[2] * scale, 0.0)


def prefetch_kernel(own, valid, guide, own_out, masks, perm, flip, guide_out, valid_in, guide_in, sems):
    copies = [
        pltpu.make_async_copy(src, dst, sems.at[i])
        for i, (src, dst) in enumerate([(own, own_out), (guide, guide_in), (valid, valid_in)])
    ]
    for copy in copies:
        copy.start()
    perm[...] = jnp.where(
        iota((SPAN, WIDE), 1) == WIDE - 1 - iota((SPAN, WIDE), 0), 1.0, 0.0
    ).astype(BF)
    back = 2 * LANES - 1 - iota((DISP, 2 * LANES), 0)
    flip[...] = jnp.where(iota((DISP, 2 * LANES), 1) == back, 1.0, 0.0).astype(BF)

    copies[1].wait()
    guide_out[...] = spread_guide(guide_in[...])
    copies[2].wait()
    masks[...] = valid_in[...].astype(F32)
    copies[0].wait()


def payload_kernel(own, other, masks, first, second, ref_own):
    view = lax.axis_index("view")
    first_view = view == 0
    sec_mask = masks[1:2, :].astype(BF)
    lane = iota((CHANNELS, LANES), 1)
    tails = []
    for line in range(LINES):
        at = view * LINES + line
        mine, theirs = own[at], other[at]
        lo = line * CHANNELS
        dest, start = (first, lo) if line < QUAD else (second, lo - QUAD_ROWS)
        dest[start : start + CHANNELS, :] = jnp.where(first_view, theirs, mine) * sec_mask
        ref = jnp.where(first_view, mine, theirs)
        ref_own[lo : lo + CHANNELS, :] = ref
        tail = ref[:, BLOCK - LANES :].astype(F32)
        slot = line % PACK
        turn = (HALO * (slot + 1)) % LANES
        if turn:
            tail = pltpu.roll(tail, turn, 1)
        if slot:
            tails[-1] = jnp.where(lane >= HALO * slot, tail, tails[-1])
        else:
            tails.append(tail)
    for i, tail in enumerate(tails):
        first[QUAD_ROWS:MASK_AT, i * LANES : (i + 1) * LANES] = tail.astype(BF)
    first[MASK_AT:, :] = jnp.broadcast_to(masks[0:1, :], (16, BLOCK)).astype(BF)


def shifted(left, mine, lo, off):
    ch_lane = iota((CHANNELS, LANES), 1)
    tiles = [
        src[lo : lo + CHANNELS, i * LANES : (i + 1) * LANES].astype(F32)
        for src in (left, mine)
        for i in range(2)
    ]
    tiles = [pltpu.roll(tile, off, 1) for tile in tiles]
    tiles = [jnp.where(ch_lane < off, tiles[max(i - 1, 0)], tiles[i]).astype(BF) for i in range(4)]
    return jnp.concatenate(tiles, axis=1)


def line_costs(lhs, rhs, slot, skew, cost_rows):
    diagonal = iota((8, LANES), 1) - iota((8, LANES), 0)
    for chunk in range(3):
        rows = min(LANES, SPAN - chunk * LANES)
        first = max(1 - chunk, 0)
        last = 3 - chunk
        products = jnp.dot(
            lhs[chunk * LANES : chunk * LANES + rows],
            rhs[:, first * LANES : (last + 1) * LANES],
            preferred_element_type=F32,
        )
        for j in range(rows // 8):
            tiles = [
                pltpu.roll(
                    products[8 * j : 8 * j + 8, i * LANES : (i + 1) * LANES],
                    8 * j, 1, stride=1, stride_axis=0,
                )
                for i in range(last + 1 - first)
            ]
            if len(tiles) < 3:
                tiles = [tiles[0]] + tiles
            beyond = diagonal >= 8 * j
            at = chunk * LANES + 8 * j
            skew[slot, 0, at : at + 8, :] = jnp.where(beyond, tiles[1], tiles[0])
            skew[slot, 1, at : at + 8, :] = jnp.where(beyond, tiles[2], tiles[1])
    for t in range(RUN):
        at = t * QUAD_LANES + slot * PARTS
        for v in range(2):
            cost_rows[at : at + PARTS, v * LANES : (v + 1) * LANES] = skew[
                slot, v, pl.ds(t, PARTS, stride=RUN), :
            ].astype(BF)


def early_kernel(
    offsets, ref_own, mine, left, masks, perm, guide, wts, cost_rows, lhs_out,
    ref_rows, ref_cols, gate_rows, skew
):
    base = lax.axis_index("view") * LINES
    low = jnp.where(lax.axis_index("cols") == 0, HALO, 0)
    for line in range(LINES):
        lo = line * CHANNELS
        ref_rows[lo : lo + CHANNELS, LANES:] = ref_own[lo : lo + CHANNELS, :]
        half = line // PACK
        packed = left[QUAD_ROWS:MASK_AT, half * LANES : (half + 1) * LANES].astype(F32)
        turn = (LANES - HALO) - HALO * (line % PACK)
        if turn:
            packed = pltpu.roll(packed, turn, 1)
        ref_rows[lo : lo + CHANNELS, :LANES] = packed.astype(BF)

    mask_left = left[MASK_AT : MASK_AT + 1, BLOCK - LANES :].astype(F32)
    ref_mask = jnp.concatenate([mask_left, masks[0:1, :]], axis=1)
    ref_mask = jnp.broadcast_to(ref_mask * (1.0 / math.sqrt(CHANNELS)), (LANES, WIDE))
    mask_cols = dot_t(perm[...], ref_mask.astype(BF))
    half_lane = iota((PARTS, LANES), 1) < CHANNELS
    span_lane = iota((SPAN, LANES), 1) < CHANNELS

    for quad in range(LINES // QUAD):
        ref_t = dot_t(perm[...], ref_rows[quad * QUAD_ROWS : (quad + 1) * QUAD_ROWS, :])
        for pair in range(QUAD // 2):
            cols = ref_t[:, pair * LANES : (pair + 1) * LANES]
            slot = quad * 2 + pair
            ref_cols[slot] = cols
            masked = cols * mask_cols
            if quad == 0:
                rhs = jnp.concatenate(
                    [
                        shifted(left, mine, line * CHANNELS, offsets[base + line])
                        for line in (2 * slot, 2 * slot + 1)
                    ],
                    axis=0,
                )
            for side in range(2):
                line = 2 * slot + side
                for t in range(RUN):
                    picked = ref_cols[slot, pl.ds(t, PARTS, stride=RUN), :]
                    picked = jnp.where(half_lane if side == 0 else ~half_lane, picked, 0.0)
                    at = t * LANES + line * PARTS
                    gate_rows[at : at + PARTS, :] = picked.astype(BF)
                lhs = jnp.where(span_lane if side == 0 else ~span_lane, masked, 0.0).astype(BF)
                if quad == 0:
                    line_costs(lhs, rhs, line, skew, cost_rows)
                else:
                    lhs_out[line - QUAD] = lhs

    place = iota((KEYS, LANES), 1)
    x_base = SPAN - 1 - RUN * (place & (PARTS - 1))
    row = iota((KEYS, LANES), 0)
    reach = jnp.where(row >= 2 * GROUPS, 9, jnp.where(row >= GROUPS, 3, 1))
    room_left = x_base - reach - low
    room_right = x_base + reach - SPAN
    for two in range(RUN // 2):
        at = 2 * two * LANES
        logits = dot_t(guide[...], gate_rows[at : at + 2 * LANES, :])
        for i in range(2):
            t = 2 * two + i
            normalise(logits[:, i * LANES : (i + 1) * LANES], wts, t, room_left, room_right)


def late_kernel(
    offsets, mine, left, lhs, early_rows, wts, flip, out, skew, cost_rows, vol, vals, turned
):
    base = lax.axis_index("view") * LINES
    for pair in range(QUAD // 2):
        rhs = jnp.concatenate(
            [
                shifted(left, mine, line * CHANNELS, offsets[base + QUAD + line])
                for line in (2 * pair, 2 * pair + 1)
            ],
            axis=0,
        )
        for line in (2 * pair, 2 * pair + 1):
            line_costs(lhs[line], rhs, line, skew, cost_rows)

    for two in range(RUN // 2):
        rows = []
        for t in (2 * two, 2 * two + 1):
            for part in (early_rows, cost_rows):
                rows.append(part[t * QUAD_LANES : (t + 1) * QUAD_LANES, :])
        costs = dot_t(flip[...], jnp.concatenate(rows, axis=0))
        vol[2 * two] = costs[:, :LANES]
        vol[2 * two + 1] = costs[:, LANES:]

    def aggregate(group, carry):
        for half in range(2):
            at = pl.multiple_of(group * DGROUP + half * 8, 8)
            v = [vol[t, pl.ds(at, 8), :] for t in range(RUN)]
            for layer in range(LAYERS):
                s = 3**layer
                before = [v[t + s] if t + s < RUN else pltpu.roll(v[t + s - RUN], LANES - 1, 1) for t in range(RUN)]
                after = [v[t - s] if t >= s else pltpu.roll(v[t - s + RUN], 1, 1) for t in range(RUN)]
                fresh = []
                for t in range(RUN):
                    w = [wts[t, pl.ds(k * KEYS + layer * GROUPS + group, 1), :] for k in range(3)]
                    fresh.append(w[0] * before[t] + w[1] * v[t] + w[2] * after[t])
                v = fresh
            for t in range(RUN):
                vol[t, pl.ds(at, 8), :] = v[t]
        return carry

    lax.fori_loop(0, GROUPS, aggregate, 0)

    vals[...] = jnp.zeros((LANES, LANES), F32)
    sub = iota((8, LANES), 0).astype(F32)
    line_of = iota((1, LANES), 1) >> 4
    offs = jnp.zeros((1, LANES), F32)
    for line in range(LINES):
        offs = jnp.where(line_of == line, offsets[base + line].astype(F32), offs)

    def softmax(t, carry):
        v = [vol[t, 8 * i : 8 * i + 8, :] for i in range(DISP // 8)]
        top = v
        while len(top) > 1:
            top = [jnp.maximum(a, b) for a, b in zip(top[::2], top[1::2])] + top[len(top) & ~1 :]
        top = jnp.max(top[0], axis=0, keepdims=True)
        e = [jnp.exp(SHARPNESS * (a - top)) for a in v]
        total = e[0]
        moment = jnp.zeros((8, LANES), F32)
        for i in range(1, DISP // 8):
            total = total + e[i]
            moment = moment + float(8 * i) * e[i]
        moment = jnp.sum(moment + sub * total, axis=0, keepdims=True)
        total = jnp.sum(total, axis=0, keepdims=True)
        vals[pl.ds(RUN - 1 - t, 1), :] = (moment / total + offs) * (1.0 / DISP)
        return carry

    lax.fori_loop(0, RUN, softmax, 0)

    turned[...] = jnp.transpose(vals[...])
    lane = iota((8, LANES), 1)
    result = [jnp.zeros((8, LANES), F32) for _ in range(WIDE // LANES)]
    for part in range(PARTS):
        piece = turned[pl.ds(part, LINES, stride=PARTS), :]
        start = (RUN * (PARTS - 1 - part) - HALO) % WIDE
        tile, turn = divmod(start, LANES)
        if turn:
            piece = pltpu.roll(piece, turn, 1)
        if turn + RUN > LANES:
            after = (tile + 1) % len(result)
            result[after] = result[after] + jnp.where(lane < turn, piece, 0.0)
            piece = jnp.where(lane >= turn, piece, 0.0)
        result[tile] = result[tile] + piece
    for tile, value in enumerate(result):
        out[:, tile * LANES : (tile + 1) * LANES] = value


def join(pieces, sub, n):
    block = lax.axis_index("cols")
    pieces = pieces.reshape(n, 2, LINES, WIDE)
    start = (0, block // (n // 2), (block % (n // 2)) * sub, 0)
    pieces = lax.dynamic_slice(pieces, start, (n, 1, sub, WIDE))[:, 0]
    main = pieces[:, :, :BLOCK]
    tail = jnp.pad(pieces[1:, :, BLOCK:], ((0, 1), (0, 0), (LANES, 0)))
    place = (n, sub, BLOCK)
    keep = (iota(place, 2) < BLOCK - CUT) | (iota(place, 0) == n - 1)
    joined = jnp.where(keep, main, tail)
    return jnp.transpose(joined, (1, 0, 2)).reshape(1, sub, n * BLOCK)


def halo_plan(features, valid_cols, offsets, guide_weight):
    own = features[0]
    n = lax.axis_size("cols")
    right = [(c, c + 1) for c in range(n - 1)]
    other = lax.ppermute(own, "view", [(0, 1), (1, 0)])
    near, masks, perm, flip, guide = call(
        prefetch_kernel,
        [(own.shape, BF), (valid_cols.shape, F32), ((SPAN, WIDE), BF), ((DISP, 2 * LANES), BF), ((3 * KEYS, LANES), BF)],
        [pltpu.VMEM(valid_cols.shape, jnp.int32), pltpu.VMEM(guide_weight.shape, BF), pltpu.SemaphoreType.DMA((3,))],
        0, (own, valid_cols, guide_weight), 100_000_000, pl.ANY, 24, pltpu.VMEM,
    )
    first, second, ref_own = call(
        payload_kernel,
        [((PAYLOAD, BLOCK), BF), ((QUAD_ROWS, BLOCK), BF), ((SEC_ROWS, BLOCK), BF)],
        [], 0, (near, other, masks),
    )
    left_first = lax.ppermute(first, "cols", right)
    left_second = lax.ppermute(second, "cols", right)
    quad_rows = (RUN * QUAD_LANES, 2 * LANES)
    skew = pltpu.VMEM((QUAD, 2, SPAN, LANES), F32)
    square = pltpu.VMEM((LANES, LANES), F32)
    wts, early_rows, lhs = call(
        early_kernel,
        [((RUN, 3 * KEYS, LANES), F32), (quad_rows, BF), ((QUAD, SPAN, LANES), BF)],
        [pltpu.VMEM((SEC_ROWS, WIDE), BF), pltpu.VMEM((QUAD, SPAN, LANES), F32), pltpu.VMEM((RUN * LANES, LANES), BF), skew],
        1, (offsets, ref_own, first, left_first, masks, perm, guide), 1_000_000_000,
    )
    (result,) = call(
        late_kernel,
        [((LINES, WIDE), F32)],
        [skew, pltpu.VMEM(quad_rows, BF), pltpu.VMEM((RUN, DISP, LANES), F32), square, square],
        1, (offsets, second, left_second, lhs, early_rows, wts, flip), 1_000_000_000,
    )
    copies = jnp.broadcast_to(result[None], (2 * n, LINES, WIDE))
    pieces = lax.all_to_all(copies, ("cols", "view"), split_axis=0, concat_axis=0, tiled=True)
    return join(pieces, own.shape[0] // n, n)


LINE_RUN = 16
PAIR = 2
LINE_PARTS = LANES // PAIR


MASKS = 8


def pack_kernel(key, own, *rest):
    out = rest[-1]
    me = 2 * lax.axis_index("cols") + lax.axis_index("view")
    rows = PAIR * CHANNELS
    out[:rows, :] = own[me ^ key]
    if out.shape[0] > rows:
        masks = rest[0][...].astype(F32)
        out[rows:, :] = jnp.where(
            iota((MASKS, BLOCK), 0) < MASKS // 2, masks[0:1, :], masks[1:2, :]
        ).astype(BF)


def constants_kernel(offsets, guide, valid, order, flip, guide_out, spread, masks):
    masks[...] = valid[...].astype(F32)
    row = iota((LANES, LANES), 0)
    from_lane = LANES - 1 - LINE_RUN * (row & 7) - (row >> 3)
    order[...] = jnp.where(iota((LANES, LANES), 1) == from_lane, 1.0, 0.0).astype(BF)
    back = 2 * LANES - 1 - iota((DISP, 2 * LANES), 0)
    flip[...] = jnp.where(iota((DISP, 2 * LANES), 1) == back, 1.0, 0.0).astype(BF)
    guide_out[...] = spread_guide(guide[...])
    block_of = LINE_PARTS - 1 - (iota(spread.shape, 1) >> 4)
    here = (iota(spread.shape, 0) & (LINE_PARTS - 1)) == block_of
    spread[...] = jnp.where(here, 1.0, 0.0).astype(BF)


def lines_kernel(
    offsets, order, flip, guide, spread, *rest
):
    pieces, (out, blocks, valid, gate_rows, cost_rows, vol, done, wts) = rest[:-8], rest[-8:]
    near, pieces = pieces[0], pieces[1:]
    tiles = len(pieces)
    width = tiles * LANES
    me = 2 * lax.axis_index("cols") + lax.axis_index("view")
    rows = PAIR * CHANNELS
    for key, piece in enumerate(pieces):
        blocks[me ^ key] = piece[:rows, :]
        if piece.shape[0] > rows:
            masks = piece[rows:, :].astype(F32)
            valid[(me ^ key) // 2] = jnp.concatenate([masks[0:1], masks[MASKS // 2 : MASKS // 2 + 1]], axis=0)
    valid[me // 2] = near[...]
    at = PAIR * me
    offs = [offsets[at + i] for i in range(PAIR)]
    ch_lane = iota((CHANNELS, LANES), 1)
    diagonal = iota((8, LANES), 1) - LINE_RUN * iota((8, LANES), 0)
    low_half = iota((LANES, LANES), 1) < CHANNELS
    scale = 1.0 / math.sqrt(CHANNELS)
    empty = jnp.zeros((CHANNELS, LANES), F32)

    def mask_of(view, w):
        lo = (w % 2) * LANES
        return valid[w // 2, view : view + 1, lo : lo + LANES]

    for i in range(PAIR):

        def tile_of(view, w):
            lo = (w % 2) * LANES
            return blocks[2 * (w // 2) + view, i * CHANNELS : (i + 1) * CHANNELS, lo : lo + LANES]

        off = offs[i]
        rolled = [pltpu.roll(tile_of(1, w).astype(F32) * mask_of(1, w), off, 1) for w in range(tiles)]
        shifted = [empty.astype(BF)] * 2
        for w in range(tiles):
            shifted.append(jnp.where(ch_lane < off, rolled[w - 1] if w else empty, rolled[w]).astype(BF))
        shifted = [jnp.concatenate([tile, tile], axis=0) for tile in shifted]
        for quad in range(tiles // 4):
            refs = [tile_of(0, 4 * quad + q) for q in range(4)]
            masked = [refs[q] * (mask_of(0, 4 * quad + q) * scale).astype(BF) for q in range(4)]
            cols = dot_t(order[...], jnp.concatenate(refs, axis=0))
            masked = dot_t(order[...], jnp.concatenate(masked, axis=0))
            for two in range(2):
                lo = two * LANES
                gates, products = [], []
                for side in range(2):
                    w = 4 * quad + 2 * two + side
                    keep = low_half if side == 0 else ~low_half
                    gates.append(jnp.where(keep, cols[:, lo : lo + LANES], 0.0))
                    lhs = jnp.where(keep, masked[:, lo : lo + LANES], 0.0).astype(BF)
                    rhs = jnp.concatenate(shifted[w : w + 3], axis=1)
                    products.append(jnp.dot(lhs, rhs, preferred_element_type=F32))
                place = i * LINE_PARTS + 8 * (tiles - 2 - 4 * quad - 2 * two)
                for t in range(LINE_RUN):
                    row = t * LANES + place
                    r = 8 * t
                    gate_rows[row : row + 16, :] = jnp.concatenate(
                        [gates[1][r : r + 8], gates[0][r : r + 8]], axis=0
                    ).astype(BF)
                    beyond = diagonal >= t
                    both = []
                    for side in (1, 0):
                        turned = [
                            pltpu.roll(
                                products[side][r : r + 8, m * LANES : (m + 1) * LANES],
                                t, 1, stride=LINE_RUN, stride_axis=0,
                            )
                            for m in range(3)
                        ]
                        both.append(
                            jnp.concatenate(
                                [jnp.where(beyond, turned[1], turned[0]), jnp.where(beyond, turned[2], turned[1])],
                                axis=1,
                            )
                        )
                    cost_rows[row : row + 16, :] = jnp.concatenate(both, axis=0).astype(BF)

    x_base = width - 1 - LINE_RUN * (iota((KEYS, LANES), 1) & (LINE_PARTS - 1))
    row = iota((KEYS, LANES), 0)
    reach = jnp.where(row >= 2 * GROUPS, 9, jnp.where(row >= GROUPS, 3, 1))
    room_left = x_base - reach
    room_right = x_base + reach - width
    for two in range(LINE_RUN // 2):
        lo = 2 * two * LANES
        costs = dot_t(flip[...], cost_rows[lo : lo + 2 * LANES, :])
        logits = dot_t(guide[...], gate_rows[lo : lo + 2 * LANES, :])
        for i in range(2):
            t = 2 * two + i
            vol[t] = costs[:, i * LANES : (i + 1) * LANES]
            normalise(logits[:, i * LANES : (i + 1) * LANES], wts, t, room_left, room_right)

    for group in range(GROUPS):
        for at in (group * DGROUP, group * DGROUP + 8):
            v = [vol[t, at : at + 8, :] for t in range(LINE_RUN)]
            for layer in range(LAYERS):
                s = 3**layer
                fresh = []
                for t in range(LINE_RUN):
                    rows = [k * KEYS + layer * GROUPS + group for k in range(3)]
                    w = [wts[t, r : r + 1, :] for r in rows]
                    blk, r = divmod(t + s, LINE_RUN)
                    before = pltpu.roll(v[r], LANES - blk, 1) if blk else v[r]
                    blk, r = divmod(t - s, LINE_RUN)
                    after = pltpu.roll(v[r], -blk, 1) if blk else v[r]
                    fresh.append(w[0] * before + w[1] * v[t] + w[2] * after)
                v = fresh
            for t in range(LINE_RUN):
                done[t, at : at + 8, :] = v[t]

    sub = iota((8, LANES), 0)
    results = []
    for block in range(LINE_RUN // 8):
        totals = jnp.zeros((8, LANES), F32)
        moments = totals
        for s in range(8):
            t = LINE_RUN - 1 - (8 * block + s)
            v = [done[t, 8 * i : 8 * i + 8, :] for i in range(DISP // 8)]
            top = v
            while len(top) > 1:
                top = [jnp.maximum(a, b) for a, b in zip(top[::2], top[1::2])] + top[len(top) & ~1 :]
            top = jnp.max(top[0], axis=0, keepdims=True)
            total = jnp.zeros((8, LANES), F32)
            moment = total
            for i in range(DISP // 8):
                e = jnp.exp(SHARPNESS * (v[i] - top))
                total = total + e
                if i:
                    moment = moment + float(8 * i) * e
            moment = moment + sub.astype(F32) * total
            totals = jnp.where(sub == s, jnp.sum(total, axis=0, keepdims=True), totals)
            moments = jnp.where(sub == s, jnp.sum(moment, axis=0, keepdims=True), moments)
        lane_line = iota((8, LANES), 1) >> 6
        shift = jnp.zeros((8, LANES), F32)
        for i in range(PAIR):
            shift = jnp.where(lane_line == i, offs[i].astype(F32), shift)
        results.append((moments / totals + shift) * (1.0 / DISP))
    vals = jnp.concatenate(results, axis=0)
    lane_line = iota((LINE_RUN, LANES), 1) >> 6
    both = jnp.concatenate([jnp.where(lane_line == i, vals, 0.0) for i in range(PAIR)], axis=0)
    high = both.astype(BF)
    rest = both - high.astype(F32)
    middle = rest.astype(BF)
    low = (rest - middle.astype(F32)).astype(BF)
    pieces = jnp.dot(
        jnp.concatenate([high, middle, low], axis=0), spread[...], preferred_element_type=F32
    )
    size = PAIR * LINE_RUN
    pieces = pieces[:size] + pieces[size : 2 * size] + pieces[2 * size :]
    wanted = iota((LINE_RUN, width), 0) == (iota((LINE_RUN, width), 1) & (LINE_RUN - 1))
    for i in range(PAIR):
        piece = jnp.where(wanted, pieces[i * LINE_RUN : (i + 1) * LINE_RUN], 0.0)
        out[i : i + 1, :] = jnp.sum(piece, axis=0, keepdims=True)


def lines_plan(features, valid_cols, offsets, guide_weight):
    n = lax.axis_size("cols")
    devices = 2 * n
    width = n * BLOCK
    rows = PAIR * CHANNELS
    own = features.reshape(devices, rows, BLOCK)
    pieces = [None] * devices
    gone = ()
    for key, after in ((6, None), (4, None), (1, None), (2, None), (7, None), (5, 1), (3, 2), (0, None)):
        masked = key % 2 and key > 1
        (piece,) = call(
            functools.partial(pack_kernel, key),
            [((rows + (MASKS if masked else 0), BLOCK), BF)],
            [], 0,
            (own,) + ((valid_cols,) if masked else ()) + gone + (() if after is None else (pieces[after],)),
            1_000_000,
        )
        gone = (piece,)
        moves = [(i, i ^ key) for i in range(devices)]
        pieces[key] = lax.ppermute(piece, ("cols", "view"), moves) if key else piece
    consts = call(
        constants_kernel,
        [
            ((LANES, LANES), BF), ((DISP, 2 * LANES), BF), ((3 * KEYS, LANES), BF), ((LANES, width), BF),
            (valid_cols.shape, F32),
        ],
        [], 1, (offsets, guide_weight, valid_cols), 1_000_000,
    )
    (rows,) = call(
        lines_kernel,
        [((PAIR, width), F32)],
        [
            pltpu.VMEM((devices, rows, BLOCK), BF),
            pltpu.VMEM((n,) + valid_cols.shape, F32),
            pltpu.VMEM((LINE_RUN * LANES, LANES), BF),
            pltpu.VMEM((LINE_RUN * LANES, 2 * LANES), BF),
            pltpu.VMEM((LINE_RUN, DISP, LANES), F32),
            pltpu.VMEM((LINE_RUN, DISP, LANES), F32),
            pltpu.VMEM((LINE_RUN, 3 * KEYS, LANES), F32),
        ],
        1, (offsets, *consts, *pieces), 1_000_000_000,
    )
    return lax.all_gather(rows, "view", axis=0, tiled=True)[None]


def on_device(features, valid_cols, offsets, guide_weight):
    n = lax.axis_size("cols")
    lines = features.shape[1]
    if lines == 2 * PAIR * n and n * BLOCK == LINE_RUN * LINE_PARTS:
        return lines_plan(features, valid_cols, offsets, guide_weight)
    return halo_plan(features, valid_cols, offsets, guide_weight)


def solution(mesh):
    return jax.shard_map(
        on_device,
        mesh=mesh,
        in_specs=(
            P("view", ("tiles", "lines"), None, "cols"),
            P(None, ("tiles", "cols")),
            P(("tiles", "lines")),
            P(),
        ),
        out_specs=P(("tiles", "lines"), "cols", None),
        check_vma=False,
    )
```

```python
import functools
import math

import jax
import jax.numpy as jnp
from jax import lax
from jax.experimental import pallas as pl
from jax.experimental.pallas import tpu as pltpu
from jax.sharding import PartitionSpec as P

DISP = 192
DGROUP = 16
GROUPS = DISP // DGROUP
LAYERS = 3
SHARPNESS = 2.0
HALO = 32
LANES = 128
LINES = 8
CHANNELS = 64
BLOCK = 256
SPAN = BLOCK + HALO
PARTS = LANES // LINES
RUN = SPAN // PARTS
KEYS = 40
WIDE = BLOCK + LANES
SEC_ROWS = LINES * CHANNELS
QUAD_ROWS = SEC_ROWS // 2
MASK_AT = QUAD_ROWS + CHANNELS
PAYLOAD = MASK_AT + 16
QUAD = LINES // 2
QUAD_LANES = LANES // 2
PACK = LANES // HALO
CUT = 16

BF = jnp.bfloat16
F32 = jnp.float32


def iota(shape, dim):
    return lax.broadcasted_iota(jnp.int32, shape, dim)


def dot_t(a, b):
    return lax.dot_general(a, b, (((1,), (1,)), ((), ())), preferred_element_type=F32)


def call(kernel, outs, scratch, smem, args, flops=0, space=pltpu.VMEM, limit=24, to=None):
    specs = [pl.BlockSpec(memory_space=pltpu.SMEM)] * smem
    specs += [pl.BlockSpec(memory_space=space)] * (len(args) - smem)
    return pl.pallas_call(
        kernel,
        out_shape=[jax.ShapeDtypeStruct(shape, dtype) for shape, dtype in outs],
        in_specs=specs,
        out_specs=[pl.BlockSpec(memory_space=to or space)] * len(outs),
        scratch_shapes=scratch,
        compiler_params=pltpu.CompilerParams(vmem_limit_bytes=limit * 1024 * 1024),
        cost_estimate=pl.CostEstimate(flops=flops, bytes_accessed=1_000_000, transcendentals=0),
    )(*args)


def spread_guide(guide):
    keys = LAYERS * 3 * GROUPS
    row = iota((3 * KEYS, keys), 0)
    tap = jnp.where(row >= KEYS, 1, 0) + jnp.where(row >= 2 * KEYS, 1, 0)
    row = row - KEYS * tap
    layer = jnp.where(row >= GROUPS, 1, 0) + jnp.where(row >= 2 * GROUPS, 1, 0)
    key = 2 * GROUPS * layer + GROUPS * tap + row
    chosen = jnp.where((iota((3 * KEYS, keys), 1) == key) & (row < 3 * GROUPS), 1.0, 0.0).astype(BF)
    guide_t = dot_t(chosen, guide).astype(BF)
    return jnp.concatenate([guide_t, guide_t], axis=1)


def normalise(z, wts, t, room_left, room_right):
    z = (0.55 + 0.45 * jnp.tanh(0.5 * z)).astype(BF).astype(F32)
    taps = [z[k * KEYS : (k + 1) * KEYS] for k in range(3)]
    scale = 1.0 / (taps[0] + taps[1] + taps[2])
    wts[t, 0:KEYS, :] = jnp.where(room_left >= t, taps[0] * scale, 0.0)
    wts[t, KEYS : 2 * KEYS, :] = taps[1] * scale
    wts[t, 2 * KEYS : 3 * KEYS, :] = jnp.where(room_right < t, taps[2] * scale, 0.0)


def prefetch_kernel(own, valid, guide, own_out, masks, perm, flip, guide_out, valid_in, guide_in, sems):
    copies = [
        pltpu.make_async_copy(src, dst, sems.at[i])
        for i, (src, dst) in enumerate([(own, own_out), (guide, guide_in), (valid, valid_in)])
    ]
    for copy in copies:
        copy.start()
    perm[...] = jnp.where(
        iota((SPAN, WIDE), 1) == WIDE - 1 - iota((SPAN, WIDE), 0), 1.0, 0.0
    ).astype(BF)
    back = 2 * LANES - 1 - iota((DISP, 2 * LANES), 0)
    flip[...] = jnp.where(iota((DISP, 2 * LANES), 1) == back, 1.0, 0.0).astype(BF)

    copies[1].wait()
    guide_out[...] = spread_guide(guide_in[...])
    copies[2].wait()
    masks[...] = valid_in[...].astype(F32)
    copies[0].wait()


def payload_kernel(own, other, masks, first, second, ref_own):
    view = lax.axis_index("view")
    first_view = view == 0
    sec_mask = masks[1:2, :].astype(BF)
    lane = iota((CHANNELS, LANES), 1)
    tails = []
    for line in range(LINES):
        at = view * LINES + line
        mine, theirs = own[at], other[at]
        lo = line * CHANNELS
        dest, start = (first, lo) if line < QUAD else (second, lo - QUAD_ROWS)
        dest[start : start + CHANNELS, :] = jnp.where(first_view, theirs, mine) * sec_mask
        ref = jnp.where(first_view, mine, theirs)
        ref_own[lo : lo + CHANNELS, :] = ref
        tail = ref[:, BLOCK - LANES :].astype(F32)
        slot = line % PACK
        turn = (HALO * (slot + 1)) % LANES
        if turn:
            tail = pltpu.roll(tail, turn, 1)
        if slot:
            tails[-1] = jnp.where(lane >= HALO * slot, tail, tails[-1])
        else:
            tails.append(tail)
    for i, tail in enumerate(tails):
        first[QUAD_ROWS:MASK_AT, i * LANES : (i + 1) * LANES] = tail.astype(BF)
    first[MASK_AT:, :] = jnp.broadcast_to(masks[0:1, :], (16, BLOCK)).astype(BF)


def shifted(left, mine, lo, off):
    ch_lane = iota((CHANNELS, LANES), 1)
    tiles = [
        src[lo : lo + CHANNELS, i * LANES : (i + 1) * LANES].astype(F32)
        for src in (left, mine)
        for i in range(2)
    ]
    tiles = [pltpu.roll(tile, off, 1) for tile in tiles]
    tiles = [jnp.where(ch_lane < off, tiles[max(i - 1, 0)], tiles[i]).astype(BF) for i in range(4)]
    return jnp.concatenate(tiles, axis=1)


def line_costs(lhs, rhs, slot, skew, cost_rows):
    diagonal = iota((8, LANES), 1) - iota((8, LANES), 0)
    for chunk in range(3):
        rows = min(LANES, SPAN - chunk * LANES)
        first = max(1 - chunk, 0)
        last = 3 - chunk
        products = jnp.dot(
            lhs[chunk * LANES : chunk * LANES + rows],
            rhs[:, first * LANES : (last + 1) * LANES],
            preferred_element_type=F32,
        )
        for j in range(rows // 8):
            tiles = [
                pltpu.roll(
                    products[8 * j : 8 * j + 8, i * LANES : (i + 1) * LANES],
                    8 * j, 1, stride=1, stride_axis=0,
                )
                for i in range(last + 1 - first)
            ]
            if len(tiles) < 3:
                tiles = [tiles[0]] + tiles
            beyond = diagonal >= 8 * j
            at = chunk * LANES + 8 * j
            skew[slot, 0, at : at + 8, :] = jnp.where(beyond, tiles[1], tiles[0])
            skew[slot, 1, at : at + 8, :] = jnp.where(beyond, tiles[2], tiles[1])
    for t in range(RUN):
        at = t * QUAD_LANES + slot * PARTS
        for v in range(2):
            cost_rows[at : at + PARTS, v * LANES : (v + 1) * LANES] = skew[
                slot, v, pl.ds(t, PARTS, stride=RUN), :
            ].astype(BF)


def early_kernel(
    offsets, ref_own, mine, left, masks, perm, guide, wts, cost_rows, lhs_out,
    ref_rows, ref_cols, gate_rows, skew
):
    base = lax.axis_index("view") * LINES
    low = jnp.where(lax.axis_index("cols") == 0, HALO, 0)
    for line in range(LINES):
        lo = line * CHANNELS
        ref_rows[lo : lo + CHANNELS, LANES:] = ref_own[lo : lo + CHANNELS, :]
        half = line // PACK
        packed = left[QUAD_ROWS:MASK_AT, half * LANES : (half + 1) * LANES].astype(F32)
        turn = (LANES - HALO) - HALO * (line % PACK)
        if turn:
            packed = pltpu.roll(packed, turn, 1)
        ref_rows[lo : lo + CHANNELS, :LANES] = packed.astype(BF)

    mask_left = left[MASK_AT : MASK_AT + 1, BLOCK - LANES :].astype(F32)
    ref_mask = jnp.concatenate([mask_left, masks[0:1, :]], axis=1)
    ref_mask = jnp.broadcast_to(ref_mask * (1.0 / math.sqrt(CHANNELS)), (LANES, WIDE))
    mask_cols = dot_t(perm[...], ref_mask.astype(BF))
    half_lane = iota((PARTS, LANES), 1) < CHANNELS
    span_lane = iota((SPAN, LANES), 1) < CHANNELS

    for quad in range(LINES // QUAD):
        ref_t = dot_t(perm[...], ref_rows[quad * QUAD_ROWS : (quad + 1) * QUAD_ROWS, :])
        for pair in range(QUAD // 2):
            cols = ref_t[:, pair * LANES : (pair + 1) * LANES]
            slot = quad * 2 + pair
            ref_cols[slot] = cols
            masked = cols * mask_cols
            if quad == 0:
                rhs = jnp.concatenate(
                    [
                        shifted(left, mine, line * CHANNELS, offsets[base + line])
                        for line in (2 * slot, 2 * slot + 1)
                    ],
                    axis=0,
                )
            for side in range(2):
                line = 2 * slot + side
                for t in range(RUN):
                    picked = ref_cols[slot, pl.ds(t, PARTS, stride=RUN), :]
                    picked = jnp.where(half_lane if side == 0 else ~half_lane, picked, 0.0)
                    at = t * LANES + line * PARTS
                    gate_rows[at : at + PARTS, :] = picked.astype(BF)
                lhs = jnp.where(span_lane if side == 0 else ~span_lane, masked, 0.0).astype(BF)
                if quad == 0:
                    line_costs(lhs, rhs, line, skew, cost_rows)
                else:
                    lhs_out[line - QUAD] = lhs

    place = iota((KEYS, LANES), 1)
    x_base = SPAN - 1 - RUN * (place & (PARTS - 1))
    row = iota((KEYS, LANES), 0)
    reach = jnp.where(row >= 2 * GROUPS, 9, jnp.where(row >= GROUPS, 3, 1))
    room_left = x_base - reach - low
    room_right = x_base + reach - SPAN
    for two in range(RUN // 2):
        at = 2 * two * LANES
        logits = dot_t(guide[...], gate_rows[at : at + 2 * LANES, :])
        for i in range(2):
            t = 2 * two + i
            normalise(logits[:, i * LANES : (i + 1) * LANES], wts, t, room_left, room_right)


def late_kernel(
    offsets, mine, left, lhs, early_rows, wts, flip, out, skew, cost_rows, vol, vals, turned
):
    base = lax.axis_index("view") * LINES
    for pair in range(QUAD // 2):
        rhs = jnp.concatenate(
            [
                shifted(left, mine, line * CHANNELS, offsets[base + QUAD + line])
                for line in (2 * pair, 2 * pair + 1)
            ],
            axis=0,
        )
        for line in (2 * pair, 2 * pair + 1):
            line_costs(lhs[line], rhs, line, skew, cost_rows)

    for two in range(RUN // 2):
        rows = []
        for t in (2 * two, 2 * two + 1):
            for part in (early_rows, cost_rows):
                rows.append(part[t * QUAD_LANES : (t + 1) * QUAD_LANES, :])
        costs = dot_t(flip[...], jnp.concatenate(rows, axis=0))
        vol[2 * two] = costs[:, :LANES]
        vol[2 * two + 1] = costs[:, LANES:]

    def aggregate(group, carry):
        for half in range(2):
            at = pl.multiple_of(group * DGROUP + half * 8, 8)
            v = [vol[t, pl.ds(at, 8), :] for t in range(RUN)]
            for layer in range(LAYERS):
                s = 3**layer
                before = [v[t + s] if t + s < RUN else pltpu.roll(v[t + s - RUN], LANES - 1, 1) for t in range(RUN)]
                after = [v[t - s] if t >= s else pltpu.roll(v[t - s + RUN], 1, 1) for t in range(RUN)]
                fresh = []
                for t in range(RUN):
                    w = [wts[t, pl.ds(k * KEYS + layer * GROUPS + group, 1), :] for k in range(3)]
                    fresh.append(w[0] * before[t] + w[1] * v[t] + w[2] * after[t])
                v = fresh
            for t in range(RUN):
                vol[t, pl.ds(at, 8), :] = v[t]
        return carry

    lax.fori_loop(0, GROUPS, aggregate, 0)

    vals[...] = jnp.zeros((LANES, LANES), F32)
    sub = iota((8, LANES), 0).astype(F32)
    line_of = iota((1, LANES), 1) >> 4
    offs = jnp.zeros((1, LANES), F32)
    for line in range(LINES):
        offs = jnp.where(line_of == line, offsets[base + line].astype(F32), offs)

    def softmax(t, carry):
        v = [vol[t, 8 * i : 8 * i + 8, :] for i in range(DISP // 8)]
        top = v
        while len(top) > 1:
            top = [jnp.maximum(a, b) for a, b in zip(top[::2], top[1::2])] + top[len(top) & ~1 :]
        top = jnp.max(top[0], axis=0, keepdims=True)
        e = [jnp.exp(SHARPNESS * (a - top)) for a in v]
        total = e[0]
        moment = jnp.zeros((8, LANES), F32)
        for i in range(1, DISP // 8):
            total = total + e[i]
            moment = moment + float(8 * i) * e[i]
        moment = jnp.sum(moment + sub * total, axis=0, keepdims=True)
        total = jnp.sum(total, axis=0, keepdims=True)
        vals[pl.ds(RUN - 1 - t, 1), :] = (moment / total + offs) * (1.0 / DISP)
        return carry

    lax.fori_loop(0, RUN, softmax, 0)

    turned[...] = jnp.transpose(vals[...])
    lane = iota((8, LANES), 1)
    result = [jnp.zeros((8, LANES), F32) for _ in range(WIDE // LANES)]
    for part in range(PARTS):
        piece = turned[pl.ds(part, LINES, stride=PARTS), :]
        start = (RUN * (PARTS - 1 - part) - HALO) % WIDE
        tile, turn = divmod(start, LANES)
        if turn:
            piece = pltpu.roll(piece, turn, 1)
        if turn + RUN > LANES:
            after = (tile + 1) % len(result)
            result[after] = result[after] + jnp.where(lane < turn, piece, 0.0)
            piece = jnp.where(lane >= turn, piece, 0.0)
        result[tile] = result[tile] + piece
    for tile, value in enumerate(result):
        out[:, tile * LANES : (tile + 1) * LANES] = value


def join(pieces, sub, n):
    block = lax.axis_index("cols")
    pieces = pieces.reshape(n, 2, LINES, WIDE)
    start = (0, block // (n // 2), (block % (n // 2)) * sub, 0)
    pieces = lax.dynamic_slice(pieces, start, (n, 1, sub, WIDE))[:, 0]
    main = pieces[:, :, :BLOCK]
    tail = jnp.pad(pieces[1:, :, BLOCK:], ((0, 1), (0, 0), (LANES, 0)))
    place = (n, sub, BLOCK)
    keep = (iota(place, 2) < BLOCK - CUT) | (iota(place, 0) == n - 1)
    joined = jnp.where(keep, main, tail)
    return jnp.transpose(joined, (1, 0, 2)).reshape(1, sub, n * BLOCK)


def halo_plan(features, valid_cols, offsets, guide_weight):
    own = features[0]
    n = lax.axis_size("cols")
    right = [(c, c + 1) for c in range(n - 1)]
    other = lax.ppermute(own, "view", [(0, 1), (1, 0)])
    near, masks, perm, flip, guide = call(
        prefetch_kernel,
        [(own.shape, BF), (valid_cols.shape, F32), ((SPAN, WIDE), BF), ((DISP, 2 * LANES), BF), ((3 * KEYS, LANES), BF)],
        [pltpu.VMEM(valid_cols.shape, jnp.int32), pltpu.VMEM(guide_weight.shape, BF), pltpu.SemaphoreType.DMA((3,))],
        0, (own, valid_cols, guide_weight), 100_000_000, pl.ANY, 24, pltpu.VMEM,
    )
    first, second, ref_own = call(
        payload_kernel,
        [((PAYLOAD, BLOCK), BF), ((QUAD_ROWS, BLOCK), BF), ((SEC_ROWS, BLOCK), BF)],
        [], 0, (near, other, masks),
    )
    left_first = lax.ppermute(first, "cols", right)
    left_second = lax.ppermute(second, "cols", right)
    quad_rows = (RUN * QUAD_LANES, 2 * LANES)
    skew = pltpu.VMEM((QUAD, 2, SPAN, LANES), F32)
    square = pltpu.VMEM((LANES, LANES), F32)
    wts, early_rows, lhs = call(
        early_kernel,
        [((RUN, 3 * KEYS, LANES), F32), (quad_rows, BF), ((QUAD, SPAN, LANES), BF)],
        [pltpu.VMEM((SEC_ROWS, WIDE), BF), pltpu.VMEM((QUAD, SPAN, LANES), F32), pltpu.VMEM((RUN * LANES, LANES), BF), skew],
        1, (offsets, ref_own, first, left_first, masks, perm, guide), 1_000_000_000,
    )
    (result,) = call(
        late_kernel,
        [((LINES, WIDE), F32)],
        [skew, pltpu.VMEM(quad_rows, BF), pltpu.VMEM((RUN, DISP, LANES), F32), square, square],
        1, (offsets, second, left_second, lhs, early_rows, wts, flip), 1_000_000_000,
    )
    copies = jnp.broadcast_to(result[None], (2 * n, LINES, WIDE))
    pieces = lax.all_to_all(copies, ("cols", "view"), split_axis=0, concat_axis=0, tiled=True)
    return join(pieces, own.shape[0] // n, n)


LINE_RUN = 16
PAIR = 2
LINE_PARTS = LANES // PAIR


MASKS = 8


def pack_kernel(key, own, *rest):
    out = rest[-1]
    me = 2 * lax.axis_index("cols") + lax.axis_index("view")
    rows = PAIR * CHANNELS
    out[:rows, :] = own[me ^ key]
    if out.shape[0] > rows:
        masks = rest[0][...].astype(F32)
        out[rows:, :] = jnp.where(
            iota((MASKS, BLOCK), 0) < MASKS // 2, masks[0:1, :], masks[1:2, :]
        ).astype(BF)


def constants_kernel(offsets, guide, valid, order, flip, guide_out, spread, masks):
    masks[...] = valid[...].astype(F32)
    row = iota((LANES, LANES), 0)
    from_lane = LANES - 1 - LINE_RUN * (row & 7) - (row >> 3)
    order[...] = jnp.where(iota((LANES, LANES), 1) == from_lane, 1.0, 0.0).astype(BF)
    back = 2 * LANES - 1 - iota((DISP, 2 * LANES), 0)
    flip[...] = jnp.where(iota((DISP, 2 * LANES), 1) == back, 1.0, 0.0).astype(BF)
    guide_out[...] = spread_guide(guide[...])
    block_of = LINE_PARTS - 1 - (iota(spread.shape, 1) >> 4)
    here = (iota(spread.shape, 0) & (LINE_PARTS - 1)) == block_of
    spread[...] = jnp.where(here, 1.0, 0.0).astype(BF)


def lines_kernel(
    offsets, order, flip, guide, spread, *rest
):
    pieces, (out, blocks, valid, gate_rows, cost_rows, vol, done, wts) = rest[:-8], rest[-8:]
    near, pieces = pieces[0], pieces[1:]
    tiles = len(pieces)
    width = tiles * LANES
    me = 2 * lax.axis_index("cols") + lax.axis_index("view")
    rows = PAIR * CHANNELS
    for key, piece in enumerate(pieces):
        blocks[me ^ key] = piece[:rows, :]
        if piece.shape[0] > rows:
            masks = piece[rows:, :].astype(F32)
            valid[(me ^ key) // 2] = jnp.concatenate([masks[0:1], masks[MASKS // 2 : MASKS // 2 + 1]], axis=0)
    valid[me // 2] = near[...]
    at = PAIR * me
    offs = [offsets[at + i] for i in range(PAIR)]
    ch_lane = iota((CHANNELS, LANES), 1)
    diagonal = iota((8, LANES), 1) - LINE_RUN * iota((8, LANES), 0)
    low_half = iota((LANES, LANES), 1) < CHANNELS
    scale = 1.0 / math.sqrt(CHANNELS)
    empty = jnp.zeros((CHANNELS, LANES), F32)

    def mask_of(view, w):
        lo = (w % 2) * LANES
        return valid[w // 2, view : view + 1, lo : lo + LANES]

    for i in range(PAIR):

        def tile_of(view, w):
            lo = (w % 2) * LANES
            return blocks[2 * (w // 2) + view, i * CHANNELS : (i + 1) * CHANNELS, lo : lo + LANES]

        off = offs[i]
        rolled = [pltpu.roll(tile_of(1, w).astype(F32) * mask_of(1, w), off, 1) for w in range(tiles)]
        shifted = [empty.astype(BF)] * 2
        for w in range(tiles):
            shifted.append(jnp.where(ch_lane < off, rolled[w - 1] if w else empty, rolled[w]).astype(BF))
        shifted = [jnp.concatenate([tile, tile], axis=0) for tile in shifted]
        for quad in range(tiles // 4):
            refs = [tile_of(0, 4 * quad + q) for q in range(4)]
            masked = [refs[q] * (mask_of(0, 4 * quad + q) * scale).astype(BF) for q in range(4)]
            cols = dot_t(order[...], jnp.concatenate(refs, axis=0))
            masked = dot_t(order[...], jnp.concatenate(masked, axis=0))
            for two in range(2):
                lo = two * LANES
                gates, products = [], []
                for side in range(2):
                    w = 4 * quad + 2 * two + side
                    keep = low_half if side == 0 else ~low_half
                    gates.append(jnp.where(keep, cols[:, lo : lo + LANES], 0.0))
                    lhs = jnp.where(keep, masked[:, lo : lo + LANES], 0.0).astype(BF)
                    rhs = jnp.concatenate(shifted[w : w + 3], axis=1)
                    products.append(jnp.dot(lhs, rhs, preferred_element_type=F32))
                place = i * LINE_PARTS + 8 * (tiles - 2 - 4 * quad - 2 * two)
                for t in range(LINE_RUN):
                    row = t * LANES + place
                    r = 8 * t
                    gate_rows[row : row + 16, :] = jnp.concatenate(
                        [gates[1][r : r + 8], gates[0][r : r + 8]], axis=0
                    ).astype(BF)
                    beyond = diagonal >= t
                    both = []
                    for side in (1, 0):
                        turned = [
                            pltpu.roll(
                                products[side][r : r + 8, m * LANES : (m + 1) * LANES],
                                t, 1, stride=LINE_RUN, stride_axis=0,
                            )
                            for m in range(3)
                        ]
                        both.append(
                            jnp.concatenate(
                                [jnp.where(beyond, turned[1], turned[0]), jnp.where(beyond, turned[2], turned[1])],
                                axis=1,
                            )
                        )
                    cost_rows[row : row + 16, :] = jnp.concatenate(both, axis=0).astype(BF)

    x_base = width - 1 - LINE_RUN * (iota((KEYS, LANES), 1) & (LINE_PARTS - 1))
    row = iota((KEYS, LANES), 0)
    reach = jnp.where(row >= 2 * GROUPS, 9, jnp.where(row >= GROUPS, 3, 1))
    room_left = x_base - reach
    room_right = x_base + reach - width
    for two in range(LINE_RUN // 2):
        lo = 2 * two * LANES
        costs = dot_t(flip[...], cost_rows[lo : lo + 2 * LANES, :])
        logits = dot_t(guide[...], gate_rows[lo : lo + 2 * LANES, :])
        for i in range(2):
            t = 2 * two + i
            vol[t] = costs[:, i * LANES : (i + 1) * LANES]
            normalise(logits[:, i * LANES : (i + 1) * LANES], wts, t, room_left, room_right)

    for group in range(GROUPS):
        for at in (group * DGROUP, group * DGROUP + 8):
            v = [vol[t, at : at + 8, :] for t in range(LINE_RUN)]
            for layer in range(LAYERS):
                s = 3**layer
                fresh = []
                for t in range(LINE_RUN):
                    rows = [k * KEYS + layer * GROUPS + group for k in range(3)]
                    w = [wts[t, r : r + 1, :] for r in rows]
                    blk, r = divmod(t + s, LINE_RUN)
                    before = pltpu.roll(v[r], LANES - blk, 1) if blk else v[r]
                    blk, r = divmod(t - s, LINE_RUN)
                    after = pltpu.roll(v[r], -blk, 1) if blk else v[r]
                    fresh.append(w[0] * before + w[1] * v[t] + w[2] * after)
                v = fresh
            for t in range(LINE_RUN):
                done[t, at : at + 8, :] = v[t]

    sub = iota((8, LANES), 0)
    results = []
    for block in range(LINE_RUN // 8):
        totals = jnp.zeros((8, LANES), F32)
        moments = totals
        for s in range(8):
            t = LINE_RUN - 1 - (8 * block + s)
            v = [done[t, 8 * i : 8 * i + 8, :] for i in range(DISP // 8)]
            top = v
            while len(top) > 1:
                top = [jnp.maximum(a, b) for a, b in zip(top[::2], top[1::2])] + top[len(top) & ~1 :]
            top = jnp.max(top[0], axis=0, keepdims=True)
            total = jnp.zeros((8, LANES), F32)
            moment = total
            for i in range(DISP // 8):
                e = jnp.exp(SHARPNESS * (v[i] - top))
                total = total + e
                if i:
                    moment = moment + float(8 * i) * e
            moment = moment + sub.astype(F32) * total
            totals = jnp.where(sub == s, jnp.sum(total, axis=0, keepdims=True), totals)
            moments = jnp.where(sub == s, jnp.sum(moment, axis=0, keepdims=True), moments)
        lane_line = iota((8, LANES), 1) >> 6
        shift = jnp.zeros((8, LANES), F32)
        for i in range(PAIR):
            shift = jnp.where(lane_line == i, offs[i].astype(F32), shift)
        results.append((moments / totals + shift) * (1.0 / DISP))
    vals = jnp.concatenate(results, axis=0)
    lane_line = iota((LINE_RUN, LANES), 1) >> 6
    both = jnp.concatenate([jnp.where(lane_line == i, vals, 0.0) for i in range(PAIR)], axis=0)
    high = both.astype(BF)
    rest = both - high.astype(F32)
    middle = rest.astype(BF)
    low = (rest - middle.astype(F32)).astype(BF)
    pieces = jnp.dot(
        jnp.concatenate([high, middle, low], axis=0), spread[...], preferred_element_type=F32
    )
    size = PAIR * LINE_RUN
    pieces = pieces[:size] + pieces[size : 2 * size] + pieces[2 * size :]
    wanted = iota((LINE_RUN, width), 0) == (iota((LINE_RUN, width), 1) & (LINE_RUN - 1))
    for i in range(PAIR):
        piece = jnp.where(wanted, pieces[i * LINE_RUN : (i + 1) * LINE_RUN], 0.0)
        out[i : i + 1, :] = jnp.sum(piece, axis=0, keepdims=True)


def lines_plan(features, valid_cols, offsets, guide_weight):
    n = lax.axis_size("cols")
    devices = 2 * n
    width = n * BLOCK
    rows = PAIR * CHANNELS
    own = features.reshape(devices, rows, BLOCK)
    pieces = [None] * devices
    gone = ()
    for key in (1, 2, 6, 4, 7, 5, 3, 0):
        masked = key % 2 and key > 1
        (piece,) = call(
            functools.partial(pack_kernel, key),
            [((rows + (MASKS if masked else 0), BLOCK), BF)],
            [], 0,
            (own,) + ((valid_cols,) if masked else ()) + gone,
            1_000_000,
        )
        gone = (piece,)
        moves = [(i, i ^ key) for i in range(devices)]
        pieces[key] = lax.ppermute(piece, ("cols", "view"), moves) if key else piece
    consts = call(
        constants_kernel,
        [
            ((LANES, LANES), BF), ((DISP, 2 * LANES), BF), ((3 * KEYS, LANES), BF), ((LANES, width), BF),
            (valid_cols.shape, F32),
        ],
        [], 1, (offsets, guide_weight, valid_cols), 1_000_000,
    )
    (rows,) = call(
        lines_kernel,
        [((PAIR, width), F32)],
        [
            pltpu.VMEM((devices, rows, BLOCK), BF),
            pltpu.VMEM((n,) + valid_cols.shape, F32),
            pltpu.VMEM((LINE_RUN * LANES, LANES), BF),
            pltpu.VMEM((LINE_RUN * LANES, 2 * LANES), BF),
            pltpu.VMEM((LINE_RUN, DISP, LANES), F32),
            pltpu.VMEM((LINE_RUN, DISP, LANES), F32),
            pltpu.VMEM((LINE_RUN, 3 * KEYS, LANES), F32),
        ],
        1, (offsets, *consts, *pieces), 1_000_000_000,
    )
    return lax.all_gather(rows, "view", axis=0, tiled=True)[None]


def on_device(features, valid_cols, offsets, guide_weight):
    n = lax.axis_size("cols")
    lines = features.shape[1]
    if lines == 2 * PAIR * n and n * BLOCK == LINE_RUN * LINE_PARTS:
        return lines_plan(features, valid_cols, offsets, guide_weight)
    return halo_plan(features, valid_cols, offsets, guide_weight)


def solution(mesh):
    return jax.shard_map(
        on_device,
        mesh=mesh,
        in_specs=(
            P("view", ("tiles", "lines"), None, "cols"),
            P(None, ("tiles", "cols")),
            P(("tiles", "lines")),
            P(),
        ),
        out_specs=P(("tiles", "lines"), "cols", None),
        check_vma=False,
    )
```

```python
import functools
import math

import jax
import jax.numpy as jnp
from jax import lax
from jax.experimental import pallas as pl
from jax.experimental.pallas import tpu as pltpu
from jax.sharding import PartitionSpec as P

DISP = 192
DGROUP = 16
GROUPS = DISP // DGROUP
LAYERS = 3
SHARPNESS = 2.0
HALO = 32
LANES = 128
LINES = 8
CHANNELS = 64
BLOCK = 256
SPAN = BLOCK + HALO
PARTS = LANES // LINES
RUN = SPAN // PARTS
KEYS = 40
WIDE = BLOCK + LANES
SEC_ROWS = LINES * CHANNELS
QUAD_ROWS = SEC_ROWS // 2
MASK_AT = QUAD_ROWS + CHANNELS
PAYLOAD = MASK_AT + 16
QUAD = LINES // 2
QUAD_LANES = LANES // 2
PACK = LANES // HALO
CUT = 16

BF = jnp.bfloat16
F32 = jnp.float32


def iota(shape, dim):
    return lax.broadcasted_iota(jnp.int32, shape, dim)


def dot_t(a, b):
    return lax.dot_general(a, b, (((1,), (1,)), ((), ())), preferred_element_type=F32)


def call(kernel, outs, scratch, smem, args, flops=0, space=pltpu.VMEM, limit=24, to=None):
    specs = [pl.BlockSpec(memory_space=pltpu.SMEM)] * smem
    specs += [pl.BlockSpec(memory_space=space)] * (len(args) - smem)
    return pl.pallas_call(
        kernel,
        out_shape=[jax.ShapeDtypeStruct(shape, dtype) for shape, dtype in outs],
        in_specs=specs,
        out_specs=[pl.BlockSpec(memory_space=to or space)] * len(outs),
        scratch_shapes=scratch,
        compiler_params=pltpu.CompilerParams(vmem_limit_bytes=limit * 1024 * 1024),
        cost_estimate=pl.CostEstimate(flops=flops, bytes_accessed=1_000_000, transcendentals=0),
    )(*args)


def spread_guide(guide):
    keys = LAYERS * 3 * GROUPS
    row = iota((3 * KEYS, keys), 0)
    tap = jnp.where(row >= KEYS, 1, 0) + jnp.where(row >= 2 * KEYS, 1, 0)
    row = row - KEYS * tap
    layer = jnp.where(row >= GROUPS, 1, 0) + jnp.where(row >= 2 * GROUPS, 1, 0)
    key = 2 * GROUPS * layer + GROUPS * tap + row
    chosen = jnp.where((iota((3 * KEYS, keys), 1) == key) & (row < 3 * GROUPS), 1.0, 0.0).astype(BF)
    guide_t = dot_t(chosen, guide).astype(BF)
    return jnp.concatenate([guide_t, guide_t], axis=1)


def normalise(z, wts, t, room_left, room_right):
    z = (0.55 + 0.45 * jnp.tanh(0.5 * z)).astype(BF).astype(F32)
    taps = [z[k * KEYS : (k + 1) * KEYS] for k in range(3)]
    scale = 1.0 / (taps[0] + taps[1] + taps[2])
    wts[t, 0:KEYS, :] = jnp.where(room_left >= t, taps[0] * scale, 0.0)
    wts[t, KEYS : 2 * KEYS, :] = taps[1] * scale
    wts[t, 2 * KEYS : 3 * KEYS, :] = jnp.where(room_right < t, taps[2] * scale, 0.0)


def prefetch_kernel(own, valid, guide, own_out, masks, perm, flip, guide_out, valid_in, guide_in, sems):
    copies = [
        pltpu.make_async_copy(src, dst, sems.at[i])
        for i, (src, dst) in enumerate([(own, own_out), (guide, guide_in), (valid, valid_in)])
    ]
    for copy in copies:
        copy.start()
    perm[...] = jnp.where(
        iota((SPAN, WIDE), 1) == WIDE - 1 - iota((SPAN, WIDE), 0), 1.0, 0.0
    ).astype(BF)
    back = 2 * LANES - 1 - iota((DISP, 2 * LANES), 0)
    flip[...] = jnp.where(iota((DISP, 2 * LANES), 1) == back, 1.0, 0.0).astype(BF)

    copies[1].wait()
    guide_out[...] = spread_guide(guide_in[...])
    copies[2].wait()
    masks[...] = valid_in[...].astype(F32)
    copies[0].wait()


def payload_kernel(own, other, masks, first, second, ref_own):
    view = lax.axis_index("view")
    first_view = view == 0
    sec_mask = masks[1:2, :].astype(BF)
    lane = iota((CHANNELS, LANES), 1)
    tails = []
    for line in range(LINES):
        at = view * LINES + line
        mine, theirs = own[at], other[at]
        lo = line * CHANNELS
        dest, start = (first, lo) if line < QUAD else (second, lo - QUAD_ROWS)
        dest[start : start + CHANNELS, :] = jnp.where(first_view, theirs, mine) * sec_mask
        ref = jnp.where(first_view, mine, theirs)
        ref_own[lo : lo + CHANNELS, :] = ref
        tail = ref[:, BLOCK - LANES :].astype(F32)
        slot = line % PACK
        turn = (HALO * (slot + 1)) % LANES
        if turn:
            tail = pltpu.roll(tail, turn, 1)
        if slot:
            tails[-1] = jnp.where(lane >= HALO * slot, tail, tails[-1])
        else:
            tails.append(tail)
    for i, tail in enumerate(tails):
        first[QUAD_ROWS:MASK_AT, i * LANES : (i + 1) * LANES] = tail.astype(BF)
    first[MASK_AT:, :] = jnp.broadcast_to(masks[0:1, :], (16, BLOCK)).astype(BF)


def shifted(left, mine, lo, off):
    ch_lane = iota((CHANNELS, LANES), 1)
    tiles = [
        src[lo : lo + CHANNELS, i * LANES : (i + 1) * LANES].astype(F32)
        for src in (left, mine)
        for i in range(2)
    ]
    tiles = [pltpu.roll(tile, off, 1) for tile in tiles]
    tiles = [jnp.where(ch_lane < off, tiles[max(i - 1, 0)], tiles[i]).astype(BF) for i in range(4)]
    return jnp.concatenate(tiles, axis=1)


def line_costs(lhs, rhs, slot, skew, cost_rows):
    diagonal = iota((8, LANES), 1) - iota((8, LANES), 0)
    for chunk in range(3):
        rows = min(LANES, SPAN - chunk * LANES)
        first = max(1 - chunk, 0)
        last = 3 - chunk
        products = jnp.dot(
            lhs[chunk * LANES : chunk * LANES + rows],
            rhs[:, first * LANES : (last + 1) * LANES],
            preferred_element_type=F32,
        )
        for j in range(rows // 8):
            tiles = [
                pltpu.roll(
                    products[8 * j : 8 * j + 8, i * LANES : (i + 1) * LANES],
                    8 * j, 1, stride=1, stride_axis=0,
                )
                for i in range(last + 1 - first)
            ]
            if len(tiles) < 3:
                tiles = [tiles[0]] + tiles
            beyond = diagonal >= 8 * j
            at = chunk * LANES + 8 * j
            skew[slot, 0, at : at + 8, :] = jnp.where(beyond, tiles[1], tiles[0])
            skew[slot, 1, at : at + 8, :] = jnp.where(beyond, tiles[2], tiles[1])
    for t in range(RUN):
        at = t * QUAD_LANES + slot * PARTS
        for v in range(2):
            cost_rows[at : at + PARTS, v * LANES : (v + 1) * LANES] = skew[
                slot, v, pl.ds(t, PARTS, stride=RUN), :
            ].astype(BF)


def early_kernel(
    offsets, ref_own, mine, left, masks, perm, guide, wts, cost_rows, lhs_out,
    ref_rows, ref_cols, gate_rows, skew
):
    base = lax.axis_index("view") * LINES
    low = jnp.where(lax.axis_index("cols") == 0, HALO, 0)
    for line in range(LINES):
        lo = line * CHANNELS
        ref_rows[lo : lo + CHANNELS, LANES:] = ref_own[lo : lo + CHANNELS, :]
        half = line // PACK
        packed = left[QUAD_ROWS:MASK_AT, half * LANES : (half + 1) * LANES].astype(F32)
        turn = (LANES - HALO) - HALO * (line % PACK)
        if turn:
            packed = pltpu.roll(packed, turn, 1)
        ref_rows[lo : lo + CHANNELS, :LANES] = packed.astype(BF)

    mask_left = left[MASK_AT : MASK_AT + 1, BLOCK - LANES :].astype(F32)
    ref_mask = jnp.concatenate([mask_left, masks[0:1, :]], axis=1)
    ref_mask = jnp.broadcast_to(ref_mask * (1.0 / math.sqrt(CHANNELS)), (LANES, WIDE))
    mask_cols = dot_t(perm[...], ref_mask.astype(BF))
    half_lane = iota((PARTS, LANES), 1) < CHANNELS
    span_lane = iota((SPAN, LANES), 1) < CHANNELS

    for quad in range(LINES // QUAD):
        ref_t = dot_t(perm[...], ref_rows[quad * QUAD_ROWS : (quad + 1) * QUAD_ROWS, :])
        for pair in range(QUAD // 2):
            cols = ref_t[:, pair * LANES : (pair + 1) * LANES]
            slot = quad * 2 + pair
            ref_cols[slot] = cols
            masked = cols * mask_cols
            if quad == 0:
                rhs = jnp.concatenate(
                    [
                        shifted(left, mine, line * CHANNELS, offsets[base + line])
                        for line in (2 * slot, 2 * slot + 1)
                    ],
                    axis=0,
                )
            for side in range(2):
                line = 2 * slot + side
                for t in range(RUN):
                    picked = ref_cols[slot, pl.ds(t, PARTS, stride=RUN), :]
                    picked = jnp.where(half_lane if side == 0 else ~half_lane, picked, 0.0)
                    at = t * LANES + line * PARTS
                    gate_rows[at : at + PARTS, :] = picked.astype(BF)
                lhs = jnp.where(span_lane if side == 0 else ~span_lane, masked, 0.0).astype(BF)
                if quad == 0:
                    line_costs(lhs, rhs, line, skew, cost_rows)
                else:
                    lhs_out[line - QUAD] = lhs

    place = iota((KEYS, LANES), 1)
    x_base = SPAN - 1 - RUN * (place & (PARTS - 1))
    row = iota((KEYS, LANES), 0)
    reach = jnp.where(row >= 2 * GROUPS, 9, jnp.where(row >= GROUPS, 3, 1))
    room_left = x_base - reach - low
    room_right = x_base + reach - SPAN
    for two in range(RUN // 2):
        at = 2 * two * LANES
        logits = dot_t(guide[...], gate_rows[at : at + 2 * LANES, :])
        for i in range(2):
            t = 2 * two + i
            normalise(logits[:, i * LANES : (i + 1) * LANES], wts, t, room_left, room_right)


def late_kernel(
    offsets, mine, left, lhs, early_rows, wts, flip, out, skew, cost_rows, vol, vals, turned
):
    base = lax.axis_index("view") * LINES
    for pair in range(QUAD // 2):
        rhs = jnp.concatenate(
            [
                shifted(left, mine, line * CHANNELS, offsets[base + QUAD + line])
                for line in (2 * pair, 2 * pair + 1)
            ],
            axis=0,
        )
        for line in (2 * pair, 2 * pair + 1):
            line_costs(lhs[line], rhs, line, skew, cost_rows)

    for two in range(RUN // 2):
        rows = []
        for t in (2 * two, 2 * two + 1):
            for part in (early_rows, cost_rows):
                rows.append(part[t * QUAD_LANES : (t + 1) * QUAD_LANES, :])
        costs = dot_t(flip[...], jnp.concatenate(rows, axis=0))
        vol[2 * two] = costs[:, :LANES]
        vol[2 * two + 1] = costs[:, LANES:]

    def aggregate(group, carry):
        for half in range(2):
            at = pl.multiple_of(group * DGROUP + half * 8, 8)
            v = [vol[t, pl.ds(at, 8), :] for t in range(RUN)]
            for layer in range(LAYERS):
                s = 3**layer
                before = [v[t + s] if t + s < RUN else pltpu.roll(v[t + s - RUN], LANES - 1, 1) for t in range(RUN)]
                after = [v[t - s] if t >= s else pltpu.roll(v[t - s + RUN], 1, 1) for t in range(RUN)]
                fresh = []
                for t in range(RUN):
                    w = [wts[t, pl.ds(k * KEYS + layer * GROUPS + group, 1), :] for k in range(3)]
                    fresh.append(w[0] * before[t] + w[1] * v[t] + w[2] * after[t])
                v = fresh
            for t in range(RUN):
                vol[t, pl.ds(at, 8), :] = v[t]
        return carry

    lax.fori_loop(0, GROUPS, aggregate, 0)

    vals[...] = jnp.zeros((LANES, LANES), F32)
    sub = iota((8, LANES), 0).astype(F32)
    line_of = iota((1, LANES), 1) >> 4
    offs = jnp.zeros((1, LANES), F32)
    for line in range(LINES):
        offs = jnp.where(line_of == line, offsets[base + line].astype(F32), offs)

    def softmax(t, carry):
        v = [vol[t, 8 * i : 8 * i + 8, :] for i in range(DISP // 8)]
        top = v
        while len(top) > 1:
            top = [jnp.maximum(a, b) for a, b in zip(top[::2], top[1::2])] + top[len(top) & ~1 :]
        top = jnp.max(top[0], axis=0, keepdims=True)
        e = [jnp.exp(SHARPNESS * (a - top)) for a in v]
        total = e[0]
        moment = jnp.zeros((8, LANES), F32)
        for i in range(1, DISP // 8):
            total = total + e[i]
            moment = moment + float(8 * i) * e[i]
        moment = jnp.sum(moment + sub * total, axis=0, keepdims=True)
        total = jnp.sum(total, axis=0, keepdims=True)
        vals[pl.ds(RUN - 1 - t, 1), :] = (moment / total + offs) * (1.0 / DISP)
        return carry

    lax.fori_loop(0, RUN, softmax, 0)

    turned[...] = jnp.transpose(vals[...])
    lane = iota((8, LANES), 1)
    result = [jnp.zeros((8, LANES), F32) for _ in range(WIDE // LANES)]
    for part in range(PARTS):
        piece = turned[pl.ds(part, LINES, stride=PARTS), :]
        start = (RUN * (PARTS - 1 - part) - HALO) % WIDE
        tile, turn = divmod(start, LANES)
        if turn:
            piece = pltpu.roll(piece, turn, 1)
        if turn + RUN > LANES:
            after = (tile + 1) % len(result)
            result[after] = result[after] + jnp.where(lane < turn, piece, 0.0)
            piece = jnp.where(lane >= turn, piece, 0.0)
        result[tile] = result[tile] + piece
    for tile, value in enumerate(result):
        out[:, tile * LANES : (tile + 1) * LANES] = value


def join(pieces, sub, n):
    block = lax.axis_index("cols")
    pieces = pieces.reshape(n, 2, LINES, WIDE)
    start = (0, block // (n // 2), (block % (n // 2)) * sub, 0)
    pieces = lax.dynamic_slice(pieces, start, (n, 1, sub, WIDE))[:, 0]
    main = pieces[:, :, :BLOCK]
    tail = jnp.pad(pieces[1:, :, BLOCK:], ((0, 1), (0, 0), (LANES, 0)))
    place = (n, sub, BLOCK)
    keep = (iota(place, 2) < BLOCK - CUT) | (iota(place, 0) == n - 1)
    joined = jnp.where(keep, main, tail)
    return jnp.transpose(joined, (1, 0, 2)).reshape(1, sub, n * BLOCK)


def halo_plan(features, valid_cols, offsets, guide_weight):
    own = features[0]
    n = lax.axis_size("cols")
    right = [(c, c + 1) for c in range(n - 1)]
    other = lax.ppermute(own, "view", [(0, 1), (1, 0)])
    near, masks, perm, flip, guide = call(
        prefetch_kernel,
        [(own.shape, BF), (valid_cols.shape, F32), ((SPAN, WIDE), BF), ((DISP, 2 * LANES), BF), ((3 * KEYS, LANES), BF)],
        [pltpu.VMEM(valid_cols.shape, jnp.int32), pltpu.VMEM(guide_weight.shape, BF), pltpu.SemaphoreType.DMA((3,))],
        0, (own, valid_cols, guide_weight), 100_000_000, pl.ANY, 24, pltpu.VMEM,
    )
    first, second, ref_own = call(
        payload_kernel,
        [((PAYLOAD, BLOCK), BF), ((QUAD_ROWS, BLOCK), BF), ((SEC_ROWS, BLOCK), BF)],
        [], 0, (near, other, masks),
    )
    left_first = lax.ppermute(first, "cols", right)
    left_second = lax.ppermute(second, "cols", right)
    quad_rows = (RUN * QUAD_LANES, 2 * LANES)
    skew = pltpu.VMEM((QUAD, 2, SPAN, LANES), F32)
    square = pltpu.VMEM((LANES, LANES), F32)
    wts, early_rows, lhs = call(
        early_kernel,
        [((RUN, 3 * KEYS, LANES), F32), (quad_rows, BF), ((QUAD, SPAN, LANES), BF)],
        [pltpu.VMEM((SEC_ROWS, WIDE), BF), pltpu.VMEM((QUAD, SPAN, LANES), F32), pltpu.VMEM((RUN * LANES, LANES), BF), skew],
        1, (offsets, ref_own, first, left_first, masks, perm, guide), 1_000_000_000,
    )
    (result,) = call(
        late_kernel,
        [((LINES, WIDE), F32)],
        [skew, pltpu.VMEM(quad_rows, BF), pltpu.VMEM((RUN, DISP, LANES), F32), square, square],
        1, (offsets, second, left_second, lhs, early_rows, wts, flip), 1_000_000_000,
    )
    copies = jnp.broadcast_to(result[None], (2 * n, LINES, WIDE))
    pieces = lax.all_to_all(copies, ("cols", "view"), split_axis=0, concat_axis=0, tiled=True)
    return join(pieces, own.shape[0] // n, n)


LINE_RUN = 16
PAIR = 2
LINE_PARTS = LANES // PAIR


MASKS = 8
GATE_FLOOR = 11.0 / 9.0


def pack_kernel(key, own, *rest):
    out = rest[-1]
    me = 2 * lax.axis_index("cols") + lax.axis_index("view")
    rows = PAIR * CHANNELS
    out[:rows, :] = own[me ^ key]
    if out.shape[0] > rows:
        masks = rest[0][...].astype(F32)
        out[rows:, :] = jnp.where(
            iota((MASKS, BLOCK), 0) < MASKS // 2, masks[0:1, :], masks[1:2, :]
        ).astype(BF)


def constants_kernel(offsets, guide, valid, order, flip, guide_out, spread, masks):
    masks[...] = valid[...].astype(F32)
    row = iota((LANES, LANES), 0)
    from_lane = LANES - 1 - LINE_RUN * (row & 7) - (row >> 3)
    order[...] = jnp.where(iota((LANES, LANES), 1) == from_lane, 1.0, 0.0).astype(BF)
    back = 2 * LANES - 1 - iota((DISP, 2 * LANES), 0)
    flip[...] = jnp.where(iota((DISP, 2 * LANES), 1) == back, 1.0, 0.0).astype(BF)
    guide_out[...] = spread_guide(guide[...]) * 0.5
    block_of = LINE_PARTS - 1 - (iota(spread.shape, 1) >> 4)
    here = (iota(spread.shape, 0) & (LINE_PARTS - 1)) == block_of
    spread[...] = jnp.where(here, 1.0, 0.0).astype(BF)


def lines_kernel(
    offsets, order, flip, guide, spread, *rest
):
    pieces, (out, blocks, valid, gate_rows, cost_rows, vol, done, wts) = rest[:-8], rest[-8:]
    near, pieces = pieces[0], pieces[1:]
    tiles = len(pieces)
    width = tiles * LANES
    me = 2 * lax.axis_index("cols") + lax.axis_index("view")
    rows = PAIR * CHANNELS
    for key, piece in enumerate(pieces):
        blocks[me ^ key] = piece[:rows, :]
        if piece.shape[0] > rows:
            masks = piece[rows:, :].astype(F32)
            valid[(me ^ key) // 2] = jnp.concatenate([masks[0:1], masks[MASKS // 2 : MASKS // 2 + 1]], axis=0)
    valid[me // 2] = near[...]
    at = PAIR * me
    offs = [offsets[at + i] for i in range(PAIR)]
    ch_lane = iota((CHANNELS, LANES), 1)
    diagonal = iota((8, LANES), 1) - LINE_RUN * iota((8, LANES), 0)
    low_half = iota((LANES, LANES), 1) < CHANNELS
    scale = 1.0 / math.sqrt(CHANNELS)
    empty = jnp.zeros((CHANNELS, LANES), F32)

    def mask_of(view, w):
        lo = (w % 2) * LANES
        return valid[w // 2, view : view + 1, lo : lo + LANES]

    for i in range(PAIR):

        def tile_of(view, w):
            lo = (w % 2) * LANES
            return blocks[2 * (w // 2) + view, i * CHANNELS : (i + 1) * CHANNELS, lo : lo + LANES]

        off = offs[i]
        rolled = [pltpu.roll(tile_of(1, w).astype(F32) * mask_of(1, w), off, 1) for w in range(tiles)]
        shifted = [empty.astype(BF)] * 2
        for w in range(tiles):
            shifted.append(jnp.where(ch_lane < off, rolled[w - 1] if w else empty, rolled[w]).astype(BF))
        for quad in range(tiles // 4):
            refs = [tile_of(0, 4 * quad + q) for q in range(4)]
            masked = [refs[q] * (mask_of(0, 4 * quad + q) * scale).astype(BF) for q in range(4)]
            cols = dot_t(order[...], jnp.concatenate(refs, axis=0))
            masked = dot_t(order[...], jnp.concatenate(masked, axis=0))
            for two in range(2):
                lo = two * LANES
                gates, products = [], []
                lhs = masked[:, lo : lo + LANES].astype(BF)
                for side in range(2):
                    w = 4 * quad + 2 * two + side
                    keep = low_half if side == 0 else ~low_half
                    gates.append(jnp.where(keep, cols[:, lo : lo + LANES], 0.0))
                    window = jnp.concatenate(shifted[w : w + 3], axis=1)
                    rhs = [jnp.zeros_like(window)] * 2
                    rhs[side] = window
                    rhs = jnp.concatenate(rhs, axis=0)
                    products.append(jnp.dot(lhs, rhs, preferred_element_type=F32))
                place = i * LINE_PARTS + 8 * (tiles - 2 - 4 * quad - 2 * two)
                for t in range(LINE_RUN):
                    row = t * LANES + place
                    r = 8 * t
                    gate_rows[row : row + 16, :] = jnp.concatenate(
                        [gates[1][r : r + 8], gates[0][r : r + 8]], axis=0
                    ).astype(BF)
                    beyond = diagonal >= t
                    both = []
                    for side in (1, 0):
                        turned = [
                            pltpu.roll(
                                products[side][r : r + 8, m * LANES : (m + 1) * LANES],
                                t, 1, stride=LINE_RUN, stride_axis=0,
                            )
                            for m in range(3)
                        ]
                        both.append(
                            jnp.concatenate(
                                [jnp.where(beyond, turned[1], turned[0]), jnp.where(beyond, turned[2], turned[1])],
                                axis=1,
                            )
                        )
                    cost_rows[row : row + 16, :] = jnp.concatenate(both, axis=0).astype(BF)

    x_base = width - 1 - LINE_RUN * (iota((KEYS, LANES), 1) & (LINE_PARTS - 1))
    row = iota((KEYS, LANES), 0)
    reach = jnp.where(row >= 2 * GROUPS, 9, jnp.where(row >= GROUPS, 3, 1))
    room_left = x_base - reach
    room_right = x_base + reach - width
    unit = jnp.where(row >= 2 * GROUPS, SHARPNESS / math.log(2.0), 1.0)
    for two in range(LINE_RUN // 2):
        lo = 2 * two * LANES
        costs = dot_t(flip[...], cost_rows[lo : lo + 2 * LANES, :])
        logits = dot_t(guide[...], gate_rows[lo : lo + 2 * LANES, :])
        for i in range(2):
            t = 2 * two + i
            vol[t] = costs[:, i * LANES : (i + 1) * LANES]
            z = jnp.tanh(logits[:, i * LANES : (i + 1) * LANES]) + GATE_FLOOR
            taps = [z[m * KEYS : (m + 1) * KEYS] for m in range(3)]
            factor = unit / (taps[0] + taps[1] + taps[2])
            taps = [tap * factor for tap in taps]
            if t >= LINE_RUN - 9:
                taps[0] = jnp.where(room_left >= t, taps[0], 0.0)
            if t < 9:
                taps[2] = jnp.where(room_right < t, taps[2], 0.0)
            for m in range(3):
                wts[t, m * KEYS : (m + 1) * KEYS, :] = taps[m]

    for group in range(GROUPS):
        for at in (group * DGROUP, group * DGROUP + 8):
            v = [vol[t, at : at + 8, :] for t in range(LINE_RUN)]
            for layer in range(LAYERS):
                s = 3**layer
                fresh = []
                for t in range(LINE_RUN):
                    rows = [k * KEYS + layer * GROUPS + group for k in range(3)]
                    w = [wts[t, r : r + 1, :] for r in rows]
                    blk, r = divmod(t + s, LINE_RUN)
                    before = pltpu.roll(v[r], LANES - blk, 1) if blk else v[r]
                    blk, r = divmod(t - s, LINE_RUN)
                    after = pltpu.roll(v[r], -blk, 1) if blk else v[r]
                    fresh.append(w[0] * before + w[1] * v[t] + w[2] * after)
                v = fresh
            for t in range(LINE_RUN):
                done[t, at : at + 8, :] = v[t]

    sub = iota((8, LANES), 0)
    results = []
    for block in range(LINE_RUN // 8):
        totals = jnp.zeros((8, LANES), F32)
        moments = totals
        for s in range(8):
            t = LINE_RUN - 1 - (8 * block + s)
            v = [done[t, 8 * i : 8 * i + 8, :] for i in range(DISP // 8)]
            top = v
            while len(top) > 1:
                top = [jnp.maximum(a, b) for a, b in zip(top[::2], top[1::2])] + top[len(top) & ~1 :]
            top = jnp.max(top[0], axis=0, keepdims=True)
            total = jnp.exp2(v[-1] - top)
            moment = total
            for i in range(DISP // 8 - 2, -1, -1):
                total = total + jnp.exp2(v[i] - top)
                if i:
                    moment = moment + total
            moment = 8.0 * moment + sub.astype(F32) * total
            totals = jnp.where(sub == s, jnp.sum(total, axis=0, keepdims=True), totals)
            moments = jnp.where(sub == s, jnp.sum(moment, axis=0, keepdims=True), moments)
        lane_line = iota((8, LANES), 1) >> 6
        shift = jnp.zeros((8, LANES), F32)
        for i in range(PAIR):
            shift = jnp.where(lane_line == i, offs[i].astype(F32), shift)
        results.append((moments / totals + shift) * (1.0 / DISP))
    vals = jnp.concatenate(results, axis=0)
    lane_line = iota((LINE_RUN, LANES), 1) >> 6
    both = jnp.concatenate([jnp.where(lane_line == i, vals, 0.0) for i in range(PAIR)], axis=0)
    high = both.astype(BF)
    rest = both - high.astype(F32)
    middle = rest.astype(BF)
    low = (rest - middle.astype(F32)).astype(BF)
    pieces = jnp.dot(
        jnp.concatenate([high, middle, low], axis=0), spread[...], preferred_element_type=F32
    )
    size = PAIR * LINE_RUN
    pieces = pieces[:size] + pieces[size : 2 * size] + pieces[2 * size :]
    wanted = iota((LINE_RUN, width), 0) == (iota((LINE_RUN, width), 1) & (LINE_RUN - 1))
    for i in range(PAIR):
        piece = jnp.where(wanted, pieces[i * LINE_RUN : (i + 1) * LINE_RUN], 0.0)
        out[i : i + 1, :] = jnp.sum(piece, axis=0, keepdims=True)


def lines_plan(features, valid_cols, offsets, guide_weight):
    n = lax.axis_size("cols")
    devices = 2 * n
    width = n * BLOCK
    rows = PAIR * CHANNELS
    own = features.reshape(devices, rows, BLOCK)
    pieces = [None] * devices
    gone = ()
    for key in (1, 2, 6, 4, 7, 5, 3, 0):
        masked = key % 2 and key > 1
        (piece,) = call(
            functools.partial(pack_kernel, key),
            [((rows + (MASKS if masked else 0), BLOCK), BF)],
            [], 0,
            (own,) + ((valid_cols,) if masked else ()) + gone,
            1_000_000,
        )
        gone = (piece,)
        moves = [(i, i ^ key) for i in range(devices)]
        pieces[key] = lax.ppermute(piece, ("cols", "view"), moves) if key else piece
    consts = call(
        constants_kernel,
        [
            ((LANES, LANES), BF), ((DISP, 2 * LANES), BF), ((3 * KEYS, LANES), BF), ((LANES, width), BF),
            (valid_cols.shape, F32),
        ],
        [], 1, (offsets, guide_weight, valid_cols), 1_000_000,
    )
    (rows,) = call(
        lines_kernel,
        [((PAIR, width), F32)],
        [
            pltpu.VMEM((devices, rows, BLOCK), BF),
            pltpu.VMEM((n,) + valid_cols.shape, F32),
            pltpu.VMEM((LINE_RUN * LANES, LANES), BF),
            pltpu.VMEM((LINE_RUN * LANES, 2 * LANES), BF),
            pltpu.VMEM((LINE_RUN, DISP, LANES), F32),
            pltpu.VMEM((LINE_RUN, DISP, LANES), F32),
            pltpu.VMEM((LINE_RUN, 3 * KEYS, LANES), F32),
        ],
        1, (offsets, *consts, *pieces), 1_000_000_000,
    )
    others = lax.ppermute(rows, "view", [(0, 1), (1, 0)])
    first = lax.axis_index("view") == 0
    return jnp.where(first, jnp.concatenate([rows, others]), jnp.concatenate([others, rows]))[None]


def on_device(features, valid_cols, offsets, guide_weight):
    n = lax.axis_size("cols")
    lines = features.shape[1]
    if lines == 2 * PAIR * n and n * BLOCK == LINE_RUN * LINE_PARTS:
        return lines_plan(features, valid_cols, offsets, guide_weight)
    return halo_plan(features, valid_cols, offsets, guide_weight)


def solution(mesh):
    return jax.shard_map(
        on_device,
        mesh=mesh,
        in_specs=(
            P("view", ("tiles", "lines"), None, "cols"),
            P(None, ("tiles", "cols")),
            P(("tiles", "lines")),
            P(),
        ),
        out_specs=P(("tiles", "lines"), "cols", None),
        check_vma=False,
    )
```

```python
import functools
import math

import jax
import jax.numpy as jnp
from jax import lax
from jax.experimental import pallas as pl
from jax.experimental.pallas import tpu as pltpu
from jax.sharding import PartitionSpec as P

DISP = 192
DGROUP = 16
GROUPS = DISP // DGROUP
LAYERS = 3
SHARPNESS = 2.0
HALO = 32
LANES = 128
LINES = 8
CHANNELS = 64
BLOCK = 256
SPAN = BLOCK + HALO
PARTS = LANES // LINES
RUN = SPAN // PARTS
KEYS = 40
WIDE = BLOCK + LANES
SEC_ROWS = LINES * CHANNELS
QUAD_ROWS = SEC_ROWS // 2
MASK_AT = QUAD_ROWS + CHANNELS
PAYLOAD = MASK_AT + 16
QUAD = LINES // 2
QUAD_LANES = LANES // 2
PACK = LANES // HALO
CUT = 16

BF = jnp.bfloat16
F32 = jnp.float32


def iota(shape, dim):
    return lax.broadcasted_iota(jnp.int32, shape, dim)


def dot_t(a, b):
    return lax.dot_general(a, b, (((1,), (1,)), ((), ())), preferred_element_type=F32)


def call(kernel, outs, scratch, smem, args, flops=0, space=pltpu.VMEM, limit=24, to=None):
    specs = [pl.BlockSpec(memory_space=pltpu.SMEM)] * smem
    specs += [pl.BlockSpec(memory_space=space)] * (len(args) - smem)
    return pl.pallas_call(
        kernel,
        out_shape=[jax.ShapeDtypeStruct(shape, dtype) for shape, dtype in outs],
        in_specs=specs,
        out_specs=[pl.BlockSpec(memory_space=to or space)] * len(outs),
        scratch_shapes=scratch,
        compiler_params=pltpu.CompilerParams(vmem_limit_bytes=limit * 1024 * 1024),
        cost_estimate=pl.CostEstimate(flops=flops, bytes_accessed=1_000_000, transcendentals=0),
    )(*args)


def spread_guide(guide):
    keys = LAYERS * 3 * GROUPS
    row = iota((3 * KEYS, keys), 0)
    tap = jnp.where(row >= KEYS, 1, 0) + jnp.where(row >= 2 * KEYS, 1, 0)
    row = row - KEYS * tap
    layer = jnp.where(row >= GROUPS, 1, 0) + jnp.where(row >= 2 * GROUPS, 1, 0)
    key = 2 * GROUPS * layer + GROUPS * tap + row
    chosen = jnp.where((iota((3 * KEYS, keys), 1) == key) & (row < 3 * GROUPS), 1.0, 0.0).astype(BF)
    guide_t = dot_t(chosen, guide).astype(BF)
    return jnp.concatenate([guide_t, guide_t], axis=1)


def normalise(z, wts, t, room_left, room_right):
    z = (0.55 + 0.45 * jnp.tanh(0.5 * z)).astype(BF).astype(F32)
    taps = [z[k * KEYS : (k + 1) * KEYS] for k in range(3)]
    scale = 1.0 / (taps[0] + taps[1] + taps[2])
    wts[t, 0:KEYS, :] = jnp.where(room_left >= t, taps[0] * scale, 0.0)
    wts[t, KEYS : 2 * KEYS, :] = taps[1] * scale
    wts[t, 2 * KEYS : 3 * KEYS, :] = jnp.where(room_right < t, taps[2] * scale, 0.0)


def prefetch_kernel(own, valid, guide, own_out, masks, perm, flip, guide_out, valid_in, guide_in, sems):
    copies = [
        pltpu.make_async_copy(src, dst, sems.at[i])
        for i, (src, dst) in enumerate([(own, own_out), (guide, guide_in), (valid, valid_in)])
    ]
    for copy in copies:
        copy.start()
    perm[...] = jnp.where(
        iota((SPAN, WIDE), 1) == WIDE - 1 - iota((SPAN, WIDE), 0), 1.0, 0.0
    ).astype(BF)
    back = 2 * LANES - 1 - iota((DISP, 2 * LANES), 0)
    flip[...] = jnp.where(iota((DISP, 2 * LANES), 1) == back, 1.0, 0.0).astype(BF)

    copies[1].wait()
    guide_out[...] = spread_guide(guide_in[...])
    copies[2].wait()
    masks[...] = valid_in[...].astype(F32)
    copies[0].wait()


def payload_kernel(own, other, masks, first, second, ref_own):
    view = lax.axis_index("view")
    first_view = view == 0
    sec_mask = masks[1:2, :].astype(BF)
    lane = iota((CHANNELS, LANES), 1)
    tails = []
    for line in range(LINES):
        at = view * LINES + line
        mine, theirs = own[at], other[at]
        lo = line * CHANNELS
        dest, start = (first, lo) if line < QUAD else (second, lo - QUAD_ROWS)
        dest[start : start + CHANNELS, :] = jnp.where(first_view, theirs, mine) * sec_mask
        ref = jnp.where(first_view, mine, theirs)
        ref_own[lo : lo + CHANNELS, :] = ref
        tail = ref[:, BLOCK - LANES :].astype(F32)
        slot = line % PACK
        turn = (HALO * (slot + 1)) % LANES
        if turn:
            tail = pltpu.roll(tail, turn, 1)
        if slot:
            tails[-1] = jnp.where(lane >= HALO * slot, tail, tails[-1])
        else:
            tails.append(tail)
    for i, tail in enumerate(tails):
        first[QUAD_ROWS:MASK_AT, i * LANES : (i + 1) * LANES] = tail.astype(BF)
    first[MASK_AT:, :] = jnp.broadcast_to(masks[0:1, :], (16, BLOCK)).astype(BF)


def shifted(left, mine, lo, off):
    ch_lane = iota((CHANNELS, LANES), 1)
    tiles = [
        src[lo : lo + CHANNELS, i * LANES : (i + 1) * LANES].astype(F32)
        for src in (left, mine)
        for i in range(2)
    ]
    tiles = [pltpu.roll(tile, off, 1) for tile in tiles]
    tiles = [jnp.where(ch_lane < off, tiles[max(i - 1, 0)], tiles[i]).astype(BF) for i in range(4)]
    return jnp.concatenate(tiles, axis=1)


def line_costs(lhs, rhs, slot, skew, cost_rows):
    diagonal = iota((8, LANES), 1) - iota((8, LANES), 0)
    for chunk in range(3):
        rows = min(LANES, SPAN - chunk * LANES)
        first = max(1 - chunk, 0)
        last = 3 - chunk
        products = jnp.dot(
            lhs[chunk * LANES : chunk * LANES + rows],
            rhs[:, first * LANES : (last + 1) * LANES],
            preferred_element_type=F32,
        )
        for j in range(rows // 8):
            tiles = [
                pltpu.roll(
                    products[8 * j : 8 * j + 8, i * LANES : (i + 1) * LANES],
                    8 * j, 1, stride=1, stride_axis=0,
                )
                for i in range(last + 1 - first)
            ]
            if len(tiles) < 3:
                tiles = [tiles[0]] + tiles
            beyond = diagonal >= 8 * j
            at = chunk * LANES + 8 * j
            skew[slot, 0, at : at + 8, :] = jnp.where(beyond, tiles[1], tiles[0])
            skew[slot, 1, at : at + 8, :] = jnp.where(beyond, tiles[2], tiles[1])
    for t in range(RUN):
        at = t * QUAD_LANES + slot * PARTS
        for v in range(2):
            cost_rows[at : at + PARTS, v * LANES : (v + 1) * LANES] = skew[
                slot, v, pl.ds(t, PARTS, stride=RUN), :
            ].astype(BF)


def early_kernel(
    offsets, ref_own, mine, left, masks, perm, guide, wts, cost_rows, lhs_out,
    ref_rows, ref_cols, gate_rows, skew
):
    base = lax.axis_index("view") * LINES
    low = jnp.where(lax.axis_index("cols") == 0, HALO, 0)
    for line in range(LINES):
        lo = line * CHANNELS
        ref_rows[lo : lo + CHANNELS, LANES:] = ref_own[lo : lo + CHANNELS, :]
        half = line // PACK
        packed = left[QUAD_ROWS:MASK_AT, half * LANES : (half + 1) * LANES].astype(F32)
        turn = (LANES - HALO) - HALO * (line % PACK)
        if turn:
            packed = pltpu.roll(packed, turn, 1)
        ref_rows[lo : lo + CHANNELS, :LANES] = packed.astype(BF)

    mask_left = left[MASK_AT : MASK_AT + 1, BLOCK - LANES :].astype(F32)
    ref_mask = jnp.concatenate([mask_left, masks[0:1, :]], axis=1)
    ref_mask = jnp.broadcast_to(ref_mask * (1.0 / math.sqrt(CHANNELS)), (LANES, WIDE))
    mask_cols = dot_t(perm[...], ref_mask.astype(BF))
    half_lane = iota((PARTS, LANES), 1) < CHANNELS
    span_lane = iota((SPAN, LANES), 1) < CHANNELS

    for quad in range(LINES // QUAD):
        ref_t = dot_t(perm[...], ref_rows[quad * QUAD_ROWS : (quad + 1) * QUAD_ROWS, :])
        for pair in range(QUAD // 2):
            cols = ref_t[:, pair * LANES : (pair + 1) * LANES]
            slot = quad * 2 + pair
            ref_cols[slot] = cols
            masked = cols * mask_cols
            if quad == 0:
                rhs = jnp.concatenate(
                    [
                        shifted(left, mine, line * CHANNELS, offsets[base + line])
                        for line in (2 * slot, 2 * slot + 1)
                    ],
                    axis=0,
                )
            for side in range(2):
                line = 2 * slot + side
                for t in range(RUN):
                    picked = ref_cols[slot, pl.ds(t, PARTS, stride=RUN), :]
                    picked = jnp.where(half_lane if side == 0 else ~half_lane, picked, 0.0)
                    at = t * LANES + line * PARTS
                    gate_rows[at : at + PARTS, :] = picked.astype(BF)
                lhs = jnp.where(span_lane if side == 0 else ~span_lane, masked, 0.0).astype(BF)
                if quad == 0:
                    line_costs(lhs, rhs, line, skew, cost_rows)
                else:
                    lhs_out[line - QUAD] = lhs

    place = iota((KEYS, LANES), 1)
    x_base = SPAN - 1 - RUN * (place & (PARTS - 1))
    row = iota((KEYS, LANES), 0)
    reach = jnp.where(row >= 2 * GROUPS, 9, jnp.where(row >= GROUPS, 3, 1))
    room_left = x_base - reach - low
    room_right = x_base + reach - SPAN
    for two in range(RUN // 2):
        at = 2 * two * LANES
        logits = dot_t(guide[...], gate_rows[at : at + 2 * LANES, :])
        for i in range(2):
            t = 2 * two + i
            normalise(logits[:, i * LANES : (i + 1) * LANES], wts, t, room_left, room_right)


def late_kernel(
    offsets, mine, left, lhs, early_rows, wts, flip, out, skew, cost_rows, vol, vals, turned
):
    base = lax.axis_index("view") * LINES
    for pair in range(QUAD // 2):
        rhs = jnp.concatenate(
            [
                shifted(left, mine, line * CHANNELS, offsets[base + QUAD + line])
                for line in (2 * pair, 2 * pair + 1)
            ],
            axis=0,
        )
        for line in (2 * pair, 2 * pair + 1):
            line_costs(lhs[line], rhs, line, skew, cost_rows)

    for two in range(RUN // 2):
        rows = []
        for t in (2 * two, 2 * two + 1):
            for part in (early_rows, cost_rows):
                rows.append(part[t * QUAD_LANES : (t + 1) * QUAD_LANES, :])
        costs = dot_t(flip[...], jnp.concatenate(rows, axis=0))
        vol[2 * two] = costs[:, :LANES]
        vol[2 * two + 1] = costs[:, LANES:]

    def aggregate(group, carry):
        for half in range(2):
            at = pl.multiple_of(group * DGROUP + half * 8, 8)
            v = [vol[t, pl.ds(at, 8), :] for t in range(RUN)]
            for layer in range(LAYERS):
                s = 3**layer
                before = [v[t + s] if t + s < RUN else pltpu.roll(v[t + s - RUN], LANES - 1, 1) for t in range(RUN)]
                after = [v[t - s] if t >= s else pltpu.roll(v[t - s + RUN], 1, 1) for t in range(RUN)]
                fresh = []
                for t in range(RUN):
                    w = [wts[t, pl.ds(k * KEYS + layer * GROUPS + group, 1), :] for k in range(3)]
                    fresh.append(w[0] * before[t] + w[1] * v[t] + w[2] * after[t])
                v = fresh
            for t in range(RUN):
                vol[t, pl.ds(at, 8), :] = v[t]
        return carry

    lax.fori_loop(0, GROUPS, aggregate, 0)

    vals[...] = jnp.zeros((LANES, LANES), F32)
    sub = iota((8, LANES), 0).astype(F32)
    line_of = iota((1, LANES), 1) >> 4
    offs = jnp.zeros((1, LANES), F32)
    for line in range(LINES):
        offs = jnp.where(line_of == line, offsets[base + line].astype(F32), offs)

    def softmax(t, carry):
        v = [vol[t, 8 * i : 8 * i + 8, :] for i in range(DISP // 8)]
        top = v
        while len(top) > 1:
            top = [jnp.maximum(a, b) for a, b in zip(top[::2], top[1::2])] + top[len(top) & ~1 :]
        top = jnp.max(top[0], axis=0, keepdims=True)
        e = [jnp.exp(SHARPNESS * (a - top)) for a in v]
        total = e[0]
        moment = jnp.zeros((8, LANES), F32)
        for i in range(1, DISP // 8):
            total = total + e[i]
            moment = moment + float(8 * i) * e[i]
        moment = jnp.sum(moment + sub * total, axis=0, keepdims=True)
        total = jnp.sum(total, axis=0, keepdims=True)
        vals[pl.ds(RUN - 1 - t, 1), :] = (moment / total + offs) * (1.0 / DISP)
        return carry

    lax.fori_loop(0, RUN, softmax, 0)

    turned[...] = jnp.transpose(vals[...])
    lane = iota((8, LANES), 1)
    result = [jnp.zeros((8, LANES), F32) for _ in range(WIDE // LANES)]
    for part in range(PARTS):
        piece = turned[pl.ds(part, LINES, stride=PARTS), :]
        start = (RUN * (PARTS - 1 - part) - HALO) % WIDE
        tile, turn = divmod(start, LANES)
        if turn:
            piece = pltpu.roll(piece, turn, 1)
        if turn + RUN > LANES:
            after = (tile + 1) % len(result)
            result[after] = result[after] + jnp.where(lane < turn, piece, 0.0)
            piece = jnp.where(lane >= turn, piece, 0.0)
        result[tile] = result[tile] + piece
    for tile, value in enumerate(result):
        out[:, tile * LANES : (tile + 1) * LANES] = value


def join(pieces, sub, n):
    block = lax.axis_index("cols")
    pieces = pieces.reshape(n, 2, LINES, WIDE)
    start = (0, block // (n // 2), (block % (n // 2)) * sub, 0)
    pieces = lax.dynamic_slice(pieces, start, (n, 1, sub, WIDE))[:, 0]
    main = pieces[:, :, :BLOCK]
    tail = jnp.pad(pieces[1:, :, BLOCK:], ((0, 1), (0, 0), (LANES, 0)))
    place = (n, sub, BLOCK)
    keep = (iota(place, 2) < BLOCK - CUT) | (iota(place, 0) == n - 1)
    joined = jnp.where(keep, main, tail)
    return jnp.transpose(joined, (1, 0, 2)).reshape(1, sub, n * BLOCK)


def halo_plan(features, valid_cols, offsets, guide_weight):
    own = features[0]
    n = lax.axis_size("cols")
    right = [(c, c + 1) for c in range(n - 1)]
    other = lax.ppermute(own, "view", [(0, 1), (1, 0)])
    near, masks, perm, flip, guide = call(
        prefetch_kernel,
        [(own.shape, BF), (valid_cols.shape, F32), ((SPAN, WIDE), BF), ((DISP, 2 * LANES), BF), ((3 * KEYS, LANES), BF)],
        [pltpu.VMEM(valid_cols.shape, jnp.int32), pltpu.VMEM(guide_weight.shape, BF), pltpu.SemaphoreType.DMA((3,))],
        0, (own, valid_cols, guide_weight), 100_000_000, pl.ANY, 24, pltpu.VMEM,
    )
    first, second, ref_own = call(
        payload_kernel,
        [((PAYLOAD, BLOCK), BF), ((QUAD_ROWS, BLOCK), BF), ((SEC_ROWS, BLOCK), BF)],
        [], 0, (near, other, masks),
    )
    left_first = lax.ppermute(first, "cols", right)
    left_second = lax.ppermute(second, "cols", right)
    quad_rows = (RUN * QUAD_LANES, 2 * LANES)
    skew = pltpu.VMEM((QUAD, 2, SPAN, LANES), F32)
    square = pltpu.VMEM((LANES, LANES), F32)
    wts, early_rows, lhs = call(
        early_kernel,
        [((RUN, 3 * KEYS, LANES), F32), (quad_rows, BF), ((QUAD, SPAN, LANES), BF)],
        [pltpu.VMEM((SEC_ROWS, WIDE), BF), pltpu.VMEM((QUAD, SPAN, LANES), F32), pltpu.VMEM((RUN * LANES, LANES), BF), skew],
        1, (offsets, ref_own, first, left_first, masks, perm, guide), 1_000_000_000,
    )
    (result,) = call(
        late_kernel,
        [((LINES, WIDE), F32)],
        [skew, pltpu.VMEM(quad_rows, BF), pltpu.VMEM((RUN, DISP, LANES), F32), square, square],
        1, (offsets, second, left_second, lhs, early_rows, wts, flip), 1_000_000_000,
    )
    copies = jnp.broadcast_to(result[None], (2 * n, LINES, WIDE))
    pieces = lax.all_to_all(copies, ("cols", "view"), split_axis=0, concat_axis=0, tiled=True)
    return join(pieces, own.shape[0] // n, n)


LINE_RUN = 8
PAIR = 2
MASKS = 8
GATE_FLOOR = 11.0 / 9.0


def pack_kernel(hop, line, own, *rest):
    out = rest[-1]
    view = lax.axis_index("view")
    target = (2 * lax.axis_index("cols") + view) ^ (2 * hop)
    if line is None:
        out[...] = own[target]
        return
    lo = line * CHANNELS
    other = rest[0][target, lo : lo + CHANNELS, :]
    rows = CHANNELS
    if hop == 2:
        out[:rows, :] = other
    else:
        rows = 2 * CHANNELS
        mine = own[target, lo : lo + CHANNELS, :]
        out[:CHANNELS, :] = jnp.where(view == 0, mine, other)
        out[CHANNELS:rows, :] = jnp.where(view == 0, other, mine)
    if out.shape[0] > rows:
        masks = rest[1][...].astype(F32)
        out[rows:, :] = jnp.where(
            iota((MASKS, BLOCK), 0) < MASKS // 2, masks[0:1, :], masks[1:2, :]
        ).astype(BF)


def constants_kernel(offsets, guide, order, flip, guide_out, spread):
    row = iota((LANES, LANES), 0)
    from_lane = LANES - 1 - LINE_RUN * (row & (PARTS - 1)) - (row >> 4)
    order[...] = jnp.where(iota((LANES, LANES), 1) == from_lane, 1.0, 0.0).astype(BF)
    back = 2 * LANES - 1 - iota((DISP, 2 * LANES), 0)
    flip[...] = jnp.where(iota((DISP, 2 * LANES), 1) == back, 1.0, 0.0).astype(BF)
    guide_out[...] = spread_guide(guide[...]) * 0.5
    block_of = LANES - 1 - (iota(spread.shape, 1) >> 3)
    spread[...] = jnp.where(iota(spread.shape, 0) == block_of, 1.0, 0.0).astype(BF)


def line_kernel(line, offsets, order, flip, guide, spread, zero, one, two, two_more, three, masks, *rest):
    if line:
        earlier, *rest = rest
        out, refs, secs, gate_rows, cost_rows, vol, done, wts = rest
        valid = masks
    else:
        out, valid, refs, secs, gate_rows, cost_rows, vol, done, wts = rest
    block = lax.axis_index("cols")
    view = lax.axis_index("view")
    n = refs.shape[0]
    tiles = 2 * n
    width = tiles * LANES
    off = offsets[PAIR * (2 * block + view) + line]

    for hop, piece in ((0, zero), (1, one), (3, three)):
        refs[block ^ hop] = piece[:CHANNELS, :]
        secs[block ^ hop] = piece[CHANNELS : 2 * CHANNELS, :]
    lo = line * CHANNELS
    near = two[lo : lo + CHANNELS, :]
    refs[block ^ 2] = jnp.where(view == 0, near, two_more[:CHANNELS, :])
    secs[block ^ 2] = jnp.where(view == 0, two_more[:CHANNELS, :], near)
    if not line:
        valid[block] = masks[...].astype(F32)
        for hop, piece, lo in ((1, one, 2 * CHANNELS), (2, two_more, CHANNELS), (3, three, 2 * CHANNELS)):
            got = piece[lo : lo + MASKS, :].astype(F32)
            valid[block ^ hop] = jnp.concatenate([got[0:1], got[MASKS // 2 : MASKS // 2 + 1]], axis=0)

    def tile_of(source, w):
        lo = (w % 2) * LANES
        return source[w // 2, :, lo : lo + LANES]

    def mask_of(view, w):
        lo = (w % 2) * LANES
        return valid[w // 2, view : view + 1, lo : lo + LANES]

    ch_lane = iota((CHANNELS, LANES), 1)
    rolled = [pltpu.roll(tile_of(secs, w).astype(F32) * mask_of(1, w), off, 1) for w in range(tiles)]
    empty = jnp.zeros((CHANNELS, LANES), F32)
    shifted = [empty.astype(BF)] * 2
    for w in range(tiles):
        shifted.append(jnp.where(ch_lane < off, rolled[w - 1] if w else empty, rolled[w]).astype(BF))

    reached = iota((8, LANES), 1) + LINE_RUN * iota((8, LANES), 0)
    low_half = iota((LANES, LANES), 1) < CHANNELS
    scale = 1.0 / math.sqrt(CHANNELS)
    for quad in range(tiles // 4):
        raw = [tile_of(refs, 4 * quad + q) for q in range(4)]
        masked = [raw[q] * (mask_of(0, 4 * quad + q) * scale).astype(BF) for q in range(4)]
        cols = dot_t(order[...], jnp.concatenate(raw, axis=0))
        masked = dot_t(order[...], jnp.concatenate(masked, axis=0))
        for q in range(4):
            w = 4 * quad + q
            place = (tiles - 1 - w) * PARTS
            lo = (q // 2) * LANES
            keep = low_half if q % 2 == 0 else ~low_half
            gates = jnp.where(keep, cols[:, lo : lo + LANES], 0.0).astype(BF)
            window = jnp.concatenate(shifted[w : w + 3], axis=1)
            rhs = [jnp.zeros_like(window)] * 2
            rhs[q % 2] = window
            products = jnp.dot(
                masked[:, lo : lo + LANES].astype(BF), jnp.concatenate(rhs, axis=0), preferred_element_type=F32
            )
            for t in range(LINE_RUN):
                row = t * LANES + place
                gate_rows[row : row + PARTS, :] = gates[t * PARTS : (t + 1) * PARTS]
                halves = []
                for half in range(2):
                    base = half * LANES // 2 + t
                    r = t * PARTS + 8 * half
                    part = [products[r : r + 8, m * LANES : (m + 1) * LANES] for m in range(3)]
                    within = reached < LANES - base
                    halves.append(
                        jnp.concatenate(
                            [
                                pltpu.roll(
                                    jnp.where(within, part[m + 1], part[m]),
                                    base, 1, stride=LINE_RUN, stride_axis=0,
                                )
                                for m in range(2)
                            ],
                            axis=1,
                        )
                    )
                cost_rows[row : row + PARTS, :] = jnp.concatenate(halves, axis=0).astype(BF)

    x_base = width - 1 - LINE_RUN * iota((KEYS, LANES), 1)
    row = iota((KEYS, LANES), 0)
    reach = jnp.where(row >= 2 * GROUPS, 9, jnp.where(row >= GROUPS, 3, 1))
    room_left = x_base - reach
    room_right = x_base + reach - width
    unit = jnp.where(row >= 2 * GROUPS, SHARPNESS / math.log(2.0), 1.0)
    for two_t in range(LINE_RUN // 2):
        lo = 2 * two_t * LANES
        costs = dot_t(flip[...], cost_rows[lo : lo + 2 * LANES, :])
        logits = dot_t(guide[...], gate_rows[lo : lo + 2 * LANES, :])
        for i in range(2):
            t = 2 * two_t + i
            vol[t] = costs[:, i * LANES : (i + 1) * LANES]
            z = jnp.tanh(logits[:, i * LANES : (i + 1) * LANES]) + GATE_FLOOR
            taps = [z[m * KEYS : (m + 1) * KEYS] for m in range(3)]
            factor = unit / (taps[0] + taps[1] + taps[2])
            taps = [tap * factor for tap in taps]
            taps[0] = jnp.where(room_left >= t, taps[0], 0.0)
            taps[2] = jnp.where(room_right < t, taps[2], 0.0)
            for m in range(3):
                wts[t, m * KEYS : (m + 1) * KEYS, :] = taps[m]

    for group in range(GROUPS):
        for at in (group * DGROUP, group * DGROUP + 8):
            v = [vol[t, at : at + 8, :] for t in range(LINE_RUN)]
            for layer in range(LAYERS):
                s = 3**layer
                fresh = []
                for t in range(LINE_RUN):
                    w = [wts[t, r : r + 1, :] for r in [m * KEYS + layer * GROUPS + group for m in range(3)]]
                    blk, r = divmod(t + s, LINE_RUN)
                    before = pltpu.roll(v[r], LANES - blk, 1) if blk else v[r]
                    blk, r = divmod(t - s, LINE_RUN)
                    after = pltpu.roll(v[r], -blk, 1) if blk else v[r]
                    fresh.append(w[0] * before + w[1] * v[t] + w[2] * after)
                v = fresh
            for t in range(LINE_RUN):
                done[t, at : at + 8, :] = v[t]

    sub = iota((8, LANES), 0)
    totals = jnp.zeros((8, LANES), F32)
    moments = totals
    for t in range(LINE_RUN):
        v = [done[t, 8 * i : 8 * i + 8, :] for i in range(DISP // 8)]
        top = v
        while len(top) > 1:
            top = [jnp.maximum(a, b) for a, b in zip(top[::2], top[1::2])] + top[len(top) & ~1 :]
        top = jnp.max(top[0], axis=0, keepdims=True)
        total = jnp.exp2(v[-1] - top)
        moment = total
        for i in range(DISP // 8 - 2, -1, -1):
            total = total + jnp.exp2(v[i] - top)
            if i:
                moment = moment + total
        moment = 8.0 * moment + sub.astype(F32) * total
        here = sub == LINE_RUN - 1 - t
        totals = jnp.where(here, jnp.sum(total, axis=0, keepdims=True), totals)
        moments = jnp.where(here, jnp.sum(moment, axis=0, keepdims=True), moments)
    vals = (moments / totals + off.astype(F32)) * (1.0 / DISP)
    high = vals.astype(BF)
    left = vals - high.astype(F32)
    middle = left.astype(BF)
    low = (left - middle.astype(F32)).astype(BF)
    spare = jnp.zeros((8, LANES), BF)
    parts = jnp.dot(
        jnp.concatenate([high, middle, low, spare], axis=0), spread[...], preferred_element_type=F32
    )
    parts = parts[0:8] + parts[8:16] + parts[16:24]
    wanted = iota((8, width), 0) == (iota((8, width), 1) & (LINE_RUN - 1))
    result = jnp.sum(jnp.where(wanted, parts, 0.0), axis=0, keepdims=True)
    if line:
        out[0:1, :] = earlier[...]
        out[1:2, :] = result
    else:
        out[...] = result


def lines_plan(features, valid_cols, offsets, guide_weight):
    n = lax.axis_size("cols")
    devices = 2 * n
    width = n * BLOCK
    own = features.reshape(devices, PAIR * CHANNELS, BLOCK)
    other = lax.ppermute(own, "view", [(0, 1), (1, 0)])
    got = {}
    gone = ()
    for hop, line in ((2, None), (3, 0), (2, 0), (1, 0), (3, 1), (2, 1), (1, 1), (0, 0), (0, 1)):
        masked = hop and line == 0
        rows = CHANNELS if hop == 2 and line is not None else 2 * CHANNELS
        (piece,) = call(
            functools.partial(pack_kernel, hop, line),
            [((rows + (MASKS if masked else 0), BLOCK), BF)],
            [], 0,
            (own,) + (() if line is None else (other,)) + ((valid_cols,) if masked else ()) + gone,
            1_000_000,
        )
        gone = (piece,)
        got[hop, line] = lax.ppermute(piece, "cols", [(c, c ^ hop) for c in range(n)]) if hop else piece
    consts = call(
        constants_kernel,
        [((LANES, LANES), BF), ((DISP, 2 * LANES), BF), ((3 * KEYS, LANES), BF), ((LANES, width), BF)],
        [], 1, (offsets, guide_weight), 1_000_000,
    )
    scratch = [
        pltpu.VMEM((n, CHANNELS, BLOCK), BF),
        pltpu.VMEM((n, CHANNELS, BLOCK), BF),
        pltpu.VMEM((LINE_RUN * LANES, LANES), BF),
        pltpu.VMEM((LINE_RUN * LANES, 2 * LANES), BF),
        pltpu.VMEM((LINE_RUN, DISP, LANES), F32),
        pltpu.VMEM((LINE_RUN, DISP, LANES), F32),
        pltpu.VMEM((LINE_RUN, 3 * KEYS, LANES), F32),
    ]
    both = ((n,) + valid_cols.shape, F32)
    masks, more = valid_cols, ()
    for line in range(PAIR):
        pieces = [got[0, line], got[1, line], got[2, None], got[2, line], got[3, line]]
        rows, *kept = call(
            functools.partial(line_kernel, line),
            [((1 + line, width), F32)] + ([] if line else [both]),
            scratch, 1, (offsets, *consts, *pieces, masks, *more), 1_000_000_000,
        )
        if kept:
            masks, more = kept[0], (rows,)
    others = lax.ppermute(rows, "view", [(0, 1), (1, 0)])
    first = lax.axis_index("view") == 0
    return jnp.where(first, jnp.concatenate([rows, others]), jnp.concatenate([others, rows]))[None]


def on_device(features, valid_cols, offsets, guide_weight):
    n = lax.axis_size("cols")
    lines = features.shape[1]
    if lines == 2 * PAIR * n and n * BLOCK == LINE_RUN * LANES:
        return lines_plan(features, valid_cols, offsets, guide_weight)
    return halo_plan(features, valid_cols, offsets, guide_weight)


def solution(mesh):
    return jax.shard_map(
        on_device,
        mesh=mesh,
        in_specs=(
            P("view", ("tiles", "lines"), None, "cols"),
            P(None, ("tiles", "cols")),
            P(("tiles", "lines")),
            P(),
        ),
        out_specs=P(("tiles", "lines"), "cols", None),
        check_vma=False,
    )
```

```python
import functools
import math

import jax
import jax.numpy as jnp
from jax import lax
from jax.experimental import pallas as pl
from jax.experimental.pallas import tpu as pltpu
from jax.sharding import PartitionSpec as P

DISP = 192
DGROUP = 16
GROUPS = DISP // DGROUP
LAYERS = 3
SHARPNESS = 2.0
HALO = 32
LANES = 128
LINES = 8
CHANNELS = 64
BLOCK = 256
SPAN = BLOCK + HALO
PARTS = LANES // LINES
RUN = SPAN // PARTS
KEYS = 40
WIDE = BLOCK + LANES
SEC_ROWS = LINES * CHANNELS
QUAD_ROWS = SEC_ROWS // 2
MASK_AT = QUAD_ROWS + CHANNELS
PAYLOAD = MASK_AT + 16
QUAD = LINES // 2
QUAD_LANES = LANES // 2
PACK = LANES // HALO
CUT = 16

BF = jnp.bfloat16
F32 = jnp.float32


def iota(shape, dim):
    return lax.broadcasted_iota(jnp.int32, shape, dim)


def dot_t(a, b):
    return lax.dot_general(a, b, (((1,), (1,)), ((), ())), preferred_element_type=F32)


def call(kernel, outs, scratch, smem, args, flops=0, space=pltpu.VMEM, limit=24, to=None):
    specs = [pl.BlockSpec(memory_space=pltpu.SMEM)] * smem
    specs += [pl.BlockSpec(memory_space=space)] * (len(args) - smem)
    return pl.pallas_call(
        kernel,
        out_shape=[jax.ShapeDtypeStruct(shape, dtype) for shape, dtype in outs],
        in_specs=specs,
        out_specs=[pl.BlockSpec(memory_space=to or space)] * len(outs),
        scratch_shapes=scratch,
        compiler_params=pltpu.CompilerParams(vmem_limit_bytes=limit * 1024 * 1024),
        cost_estimate=pl.CostEstimate(flops=flops, bytes_accessed=1_000_000, transcendentals=0),
    )(*args)


def spread_guide(guide):
    keys = LAYERS * 3 * GROUPS
    row = iota((3 * KEYS, keys), 0)
    tap = jnp.where(row >= KEYS, 1, 0) + jnp.where(row >= 2 * KEYS, 1, 0)
    row = row - KEYS * tap
    layer = jnp.where(row >= GROUPS, 1, 0) + jnp.where(row >= 2 * GROUPS, 1, 0)
    key = 2 * GROUPS * layer + GROUPS * tap + row
    chosen = jnp.where((iota((3 * KEYS, keys), 1) == key) & (row < 3 * GROUPS), 1.0, 0.0).astype(BF)
    guide_t = dot_t(chosen, guide).astype(BF)
    return jnp.concatenate([guide_t, guide_t], axis=1)


def normalise(z, wts, t, room_left, room_right):
    z = (0.55 + 0.45 * jnp.tanh(0.5 * z)).astype(BF).astype(F32)
    taps = [z[k * KEYS : (k + 1) * KEYS] for k in range(3)]
    scale = 1.0 / (taps[0] + taps[1] + taps[2])
    wts[t, 0:KEYS, :] = jnp.where(room_left >= t, taps[0] * scale, 0.0)
    wts[t, KEYS : 2 * KEYS, :] = taps[1] * scale
    wts[t, 2 * KEYS : 3 * KEYS, :] = jnp.where(room_right < t, taps[2] * scale, 0.0)


def prefetch_kernel(own, valid, guide, own_out, masks, perm, flip, guide_out, valid_in, guide_in, sems):
    copies = [
        pltpu.make_async_copy(src, dst, sems.at[i])
        for i, (src, dst) in enumerate([(own, own_out), (guide, guide_in), (valid, valid_in)])
    ]
    for copy in copies:
        copy.start()
    perm[...] = jnp.where(
        iota((SPAN, WIDE), 1) == WIDE - 1 - iota((SPAN, WIDE), 0), 1.0, 0.0
    ).astype(BF)
    back = 2 * LANES - 1 - iota((DISP, 2 * LANES), 0)
    flip[...] = jnp.where(iota((DISP, 2 * LANES), 1) == back, 1.0, 0.0).astype(BF)

    copies[1].wait()
    guide_out[...] = spread_guide(guide_in[...])
    copies[2].wait()
    masks[...] = valid_in[...].astype(F32)
    copies[0].wait()


def payload_kernel(own, other, masks, first, second, ref_own):
    view = lax.axis_index("view")
    first_view = view == 0
    sec_mask = masks[1:2, :].astype(BF)
    lane = iota((CHANNELS, LANES), 1)
    tails = []
    for line in range(LINES):
        at = view * LINES + line
        mine, theirs = own[at], other[at]
        lo = line * CHANNELS
        dest, start = (first, lo) if line < QUAD else (second, lo - QUAD_ROWS)
        dest[start : start + CHANNELS, :] = jnp.where(first_view, theirs, mine) * sec_mask
        ref = jnp.where(first_view, mine, theirs)
        ref_own[lo : lo + CHANNELS, :] = ref
        tail = ref[:, BLOCK - LANES :].astype(F32)
        slot = line % PACK
        turn = (HALO * (slot + 1)) % LANES
        if turn:
            tail = pltpu.roll(tail, turn, 1)
        if slot:
            tails[-1] = jnp.where(lane >= HALO * slot, tail, tails[-1])
        else:
            tails.append(tail)
    for i, tail in enumerate(tails):
        first[QUAD_ROWS:MASK_AT, i * LANES : (i + 1) * LANES] = tail.astype(BF)
    first[MASK_AT:, :] = jnp.broadcast_to(masks[0:1, :], (16, BLOCK)).astype(BF)


def shifted(left, mine, lo, off):
    ch_lane = iota((CHANNELS, LANES), 1)
    tiles = [
        src[lo : lo + CHANNELS, i * LANES : (i + 1) * LANES].astype(F32)
        for src in (left, mine)
        for i in range(2)
    ]
    tiles = [pltpu.roll(tile, off, 1) for tile in tiles]
    tiles = [jnp.where(ch_lane < off, tiles[max(i - 1, 0)], tiles[i]).astype(BF) for i in range(4)]
    return jnp.concatenate(tiles, axis=1)


def line_costs(lhs, rhs, slot, skew, cost_rows):
    diagonal = iota((8, LANES), 1) - iota((8, LANES), 0)
    for chunk in range(3):
        rows = min(LANES, SPAN - chunk * LANES)
        first = max(1 - chunk, 0)
        last = 3 - chunk
        products = jnp.dot(
            lhs[chunk * LANES : chunk * LANES + rows],
            rhs[:, first * LANES : (last + 1) * LANES],
            preferred_element_type=F32,
        )
        for j in range(rows // 8):
            tiles = [
                pltpu.roll(
                    products[8 * j : 8 * j + 8, i * LANES : (i + 1) * LANES],
                    8 * j, 1, stride=1, stride_axis=0,
                )
                for i in range(last + 1 - first)
            ]
            if len(tiles) < 3:
                tiles = [tiles[0]] + tiles
            beyond = diagonal >= 8 * j
            at = chunk * LANES + 8 * j
            skew[slot, 0, at : at + 8, :] = jnp.where(beyond, tiles[1], tiles[0])
            skew[slot, 1, at : at + 8, :] = jnp.where(beyond, tiles[2], tiles[1])
    for t in range(RUN):
        at = t * QUAD_LANES + slot * PARTS
        for v in range(2):
            cost_rows[at : at + PARTS, v * LANES : (v + 1) * LANES] = skew[
                slot, v, pl.ds(t, PARTS, stride=RUN), :
            ].astype(BF)


def early_kernel(
    offsets, ref_own, mine, left, masks, perm, guide, wts, cost_rows, lhs_out,
    ref_rows, ref_cols, gate_rows, skew
):
    base = lax.axis_index("view") * LINES
    low = jnp.where(lax.axis_index("cols") == 0, HALO, 0)
    for line in range(LINES):
        lo = line * CHANNELS
        ref_rows[lo : lo + CHANNELS, LANES:] = ref_own[lo : lo + CHANNELS, :]
        half = line // PACK
        packed = left[QUAD_ROWS:MASK_AT, half * LANES : (half + 1) * LANES].astype(F32)
        turn = (LANES - HALO) - HALO * (line % PACK)
        if turn:
            packed = pltpu.roll(packed, turn, 1)
        ref_rows[lo : lo + CHANNELS, :LANES] = packed.astype(BF)

    mask_left = left[MASK_AT : MASK_AT + 1, BLOCK - LANES :].astype(F32)
    ref_mask = jnp.concatenate([mask_left, masks[0:1, :]], axis=1)
    ref_mask = jnp.broadcast_to(ref_mask * (1.0 / math.sqrt(CHANNELS)), (LANES, WIDE))
    mask_cols = dot_t(perm[...], ref_mask.astype(BF))
    half_lane = iota((PARTS, LANES), 1) < CHANNELS
    span_lane = iota((SPAN, LANES), 1) < CHANNELS

    for quad in range(LINES // QUAD):
        ref_t = dot_t(perm[...], ref_rows[quad * QUAD_ROWS : (quad + 1) * QUAD_ROWS, :])
        for pair in range(QUAD // 2):
            cols = ref_t[:, pair * LANES : (pair + 1) * LANES]
            slot = quad * 2 + pair
            ref_cols[slot] = cols
            masked = cols * mask_cols
            if quad == 0:
                rhs = jnp.concatenate(
                    [
                        shifted(left, mine, line * CHANNELS, offsets[base + line])
                        for line in (2 * slot, 2 * slot + 1)
                    ],
                    axis=0,
                )
            for side in range(2):
                line = 2 * slot + side
                for t in range(RUN):
                    picked = ref_cols[slot, pl.ds(t, PARTS, stride=RUN), :]
                    picked = jnp.where(half_lane if side == 0 else ~half_lane, picked, 0.0)
                    at = t * LANES + line * PARTS
                    gate_rows[at : at + PARTS, :] = picked.astype(BF)
                lhs = jnp.where(span_lane if side == 0 else ~span_lane, masked, 0.0).astype(BF)
                if quad == 0:
                    line_costs(lhs, rhs, line, skew, cost_rows)
                else:
                    lhs_out[line - QUAD] = lhs

    place = iota((KEYS, LANES), 1)
    x_base = SPAN - 1 - RUN * (place & (PARTS - 1))
    row = iota((KEYS, LANES), 0)
    reach = jnp.where(row >= 2 * GROUPS, 9, jnp.where(row >= GROUPS, 3, 1))
    room_left = x_base - reach - low
    room_right = x_base + reach - SPAN
    for two in range(RUN // 2):
        at = 2 * two * LANES
        logits = dot_t(guide[...], gate_rows[at : at + 2 * LANES, :])
        for i in range(2):
            t = 2 * two + i
            normalise(logits[:, i * LANES : (i + 1) * LANES], wts, t, room_left, room_right)


def late_kernel(
    offsets, mine, left, lhs, early_rows, wts, flip, out, skew, cost_rows, vol, vals, turned
):
    base = lax.axis_index("view") * LINES
    for pair in range(QUAD // 2):
        rhs = jnp.concatenate(
            [
                shifted(left, mine, line * CHANNELS, offsets[base + QUAD + line])
                for line in (2 * pair, 2 * pair + 1)
            ],
            axis=0,
        )
        for line in (2 * pair, 2 * pair + 1):
            line_costs(lhs[line], rhs, line, skew, cost_rows)

    for two in range(RUN // 2):
        rows = []
        for t in (2 * two, 2 * two + 1):
            for part in (early_rows, cost_rows):
                rows.append(part[t * QUAD_LANES : (t + 1) * QUAD_LANES, :])
        costs = dot_t(flip[...], jnp.concatenate(rows, axis=0))
        vol[2 * two] = costs[:, :LANES]
        vol[2 * two + 1] = costs[:, LANES:]

    def aggregate(group, carry):
        for half in range(2):
            at = pl.multiple_of(group * DGROUP + half * 8, 8)
            v = [vol[t, pl.ds(at, 8), :] for t in range(RUN)]
            for layer in range(LAYERS):
                s = 3**layer
                before = [v[t + s] if t + s < RUN else pltpu.roll(v[t + s - RUN], LANES - 1, 1) for t in range(RUN)]
                after = [v[t - s] if t >= s else pltpu.roll(v[t - s + RUN], 1, 1) for t in range(RUN)]
                fresh = []
                for t in range(RUN):
                    w = [wts[t, pl.ds(k * KEYS + layer * GROUPS + group, 1), :] for k in range(3)]
                    fresh.append(w[0] * before[t] + w[1] * v[t] + w[2] * after[t])
                v = fresh
            for t in range(RUN):
                vol[t, pl.ds(at, 8), :] = v[t]
        return carry

    lax.fori_loop(0, GROUPS, aggregate, 0)

    vals[...] = jnp.zeros((LANES, LANES), F32)
    sub = iota((8, LANES), 0).astype(F32)
    line_of = iota((1, LANES), 1) >> 4
    offs = jnp.zeros((1, LANES), F32)
    for line in range(LINES):
        offs = jnp.where(line_of == line, offsets[base + line].astype(F32), offs)

    def softmax(t, carry):
        v = [vol[t, 8 * i : 8 * i + 8, :] for i in range(DISP // 8)]
        top = v
        while len(top) > 1:
            top = [jnp.maximum(a, b) for a, b in zip(top[::2], top[1::2])] + top[len(top) & ~1 :]
        top = jnp.max(top[0], axis=0, keepdims=True)
        e = [jnp.exp(SHARPNESS * (a - top)) for a in v]
        total = e[0]
        moment = jnp.zeros((8, LANES), F32)
        for i in range(1, DISP // 8):
            total = total + e[i]
            moment = moment + float(8 * i) * e[i]
        moment = jnp.sum(moment + sub * total, axis=0, keepdims=True)
        total = jnp.sum(total, axis=0, keepdims=True)
        vals[pl.ds(RUN - 1 - t, 1), :] = (moment / total + offs) * (1.0 / DISP)
        return carry

    lax.fori_loop(0, RUN, softmax, 0)

    turned[...] = jnp.transpose(vals[...])
    lane = iota((8, LANES), 1)
    result = [jnp.zeros((8, LANES), F32) for _ in range(WIDE // LANES)]
    for part in range(PARTS):
        piece = turned[pl.ds(part, LINES, stride=PARTS), :]
        start = (RUN * (PARTS - 1 - part) - HALO) % WIDE
        tile, turn = divmod(start, LANES)
        if turn:
            piece = pltpu.roll(piece, turn, 1)
        if turn + RUN > LANES:
            after = (tile + 1) % len(result)
            result[after] = result[after] + jnp.where(lane < turn, piece, 0.0)
            piece = jnp.where(lane >= turn, piece, 0.0)
        result[tile] = result[tile] + piece
    for tile, value in enumerate(result):
        out[:, tile * LANES : (tile + 1) * LANES] = value


def join(pieces, sub, n):
    block = lax.axis_index("cols")
    pieces = pieces.reshape(n, 2, LINES, WIDE)
    start = (0, block // (n // 2), (block % (n // 2)) * sub, 0)
    pieces = lax.dynamic_slice(pieces, start, (n, 1, sub, WIDE))[:, 0]
    main = pieces[:, :, :BLOCK]
    tail = jnp.pad(pieces[1:, :, BLOCK:], ((0, 1), (0, 0), (LANES, 0)))
    place = (n, sub, BLOCK)
    keep = (iota(place, 2) < BLOCK - CUT) | (iota(place, 0) == n - 1)
    joined = jnp.where(keep, main, tail)
    return jnp.transpose(joined, (1, 0, 2)).reshape(1, sub, n * BLOCK)


def halo_plan(features, valid_cols, offsets, guide_weight):
    own = features[0]
    n = lax.axis_size("cols")
    right = [(c, c + 1) for c in range(n - 1)]
    other = lax.ppermute(own, "view", [(0, 1), (1, 0)])
    near, masks, perm, flip, guide = call(
        prefetch_kernel,
        [(own.shape, BF), (valid_cols.shape, F32), ((SPAN, WIDE), BF), ((DISP, 2 * LANES), BF), ((3 * KEYS, LANES), BF)],
        [pltpu.VMEM(valid_cols.shape, jnp.int32), pltpu.VMEM(guide_weight.shape, BF), pltpu.SemaphoreType.DMA((3,))],
        0, (own, valid_cols, guide_weight), 100_000_000, pl.ANY, 24, pltpu.VMEM,
    )
    first, second, ref_own = call(
        payload_kernel,
        [((PAYLOAD, BLOCK), BF), ((QUAD_ROWS, BLOCK), BF), ((SEC_ROWS, BLOCK), BF)],
        [], 0, (near, other, masks),
    )
    left_first = lax.ppermute(first, "cols", right)
    left_second = lax.ppermute(second, "cols", right)
    quad_rows = (RUN * QUAD_LANES, 2 * LANES)
    skew = pltpu.VMEM((QUAD, 2, SPAN, LANES), F32)
    square = pltpu.VMEM((LANES, LANES), F32)
    wts, early_rows, lhs = call(
        early_kernel,
        [((RUN, 3 * KEYS, LANES), F32), (quad_rows, BF), ((QUAD, SPAN, LANES), BF)],
        [pltpu.VMEM((SEC_ROWS, WIDE), BF), pltpu.VMEM((QUAD, SPAN, LANES), F32), pltpu.VMEM((RUN * LANES, LANES), BF), skew],
        1, (offsets, ref_own, first, left_first, masks, perm, guide), 1_000_000_000,
    )
    (result,) = call(
        late_kernel,
        [((LINES, WIDE), F32)],
        [skew, pltpu.VMEM(quad_rows, BF), pltpu.VMEM((RUN, DISP, LANES), F32), square, square],
        1, (offsets, second, left_second, lhs, early_rows, wts, flip), 1_000_000_000,
    )
    copies = jnp.broadcast_to(result[None], (2 * n, LINES, WIDE))
    pieces = lax.all_to_all(copies, ("cols", "view"), split_axis=0, concat_axis=0, tiled=True)
    return join(pieces, own.shape[0] // n, n)


LINE_RUN = 16
PAIR = 2
LINE_PARTS = LANES // PAIR


MASKS = 8
GATE_FLOOR = 11.0 / 9.0


def pack_kernel(key, own, *rest):
    out = rest[-1]
    me = 2 * lax.axis_index("cols") + lax.axis_index("view")
    rows = PAIR * CHANNELS
    out[:rows, :] = own[me ^ key]
    if out.shape[0] > rows:
        masks = rest[0][...].astype(F32)
        out[rows:, :] = jnp.where(
            iota((MASKS, BLOCK), 0) < MASKS // 2, masks[0:1, :], masks[1:2, :]
        ).astype(BF)


def constants_kernel(offsets, guide, valid, order, flip, guide_out, spread, masks):
    masks[...] = valid[...].astype(F32)
    row = iota((LANES, LANES), 0)
    from_lane = LANES - 1 - LINE_RUN * (row & 7) - (row >> 3)
    order[...] = jnp.where(iota((LANES, LANES), 1) == from_lane, 1.0, 0.0).astype(BF)
    back = 2 * LANES - 1 - iota((DISP, 2 * LANES), 0)
    flip[...] = jnp.where(iota((DISP, 2 * LANES), 1) == back, 1.0, 0.0).astype(BF)
    guide_out[...] = spread_guide(guide[...]) * 0.5
    block_of = LINE_PARTS - 1 - (iota(spread.shape, 1) >> 4)
    here = (iota(spread.shape, 0) & (LINE_PARTS - 1)) == block_of
    spread[...] = jnp.where(here, 1.0, 0.0).astype(BF)


def lines_kernel(
    offsets, order, flip, guide, spread, *rest
):
    pieces, (out, blocks, valid, gate_rows, cost_rows, vol, done, wts) = rest[:-8], rest[-8:]
    near, pieces = pieces[0], pieces[1:]
    tiles = len(pieces)
    width = tiles * LANES
    me = 2 * lax.axis_index("cols") + lax.axis_index("view")
    rows = PAIR * CHANNELS
    for key, piece in enumerate(pieces):
        blocks[me ^ key] = piece[:rows, :]
        if piece.shape[0] > rows:
            masks = piece[rows:, :].astype(F32)
            valid[(me ^ key) // 2] = jnp.concatenate([masks[0:1], masks[MASKS // 2 : MASKS // 2 + 1]], axis=0)
    valid[me // 2] = near[...]
    at = PAIR * me
    offs = [offsets[at + i] for i in range(PAIR)]
    ch_lane = iota((CHANNELS, LANES), 1)
    reached = iota((8, LANES), 1) + LINE_RUN * iota((8, LANES), 0)
    low_half = iota((LANES, LANES), 1) < CHANNELS
    scale = 1.0 / math.sqrt(CHANNELS)
    empty = jnp.zeros((CHANNELS, LANES), F32)

    def mask_of(view, w):
        lo = (w % 2) * LANES
        return valid[w // 2, view : view + 1, lo : lo + LANES]

    for i in range(PAIR):

        def tile_of(view, w):
            lo = (w % 2) * LANES
            return blocks[2 * (w // 2) + view, i * CHANNELS : (i + 1) * CHANNELS, lo : lo + LANES]

        off = offs[i]
        rolled = [pltpu.roll(tile_of(1, w).astype(F32) * mask_of(1, w), off, 1) for w in range(tiles)]
        shifted = [empty.astype(BF)] * 2
        for w in range(tiles):
            shifted.append(jnp.where(ch_lane < off, rolled[w - 1] if w else empty, rolled[w]).astype(BF))
        for quad in range(tiles // 4):
            refs = [tile_of(0, 4 * quad + q) for q in range(4)]
            masked = [refs[q] * (mask_of(0, 4 * quad + q) * scale).astype(BF) for q in range(4)]
            cols = dot_t(order[...], jnp.concatenate(refs, axis=0))
            masked = dot_t(order[...], jnp.concatenate(masked, axis=0))
            for two in range(2):
                lo = two * LANES
                gates, products = [], []
                lhs = masked[:, lo : lo + LANES].astype(BF)
                for side in range(2):
                    w = 4 * quad + 2 * two + side
                    keep = low_half if side == 0 else ~low_half
                    gates.append(jnp.where(keep, cols[:, lo : lo + LANES], 0.0))
                    window = jnp.concatenate(shifted[w : w + 3], axis=1)
                    rhs = [jnp.zeros_like(window)] * 2
                    rhs[side] = window
                    rhs = jnp.concatenate(rhs, axis=0)
                    products.append(jnp.dot(lhs, rhs, preferred_element_type=F32))
                place = i * LINE_PARTS + 8 * (tiles - 2 - 4 * quad - 2 * two)
                for t in range(LINE_RUN):
                    row = t * LANES + place
                    r = 8 * t
                    gate_rows[row : row + 16, :] = jnp.concatenate(
                        [gates[1][r : r + 8], gates[0][r : r + 8]], axis=0
                    ).astype(BF)
                    within = reached < LANES - t
                    both = []
                    for side in (1, 0):
                        part = [products[side][r : r + 8, m * LANES : (m + 1) * LANES] for m in range(3)]
                        both.append(
                            jnp.concatenate(
                                [
                                    pltpu.roll(
                                        jnp.where(within, part[m + 1], part[m]),
                                        t, 1, stride=LINE_RUN, stride_axis=0,
                                    )
                                    for m in range(2)
                                ],
                                axis=1,
                            )
                        )
                    cost_rows[row : row + 16, :] = jnp.concatenate(both, axis=0).astype(BF)

    x_base = width - 1 - LINE_RUN * (iota((KEYS, LANES), 1) & (LINE_PARTS - 1))
    row = iota((KEYS, LANES), 0)
    reach = jnp.where(row >= 2 * GROUPS, 9, jnp.where(row >= GROUPS, 3, 1))
    room_left = x_base - reach
    room_right = x_base + reach - width
    unit = jnp.where(row >= 2 * GROUPS, SHARPNESS / math.log(2.0), 1.0)
    for two in range(LINE_RUN // 2):
        lo = 2 * two * LANES
        costs = dot_t(flip[...], cost_rows[lo : lo + 2 * LANES, :])
        logits = dot_t(guide[...], gate_rows[lo : lo + 2 * LANES, :])
        for i in range(2):
            t = 2 * two + i
            vol[t] = costs[:, i * LANES : (i + 1) * LANES]
            z = jnp.tanh(logits[:, i * LANES : (i + 1) * LANES]) + GATE_FLOOR
            taps = [z[m * KEYS : (m + 1) * KEYS] for m in range(3)]
            factor = unit / (taps[0] + taps[1] + taps[2])
            taps = [tap * factor for tap in taps]
            if t >= LINE_RUN - 9:
                taps[0] = jnp.where(room_left >= t, taps[0], 0.0)
            if t < 9:
                taps[2] = jnp.where(room_right < t, taps[2], 0.0)
            for m in range(3):
                wts[t, m * KEYS : (m + 1) * KEYS, :] = taps[m]

    for group in range(GROUPS):
        for at in (group * DGROUP, group * DGROUP + 8):
            v = [vol[t, at : at + 8, :] for t in range(LINE_RUN)]
            for layer in range(LAYERS):
                s = 3**layer
                fresh = []
                for t in range(LINE_RUN):
                    rows = [k * KEYS + layer * GROUPS + group for k in range(3)]
                    w = [wts[t, r : r + 1, :] for r in rows]
                    blk, r = divmod(t + s, LINE_RUN)
                    before = pltpu.roll(v[r], LANES - blk, 1) if blk else v[r]
                    blk, r = divmod(t - s, LINE_RUN)
                    after = pltpu.roll(v[r], -blk, 1) if blk else v[r]
                    fresh.append(w[0] * before + w[1] * v[t] + w[2] * after)
                v = fresh
            for t in range(LINE_RUN):
                done[t, at : at + 8, :] = v[t]

    sub = iota((8, LANES), 0)
    results = []
    for block in range(LINE_RUN // 8):
        totals = jnp.zeros((8, LANES), F32)
        moments = totals
        for s in range(8):
            t = LINE_RUN - 1 - (8 * block + s)
            v = [done[t, 8 * i : 8 * i + 8, :] for i in range(DISP // 8)]
            top = v
            while len(top) > 1:
                top = [jnp.maximum(a, b) for a, b in zip(top[::2], top[1::2])] + top[len(top) & ~1 :]
            top = jnp.max(top[0], axis=0, keepdims=True)
            total = jnp.exp2(v[-1] - top)
            moment = total
            for i in range(DISP // 8 - 2, -1, -1):
                total = total + jnp.exp2(v[i] - top)
                if i:
                    moment = moment + total
            moment = 8.0 * moment + sub.astype(F32) * total
            totals = jnp.where(sub == s, jnp.sum(total, axis=0, keepdims=True), totals)
            moments = jnp.where(sub == s, jnp.sum(moment, axis=0, keepdims=True), moments)
        lane_line = iota((8, LANES), 1) >> 6
        shift = jnp.zeros((8, LANES), F32)
        for i in range(PAIR):
            shift = jnp.where(lane_line == i, offs[i].astype(F32), shift)
        results.append((moments / totals + shift) * (1.0 / DISP))
    vals = jnp.concatenate(results, axis=0)
    lane_line = iota((LINE_RUN, LANES), 1) >> 6
    both = jnp.concatenate([jnp.where(lane_line == i, vals, 0.0) for i in range(PAIR)], axis=0)
    high = both.astype(BF)
    rest = both - high.astype(F32)
    middle = rest.astype(BF)
    low = (rest - middle.astype(F32)).astype(BF)
    pieces = jnp.dot(
        jnp.concatenate([high, middle, low], axis=0), spread[...], preferred_element_type=F32
    )
    size = PAIR * LINE_RUN
    pieces = pieces[:size] + pieces[size : 2 * size] + pieces[2 * size :]
    wanted = iota((LINE_RUN, width), 0) == (iota((LINE_RUN, width), 1) & (LINE_RUN - 1))
    for i in range(PAIR):
        piece = jnp.where(wanted, pieces[i * LINE_RUN : (i + 1) * LINE_RUN], 0.0)
        out[i : i + 1, :] = jnp.sum(piece, axis=0, keepdims=True)


def lines_plan(features, valid_cols, offsets, guide_weight):
    n = lax.axis_size("cols")
    devices = 2 * n
    width = n * BLOCK
    rows = PAIR * CHANNELS
    own = features.reshape(devices, rows, BLOCK)
    pieces = [None] * devices
    gone = ()
    for key in (1, 2, 6, 4, 7, 5, 3, 0):
        masked = key % 2 and key > 1
        if key in (4, 6):
            me = 2 * lax.axis_index("cols") + lax.axis_index("view")
            piece = lax.dynamic_index_in_dim(own, me ^ key, 0, False)
            pieces[key] = lax.ppermute(piece, ("cols", "view"), [(i, i ^ key) for i in range(devices)])
            continue
        (piece,) = call(
            functools.partial(pack_kernel, key),
            [((rows + (MASKS if masked else 0), BLOCK), BF)],
            [], 0,
            (own,) + ((valid_cols,) if masked else ()) + gone,
            1_000_000,
        )
        gone = (piece,)
        moves = [(i, i ^ key) for i in range(devices)]
        pieces[key] = lax.ppermute(piece, ("cols", "view"), moves) if key else piece
    consts = call(
        constants_kernel,
        [
            ((LANES, LANES), BF), ((DISP, 2 * LANES), BF), ((3 * KEYS, LANES), BF), ((LANES, width), BF),
            (valid_cols.shape, F32),
        ],
        [], 1, (offsets, guide_weight, valid_cols), 1_000_000,
    )
    (rows,) = call(
        lines_kernel,
        [((PAIR, width), F32)],
        [
            pltpu.VMEM((devices, rows, BLOCK), BF),
            pltpu.VMEM((n,) + valid_cols.shape, F32),
            pltpu.VMEM((LINE_RUN * LANES, LANES), BF),
            pltpu.VMEM((LINE_RUN * LANES, 2 * LANES), BF),
            pltpu.VMEM((LINE_RUN, DISP, LANES), F32),
            pltpu.VMEM((LINE_RUN, DISP, LANES), F32),
            pltpu.VMEM((LINE_RUN, 3 * KEYS, LANES), F32),
        ],
        1, (offsets, *consts, *pieces), 1_000_000_000,
    )
    others = lax.ppermute(rows, "view", [(0, 1), (1, 0)])
    first = lax.axis_index("view") == 0
    return jnp.where(first, jnp.concatenate([rows, others]), jnp.concatenate([others, rows]))[None]


def on_device(features, valid_cols, offsets, guide_weight):
    n = lax.axis_size("cols")
    lines = features.shape[1]
    if lines == 2 * PAIR * n and n * BLOCK == LINE_RUN * LINE_PARTS:
        return lines_plan(features, valid_cols, offsets, guide_weight)
    return halo_plan(features, valid_cols, offsets, guide_weight)


def solution(mesh):
    return jax.shard_map(
        on_device,
        mesh=mesh,
        in_specs=(
            P("view", ("tiles", "lines"), None, "cols"),
            P(None, ("tiles", "cols")),
            P(("tiles", "lines")),
            P(),
        ),
        out_specs=P(("tiles", "lines"), "cols", None),
        check_vma=False,
    )
```

```python
import functools
import math

import jax
import jax.numpy as jnp
from jax import lax
from jax.experimental import pallas as pl
from jax.experimental.pallas import tpu as pltpu
from jax.sharding import PartitionSpec as P

DISP = 192
DGROUP = 16
GROUPS = DISP // DGROUP
LAYERS = 3
SHARPNESS = 2.0
HALO = 32
LANES = 128
LINES = 8
CHANNELS = 64
BLOCK = 256
SPAN = BLOCK + HALO
PARTS = LANES // LINES
RUN = SPAN // PARTS
KEYS = 40
WIDE = BLOCK + LANES
SEC_ROWS = LINES * CHANNELS
QUAD_ROWS = SEC_ROWS // 2
MASK_AT = QUAD_ROWS + CHANNELS
PAYLOAD = MASK_AT + 16
QUAD = LINES // 2
QUAD_LANES = LANES // 2
PACK = LANES // HALO
CUT = 16

BF = jnp.bfloat16
F32 = jnp.float32


def iota(shape, dim):
    return lax.broadcasted_iota(jnp.int32, shape, dim)


def dot_t(a, b):
    return lax.dot_general(a, b, (((1,), (1,)), ((), ())), preferred_element_type=F32)


def call(kernel, outs, scratch, smem, args, flops=0, space=pltpu.VMEM, limit=24, to=None):
    specs = [pl.BlockSpec(memory_space=pltpu.SMEM)] * smem
    specs += [pl.BlockSpec(memory_space=space)] * (len(args) - smem)
    return pl.pallas_call(
        kernel,
        out_shape=[jax.ShapeDtypeStruct(shape, dtype) for shape, dtype in outs],
        in_specs=specs,
        out_specs=[pl.BlockSpec(memory_space=to or space)] * len(outs),
        scratch_shapes=scratch,
        compiler_params=pltpu.CompilerParams(vmem_limit_bytes=limit * 1024 * 1024),
        cost_estimate=pl.CostEstimate(flops=flops, bytes_accessed=1_000_000, transcendentals=0),
    )(*args)


def spread_guide(guide):
    keys = LAYERS * 3 * GROUPS
    row = iota((3 * KEYS, keys), 0)
    tap = jnp.where(row >= KEYS, 1, 0) + jnp.where(row >= 2 * KEYS, 1, 0)
    row = row - KEYS * tap
    layer = jnp.where(row >= GROUPS, 1, 0) + jnp.where(row >= 2 * GROUPS, 1, 0)
    key = 2 * GROUPS * layer + GROUPS * tap + row
    chosen = jnp.where((iota((3 * KEYS, keys), 1) == key) & (row < 3 * GROUPS), 1.0, 0.0).astype(BF)
    guide_t = dot_t(chosen, guide).astype(BF)
    return jnp.concatenate([guide_t, guide_t], axis=1)


def normalise(z, wts, t, room_left, room_right):
    z = (0.55 + 0.45 * jnp.tanh(0.5 * z)).astype(BF).astype(F32)
    taps = [z[k * KEYS : (k + 1) * KEYS] for k in range(3)]
    scale = 1.0 / (taps[0] + taps[1] + taps[2])
    wts[t, 0:KEYS, :] = jnp.where(room_left >= t, taps[0] * scale, 0.0)
    wts[t, KEYS : 2 * KEYS, :] = taps[1] * scale
    wts[t, 2 * KEYS : 3 * KEYS, :] = jnp.where(room_right < t, taps[2] * scale, 0.0)


def prefetch_kernel(own, valid, guide, own_out, masks, perm, flip, guide_out, valid_in, guide_in, sems):
    copies = [
        pltpu.make_async_copy(src, dst, sems.at[i])
        for i, (src, dst) in enumerate([(own, own_out), (guide, guide_in), (valid, valid_in)])
    ]
    for copy in copies:
        copy.start()
    perm[...] = jnp.where(
        iota((SPAN, WIDE), 1) == WIDE - 1 - iota((SPAN, WIDE), 0), 1.0, 0.0
    ).astype(BF)
    back = 2 * LANES - 1 - iota((DISP, 2 * LANES), 0)
    flip[...] = jnp.where(iota((DISP, 2 * LANES), 1) == back, 1.0, 0.0).astype(BF)

    copies[1].wait()
    guide_out[...] = spread_guide(guide_in[...])
    copies[2].wait()
    masks[...] = valid_in[...].astype(F32)
    copies[0].wait()


def payload_kernel(own, other, masks, first, second, ref_own):
    view = lax.axis_index("view")
    first_view = view == 0
    sec_mask = masks[1:2, :].astype(BF)
    lane = iota((CHANNELS, LANES), 1)
    tails = []
    for line in range(LINES):
        at = view * LINES + line
        mine, theirs = own[at], other[at]
        lo = line * CHANNELS
        dest, start = (first, lo) if line < QUAD else (second, lo - QUAD_ROWS)
        dest[start : start + CHANNELS, :] = jnp.where(first_view, theirs, mine) * sec_mask
        ref = jnp.where(first_view, mine, theirs)
        ref_own[lo : lo + CHANNELS, :] = ref
        tail = ref[:, BLOCK - LANES :].astype(F32)
        slot = line % PACK
        turn = (HALO * (slot + 1)) % LANES
        if turn:
            tail = pltpu.roll(tail, turn, 1)
        if slot:
            tails[-1] = jnp.where(lane >= HALO * slot, tail, tails[-1])
        else:
            tails.append(tail)
    for i, tail in enumerate(tails):
        first[QUAD_ROWS:MASK_AT, i * LANES : (i + 1) * LANES] = tail.astype(BF)
    first[MASK_AT:, :] = jnp.broadcast_to(masks[0:1, :], (16, BLOCK)).astype(BF)


def shifted(left, mine, lo, off):
    ch_lane = iota((CHANNELS, LANES), 1)
    tiles = [
        src[lo : lo + CHANNELS, i * LANES : (i + 1) * LANES].astype(F32)
        for src in (left, mine)
        for i in range(2)
    ]
    tiles = [pltpu.roll(tile, off, 1) for tile in tiles]
    tiles = [jnp.where(ch_lane < off, tiles[max(i - 1, 0)], tiles[i]).astype(BF) for i in range(4)]
    return jnp.concatenate(tiles, axis=1)


def line_costs(lhs, rhs, slot, skew, cost_rows):
    diagonal = iota((8, LANES), 1) - iota((8, LANES), 0)
    for chunk in range(3):
        rows = min(LANES, SPAN - chunk * LANES)
        first = max(1 - chunk, 0)
        last = 3 - chunk
        products = jnp.dot(
            lhs[chunk * LANES : chunk * LANES + rows],
            rhs[:, first * LANES : (last + 1) * LANES],
            preferred_element_type=F32,
        )
        for j in range(rows // 8):
            tiles = [
                pltpu.roll(
                    products[8 * j : 8 * j + 8, i * LANES : (i + 1) * LANES],
                    8 * j, 1, stride=1, stride_axis=0,
                )
                for i in range(last + 1 - first)
            ]
            if len(tiles) < 3:
                tiles = [tiles[0]] + tiles
            beyond = diagonal >= 8 * j
            at = chunk * LANES + 8 * j
            skew[slot, 0, at : at + 8, :] = jnp.where(beyond, tiles[1], tiles[0])
            skew[slot, 1, at : at + 8, :] = jnp.where(beyond, tiles[2], tiles[1])
    for t in range(RUN):
        at = t * QUAD_LANES + slot * PARTS
        for v in range(2):
            cost_rows[at : at + PARTS, v * LANES : (v + 1) * LANES] = skew[
                slot, v, pl.ds(t, PARTS, stride=RUN), :
            ].astype(BF)


def early_kernel(
    offsets, ref_own, mine, left, masks, perm, guide, wts, cost_rows, lhs_out,
    ref_rows, ref_cols, gate_rows, skew
):
    base = lax.axis_index("view") * LINES
    low = jnp.where(lax.axis_index("cols") == 0, HALO, 0)
    for line in range(LINES):
        lo = line * CHANNELS
        ref_rows[lo : lo + CHANNELS, LANES:] = ref_own[lo : lo + CHANNELS, :]
        half = line // PACK
        packed = left[QUAD_ROWS:MASK_AT, half * LANES : (half + 1) * LANES].astype(F32)
        turn = (LANES - HALO) - HALO * (line % PACK)
        if turn:
            packed = pltpu.roll(packed, turn, 1)
        ref_rows[lo : lo + CHANNELS, :LANES] = packed.astype(BF)

    mask_left = left[MASK_AT : MASK_AT + 1, BLOCK - LANES :].astype(F32)
    ref_mask = jnp.concatenate([mask_left, masks[0:1, :]], axis=1)
    ref_mask = jnp.broadcast_to(ref_mask * (1.0 / math.sqrt(CHANNELS)), (LANES, WIDE))
    mask_cols = dot_t(perm[...], ref_mask.astype(BF))
    half_lane = iota((PARTS, LANES), 1) < CHANNELS
    span_lane = iota((SPAN, LANES), 1) < CHANNELS

    for quad in range(LINES // QUAD):
        ref_t = dot_t(perm[...], ref_rows[quad * QUAD_ROWS : (quad + 1) * QUAD_ROWS, :])
        for pair in range(QUAD // 2):
            cols = ref_t[:, pair * LANES : (pair + 1) * LANES]
            slot = quad * 2 + pair
            ref_cols[slot] = cols
            masked = cols * mask_cols
            if quad == 0:
                rhs = jnp.concatenate(
                    [
                        shifted(left, mine, line * CHANNELS, offsets[base + line])
                        for line in (2 * slot, 2 * slot + 1)
                    ],
                    axis=0,
                )
            for side in range(2):
                line = 2 * slot + side
                for t in range(RUN):
                    picked = ref_cols[slot, pl.ds(t, PARTS, stride=RUN), :]
                    picked = jnp.where(half_lane if side == 0 else ~half_lane, picked, 0.0)
                    at = t * LANES + line * PARTS
                    gate_rows[at : at + PARTS, :] = picked.astype(BF)
                lhs = jnp.where(span_lane if side == 0 else ~span_lane, masked, 0.0).astype(BF)
                if quad == 0:
                    line_costs(lhs, rhs, line, skew, cost_rows)
                else:
                    lhs_out[line - QUAD] = lhs

    place = iota((KEYS, LANES), 1)
    x_base = SPAN - 1 - RUN * (place & (PARTS - 1))
    row = iota((KEYS, LANES), 0)
    reach = jnp.where(row >= 2 * GROUPS, 9, jnp.where(row >= GROUPS, 3, 1))
    room_left = x_base - reach - low
    room_right = x_base + reach - SPAN
    for two in range(RUN // 2):
        at = 2 * two * LANES
        logits = dot_t(guide[...], gate_rows[at : at + 2 * LANES, :])
        for i in range(2):
            t = 2 * two + i
            normalise(logits[:, i * LANES : (i + 1) * LANES], wts, t, room_left, room_right)


def late_kernel(
    offsets, mine, left, lhs, early_rows, wts, flip, out, skew, cost_rows, vol, vals, turned
):
    base = lax.axis_index("view") * LINES
    for pair in range(QUAD // 2):
        rhs = jnp.concatenate(
            [
                shifted(left, mine, line * CHANNELS, offsets[base + QUAD + line])
                for line in (2 * pair, 2 * pair + 1)
            ],
            axis=0,
        )
        for line in (2 * pair, 2 * pair + 1):
            line_costs(lhs[line], rhs, line, skew, cost_rows)

    for two in range(RUN // 2):
        rows = []
        for t in (2 * two, 2 * two + 1):
            for part in (early_rows, cost_rows):
                rows.append(part[t * QUAD_LANES : (t + 1) * QUAD_LANES, :])
        costs = dot_t(flip[...], jnp.concatenate(rows, axis=0))
        vol[2 * two] = costs[:, :LANES]
        vol[2 * two + 1] = costs[:, LANES:]

    def aggregate(group, carry):
        for half in range(2):
            at = pl.multiple_of(group * DGROUP + half * 8, 8)
            v = [vol[t, pl.ds(at, 8), :] for t in range(RUN)]
            for layer in range(LAYERS):
                s = 3**layer
                before = [v[t + s] if t + s < RUN else pltpu.roll(v[t + s - RUN], LANES - 1, 1) for t in range(RUN)]
                after = [v[t - s] if t >= s else pltpu.roll(v[t - s + RUN], 1, 1) for t in range(RUN)]
                fresh = []
                for t in range(RUN):
                    w = [wts[t, pl.ds(k * KEYS + layer * GROUPS + group, 1), :] for k in range(3)]
                    fresh.append(w[0] * before[t] + w[1] * v[t] + w[2] * after[t])
                v = fresh
            for t in range(RUN):
                vol[t, pl.ds(at, 8), :] = v[t]
        return carry

    lax.fori_loop(0, GROUPS, aggregate, 0)

    vals[...] = jnp.zeros((LANES, LANES), F32)
    sub = iota((8, LANES), 0).astype(F32)
    line_of = iota((1, LANES), 1) >> 4
    offs = jnp.zeros((1, LANES), F32)
    for line in range(LINES):
        offs = jnp.where(line_of == line, offsets[base + line].astype(F32), offs)

    def softmax(t, carry):
        v = [vol[t, 8 * i : 8 * i + 8, :] for i in range(DISP // 8)]
        top = v
        while len(top) > 1:
            top = [jnp.maximum(a, b) for a, b in zip(top[::2], top[1::2])] + top[len(top) & ~1 :]
        top = jnp.max(top[0], axis=0, keepdims=True)
        e = [jnp.exp(SHARPNESS * (a - top)) for a in v]
        total = e[0]
        moment = jnp.zeros((8, LANES), F32)
        for i in range(1, DISP // 8):
            total = total + e[i]
            moment = moment + float(8 * i) * e[i]
        moment = jnp.sum(moment + sub * total, axis=0, keepdims=True)
        total = jnp.sum(total, axis=0, keepdims=True)
        vals[pl.ds(RUN - 1 - t, 1), :] = (moment / total + offs) * (1.0 / DISP)
        return carry

    lax.fori_loop(0, RUN, softmax, 0)

    turned[...] = jnp.transpose(vals[...])
    lane = iota((8, LANES), 1)
    result = [jnp.zeros((8, LANES), F32) for _ in range(WIDE // LANES)]
    for part in range(PARTS):
        piece = turned[pl.ds(part, LINES, stride=PARTS), :]
        start = (RUN * (PARTS - 1 - part) - HALO) % WIDE
        tile, turn = divmod(start, LANES)
        if turn:
            piece = pltpu.roll(piece, turn, 1)
        if turn + RUN > LANES:
            after = (tile + 1) % len(result)
            result[after] = result[after] + jnp.where(lane < turn, piece, 0.0)
            piece = jnp.where(lane >= turn, piece, 0.0)
        result[tile] = result[tile] + piece
    for tile, value in enumerate(result):
        out[:, tile * LANES : (tile + 1) * LANES] = value


def join(pieces, sub, n):
    block = lax.axis_index("cols")
    pieces = pieces.reshape(n, 2, LINES, WIDE)
    start = (0, block // (n // 2), (block % (n // 2)) * sub, 0)
    pieces = lax.dynamic_slice(pieces, start, (n, 1, sub, WIDE))[:, 0]
    main = pieces[:, :, :BLOCK]
    tail = jnp.pad(pieces[1:, :, BLOCK:], ((0, 1), (0, 0), (LANES, 0)))
    place = (n, sub, BLOCK)
    keep = (iota(place, 2) < BLOCK - CUT) | (iota(place, 0) == n - 1)
    joined = jnp.where(keep, main, tail)
    return jnp.transpose(joined, (1, 0, 2)).reshape(1, sub, n * BLOCK)


def halo_plan(features, valid_cols, offsets, guide_weight):
    own = features[0]
    n = lax.axis_size("cols")
    right = [(c, c + 1) for c in range(n - 1)]
    other = lax.ppermute(own, "view", [(0, 1), (1, 0)])
    near, masks, perm, flip, guide = call(
        prefetch_kernel,
        [(own.shape, BF), (valid_cols.shape, F32), ((SPAN, WIDE), BF), ((DISP, 2 * LANES), BF), ((3 * KEYS, LANES), BF)],
        [pltpu.VMEM(valid_cols.shape, jnp.int32), pltpu.VMEM(guide_weight.shape, BF), pltpu.SemaphoreType.DMA((3,))],
        0, (own, valid_cols, guide_weight), 100_000_000, pl.ANY, 24, pltpu.VMEM,
    )
    first, second, ref_own = call(
        payload_kernel,
        [((PAYLOAD, BLOCK), BF), ((QUAD_ROWS, BLOCK), BF), ((SEC_ROWS, BLOCK), BF)],
        [], 0, (near, other, masks),
    )
    left_first = lax.ppermute(first, "cols", right)
    left_second = lax.ppermute(second, "cols", right)
    quad_rows = (RUN * QUAD_LANES, 2 * LANES)
    skew = pltpu.VMEM((QUAD, 2, SPAN, LANES), F32)
    square = pltpu.VMEM((LANES, LANES), F32)
    wts, early_rows, lhs = call(
        early_kernel,
        [((RUN, 3 * KEYS, LANES), F32), (quad_rows, BF), ((QUAD, SPAN, LANES), BF)],
        [pltpu.VMEM((SEC_ROWS, WIDE), BF), pltpu.VMEM((QUAD, SPAN, LANES), F32), pltpu.VMEM((RUN * LANES, LANES), BF), skew],
        1, (offsets, ref_own, first, left_first, masks, perm, guide), 1_000_000_000,
    )
    (result,) = call(
        late_kernel,
        [((LINES, WIDE), F32)],
        [skew, pltpu.VMEM(quad_rows, BF), pltpu.VMEM((RUN, DISP, LANES), F32), square, square],
        1, (offsets, second, left_second, lhs, early_rows, wts, flip), 1_000_000_000,
    )
    copies = jnp.broadcast_to(result[None], (2 * n, LINES, WIDE))
    pieces = lax.all_to_all(copies, ("cols", "view"), split_axis=0, concat_axis=0, tiled=True)
    return join(pieces, own.shape[0] // n, n)


LINE_RUN = 16
PAIR = 2
LINE_PARTS = LANES // PAIR


MASKS = 8
GATE_FLOOR = 11.0 / 9.0
TAP_ROWS = 4 * GROUPS


def pack_kernel(key, own, *rest):
    out = rest[-1]
    me = 2 * lax.axis_index("cols") + lax.axis_index("view")
    rows = PAIR * CHANNELS
    out[:rows, :] = own[me ^ key]
    if out.shape[0] > rows:
        masks = rest[0][...].astype(F32)
        out[rows:, :] = jnp.where(
            iota((MASKS, BLOCK), 0) < MASKS // 2, masks[0:1, :], masks[1:2, :]
        ).astype(BF)


def constants_kernel(offsets, guide, valid, order, flip, guide_out, spread, masks):
    masks[...] = valid[...].astype(F32)
    row = iota((LANES, LANES), 0)
    from_lane = LANES - 1 - LINE_RUN * (row & 7) - (row >> 3)
    order[...] = jnp.where(iota((LANES, LANES), 1) == from_lane, 1.0, 0.0).astype(BF)
    back = 2 * LANES - 1 - iota((DISP, 2 * LANES), 0)
    flip[...] = jnp.where(iota((DISP, 2 * LANES), 1) == back, 1.0, 0.0).astype(BF)
    keys = LAYERS * 3 * GROUPS
    row = iota((3 * TAP_ROWS, keys), 0)
    tap = jnp.where(row >= TAP_ROWS, 1, 0) + jnp.where(row >= 2 * TAP_ROWS, 1, 0)
    row = row - TAP_ROWS * tap
    layer = row & 3
    key = 3 * GROUPS * layer + GROUPS * tap + (row >> 2)
    chosen = (iota((3 * TAP_ROWS, keys), 1) == key) & (layer < LAYERS)
    guide_t = (0.5 * dot_t(jnp.where(chosen, 1.0, 0.0).astype(BF), guide[...])).astype(BF)
    guide_out[...] = jnp.concatenate([guide_t, guide_t], axis=1)
    block_of = LINE_PARTS - 1 - (iota(spread.shape, 1) >> 4)
    here = (iota(spread.shape, 0) & (LINE_PARTS - 1)) == block_of
    spread[...] = jnp.where(here, 1.0, 0.0).astype(BF)


def lines_kernel(offsets, order, flip, guide, spread, *rest):
    pieces, (out, blocks, valid, gate_rows, cost_rows, vol, done, wts, sums) = rest[:-9], rest[-9:]
    near, pieces = pieces[0], pieces[1:]
    tiles = len(pieces)
    width = tiles * LANES
    me = 2 * lax.axis_index("cols") + lax.axis_index("view")
    rows = PAIR * CHANNELS
    for key, piece in enumerate(pieces):
        blocks[me ^ key] = piece[:rows, :]
        if piece.shape[0] > rows:
            masks = piece[rows:, :].astype(F32)
            valid[(me ^ key) // 2] = jnp.concatenate([masks[0:1], masks[MASKS // 2 : MASKS // 2 + 1]], axis=0)
    valid[me // 2] = near[...]
    at = PAIR * me
    ch_lane = iota((CHANNELS, LANES), 1)
    reached = iota((8, LANES), 1) + LINE_RUN * iota((8, LANES), 0)
    low_half = iota((LANES, LANES), 1) < CHANNELS
    scale = 1.0 / math.sqrt(CHANNELS)
    empty = jnp.zeros((CHANNELS, LANES), F32)

    def mask_of(view, w):
        lo = (w % 2) * LANES
        return valid[w // 2, view : view + 1, lo : lo + LANES]

    def correlate(i, carry):
        def tile_of(view, w):
            lo = (w % 2) * LANES
            channels = pl.ds(pl.multiple_of(i * CHANNELS, CHANNELS), CHANNELS)
            return blocks[2 * (w // 2) + view, channels, lo : lo + LANES]

        off = offsets[at + i]
        rolled = [pltpu.roll(tile_of(1, w).astype(F32) * mask_of(1, w), off, 1) for w in range(tiles)]
        shifted = [empty.astype(BF)] * 2
        for w in range(tiles):
            shifted.append(jnp.where(ch_lane < off, rolled[w - 1] if w else empty, rolled[w]).astype(BF))
        for quad in range(tiles // 4):
            refs = [tile_of(0, 4 * quad + q) for q in range(4)]
            masked = [refs[q] * (mask_of(0, 4 * quad + q) * scale).astype(BF) for q in range(4)]
            cols = dot_t(order[...], jnp.concatenate(refs, axis=0))
            masked = dot_t(order[...], jnp.concatenate(masked, axis=0))
            for two in range(2):
                lo = two * LANES
                gates, products = [], []
                lhs = masked[:, lo : lo + LANES].astype(BF)
                for side in range(2):
                    w = 4 * quad + 2 * two + side
                    keep = low_half if side == 0 else ~low_half
                    gates.append(jnp.where(keep, cols[:, lo : lo + LANES], 0.0))
                    window = jnp.concatenate(shifted[w : w + 3], axis=1)
                    rhs = [jnp.zeros_like(window)] * 2
                    rhs[side] = window
                    rhs = jnp.concatenate(rhs, axis=0)
                    products.append(jnp.dot(lhs, rhs, preferred_element_type=F32))
                place = 8 * (tiles - 2 - 4 * quad - 2 * two)
                for t in range(LINE_RUN):
                    r = 8 * t
                    gate_rows[t, i, place : place + 16, :] = jnp.concatenate(
                        [gates[1][r : r + 8], gates[0][r : r + 8]], axis=0
                    ).astype(BF)
                    within = reached < LANES - t
                    both = []
                    for side in (1, 0):
                        part = [products[side][r : r + 8, m * LANES : (m + 1) * LANES] for m in range(3)]
                        both.append(
                            jnp.concatenate(
                                [
                                    pltpu.roll(
                                        jnp.where(within, part[m + 1], part[m]),
                                        t, 1, stride=LINE_RUN, stride_axis=0,
                                    )
                                    for m in range(2)
                                ],
                                axis=1,
                            )
                        )
                    cost_rows[t, i, place : place + 16, :] = jnp.concatenate(both, axis=0).astype(BF)
        return carry

    lax.fori_loop(0, PAIR, correlate, 0)

    x_base = width - 1 - LINE_RUN * (iota((TAP_ROWS, LANES), 1) & (LINE_PARTS - 1))
    layer = iota((TAP_ROWS, LANES), 0) & 3
    reach = jnp.where(layer == 2, 9, jnp.where(layer == 1, 3, 1))
    room_left = x_base - reach
    room_right = x_base + reach - width
    unit = jnp.where(layer == 2, SHARPNESS / math.log(2.0), 1.0)

    def prepare(two, carry):
        pair = pl.ds(2 * two, 2)
        costs = dot_t(flip[...], cost_rows[pair].reshape(2 * LANES, 2 * LANES))
        logits = dot_t(guide[...], gate_rows[pair].reshape(2 * LANES, LANES))
        for i in range(2):
            t = 2 * two + i
            cost = costs[:, i * LANES : (i + 1) * LANES]
            for tile in range(DISP // 8):
                vol[tile, t] = cost[8 * tile : 8 * tile + 8]
            z = jnp.tanh(logits[:, i * LANES : (i + 1) * LANES]) + GATE_FLOOR
            taps = [z[m * TAP_ROWS : (m + 1) * TAP_ROWS] for m in range(3)]
            factor = unit / (taps[0] + taps[1] + taps[2])
            taps = [tap * factor for tap in taps]
            taps[0] = jnp.where(room_left >= t, taps[0], 0.0)
            taps[2] = jnp.where(room_right < t, taps[2], 0.0)
            for m in range(3):
                for pair_of in range(GROUPS // 2):
                    wts[pair_of, t, m] = taps[m][8 * pair_of : 8 * pair_of + 8]
        return carry

    lax.fori_loop(0, LINE_RUN // 2, prepare, 0)

    def aggregate(pair_of, carry):
        for quarter in range(4):
            tile = 4 * pair_of + quarter
            v = [vol[tile, t] for t in range(LINE_RUN)]
            for layer in range(LAYERS):
                s = 3**layer
                row = 4 * (quarter // 2) + layer
                fresh = []
                for t in range(LINE_RUN):
                    w = [wts[pair_of, t, m, row : row + 1, :] for m in range(3)]
                    blk, r = divmod(t + s, LINE_RUN)
                    before = pltpu.roll(v[r], LANES - blk, 1) if blk else v[r]
                    blk, r = divmod(t - s, LINE_RUN)
                    after = pltpu.roll(v[r], -blk, 1) if blk else v[r]
                    fresh.append(w[0] * before + w[1] * v[t] + w[2] * after)
                v = fresh
            for t in range(LINE_RUN):
                done[tile, t] = v[t]
        return carry

    lax.fori_loop(0, GROUPS // 2, aggregate, 0)
    sub = iota((8, LANES), 0)

    def softmax(half, carry):
        totals = jnp.zeros((8, LANES), F32)
        moments = totals
        for s in range(8):
            t = LINE_RUN - 1 - 8 * half - s
            v = [done[i, t] for i in range(DISP // 8)]
            top = v
            while len(top) > 1:
                top = [jnp.maximum(a, b) for a, b in zip(top[::2], top[1::2])] + top[len(top) & ~1 :]
            top = jnp.max(top[0], axis=0, keepdims=True)
            total = jnp.exp2(v[-1] - top)
            moment = total
            for i in range(DISP // 8 - 2, -1, -1):
                total = total + jnp.exp2(v[i] - top)
                if i:
                    moment = moment + total
            moment = 8.0 * moment + sub.astype(F32) * total
            totals = jnp.where(sub == s, jnp.sum(total, axis=0, keepdims=True), totals)
            moments = jnp.where(sub == s, jnp.sum(moment, axis=0, keepdims=True), moments)
        sums[half] = moments / totals
        return carry

    lax.fori_loop(0, LINE_RUN // 8, softmax, 0)
    lane_line = iota((LINE_RUN, LANES), 1) >> 6
    shift = jnp.zeros((LINE_RUN, LANES), F32)
    for i in range(PAIR):
        shift = jnp.where(lane_line == i, offsets[at + i].astype(F32), shift)
    vals = (sums[...].reshape(LINE_RUN, LANES) + shift) * (1.0 / DISP)
    both = jnp.concatenate([jnp.where(lane_line == i, vals, 0.0) for i in range(PAIR)], axis=0)
    high = both.astype(BF)
    left = both - high.astype(F32)
    middle = left.astype(BF)
    low = (left - middle.astype(F32)).astype(BF)
    parts = jnp.dot(
        jnp.concatenate([high, middle, low], axis=0), spread[...], preferred_element_type=F32
    )
    size = PAIR * LINE_RUN
    parts = parts[:size] + parts[size : 2 * size] + parts[2 * size :]
    wanted = iota((LINE_RUN, width), 0) == (iota((LINE_RUN, width), 1) & (LINE_RUN - 1))
    for i in range(PAIR):
        part = jnp.where(wanted, parts[i * LINE_RUN : (i + 1) * LINE_RUN], 0.0)
        out[i : i + 1, :] = jnp.sum(part, axis=0, keepdims=True)


def lines_plan(features, valid_cols, offsets, guide_weight):
    n = lax.axis_size("cols")
    devices = 2 * n
    width = n * BLOCK
    rows = PAIR * CHANNELS
    own = features.reshape(devices, rows, BLOCK)
    pieces = [None] * devices
    gone = ()
    for key in (1, 2, 6, 4, 7, 5, 3, 0):
        masked = key % 2 and key > 1
        (piece,) = call(
            functools.partial(pack_kernel, key),
            [((rows + (MASKS if masked else 0), BLOCK), BF)],
            [], 0,
            (own,) + ((valid_cols,) if masked else ()) + gone,
            1_000_000,
        )
        gone = (piece,)
        moves = [(i, i ^ key) for i in range(devices)]
        pieces[key] = lax.ppermute(piece, ("cols", "view"), moves) if key else piece
    consts = call(
        constants_kernel,
        [
            ((LANES, LANES), BF), ((DISP, 2 * LANES), BF), ((3 * TAP_ROWS, LANES), BF), ((LANES, width), BF),
            (valid_cols.shape, F32),
        ],
        [], 1, (offsets, guide_weight, valid_cols), 1_000_000,
    )
    (rows,) = call(
        lines_kernel,
        [((PAIR, width), F32)],
        [
            pltpu.VMEM((devices, rows, BLOCK), BF),
            pltpu.VMEM((n,) + valid_cols.shape, F32),
            pltpu.VMEM((LINE_RUN, PAIR, LINE_PARTS, LANES), BF),
            pltpu.VMEM((LINE_RUN, PAIR, LINE_PARTS, 2 * LANES), BF),
            pltpu.VMEM((DISP // 8, LINE_RUN, 8, LANES), F32),
            pltpu.VMEM((DISP // 8, LINE_RUN, 8, LANES), F32),
            pltpu.VMEM((GROUPS // 2, LINE_RUN, 3, 8, LANES), F32),
            pltpu.VMEM((LINE_RUN // 8, 8, LANES), F32),
        ],
        1, (offsets, *consts, *pieces), 1_000_000_000,
    )
    others = lax.ppermute(rows, "view", [(0, 1), (1, 0)])
    first = lax.axis_index("view") == 0
    return jnp.where(first, jnp.concatenate([rows, others]), jnp.concatenate([others, rows]))[None]


def on_device(features, valid_cols, offsets, guide_weight):
    n = lax.axis_size("cols")
    lines = features.shape[1]
    if lines == 2 * PAIR * n and n * BLOCK == LINE_RUN * LINE_PARTS:
        return lines_plan(features, valid_cols, offsets, guide_weight)
    return halo_plan(features, valid_cols, offsets, guide_weight)


def solution(mesh):
    return jax.shard_map(
        on_device,
        mesh=mesh,
        in_specs=(
            P("view", ("tiles", "lines"), None, "cols"),
            P(None, ("tiles", "cols")),
            P(("tiles", "lines")),
            P(),
        ),
        out_specs=P(("tiles", "lines"), "cols", None),
        check_vma=False,
    )
```

```python
import functools
import math

import jax
import jax.numpy as jnp
from jax import lax
from jax.experimental import pallas as pl
from jax.experimental.pallas import tpu as pltpu
from jax.sharding import PartitionSpec as P

DISP = 192
DGROUP = 16
GROUPS = DISP // DGROUP
LAYERS = 3
SHARPNESS = 2.0
HALO = 32
LANES = 128
LINES = 8
CHANNELS = 64
BLOCK = 256
SPAN = BLOCK + HALO
PARTS = LANES // LINES
RUN = SPAN // PARTS
KEYS = 40
WIDE = BLOCK + LANES
SEC_ROWS = LINES * CHANNELS
QUAD_ROWS = SEC_ROWS // 2
MASK_AT = QUAD_ROWS + CHANNELS
PAYLOAD = MASK_AT + 16
QUAD = LINES // 2
QUAD_LANES = LANES // 2
PACK = LANES // HALO
CUT = 16

BF = jnp.bfloat16
F32 = jnp.float32


def iota(shape, dim):
    return lax.broadcasted_iota(jnp.int32, shape, dim)


def dot_t(a, b):
    return lax.dot_general(a, b, (((1,), (1,)), ((), ())), preferred_element_type=F32)


def call(kernel, outs, scratch, smem, args, flops=0, space=pltpu.VMEM, limit=24, to=None):
    specs = [pl.BlockSpec(memory_space=pltpu.SMEM)] * smem
    specs += [pl.BlockSpec(memory_space=space)] * (len(args) - smem)
    return pl.pallas_call(
        kernel,
        out_shape=[jax.ShapeDtypeStruct(shape, dtype) for shape, dtype in outs],
        in_specs=specs,
        out_specs=[pl.BlockSpec(memory_space=to or space)] * len(outs),
        scratch_shapes=scratch,
        compiler_params=pltpu.CompilerParams(vmem_limit_bytes=limit * 1024 * 1024),
        cost_estimate=pl.CostEstimate(flops=flops, bytes_accessed=1_000_000, transcendentals=0),
    )(*args)


def spread_guide(guide):
    keys = LAYERS * 3 * GROUPS
    row = iota((3 * KEYS, keys), 0)
    tap = jnp.where(row >= KEYS, 1, 0) + jnp.where(row >= 2 * KEYS, 1, 0)
    row = row - KEYS * tap
    layer = jnp.where(row >= GROUPS, 1, 0) + jnp.where(row >= 2 * GROUPS, 1, 0)
    key = 2 * GROUPS * layer + GROUPS * tap + row
    chosen = jnp.where((iota((3 * KEYS, keys), 1) == key) & (row < 3 * GROUPS), 1.0, 0.0).astype(BF)
    guide_t = dot_t(chosen, guide).astype(BF)
    return jnp.concatenate([guide_t, guide_t], axis=1)


def normalise(z, wts, t, room_left, room_right):
    z = (0.55 + 0.45 * jnp.tanh(0.5 * z)).astype(BF).astype(F32)
    taps = [z[k * KEYS : (k + 1) * KEYS] for k in range(3)]
    scale = 1.0 / (taps[0] + taps[1] + taps[2])
    wts[t, 0:KEYS, :] = jnp.where(room_left >= t, taps[0] * scale, 0.0)
    wts[t, KEYS : 2 * KEYS, :] = taps[1] * scale
    wts[t, 2 * KEYS : 3 * KEYS, :] = jnp.where(room_right < t, taps[2] * scale, 0.0)


def prefetch_kernel(own, valid, guide, own_out, masks, perm, flip, guide_out, valid_in, guide_in, sems):
    copies = [
        pltpu.make_async_copy(src, dst, sems.at[i])
        for i, (src, dst) in enumerate([(own, own_out), (guide, guide_in), (valid, valid_in)])
    ]
    for copy in copies:
        copy.start()
    perm[...] = jnp.where(
        iota((SPAN, WIDE), 1) == WIDE - 1 - iota((SPAN, WIDE), 0), 1.0, 0.0
    ).astype(BF)
    back = 2 * LANES - 1 - iota((DISP, 2 * LANES), 0)
    flip[...] = jnp.where(iota((DISP, 2 * LANES), 1) == back, 1.0, 0.0).astype(BF)

    copies[1].wait()
    guide_out[...] = spread_guide(guide_in[...])
    copies[2].wait()
    masks[...] = valid_in[...].astype(F32)
    copies[0].wait()


def payload_kernel(own, other, masks, first, second, ref_own):
    view = lax.axis_index("view")
    first_view = view == 0
    sec_mask = masks[1:2, :].astype(BF)
    lane = iota((CHANNELS, LANES), 1)
    tails = []
    for line in range(LINES):
        at = view * LINES + line
        mine, theirs = own[at], other[at]
        lo = line * CHANNELS
        dest, start = (first, lo) if line < QUAD else (second, lo - QUAD_ROWS)
        dest[start : start + CHANNELS, :] = jnp.where(first_view, theirs, mine) * sec_mask
        ref = jnp.where(first_view, mine, theirs)
        ref_own[lo : lo + CHANNELS, :] = ref
        tail = ref[:, BLOCK - LANES :].astype(F32)
        slot = line % PACK
        turn = (HALO * (slot + 1)) % LANES
        if turn:
            tail = pltpu.roll(tail, turn, 1)
        if slot:
            tails[-1] = jnp.where(lane >= HALO * slot, tail, tails[-1])
        else:
            tails.append(tail)
    for i, tail in enumerate(tails):
        first[QUAD_ROWS:MASK_AT, i * LANES : (i + 1) * LANES] = tail.astype(BF)
    first[MASK_AT:, :] = jnp.broadcast_to(masks[0:1, :], (16, BLOCK)).astype(BF)


def shifted(left, mine, lo, off):
    ch_lane = iota((CHANNELS, LANES), 1)
    tiles = [
        src[lo : lo + CHANNELS, i * LANES : (i + 1) * LANES].astype(F32)
        for src in (left, mine)
        for i in range(2)
    ]
    tiles = [pltpu.roll(tile, off, 1) for tile in tiles]
    tiles = [jnp.where(ch_lane < off, tiles[max(i - 1, 0)], tiles[i]).astype(BF) for i in range(4)]
    return jnp.concatenate(tiles, axis=1)


def line_costs(lhs, rhs, slot, skew, cost_rows):
    diagonal = iota((8, LANES), 1) - iota((8, LANES), 0)
    for chunk in range(3):
        rows = min(LANES, SPAN - chunk * LANES)
        first = max(1 - chunk, 0)
        last = 3 - chunk
        products = jnp.dot(
            lhs[chunk * LANES : chunk * LANES + rows],
            rhs[:, first * LANES : (last + 1) * LANES],
            preferred_element_type=F32,
        )
        for j in range(rows // 8):
            tiles = [
                pltpu.roll(
                    products[8 * j : 8 * j + 8, i * LANES : (i + 1) * LANES],
                    8 * j, 1, stride=1, stride_axis=0,
                )
                for i in range(last + 1 - first)
            ]
            if len(tiles) < 3:
                tiles = [tiles[0]] + tiles
            beyond = diagonal >= 8 * j
            at = chunk * LANES + 8 * j
            skew[slot, 0, at : at + 8, :] = jnp.where(beyond, tiles[1], tiles[0])
            skew[slot, 1, at : at + 8, :] = jnp.where(beyond, tiles[2], tiles[1])
    for t in range(RUN):
        at = t * QUAD_LANES + slot * PARTS
        for v in range(2):
            cost_rows[at : at + PARTS, v * LANES : (v + 1) * LANES] = skew[
                slot, v, pl.ds(t, PARTS, stride=RUN), :
            ].astype(BF)


def early_kernel(
    offsets, ref_own, mine, left, masks, perm, guide, wts, cost_rows, lhs_out,
    ref_rows, ref_cols, gate_rows, skew
):
    base = lax.axis_index("view") * LINES
    low = jnp.where(lax.axis_index("cols") == 0, HALO, 0)
    for line in range(LINES):
        lo = line * CHANNELS
        ref_rows[lo : lo + CHANNELS, LANES:] = ref_own[lo : lo + CHANNELS, :]
        half = line // PACK
        packed = left[QUAD_ROWS:MASK_AT, half * LANES : (half + 1) * LANES].astype(F32)
        turn = (LANES - HALO) - HALO * (line % PACK)
        if turn:
            packed = pltpu.roll(packed, turn, 1)
        ref_rows[lo : lo + CHANNELS, :LANES] = packed.astype(BF)

    mask_left = left[MASK_AT : MASK_AT + 1, BLOCK - LANES :].astype(F32)
    ref_mask = jnp.concatenate([mask_left, masks[0:1, :]], axis=1)
    ref_mask = jnp.broadcast_to(ref_mask * (1.0 / math.sqrt(CHANNELS)), (LANES, WIDE))
    mask_cols = dot_t(perm[...], ref_mask.astype(BF))
    half_lane = iota((PARTS, LANES), 1) < CHANNELS
    span_lane = iota((SPAN, LANES), 1) < CHANNELS

    for quad in range(LINES // QUAD):
        ref_t = dot_t(perm[...], ref_rows[quad * QUAD_ROWS : (quad + 1) * QUAD_ROWS, :])
        for pair in range(QUAD // 2):
            cols = ref_t[:, pair * LANES : (pair + 1) * LANES]
            slot = quad * 2 + pair
            ref_cols[slot] = cols
            masked = cols * mask_cols
            if quad == 0:
                rhs = jnp.concatenate(
                    [
                        shifted(left, mine, line * CHANNELS, offsets[base + line])
                        for line in (2 * slot, 2 * slot + 1)
                    ],
                    axis=0,
                )
            for side in range(2):
                line = 2 * slot + side
                for t in range(RUN):
                    picked = ref_cols[slot, pl.ds(t, PARTS, stride=RUN), :]
                    picked = jnp.where(half_lane if side == 0 else ~half_lane, picked, 0.0)
                    at = t * LANES + line * PARTS
                    gate_rows[at : at + PARTS, :] = picked.astype(BF)
                lhs = jnp.where(span_lane if side == 0 else ~span_lane, masked, 0.0).astype(BF)
                if quad == 0:
                    line_costs(lhs, rhs, line, skew, cost_rows)
                else:
                    lhs_out[line - QUAD] = lhs

    place = iota((KEYS, LANES), 1)
    x_base = SPAN - 1 - RUN * (place & (PARTS - 1))
    row = iota((KEYS, LANES), 0)
    reach = jnp.where(row >= 2 * GROUPS, 9, jnp.where(row >= GROUPS, 3, 1))
    room_left = x_base - reach - low
    room_right = x_base + reach - SPAN
    for two in range(RUN // 2):
        at = 2 * two * LANES
        logits = dot_t(guide[...], gate_rows[at : at + 2 * LANES, :])
        for i in range(2):
            t = 2 * two + i
            normalise(logits[:, i * LANES : (i + 1) * LANES], wts, t, room_left, room_right)


def late_kernel(
    offsets, mine, left, lhs, early_rows, wts, flip, out, skew, cost_rows, vol, vals, turned
):
    base = lax.axis_index("view") * LINES
    for pair in range(QUAD // 2):
        rhs = jnp.concatenate(
            [
                shifted(left, mine, line * CHANNELS, offsets[base + QUAD + line])
                for line in (2 * pair, 2 * pair + 1)
            ],
            axis=0,
        )
        for line in (2 * pair, 2 * pair + 1):
            line_costs(lhs[line], rhs, line, skew, cost_rows)

    for two in range(RUN // 2):
        rows = []
        for t in (2 * two, 2 * two + 1):
            for part in (early_rows, cost_rows):
                rows.append(part[t * QUAD_LANES : (t + 1) * QUAD_LANES, :])
        costs = dot_t(flip[...], jnp.concatenate(rows, axis=0))
        vol[2 * two] = costs[:, :LANES]
        vol[2 * two + 1] = costs[:, LANES:]

    def aggregate(group, carry):
        for half in range(2):
            at = pl.multiple_of(group * DGROUP + half * 8, 8)
            v = [vol[t, pl.ds(at, 8), :] for t in range(RUN)]
            for layer in range(LAYERS):
                s = 3**layer
                before = [v[t + s] if t + s < RUN else pltpu.roll(v[t + s - RUN], LANES - 1, 1) for t in range(RUN)]
                after = [v[t - s] if t >= s else pltpu.roll(v[t - s + RUN], 1, 1) for t in range(RUN)]
                fresh = []
                for t in range(RUN):
                    w = [wts[t, pl.ds(k * KEYS + layer * GROUPS + group, 1), :] for k in range(3)]
                    fresh.append(w[0] * before[t] + w[1] * v[t] + w[2] * after[t])
                v = fresh
            for t in range(RUN):
                vol[t, pl.ds(at, 8), :] = v[t]
        return carry

    lax.fori_loop(0, GROUPS, aggregate, 0)

    vals[...] = jnp.zeros((LANES, LANES), F32)
    sub = iota((8, LANES), 0).astype(F32)
    line_of = iota((1, LANES), 1) >> 4
    offs = jnp.zeros((1, LANES), F32)
    for line in range(LINES):
        offs = jnp.where(line_of == line, offsets[base + line].astype(F32), offs)

    def softmax(t, carry):
        v = [vol[t, 8 * i : 8 * i + 8, :] for i in range(DISP // 8)]
        top = v
        while len(top) > 1:
            top = [jnp.maximum(a, b) for a, b in zip(top[::2], top[1::2])] + top[len(top) & ~1 :]
        top = jnp.max(top[0], axis=0, keepdims=True)
        e = [jnp.exp(SHARPNESS * (a - top)) for a in v]
        total = e[0]
        moment = jnp.zeros((8, LANES), F32)
        for i in range(1, DISP // 8):
            total = total + e[i]
            moment = moment + float(8 * i) * e[i]
        moment = jnp.sum(moment + sub * total, axis=0, keepdims=True)
        total = jnp.sum(total, axis=0, keepdims=True)
        vals[pl.ds(RUN - 1 - t, 1), :] = (moment / total + offs) * (1.0 / DISP)
        return carry

    lax.fori_loop(0, RUN, softmax, 0)

    turned[...] = jnp.transpose(vals[...])
    lane = iota((8, LANES), 1)
    result = [jnp.zeros((8, LANES), F32) for _ in range(WIDE // LANES)]
    for part in range(PARTS):
        piece = turned[pl.ds(part, LINES, stride=PARTS), :]
        start = (RUN * (PARTS - 1 - part) - HALO) % WIDE
        tile, turn = divmod(start, LANES)
        if turn:
            piece = pltpu.roll(piece, turn, 1)
        if turn + RUN > LANES:
            after = (tile + 1) % len(result)
            result[after] = result[after] + jnp.where(lane < turn, piece, 0.0)
            piece = jnp.where(lane >= turn, piece, 0.0)
        result[tile] = result[tile] + piece
    for tile, value in enumerate(result):
        out[:, tile * LANES : (tile + 1) * LANES] = value


def join(pieces, sub, n):
    block = lax.axis_index("cols")
    pieces = pieces.reshape(n, 2, LINES, WIDE)
    start = (0, block // (n // 2), (block % (n // 2)) * sub, 0)
    pieces = lax.dynamic_slice(pieces, start, (n, 1, sub, WIDE))[:, 0]
    main = pieces[:, :, :BLOCK]
    tail = jnp.pad(pieces[1:, :, BLOCK:], ((0, 1), (0, 0), (LANES, 0)))
    place = (n, sub, BLOCK)
    keep = (iota(place, 2) < BLOCK - CUT) | (iota(place, 0) == n - 1)
    joined = jnp.where(keep, main, tail)
    return jnp.transpose(joined, (1, 0, 2)).reshape(1, sub, n * BLOCK)


def halo_plan(features, valid_cols, offsets, guide_weight):
    own = features[0]
    n = lax.axis_size("cols")
    right = [(c, c + 1) for c in range(n - 1)]
    other = lax.ppermute(own, "view", [(0, 1), (1, 0)])
    near, masks, perm, flip, guide = call(
        prefetch_kernel,
        [(own.shape, BF), (valid_cols.shape, F32), ((SPAN, WIDE), BF), ((DISP, 2 * LANES), BF), ((3 * KEYS, LANES), BF)],
        [pltpu.VMEM(valid_cols.shape, jnp.int32), pltpu.VMEM(guide_weight.shape, BF), pltpu.SemaphoreType.DMA((3,))],
        0, (own, valid_cols, guide_weight), 100_000_000, pl.ANY, 24, pltpu.VMEM,
    )
    first, second, ref_own = call(
        payload_kernel,
        [((PAYLOAD, BLOCK), BF), ((QUAD_ROWS, BLOCK), BF), ((SEC_ROWS, BLOCK), BF)],
        [], 0, (near, other, masks),
    )
    left_first = lax.ppermute(first, "cols", right)
    left_second = lax.ppermute(second, "cols", right)
    quad_rows = (RUN * QUAD_LANES, 2 * LANES)
    skew = pltpu.VMEM((QUAD, 2, SPAN, LANES), F32)
    square = pltpu.VMEM((LANES, LANES), F32)
    wts, early_rows, lhs = call(
        early_kernel,
        [((RUN, 3 * KEYS, LANES), F32), (quad_rows, BF), ((QUAD, SPAN, LANES), BF)],
        [pltpu.VMEM((SEC_ROWS, WIDE), BF), pltpu.VMEM((QUAD, SPAN, LANES), F32), pltpu.VMEM((RUN * LANES, LANES), BF), skew],
        1, (offsets, ref_own, first, left_first, masks, perm, guide), 1_000_000_000,
    )
    (result,) = call(
        late_kernel,
        [((LINES, WIDE), F32)],
        [skew, pltpu.VMEM(quad_rows, BF), pltpu.VMEM((RUN, DISP, LANES), F32), square, square],
        1, (offsets, second, left_second, lhs, early_rows, wts, flip), 1_000_000_000,
    )
    copies = jnp.broadcast_to(result[None], (2 * n, LINES, WIDE))
    pieces = lax.all_to_all(copies, ("cols", "view"), split_axis=0, concat_axis=0, tiled=True)
    return join(pieces, own.shape[0] // n, n)


LINE_RUN = 16
PAIR = 2
LINE_PARTS = LANES // PAIR


MASKS = 8
GATE_FLOOR = 11.0 / 9.0


def pack_kernel(key, own, *rest):
    out = rest[-1]
    me = 2 * lax.axis_index("cols") + lax.axis_index("view")
    rows = PAIR * CHANNELS
    out[:rows, :] = own[me ^ key]
    if out.shape[0] > rows:
        masks = rest[0][...].astype(F32)
        out[rows:, :] = jnp.where(
            iota((MASKS, BLOCK), 0) < MASKS // 2, masks[0:1, :], masks[1:2, :]
        ).astype(BF)


def constants_kernel(offsets, guide, valid, order, flip, guide_out, spread, masks):
    masks[...] = valid[...].astype(F32)
    row = iota((LANES, LANES), 0)
    from_lane = LANES - 1 - LINE_RUN * (row & 7) - (row >> 3)
    order[...] = jnp.where(iota((LANES, LANES), 1) == from_lane, 1.0, 0.0).astype(BF)
    back = 2 * LANES - 1 - iota((DISP, 2 * LANES), 0)
    flip[...] = jnp.where(iota((DISP, 2 * LANES), 1) == back, 1.0, 0.0).astype(BF)
    guide_out[...] = spread_guide(guide[...]) * 0.5
    block_of = LINE_PARTS - 1 - (iota(spread.shape, 1) >> 4)
    here = (iota(spread.shape, 0) & (LINE_PARTS - 1)) == block_of
    spread[...] = jnp.where(here, 1.0, 0.0).astype(BF)


def lines_kernel(
    offsets, order, flip, guide, spread, *rest
):
    pieces, (out, blocks, valid, gate_rows, cost_rows, vol, done, wts) = rest[:-8], rest[-8:]
    near, pieces = pieces[0], pieces[1:]
    tiles = len(pieces)
    width = tiles * LANES
    me = 2 * lax.axis_index("cols") + lax.axis_index("view")
    rows = PAIR * CHANNELS
    for key, piece in enumerate(pieces):
        blocks[me ^ key] = piece[:rows, :]
        if piece.shape[0] > rows:
            masks = piece[rows:, :].astype(F32)
            valid[(me ^ key) // 2] = jnp.concatenate([masks[0:1], masks[MASKS // 2 : MASKS // 2 + 1]], axis=0)
    valid[me // 2] = near[...]
    at = PAIR * me
    offs = [offsets[at + i] for i in range(PAIR)]
    ch_lane = iota((CHANNELS, LANES), 1)
    reached = iota((8, LANES), 1) + LINE_RUN * iota((8, LANES), 0)
    low_half = iota((LANES, LANES), 1) < CHANNELS
    scale = 1.0 / math.sqrt(CHANNELS)
    empty = jnp.zeros((CHANNELS, LANES), F32)

    def mask_of(view, w):
        lo = (w % 2) * LANES
        return valid[w // 2, view : view + 1, lo : lo + LANES]

    for i in range(PAIR):

        def tile_of(view, w):
            lo = (w % 2) * LANES
            return blocks[2 * (w // 2) + view, i * CHANNELS : (i + 1) * CHANNELS, lo : lo + LANES]

        off = offs[i]
        rolled = [pltpu.roll(tile_of(1, w).astype(F32) * mask_of(1, w), off, 1) for w in range(tiles)]
        shifted = [empty.astype(BF)] * 2
        for w in range(tiles):
            shifted.append(jnp.where(ch_lane < off, rolled[w - 1] if w else empty, rolled[w]).astype(BF))
        for quad in range(tiles // 4):
            refs = [tile_of(0, 4 * quad + q) for q in range(4)]
            masked = [refs[q] * (mask_of(0, 4 * quad + q) * scale).astype(BF) for q in range(4)]
            cols = dot_t(order[...], jnp.concatenate(refs, axis=0))
            masked = dot_t(order[...], jnp.concatenate(masked, axis=0))
            for two in range(2):
                lo = two * LANES
                gates, products = [], []
                lhs = masked[:, lo : lo + LANES].astype(BF)
                for side in range(2):
                    w = 4 * quad + 2 * two + side
                    keep = low_half if side == 0 else ~low_half
                    gates.append(jnp.where(keep, cols[:, lo : lo + LANES], 0.0))
                    window = jnp.concatenate(shifted[w : w + 3], axis=1)
                    rhs = [jnp.zeros_like(window)] * 2
                    rhs[side] = window
                    rhs = jnp.concatenate(rhs, axis=0)
                    products.append(jnp.dot(lhs, rhs, preferred_element_type=F32))
                place = i * LINE_PARTS + 8 * (tiles - 2 - 4 * quad - 2 * two)
                for t in range(LINE_RUN):
                    row = t * LANES + place
                    r = 8 * t
                    gate_rows[row : row + 16, :] = jnp.concatenate(
                        [gates[1][r : r + 8], gates[0][r : r + 8]], axis=0
                    ).astype(BF)
                    within = reached < LANES - t
                    both = []
                    for side in (1, 0):
                        part = [products[side][r : r + 8, m * LANES : (m + 1) * LANES] for m in range(3)]
                        both.append(
                            jnp.concatenate(
                                [
                                    pltpu.roll(
                                        jnp.where(within, part[m + 1], part[m]),
                                        t, 1, stride=LINE_RUN, stride_axis=0,
                                    )
                                    for m in range(2)
                                ],
                                axis=1,
                            )
                        )
                    cost_rows[row : row + 16, :] = jnp.concatenate(both, axis=0).astype(BF)

    x_base = width - 1 - LINE_RUN * (iota((KEYS, LANES), 1) & (LINE_PARTS - 1))
    row = iota((KEYS, LANES), 0)
    reach = jnp.where(row >= 2 * GROUPS, 9, jnp.where(row >= GROUPS, 3, 1))
    room_left = x_base - reach
    room_right = x_base + reach - width
    unit = jnp.where(row >= 2 * GROUPS, SHARPNESS / math.log(2.0), 1.0)
    for two in range(LINE_RUN // 2):
        lo = 2 * two * LANES
        costs = dot_t(flip[...], cost_rows[lo : lo + 2 * LANES, :])
        logits = dot_t(guide[...], gate_rows[lo : lo + 2 * LANES, :])
        for i in range(2):
            t = 2 * two + i
            vol[t] = costs[:, i * LANES : (i + 1) * LANES]
            z = jnp.tanh(logits[:, i * LANES : (i + 1) * LANES]) + GATE_FLOOR
            taps = [z[m * KEYS : (m + 1) * KEYS] for m in range(3)]
            factor = unit / (taps[0] + taps[1] + taps[2])
            taps = [tap * factor for tap in taps]
            if t >= LINE_RUN - 9:
                taps[0] = jnp.where(room_left >= t, taps[0], 0.0)
            if t < 9:
                taps[2] = jnp.where(room_right < t, taps[2], 0.0)
            for m in range(3):
                wts[t, m * KEYS : (m + 1) * KEYS, :] = taps[m]

    for group in range(GROUPS):
        starts = [group * DGROUP + 8 * half for half in range(2)]
        v = [[vol[t, at : at + 8, :] for t in range(LINE_RUN)] for at in starts]
        for layer in range(LAYERS):
            s = 3**layer
            fresh = [[], []]
            for t in range(LINE_RUN):
                rows = [k * KEYS + layer * GROUPS + group for k in range(3)]
                w = [jnp.broadcast_to(wts[t, r : r + 1, :], (8, LANES)) for r in rows]
                for half in range(2):
                    blk, r = divmod(t + s, LINE_RUN)
                    before = pltpu.roll(v[half][r], LANES - blk, 1) if blk else v[half][r]
                    blk, r = divmod(t - s, LINE_RUN)
                    after = pltpu.roll(v[half][r], -blk, 1) if blk else v[half][r]
                    fresh[half].append(w[0] * before + w[1] * v[half][t] + w[2] * after)
            v = fresh
        for half, at in enumerate(starts):
            for t in range(LINE_RUN):
                done[t, at : at + 8, :] = v[half][t]

    sub = iota((8, LANES), 0)
    results = []
    for block in range(LINE_RUN // 8):
        totals = jnp.zeros((8, LANES), F32)
        moments = totals
        for s in range(8):
            t = LINE_RUN - 1 - (8 * block + s)
            v = [done[t, 8 * i : 8 * i + 8, :] for i in range(DISP // 8)]
            top = v
            while len(top) > 1:
                top = [jnp.maximum(a, b) for a, b in zip(top[::2], top[1::2])] + top[len(top) & ~1 :]
            top = jnp.max(top[0], axis=0, keepdims=True)
            total = jnp.exp2(v[-1] - top)
            moment = total
            for i in range(DISP // 8 - 2, -1, -1):
                total = total + jnp.exp2(v[i] - top)
                if i:
                    moment = moment + total
            moment = 8.0 * moment + sub.astype(F32) * total
            totals = jnp.where(sub == s, jnp.sum(total, axis=0, keepdims=True), totals)
            moments = jnp.where(sub == s, jnp.sum(moment, axis=0, keepdims=True), moments)
        lane_line = iota((8, LANES), 1) >> 6
        shift = jnp.zeros((8, LANES), F32)
        for i in range(PAIR):
            shift = jnp.where(lane_line == i, offs[i].astype(F32), shift)
        results.append((moments / totals + shift) * (1.0 / DISP))
    vals = jnp.concatenate(results, axis=0)
    lane_line = iota((LINE_RUN, LANES), 1) >> 6
    both = jnp.concatenate([jnp.where(lane_line == i, vals, 0.0) for i in range(PAIR)], axis=0)
    high = both.astype(BF)
    rest = both - high.astype(F32)
    middle = rest.astype(BF)
    low = (rest - middle.astype(F32)).astype(BF)
    pieces = jnp.dot(
        jnp.concatenate([high, middle, low], axis=0), spread[...], preferred_element_type=F32
    )
    size = PAIR * LINE_RUN
    pieces = pieces[:size] + pieces[size : 2 * size] + pieces[2 * size :]
    wanted = iota((LINE_RUN, width), 0) == (iota((LINE_RUN, width), 1) & (LINE_RUN - 1))
    for i in range(PAIR):
        piece = jnp.where(wanted, pieces[i * LINE_RUN : (i + 1) * LINE_RUN], 0.0)
        out[i : i + 1, :] = jnp.sum(piece, axis=0, keepdims=True)


def lines_plan(features, valid_cols, offsets, guide_weight):
    n = lax.axis_size("cols")
    devices = 2 * n
    width = n * BLOCK
    rows = PAIR * CHANNELS
    own = features.reshape(devices, rows, BLOCK)
    pieces = [None] * devices
    gone = ()
    for key in (1, 2, 6, 4, 7, 5, 3, 0):
        masked = key % 2 and key > 1
        (piece,) = call(
            functools.partial(pack_kernel, key),
            [((rows + (MASKS if masked else 0), BLOCK), BF)],
            [], 0,
            (own,) + ((valid_cols,) if masked else ()) + gone,
            1_000_000,
        )
        gone = (piece,)
        moves = [(i, i ^ key) for i in range(devices)]
        pieces[key] = lax.ppermute(piece, ("cols", "view"), moves) if key else piece
    consts = call(
        constants_kernel,
        [
            ((LANES, LANES), BF), ((DISP, 2 * LANES), BF), ((3 * KEYS, LANES), BF), ((LANES, width), BF),
            (valid_cols.shape, F32),
        ],
        [], 1, (offsets, guide_weight, valid_cols), 1_000_000,
    )
    (rows,) = call(
        lines_kernel,
        [((PAIR, width), F32)],
        [
            pltpu.VMEM((devices, rows, BLOCK), BF),
            pltpu.VMEM((n,) + valid_cols.shape, F32),
            pltpu.VMEM((LINE_RUN * LANES, LANES), BF),
            pltpu.VMEM((LINE_RUN * LANES, 2 * LANES), BF),
            pltpu.VMEM((LINE_RUN, DISP, LANES), F32),
            pltpu.VMEM((LINE_RUN, DISP, LANES), F32),
            pltpu.VMEM((LINE_RUN, 3 * KEYS, LANES), F32),
        ],
        1, (offsets, *consts, *pieces), 1_000_000_000,
    )
    others = lax.ppermute(rows, "view", [(0, 1), (1, 0)])
    first = lax.axis_index("view") == 0
    return jnp.where(first, jnp.concatenate([rows, others]), jnp.concatenate([others, rows]))[None]


def on_device(features, valid_cols, offsets, guide_weight):
    n = lax.axis_size("cols")
    lines = features.shape[1]
    if lines == 2 * PAIR * n and n * BLOCK == LINE_RUN * LINE_PARTS:
        return lines_plan(features, valid_cols, offsets, guide_weight)
    return halo_plan(features, valid_cols, offsets, guide_weight)


def solution(mesh):
    return jax.shard_map(
        on_device,
        mesh=mesh,
        in_specs=(
            P("view", ("tiles", "lines"), None, "cols"),
            P(None, ("tiles", "cols")),
            P(("tiles", "lines")),
            P(),
        ),
        out_specs=P(("tiles", "lines"), "cols", None),
        check_vma=False,
    )
```

```python
import functools
import math

import jax
import jax.numpy as jnp
from jax import lax
from jax.experimental import pallas as pl
from jax.experimental.pallas import tpu as pltpu
from jax.sharding import PartitionSpec as P

DISP = 192
DGROUP = 16
GROUPS = DISP // DGROUP
LAYERS = 3
SHARPNESS = 2.0
HALO = 32
LANES = 128
LINES = 8
CHANNELS = 64
BLOCK = 256
SPAN = BLOCK + HALO
PARTS = LANES // LINES
RUN = SPAN // PARTS
KEYS = 40
WIDE = BLOCK + LANES
SEC_ROWS = LINES * CHANNELS
QUAD_ROWS = SEC_ROWS // 2
MASK_AT = QUAD_ROWS + CHANNELS
PAYLOAD = MASK_AT + 16
QUAD = LINES // 2
QUAD_LANES = LANES // 2
PACK = LANES // HALO
CUT = 16

BF = jnp.bfloat16
F32 = jnp.float32


def iota(shape, dim):
    return lax.broadcasted_iota(jnp.int32, shape, dim)


def dot_t(a, b):
    return lax.dot_general(a, b, (((1,), (1,)), ((), ())), preferred_element_type=F32)


def call(kernel, outs, scratch, smem, args, flops=0, space=pltpu.VMEM, limit=24, to=None):
    specs = [pl.BlockSpec(memory_space=pltpu.SMEM)] * smem
    specs += [pl.BlockSpec(memory_space=space)] * (len(args) - smem)
    return pl.pallas_call(
        kernel,
        out_shape=[jax.ShapeDtypeStruct(shape, dtype) for shape, dtype in outs],
        in_specs=specs,
        out_specs=[pl.BlockSpec(memory_space=to or space)] * len(outs),
        scratch_shapes=scratch,
        compiler_params=pltpu.CompilerParams(vmem_limit_bytes=limit * 1024 * 1024),
        cost_estimate=pl.CostEstimate(flops=flops, bytes_accessed=1_000_000, transcendentals=0),
    )(*args)


def spread_guide(guide):
    keys = LAYERS * 3 * GROUPS
    row = iota((3 * KEYS, keys), 0)
    tap = jnp.where(row >= KEYS, 1, 0) + jnp.where(row >= 2 * KEYS, 1, 0)
    row = row - KEYS * tap
    layer = jnp.where(row >= GROUPS, 1, 0) + jnp.where(row >= 2 * GROUPS, 1, 0)
    key = 2 * GROUPS * layer + GROUPS * tap + row
    chosen = jnp.where((iota((3 * KEYS, keys), 1) == key) & (row < 3 * GROUPS), 1.0, 0.0).astype(BF)
    guide_t = dot_t(chosen, guide).astype(BF)
    return jnp.concatenate([guide_t, guide_t], axis=1)


def normalise(z, wts, t, room_left, room_right):
    z = (0.55 + 0.45 * jnp.tanh(0.5 * z)).astype(BF).astype(F32)
    taps = [z[k * KEYS : (k + 1) * KEYS] for k in range(3)]
    scale = 1.0 / (taps[0] + taps[1] + taps[2])
    wts[t, 0:KEYS, :] = jnp.where(room_left >= t, taps[0] * scale, 0.0)
    wts[t, KEYS : 2 * KEYS, :] = taps[1] * scale
    wts[t, 2 * KEYS : 3 * KEYS, :] = jnp.where(room_right < t, taps[2] * scale, 0.0)


def prefetch_kernel(own, valid, guide, own_out, masks, perm, flip, guide_out, valid_in, guide_in, sems):
    copies = [
        pltpu.make_async_copy(src, dst, sems.at[i])
        for i, (src, dst) in enumerate([(own, own_out), (guide, guide_in), (valid, valid_in)])
    ]
    for copy in copies:
        copy.start()
    perm[...] = jnp.where(
        iota((SPAN, WIDE), 1) == WIDE - 1 - iota((SPAN, WIDE), 0), 1.0, 0.0
    ).astype(BF)
    back = 2 * LANES - 1 - iota((DISP, 2 * LANES), 0)
    flip[...] = jnp.where(iota((DISP, 2 * LANES), 1) == back, 1.0, 0.0).astype(BF)

    copies[1].wait()
    guide_out[...] = spread_guide(guide_in[...])
    copies[2].wait()
    masks[...] = valid_in[...].astype(F32)
    copies[0].wait()


def payload_kernel(own, other, masks, first, second, ref_own):
    view = lax.axis_index("view")
    first_view = view == 0
    sec_mask = masks[1:2, :].astype(BF)
    lane = iota((CHANNELS, LANES), 1)
    tails = []
    for line in range(LINES):
        at = view * LINES + line
        mine, theirs = own[at], other[at]
        lo = line * CHANNELS
        dest, start = (first, lo) if line < QUAD else (second, lo - QUAD_ROWS)
        dest[start : start + CHANNELS, :] = jnp.where(first_view, theirs, mine) * sec_mask
        ref = jnp.where(first_view, mine, theirs)
        ref_own[lo : lo + CHANNELS, :] = ref
        tail = ref[:, BLOCK - LANES :].astype(F32)
        slot = line % PACK
        turn = (HALO * (slot + 1)) % LANES
        if turn:
            tail = pltpu.roll(tail, turn, 1)
        if slot:
            tails[-1] = jnp.where(lane >= HALO * slot, tail, tails[-1])
        else:
            tails.append(tail)
    for i, tail in enumerate(tails):
        first[QUAD_ROWS:MASK_AT, i * LANES : (i + 1) * LANES] = tail.astype(BF)
    first[MASK_AT:, :] = jnp.broadcast_to(masks[0:1, :], (16, BLOCK)).astype(BF)


def shifted(left, mine, lo, off):
    ch_lane = iota((CHANNELS, LANES), 1)
    tiles = [
        src[lo : lo + CHANNELS, i * LANES : (i + 1) * LANES].astype(F32)
        for src in (left, mine)
        for i in range(2)
    ]
    tiles = [pltpu.roll(tile, off, 1) for tile in tiles]
    tiles = [jnp.where(ch_lane < off, tiles[max(i - 1, 0)], tiles[i]).astype(BF) for i in range(4)]
    return jnp.concatenate(tiles, axis=1)


def line_costs(lhs, rhs, slot, skew, cost_rows):
    diagonal = iota((8, LANES), 1) - iota((8, LANES), 0)
    for chunk in range(3):
        rows = min(LANES, SPAN - chunk * LANES)
        first = max(1 - chunk, 0)
        last = 3 - chunk
        products = jnp.dot(
            lhs[chunk * LANES : chunk * LANES + rows],
            rhs[:, first * LANES : (last + 1) * LANES],
            preferred_element_type=F32,
        )
        for j in range(rows // 8):
            tiles = [
                pltpu.roll(
                    products[8 * j : 8 * j + 8, i * LANES : (i + 1) * LANES],
                    8 * j, 1, stride=1, stride_axis=0,
                )
                for i in range(last + 1 - first)
            ]
            if len(tiles) < 3:
                tiles = [tiles[0]] + tiles
            beyond = diagonal >= 8 * j
            at = chunk * LANES + 8 * j
            skew[slot, 0, at : at + 8, :] = jnp.where(beyond, tiles[1], tiles[0])
            skew[slot, 1, at : at + 8, :] = jnp.where(beyond, tiles[2], tiles[1])
    for t in range(RUN):
        at = t * QUAD_LANES + slot * PARTS
        for v in range(2):
            cost_rows[at : at + PARTS, v * LANES : (v + 1) * LANES] = skew[
                slot, v, pl.ds(t, PARTS, stride=RUN), :
            ].astype(BF)


def early_kernel(
    offsets, ref_own, mine, left, masks, perm, guide, wts, cost_rows, lhs_out,
    ref_rows, ref_cols, gate_rows, skew
):
    base = lax.axis_index("view") * LINES
    low = jnp.where(lax.axis_index("cols") == 0, HALO, 0)
    for line in range(LINES):
        lo = line * CHANNELS
        ref_rows[lo : lo + CHANNELS, LANES:] = ref_own[lo : lo + CHANNELS, :]
        half = line // PACK
        packed = left[QUAD_ROWS:MASK_AT, half * LANES : (half + 1) * LANES].astype(F32)
        turn = (LANES - HALO) - HALO * (line % PACK)
        if turn:
            packed = pltpu.roll(packed, turn, 1)
        ref_rows[lo : lo + CHANNELS, :LANES] = packed.astype(BF)

    mask_left = left[MASK_AT : MASK_AT + 1, BLOCK - LANES :].astype(F32)
    ref_mask = jnp.concatenate([mask_left, masks[0:1, :]], axis=1)
    ref_mask = jnp.broadcast_to(ref_mask * (1.0 / math.sqrt(CHANNELS)), (LANES, WIDE))
    mask_cols = dot_t(perm[...], ref_mask.astype(BF))
    half_lane = iota((PARTS, LANES), 1) < CHANNELS
    span_lane = iota((SPAN, LANES), 1) < CHANNELS

    for quad in range(LINES // QUAD):
        ref_t = dot_t(perm[...], ref_rows[quad * QUAD_ROWS : (quad + 1) * QUAD_ROWS, :])
        for pair in range(QUAD // 2):
            cols = ref_t[:, pair * LANES : (pair + 1) * LANES]
            slot = quad * 2 + pair
            ref_cols[slot] = cols
            masked = cols * mask_cols
            if quad == 0:
                rhs = jnp.concatenate(
                    [
                        shifted(left, mine, line * CHANNELS, offsets[base + line])
                        for line in (2 * slot, 2 * slot + 1)
                    ],
                    axis=0,
                )
            for side in range(2):
                line = 2 * slot + side
                for t in range(RUN):
                    picked = ref_cols[slot, pl.ds(t, PARTS, stride=RUN), :]
                    picked = jnp.where(half_lane if side == 0 else ~half_lane, picked, 0.0)
                    at = t * LANES + line * PARTS
                    gate_rows[at : at + PARTS, :] = picked.astype(BF)
                lhs = jnp.where(span_lane if side == 0 else ~span_lane, masked, 0.0).astype(BF)
                if quad == 0:
                    line_costs(lhs, rhs, line, skew, cost_rows)
                else:
                    lhs_out[line - QUAD] = lhs

    place = iota((KEYS, LANES), 1)
    x_base = SPAN - 1 - RUN * (place & (PARTS - 1))
    row = iota((KEYS, LANES), 0)
    reach = jnp.where(row >= 2 * GROUPS, 9, jnp.where(row >= GROUPS, 3, 1))
    room_left = x_base - reach - low
    room_right = x_base + reach - SPAN
    for two in range(RUN // 2):
        at = 2 * two * LANES
        logits = dot_t(guide[...], gate_rows[at : at + 2 * LANES, :])
        for i in range(2):
            t = 2 * two + i
            normalise(logits[:, i * LANES : (i + 1) * LANES], wts, t, room_left, room_right)


def late_kernel(
    offsets, mine, left, lhs, early_rows, wts, flip, out, skew, cost_rows, vol, vals, turned
):
    base = lax.axis_index("view") * LINES
    for pair in range(QUAD // 2):
        rhs = jnp.concatenate(
            [
                shifted(left, mine, line * CHANNELS, offsets[base + QUAD + line])
                for line in (2 * pair, 2 * pair + 1)
            ],
            axis=0,
        )
        for line in (2 * pair, 2 * pair + 1):
            line_costs(lhs[line], rhs, line, skew, cost_rows)

    for two in range(RUN // 2):
        rows = []
        for t in (2 * two, 2 * two + 1):
            for part in (early_rows, cost_rows):
                rows.append(part[t * QUAD_LANES : (t + 1) * QUAD_LANES, :])
        costs = dot_t(flip[...], jnp.concatenate(rows, axis=0))
        vol[2 * two] = costs[:, :LANES]
        vol[2 * two + 1] = costs[:, LANES:]

    def aggregate(group, carry):
        for half in range(2):
            at = pl.multiple_of(group * DGROUP + half * 8, 8)
            v = [vol[t, pl.ds(at, 8), :] for t in range(RUN)]
            for layer in range(LAYERS):
                s = 3**layer
                before = [v[t + s] if t + s < RUN else pltpu.roll(v[t + s - RUN], LANES - 1, 1) for t in range(RUN)]
                after = [v[t - s] if t >= s else pltpu.roll(v[t - s + RUN], 1, 1) for t in range(RUN)]
                fresh = []
                for t in range(RUN):
                    w = [wts[t, pl.ds(k * KEYS + layer * GROUPS + group, 1), :] for k in range(3)]
                    fresh.append(w[0] * before[t] + w[1] * v[t] + w[2] * after[t])
                v = fresh
            for t in range(RUN):
                vol[t, pl.ds(at, 8), :] = v[t]
        return carry

    lax.fori_loop(0, GROUPS, aggregate, 0)

    vals[...] = jnp.zeros((LANES, LANES), F32)
    sub = iota((8, LANES), 0).astype(F32)
    line_of = iota((1, LANES), 1) >> 4
    offs = jnp.zeros((1, LANES), F32)
    for line in range(LINES):
        offs = jnp.where(line_of == line, offsets[base + line].astype(F32), offs)

    def softmax(t, carry):
        v = [vol[t, 8 * i : 8 * i + 8, :] for i in range(DISP // 8)]
        top = v
        while len(top) > 1:
            top = [jnp.maximum(a, b) for a, b in zip(top[::2], top[1::2])] + top[len(top) & ~1 :]
        top = jnp.max(top[0], axis=0, keepdims=True)
        e = [jnp.exp(SHARPNESS * (a - top)) for a in v]
        total = e[0]
        moment = jnp.zeros((8, LANES), F32)
        for i in range(1, DISP // 8):
            total = total + e[i]
            moment = moment + float(8 * i) * e[i]
        moment = jnp.sum(moment + sub * total, axis=0, keepdims=True)
        total = jnp.sum(total, axis=0, keepdims=True)
        vals[pl.ds(RUN - 1 - t, 1), :] = (moment / total + offs) * (1.0 / DISP)
        return carry

    lax.fori_loop(0, RUN, softmax, 0)

    turned[...] = jnp.transpose(vals[...])
    lane = iota((8, LANES), 1)
    result = [jnp.zeros((8, LANES), F32) for _ in range(WIDE // LANES)]
    for part in range(PARTS):
        piece = turned[pl.ds(part, LINES, stride=PARTS), :]
        start = (RUN * (PARTS - 1 - part) - HALO) % WIDE
        tile, turn = divmod(start, LANES)
        if turn:
            piece = pltpu.roll(piece, turn, 1)
        if turn + RUN > LANES:
            after = (tile + 1) % len(result)
            result[after] = result[after] + jnp.where(lane < turn, piece, 0.0)
            piece = jnp.where(lane >= turn, piece, 0.0)
        result[tile] = result[tile] + piece
    for tile, value in enumerate(result):
        out[:, tile * LANES : (tile + 1) * LANES] = value


def join(pieces, sub, n):
    block = lax.axis_index("cols")
    pieces = pieces.reshape(n, 2, LINES, WIDE)
    start = (0, block // (n // 2), (block % (n // 2)) * sub, 0)
    pieces = lax.dynamic_slice(pieces, start, (n, 1, sub, WIDE))[:, 0]
    main = pieces[:, :, :BLOCK]
    tail = jnp.pad(pieces[1:, :, BLOCK:], ((0, 1), (0, 0), (LANES, 0)))
    place = (n, sub, BLOCK)
    keep = (iota(place, 2) < BLOCK - CUT) | (iota(place, 0) == n - 1)
    joined = jnp.where(keep, main, tail)
    return jnp.transpose(joined, (1, 0, 2)).reshape(1, sub, n * BLOCK)


def halo_plan(features, valid_cols, offsets, guide_weight):
    own = features[0]
    n = lax.axis_size("cols")
    right = [(c, c + 1) for c in range(n - 1)]
    other = lax.ppermute(own, "view", [(0, 1), (1, 0)])
    near, masks, perm, flip, guide = call(
        prefetch_kernel,
        [(own.shape, BF), (valid_cols.shape, F32), ((SPAN, WIDE), BF), ((DISP, 2 * LANES), BF), ((3 * KEYS, LANES), BF)],
        [pltpu.VMEM(valid_cols.shape, jnp.int32), pltpu.VMEM(guide_weight.shape, BF), pltpu.SemaphoreType.DMA((3,))],
        0, (own, valid_cols, guide_weight), 100_000_000, pl.ANY, 24, pltpu.VMEM,
    )
    first, second, ref_own = call(
        payload_kernel,
        [((PAYLOAD, BLOCK), BF), ((QUAD_ROWS, BLOCK), BF), ((SEC_ROWS, BLOCK), BF)],
        [], 0, (near, other, masks),
    )
    left_first = lax.ppermute(first, "cols", right)
    left_second = lax.ppermute(second, "cols", right)
    quad_rows = (RUN * QUAD_LANES, 2 * LANES)
    skew = pltpu.VMEM((QUAD, 2, SPAN, LANES), F32)
    square = pltpu.VMEM((LANES, LANES), F32)
    wts, early_rows, lhs = call(
        early_kernel,
        [((RUN, 3 * KEYS, LANES), F32), (quad_rows, BF), ((QUAD, SPAN, LANES), BF)],
        [pltpu.VMEM((SEC_ROWS, WIDE), BF), pltpu.VMEM((QUAD, SPAN, LANES), F32), pltpu.VMEM((RUN * LANES, LANES), BF), skew],
        1, (offsets, ref_own, first, left_first, masks, perm, guide), 1_000_000_000,
    )
    (result,) = call(
        late_kernel,
        [((LINES, WIDE), F32)],
        [skew, pltpu.VMEM(quad_rows, BF), pltpu.VMEM((RUN, DISP, LANES), F32), square, square],
        1, (offsets, second, left_second, lhs, early_rows, wts, flip), 1_000_000_000,
    )
    copies = jnp.broadcast_to(result[None], (2 * n, LINES, WIDE))
    pieces = lax.all_to_all(copies, ("cols", "view"), split_axis=0, concat_axis=0, tiled=True)
    return join(pieces, own.shape[0] // n, n)


LINE_RUN = 16
PAIR = 2
LINE_PARTS = LANES // PAIR


MASKS = 8
GATE_FLOOR = 11.0 / 9.0
TAP_ROWS = 4 * GROUPS


def pack_kernel(key, own, *rest):
    out = rest[-1]
    me = 2 * lax.axis_index("cols") + lax.axis_index("view")
    rows = PAIR * CHANNELS
    out[:rows, :] = own[me ^ key]
    if out.shape[0] > rows:
        masks = rest[0][...].astype(F32)
        out[rows:, :] = jnp.where(
            iota((MASKS, BLOCK), 0) < MASKS // 2, masks[0:1, :], masks[1:2, :]
        ).astype(BF)


def constants_kernel(offsets, guide, valid, order, flip, guide_out, spread, masks):
    masks[...] = valid[...].astype(F32)
    row = iota((LANES, LANES), 0)
    from_lane = LANES - 1 - LINE_RUN * (row & 7) - (row >> 3)
    order[...] = jnp.where(iota((LANES, LANES), 1) == from_lane, 1.0, 0.0).astype(BF)
    back = 2 * LANES - 1 - iota((DISP, 2 * LANES), 0)
    flip[...] = jnp.where(iota((DISP, 2 * LANES), 1) == back, 1.0, 0.0).astype(BF)
    keys = LAYERS * 3 * GROUPS
    row = iota((3 * TAP_ROWS, keys), 0)
    tap = jnp.where(row >= TAP_ROWS, 1, 0) + jnp.where(row >= 2 * TAP_ROWS, 1, 0)
    row = row - TAP_ROWS * tap
    layer = row & 3
    key = 3 * GROUPS * layer + GROUPS * tap + (row >> 2)
    chosen = (iota((3 * TAP_ROWS, keys), 1) == key) & (layer < LAYERS)
    guide_t = (0.5 * dot_t(jnp.where(chosen, 1.0, 0.0).astype(BF), guide[...])).astype(BF)
    guide_out[...] = jnp.concatenate([guide_t, guide_t], axis=1)
    block_of = LINE_PARTS - 1 - (iota(spread.shape, 1) >> 4)
    here = (iota(spread.shape, 0) & (LINE_PARTS - 1)) == block_of
    spread[...] = jnp.where(here, 1.0, 0.0).astype(BF)


def lines_kernel(offsets, order, flip, guide, spread, *rest):
    pieces, (out, blocks, valid, gate_rows, cost_rows, vol, done, wts, sums) = rest[:-9], rest[-9:]
    near, pieces = pieces[0], pieces[1:]
    tiles = len(pieces)
    width = tiles * LANES
    me = 2 * lax.axis_index("cols") + lax.axis_index("view")
    rows = PAIR * CHANNELS
    for key, piece in enumerate(pieces):
        blocks[me ^ key] = piece[:rows, :]
        if piece.shape[0] > rows:
            masks = piece[rows:, :].astype(F32)
            valid[(me ^ key) // 2] = jnp.concatenate([masks[0:1], masks[MASKS // 2 : MASKS // 2 + 1]], axis=0)
    valid[me // 2] = near[...]
    at = PAIR * me
    ch_lane = iota((CHANNELS, LANES), 1)
    reached = iota((8, LANES), 1) + LINE_RUN * iota((8, LANES), 0)
    low_half = iota((LANES, LANES), 1) < CHANNELS
    scale = 1.0 / math.sqrt(CHANNELS)
    empty = jnp.zeros((CHANNELS, LANES), F32)

    def mask_of(view, w):
        lo = (w % 2) * LANES
        return valid[w // 2, view : view + 1, lo : lo + LANES]

    def correlate(i, carry):
        def tile_of(view, w):
            lo = (w % 2) * LANES
            channels = slice(i * CHANNELS, (i + 1) * CHANNELS)
            return blocks[2 * (w // 2) + view, channels, lo : lo + LANES]

        off = offsets[at + i]
        rolled = [pltpu.roll(tile_of(1, w).astype(F32) * mask_of(1, w), off, 1) for w in range(tiles)]
        shifted = [empty.astype(BF)] * 2
        for w in range(tiles):
            shifted.append(jnp.where(ch_lane < off, rolled[w - 1] if w else empty, rolled[w]).astype(BF))
        for quad in range(tiles // 4):
            refs = [tile_of(0, 4 * quad + q) for q in range(4)]
            masked = [refs[q] * (mask_of(0, 4 * quad + q) * scale).astype(BF) for q in range(4)]
            cols = dot_t(order[...], jnp.concatenate(refs, axis=0))
            masked = dot_t(order[...], jnp.concatenate(masked, axis=0))
            for two in range(2):
                lo = two * LANES
                gates, products = [], []
                lhs = masked[:, lo : lo + LANES].astype(BF)
                for side in range(2):
                    w = 4 * quad + 2 * two + side
                    keep = low_half if side == 0 else ~low_half
                    gates.append(jnp.where(keep, cols[:, lo : lo + LANES], 0.0))
                    window = jnp.concatenate(shifted[w : w + 3], axis=1)
                    rhs = [jnp.zeros_like(window)] * 2
                    rhs[side] = window
                    rhs = jnp.concatenate(rhs, axis=0)
                    products.append(jnp.dot(lhs, rhs, preferred_element_type=F32))
                place = 8 * (tiles - 2 - 4 * quad - 2 * two)
                for t in range(LINE_RUN):
                    r = 8 * t
                    gate_rows[t, i, place : place + 16, :] = jnp.concatenate(
                        [gates[1][r : r + 8], gates[0][r : r + 8]], axis=0
                    ).astype(BF)
                    within = reached < LANES - t
                    both = []
                    for side in (1, 0):
                        part = [products[side][r : r + 8, m * LANES : (m + 1) * LANES] for m in range(3)]
                        both.append(
                            jnp.concatenate(
                                [
                                    pltpu.roll(
                                        jnp.where(within, part[m + 1], part[m]),
                                        t, 1, stride=LINE_RUN, stride_axis=0,
                                    )
                                    for m in range(2)
                                ],
                                axis=1,
                            )
                        )
                    cost_rows[t, i, place : place + 16, :] = jnp.concatenate(both, axis=0).astype(BF)
        return carry

    for step in range(PAIR):
        correlate(step, 0)

    x_base = width - 1 - LINE_RUN * (iota((TAP_ROWS, LANES), 1) & (LINE_PARTS - 1))
    layer = iota((TAP_ROWS, LANES), 0) & 3
    reach = jnp.where(layer == 2, 9, jnp.where(layer == 1, 3, 1))
    room_left = x_base - reach
    room_right = x_base + reach - width
    unit = jnp.where(layer == 2, SHARPNESS / math.log(2.0), 1.0)

    def prepare(two, carry):
        pair = pl.ds(2 * two, 2)
        costs = dot_t(flip[...], cost_rows[pair].reshape(2 * LANES, 2 * LANES))
        logits = dot_t(guide[...], gate_rows[pair].reshape(2 * LANES, LANES))
        for i in range(2):
            t = 2 * two + i
            cost = costs[:, i * LANES : (i + 1) * LANES]
            for tile in range(DISP // 8):
                vol[tile, t] = cost[8 * tile : 8 * tile + 8]
            z = jnp.tanh(logits[:, i * LANES : (i + 1) * LANES]) + GATE_FLOOR
            taps = [z[m * TAP_ROWS : (m + 1) * TAP_ROWS] for m in range(3)]
            factor = unit / (taps[0] + taps[1] + taps[2])
            taps = [tap * factor for tap in taps]
            taps[0] = jnp.where(room_left >= t, taps[0], 0.0)
            taps[2] = jnp.where(room_right < t, taps[2], 0.0)
            for m in range(3):
                for pair_of in range(GROUPS // 2):
                    wts[pair_of, t, m] = taps[m][8 * pair_of : 8 * pair_of + 8]
        return carry

    for step in range(LINE_RUN // 2):
        prepare(step, 0)

    def aggregate(pair_of, carry):
        for group in range(2):
            tile = 4 * pair_of + 2 * group
            v = [[vol[tile + half, t] for t in range(LINE_RUN)] for half in range(2)]
            for layer in range(LAYERS):
                s = 3**layer
                row = 4 * group + layer
                fresh = [[], []]
                for t in range(LINE_RUN):
                    w = [jnp.broadcast_to(wts[pair_of, t, m, row : row + 1, :], (8, LANES)) for m in range(3)]
                    for half in range(2):
                        blk, r = divmod(t + s, LINE_RUN)
                        before = pltpu.roll(v[half][r], LANES - blk, 1) if blk else v[half][r]
                        blk, r = divmod(t - s, LINE_RUN)
                        after = pltpu.roll(v[half][r], -blk, 1) if blk else v[half][r]
                        fresh[half].append(w[0] * before + w[1] * v[half][t] + w[2] * after)
                v = fresh
            for half in range(2):
                for t in range(LINE_RUN):
                    done[tile + half, t] = v[half][t]
        return carry

    lax.fori_loop(0, GROUPS // 2, aggregate, 0)
    sub = iota((8, LANES), 0)

    def softmax(half, carry):
        totals = jnp.zeros((8, LANES), F32)
        moments = totals
        for s in range(8):
            t = LINE_RUN - 1 - 8 * half - s
            v = [done[i, t] for i in range(DISP // 8)]
            top = v
            while len(top) > 1:
                top = [jnp.maximum(a, b) for a, b in zip(top[::2], top[1::2])] + top[len(top) & ~1 :]
            top = jnp.max(top[0], axis=0, keepdims=True)
            total = jnp.exp2(v[-1] - top)
            moment = total
            for i in range(DISP // 8 - 2, -1, -1):
                total = total + jnp.exp2(v[i] - top)
                if i:
                    moment = moment + total
            moment = 8.0 * moment + sub.astype(F32) * total
            totals = jnp.where(sub == s, jnp.sum(total, axis=0, keepdims=True), totals)
            moments = jnp.where(sub == s, jnp.sum(moment, axis=0, keepdims=True), moments)
        sums[half] = moments / totals
        return carry

    for step in range(LINE_RUN // 8):
        softmax(step, 0)
    lane_line = iota((LINE_RUN, LANES), 1) >> 6
    shift = jnp.zeros((LINE_RUN, LANES), F32)
    for i in range(PAIR):
        shift = jnp.where(lane_line == i, offsets[at + i].astype(F32), shift)
    vals = (sums[...].reshape(LINE_RUN, LANES) + shift) * (1.0 / DISP)
    both = jnp.concatenate([jnp.where(lane_line == i, vals, 0.0) for i in range(PAIR)], axis=0)
    high = both.astype(BF)
    left = both - high.astype(F32)
    middle = left.astype(BF)
    low = (left - middle.astype(F32)).astype(BF)
    parts = jnp.dot(
        jnp.concatenate([high, middle, low], axis=0), spread[...], preferred_element_type=F32
    )
    size = PAIR * LINE_RUN
    parts = parts[:size] + parts[size : 2 * size] + parts[2 * size :]
    wanted = iota((LINE_RUN, width), 0) == (iota((LINE_RUN, width), 1) & (LINE_RUN - 1))
    for i in range(PAIR):
        part = jnp.where(wanted, parts[i * LINE_RUN : (i + 1) * LINE_RUN], 0.0)
        out[i : i + 1, :] = jnp.sum(part, axis=0, keepdims=True)


def lines_plan(features, valid_cols, offsets, guide_weight):
    n = lax.axis_size("cols")
    devices = 2 * n
    width = n * BLOCK
    rows = PAIR * CHANNELS
    own = features.reshape(devices, rows, BLOCK)
    pieces = [None] * devices
    gone = ()
    for key in (1, 2, 6, 4, 7, 5, 3, 0):
        masked = key % 2 and key > 1
        (piece,) = call(
            functools.partial(pack_kernel, key),
            [((rows + (MASKS if masked else 0), BLOCK), BF)],
            [], 0,
            (own,) + ((valid_cols,) if masked else ()) + gone,
            1_000_000,
        )
        gone = (piece,)
        moves = [(i, i ^ key) for i in range(devices)]
        pieces[key] = lax.ppermute(piece, ("cols", "view"), moves) if key else piece
    consts = call(
        constants_kernel,
        [
            ((LANES, LANES), BF), ((DISP, 2 * LANES), BF), ((3 * TAP_ROWS, LANES), BF), ((LANES, width), BF),
            (valid_cols.shape, F32),
        ],
        [], 1, (offsets, guide_weight, valid_cols), 1_000_000,
    )
    (rows,) = call(
        lines_kernel,
        [((PAIR, width), F32)],
        [
            pltpu.VMEM((devices, rows, BLOCK), BF),
            pltpu.VMEM((n,) + valid_cols.shape, F32),
            pltpu.VMEM((LINE_RUN, PAIR, LINE_PARTS, LANES), BF),
            pltpu.VMEM((LINE_RUN, PAIR, LINE_PARTS, 2 * LANES), BF),
            pltpu.VMEM((DISP // 8, LINE_RUN, 8, LANES), F32),
            pltpu.VMEM((DISP // 8, LINE_RUN, 8, LANES), F32),
            pltpu.VMEM((GROUPS // 2, LINE_RUN, 3, 8, LANES), F32),
            pltpu.VMEM((LINE_RUN // 8, 8, LANES), F32),
        ],
        1, (offsets, *consts, *pieces), 1_000_000_000,
    )
    others = lax.ppermute(rows, "view", [(0, 1), (1, 0)])
    first = lax.axis_index("view") == 0
    return jnp.where(first, jnp.concatenate([rows, others]), jnp.concatenate([others, rows]))[None]


def on_device(features, valid_cols, offsets, guide_weight):
    n = lax.axis_size("cols")
    lines = features.shape[1]
    if lines == 2 * PAIR * n and n * BLOCK == LINE_RUN * LINE_PARTS:
        return lines_plan(features, valid_cols, offsets, guide_weight)
    return halo_plan(features, valid_cols, offsets, guide_weight)


def solution(mesh):
    return jax.shard_map(
        on_device,
        mesh=mesh,
        in_specs=(
            P("view", ("tiles", "lines"), None, "cols"),
            P(None, ("tiles", "cols")),
            P(("tiles", "lines")),
            P(),
        ),
        out_specs=P(("tiles", "lines"), "cols", None),
        check_vma=False,
    )
```

```python
import functools
import math

import jax
import jax.numpy as jnp
from jax import lax
from jax.experimental import pallas as pl
from jax.experimental.pallas import tpu as pltpu
from jax.sharding import PartitionSpec as P

DISP = 192
DGROUP = 16
GROUPS = DISP // DGROUP
LAYERS = 3
SHARPNESS = 2.0
HALO = 32
LANES = 128
LINES = 8
CHANNELS = 64
BLOCK = 256
SPAN = BLOCK + HALO
PARTS = LANES // LINES
RUN = SPAN // PARTS
KEYS = 40
WIDE = BLOCK + LANES
SEC_ROWS = LINES * CHANNELS
QUAD_ROWS = SEC_ROWS // 2
MASK_AT = QUAD_ROWS + CHANNELS
PAYLOAD = MASK_AT + 16
QUAD = LINES // 2
QUAD_LANES = LANES // 2
PACK = LANES // HALO
CUT = 16

BF = jnp.bfloat16
F32 = jnp.float32


def iota(shape, dim):
    return lax.broadcasted_iota(jnp.int32, shape, dim)


def dot_t(a, b):
    return lax.dot_general(a, b, (((1,), (1,)), ((), ())), preferred_element_type=F32)


def call(kernel, outs, scratch, smem, args, flops=0, space=pltpu.VMEM, limit=24, to=None):
    specs = [pl.BlockSpec(memory_space=pltpu.SMEM)] * smem
    specs += [pl.BlockSpec(memory_space=space)] * (len(args) - smem)
    return pl.pallas_call(
        kernel,
        out_shape=[jax.ShapeDtypeStruct(shape, dtype) for shape, dtype in outs],
        in_specs=specs,
        out_specs=[pl.BlockSpec(memory_space=to or space)] * len(outs),
        scratch_shapes=scratch,
        compiler_params=pltpu.CompilerParams(vmem_limit_bytes=limit * 1024 * 1024),
        cost_estimate=pl.CostEstimate(flops=flops, bytes_accessed=1_000_000, transcendentals=0),
    )(*args)


def spread_guide(guide):
    keys = LAYERS * 3 * GROUPS
    row = iota((3 * KEYS, keys), 0)
    tap = jnp.where(row >= KEYS, 1, 0) + jnp.where(row >= 2 * KEYS, 1, 0)
    row = row - KEYS * tap
    layer = jnp.where(row >= GROUPS, 1, 0) + jnp.where(row >= 2 * GROUPS, 1, 0)
    key = 2 * GROUPS * layer + GROUPS * tap + row
    chosen = jnp.where((iota((3 * KEYS, keys), 1) == key) & (row < 3 * GROUPS), 1.0, 0.0).astype(BF)
    guide_t = dot_t(chosen, guide).astype(BF)
    return jnp.concatenate([guide_t, guide_t], axis=1)


def normalise(z, wts, t, room_left, room_right):
    z = (0.55 + 0.45 * jnp.tanh(0.5 * z)).astype(BF).astype(F32)
    taps = [z[k * KEYS : (k + 1) * KEYS] for k in range(3)]
    scale = 1.0 / (taps[0] + taps[1] + taps[2])
    wts[t, 0:KEYS, :] = jnp.where(room_left >= t, taps[0] * scale, 0.0)
    wts[t, KEYS : 2 * KEYS, :] = taps[1] * scale
    wts[t, 2 * KEYS : 3 * KEYS, :] = jnp.where(room_right < t, taps[2] * scale, 0.0)


def prefetch_kernel(own, valid, guide, own_out, masks, perm, flip, guide_out, valid_in, guide_in, sems):
    copies = [
        pltpu.make_async_copy(src, dst, sems.at[i])
        for i, (src, dst) in enumerate([(own, own_out), (guide, guide_in), (valid, valid_in)])
    ]
    for copy in copies:
        copy.start()
    perm[...] = jnp.where(
        iota((SPAN, WIDE), 1) == WIDE - 1 - iota((SPAN, WIDE), 0), 1.0, 0.0
    ).astype(BF)
    back = 2 * LANES - 1 - iota((DISP, 2 * LANES), 0)
    flip[...] = jnp.where(iota((DISP, 2 * LANES), 1) == back, 1.0, 0.0).astype(BF)

    copies[1].wait()
    guide_out[...] = spread_guide(guide_in[...])
    copies[2].wait()
    masks[...] = valid_in[...].astype(F32)
    copies[0].wait()


def payload_kernel(own, other, masks, first, second, ref_own):
    view = lax.axis_index("view")
    first_view = view == 0
    sec_mask = masks[1:2, :].astype(BF)
    lane = iota((CHANNELS, LANES), 1)
    tails = []
    for line in range(LINES):
        at = view * LINES + line
        mine, theirs = own[at], other[at]
        lo = line * CHANNELS
        dest, start = (first, lo) if line < QUAD else (second, lo - QUAD_ROWS)
        dest[start : start + CHANNELS, :] = jnp.where(first_view, theirs, mine) * sec_mask
        ref = jnp.where(first_view, mine, theirs)
        ref_own[lo : lo + CHANNELS, :] = ref
        tail = ref[:, BLOCK - LANES :].astype(F32)
        slot = line % PACK
        turn = (HALO * (slot + 1)) % LANES
        if turn:
            tail = pltpu.roll(tail, turn, 1)
        if slot:
            tails[-1] = jnp.where(lane >= HALO * slot, tail, tails[-1])
        else:
            tails.append(tail)
    for i, tail in enumerate(tails):
        first[QUAD_ROWS:MASK_AT, i * LANES : (i + 1) * LANES] = tail.astype(BF)
    first[MASK_AT:, :] = jnp.broadcast_to(masks[0:1, :], (16, BLOCK)).astype(BF)


def shifted(left, mine, lo, off):
    ch_lane = iota((CHANNELS, LANES), 1)
    tiles = [
        src[lo : lo + CHANNELS, i * LANES : (i + 1) * LANES].astype(F32)
        for src in (left, mine)
        for i in range(2)
    ]
    tiles = [pltpu.roll(tile, off, 1) for tile in tiles]
    tiles = [jnp.where(ch_lane < off, tiles[max(i - 1, 0)], tiles[i]).astype(BF) for i in range(4)]
    return jnp.concatenate(tiles, axis=1)


def line_costs(lhs, rhs, slot, skew, cost_rows):
    diagonal = iota((8, LANES), 1) - iota((8, LANES), 0)
    for chunk in range(3):
        rows = min(LANES, SPAN - chunk * LANES)
        first = max(1 - chunk, 0)
        last = 3 - chunk
        products = jnp.dot(
            lhs[chunk * LANES : chunk * LANES + rows],
            rhs[:, first * LANES : (last + 1) * LANES],
            preferred_element_type=F32,
        )
        for j in range(rows // 8):
            tiles = [
                pltpu.roll(
                    products[8 * j : 8 * j + 8, i * LANES : (i + 1) * LANES],
                    8 * j, 1, stride=1, stride_axis=0,
                )
                for i in range(last + 1 - first)
            ]
            if len(tiles) < 3:
                tiles = [tiles[0]] + tiles
            beyond = diagonal >= 8 * j
            at = chunk * LANES + 8 * j
            skew[slot, 0, at : at + 8, :] = jnp.where(beyond, tiles[1], tiles[0])
            skew[slot, 1, at : at + 8, :] = jnp.where(beyond, tiles[2], tiles[1])
    for t in range(RUN):
        at = t * QUAD_LANES + slot * PARTS
        for v in range(2):
            cost_rows[at : at + PARTS, v * LANES : (v + 1) * LANES] = skew[
                slot, v, pl.ds(t, PARTS, stride=RUN), :
            ].astype(BF)


def early_kernel(
    offsets, ref_own, mine, left, masks, perm, guide, wts, cost_rows, lhs_out,
    ref_rows, ref_cols, gate_rows, skew
):
    base = lax.axis_index("view") * LINES
    low = jnp.where(lax.axis_index("cols") == 0, HALO, 0)
    for line in range(LINES):
        lo = line * CHANNELS
        ref_rows[lo : lo + CHANNELS, LANES:] = ref_own[lo : lo + CHANNELS, :]
        half = line // PACK
        packed = left[QUAD_ROWS:MASK_AT, half * LANES : (half + 1) * LANES].astype(F32)
        turn = (LANES - HALO) - HALO * (line % PACK)
        if turn:
            packed = pltpu.roll(packed, turn, 1)
        ref_rows[lo : lo + CHANNELS, :LANES] = packed.astype(BF)

    mask_left = left[MASK_AT : MASK_AT + 1, BLOCK - LANES :].astype(F32)
    ref_mask = jnp.concatenate([mask_left, masks[0:1, :]], axis=1)
    ref_mask = jnp.broadcast_to(ref_mask * (1.0 / math.sqrt(CHANNELS)), (LANES, WIDE))
    mask_cols = dot_t(perm[...], ref_mask.astype(BF))
    half_lane = iota((PARTS, LANES), 1) < CHANNELS
    span_lane = iota((SPAN, LANES), 1) < CHANNELS

    for quad in range(LINES // QUAD):
        ref_t = dot_t(perm[...], ref_rows[quad * QUAD_ROWS : (quad + 1) * QUAD_ROWS, :])
        for pair in range(QUAD // 2):
            cols = ref_t[:, pair * LANES : (pair + 1) * LANES]
            slot = quad * 2 + pair
            ref_cols[slot] = cols
            masked = cols * mask_cols
            if quad == 0:
                rhs = jnp.concatenate(
                    [
                        shifted(left, mine, line * CHANNELS, offsets[base + line])
                        for line in (2 * slot, 2 * slot + 1)
                    ],
                    axis=0,
                )
            for side in range(2):
                line = 2 * slot + side
                for t in range(RUN):
                    picked = ref_cols[slot, pl.ds(t, PARTS, stride=RUN), :]
                    picked = jnp.where(half_lane if side == 0 else ~half_lane, picked, 0.0)
                    at = t * LANES + line * PARTS
                    gate_rows[at : at + PARTS, :] = picked.astype(BF)
                lhs = jnp.where(span_lane if side == 0 else ~span_lane, masked, 0.0).astype(BF)
                if quad == 0:
                    line_costs(lhs, rhs, line, skew, cost_rows)
                else:
                    lhs_out[line - QUAD] = lhs

    place = iota((KEYS, LANES), 1)
    x_base = SPAN - 1 - RUN * (place & (PARTS - 1))
    row = iota((KEYS, LANES), 0)
    reach = jnp.where(row >= 2 * GROUPS, 9, jnp.where(row >= GROUPS, 3, 1))
    room_left = x_base - reach - low
    room_right = x_base + reach - SPAN
    for two in range(RUN // 2):
        at = 2 * two * LANES
        logits = dot_t(guide[...], gate_rows[at : at + 2 * LANES, :])
        for i in range(2):
            t = 2 * two + i
            normalise(logits[:, i * LANES : (i + 1) * LANES], wts, t, room_left, room_right)


def late_kernel(
    offsets, mine, left, lhs, early_rows, wts, flip, out, skew, cost_rows, vol, vals, turned
):
    base = lax.axis_index("view") * LINES
    for pair in range(QUAD // 2):
        rhs = jnp.concatenate(
            [
                shifted(left, mine, line * CHANNELS, offsets[base + QUAD + line])
                for line in (2 * pair, 2 * pair + 1)
            ],
            axis=0,
        )
        for line in (2 * pair, 2 * pair + 1):
            line_costs(lhs[line], rhs, line, skew, cost_rows)

    for two in range(RUN // 2):
        rows = []
        for t in (2 * two, 2 * two + 1):
            for part in (early_rows, cost_rows):
                rows.append(part[t * QUAD_LANES : (t + 1) * QUAD_LANES, :])
        costs = dot_t(flip[...], jnp.concatenate(rows, axis=0))
        vol[2 * two] = costs[:, :LANES]
        vol[2 * two + 1] = costs[:, LANES:]

    def aggregate(group, carry):
        for half in range(2):
            at = pl.multiple_of(group * DGROUP + half * 8, 8)
            v = [vol[t, pl.ds(at, 8), :] for t in range(RUN)]
            for layer in range(LAYERS):
                s = 3**layer
                before = [v[t + s] if t + s < RUN else pltpu.roll(v[t + s - RUN], LANES - 1, 1) for t in range(RUN)]
                after = [v[t - s] if t >= s else pltpu.roll(v[t - s + RUN], 1, 1) for t in range(RUN)]
                fresh = []
                for t in range(RUN):
                    w = [wts[t, pl.ds(k * KEYS + layer * GROUPS + group, 1), :] for k in range(3)]
                    fresh.append(w[0] * before[t] + w[1] * v[t] + w[2] * after[t])
                v = fresh
            for t in range(RUN):
                vol[t, pl.ds(at, 8), :] = v[t]
        return carry

    lax.fori_loop(0, GROUPS, aggregate, 0)

    vals[...] = jnp.zeros((LANES, LANES), F32)
    sub = iota((8, LANES), 0).astype(F32)
    line_of = iota((1, LANES), 1) >> 4
    offs = jnp.zeros((1, LANES), F32)
    for line in range(LINES):
        offs = jnp.where(line_of == line, offsets[base + line].astype(F32), offs)

    def softmax(t, carry):
        v = [vol[t, 8 * i : 8 * i + 8, :] for i in range(DISP // 8)]
        top = v
        while len(top) > 1:
            top = [jnp.maximum(a, b) for a, b in zip(top[::2], top[1::2])] + top[len(top) & ~1 :]
        top = jnp.max(top[0], axis=0, keepdims=True)
        e = [jnp.exp(SHARPNESS * (a - top)) for a in v]
        total = e[0]
        moment = jnp.zeros((8, LANES), F32)
        for i in range(1, DISP // 8):
            total = total + e[i]
            moment = moment + float(8 * i) * e[i]
        moment = jnp.sum(moment + sub * total, axis=0, keepdims=True)
        total = jnp.sum(total, axis=0, keepdims=True)
        vals[pl.ds(RUN - 1 - t, 1), :] = (moment / total + offs) * (1.0 / DISP)
        return carry

    lax.fori_loop(0, RUN, softmax, 0)

    turned[...] = jnp.transpose(vals[...])
    lane = iota((8, LANES), 1)
    result = [jnp.zeros((8, LANES), F32) for _ in range(WIDE // LANES)]
    for part in range(PARTS):
        piece = turned[pl.ds(part, LINES, stride=PARTS), :]
        start = (RUN * (PARTS - 1 - part) - HALO) % WIDE
        tile, turn = divmod(start, LANES)
        if turn:
            piece = pltpu.roll(piece, turn, 1)
        if turn + RUN > LANES:
            after = (tile + 1) % len(result)
            result[after] = result[after] + jnp.where(lane < turn, piece, 0.0)
            piece = jnp.where(lane >= turn, piece, 0.0)
        result[tile] = result[tile] + piece
    for tile, value in enumerate(result):
        out[:, tile * LANES : (tile + 1) * LANES] = value


def join(pieces, sub, n):
    block = lax.axis_index("cols")
    pieces = pieces.reshape(n, 2, LINES, WIDE)
    start = (0, block // (n // 2), (block % (n // 2)) * sub, 0)
    pieces = lax.dynamic_slice(pieces, start, (n, 1, sub, WIDE))[:, 0]
    main = pieces[:, :, :BLOCK]
    tail = jnp.pad(pieces[1:, :, BLOCK:], ((0, 1), (0, 0), (LANES, 0)))
    place = (n, sub, BLOCK)
    keep = (iota(place, 2) < BLOCK - CUT) | (iota(place, 0) == n - 1)
    joined = jnp.where(keep, main, tail)
    return jnp.transpose(joined, (1, 0, 2)).reshape(1, sub, n * BLOCK)


def halo_plan(features, valid_cols, offsets, guide_weight):
    own = features[0]
    n = lax.axis_size("cols")
    right = [(c, c + 1) for c in range(n - 1)]
    other = lax.ppermute(own, "view", [(0, 1), (1, 0)])
    near, masks, perm, flip, guide = call(
        prefetch_kernel,
        [(own.shape, BF), (valid_cols.shape, F32), ((SPAN, WIDE), BF), ((DISP, 2 * LANES), BF), ((3 * KEYS, LANES), BF)],
        [pltpu.VMEM(valid_cols.shape, jnp.int32), pltpu.VMEM(guide_weight.shape, BF), pltpu.SemaphoreType.DMA((3,))],
        0, (own, valid_cols, guide_weight), 100_000_000, pl.ANY, 24, pltpu.VMEM,
    )
    first, second, ref_own = call(
        payload_kernel,
        [((PAYLOAD, BLOCK), BF), ((QUAD_ROWS, BLOCK), BF), ((SEC_ROWS, BLOCK), BF)],
        [], 0, (near, other, masks),
    )
    left_first = lax.ppermute(first, "cols", right)
    left_second = lax.ppermute(second, "cols", right)
    quad_rows = (RUN * QUAD_LANES, 2 * LANES)
    skew = pltpu.VMEM((QUAD, 2, SPAN, LANES), F32)
    square = pltpu.VMEM((LANES, LANES), F32)
    wts, early_rows, lhs = call(
        early_kernel,
        [((RUN, 3 * KEYS, LANES), F32), (quad_rows, BF), ((QUAD, SPAN, LANES), BF)],
        [pltpu.VMEM((SEC_ROWS, WIDE), BF), pltpu.VMEM((QUAD, SPAN, LANES), F32), pltpu.VMEM((RUN * LANES, LANES), BF), skew],
        1, (offsets, ref_own, first, left_first, masks, perm, guide), 1_000_000_000,
    )
    (result,) = call(
        late_kernel,
        [((LINES, WIDE), F32)],
        [skew, pltpu.VMEM(quad_rows, BF), pltpu.VMEM((RUN, DISP, LANES), F32), square, square],
        1, (offsets, second, left_second, lhs, early_rows, wts, flip), 1_000_000_000,
    )
    copies = jnp.broadcast_to(result[None], (2 * n, LINES, WIDE))
    pieces = lax.all_to_all(copies, ("cols", "view"), split_axis=0, concat_axis=0, tiled=True)
    return join(pieces, own.shape[0] // n, n)


LINE_RUN = 16
PAIR = 2
LINE_PARTS = LANES // PAIR


MASKS = 8
GATE_FLOOR = 11.0 / 9.0


def pack_kernel(key, own, *rest):
    out = rest[-1]
    me = 2 * lax.axis_index("cols") + lax.axis_index("view")
    rows = PAIR * CHANNELS
    out[:rows, :] = own[me ^ key]
    if out.shape[0] > rows:
        masks = rest[0][...].astype(F32)
        out[rows:, :] = jnp.where(
            iota((MASKS, BLOCK), 0) < MASKS // 2, masks[0:1, :], masks[1:2, :]
        ).astype(BF)


def constants_kernel(offsets, guide, valid, order, flip, guide_out, spread, masks):
    masks[...] = valid[...].astype(F32)
    row = iota((LANES, LANES), 0)
    from_lane = LANES - 1 - LINE_RUN * (row & 7) - (row >> 3)
    order[...] = jnp.where(iota((LANES, LANES), 1) == from_lane, 1.0, 0.0).astype(BF)
    back = 2 * LANES - 1 - iota((DISP, 2 * LANES), 0)
    flip[...] = jnp.where(iota((DISP, 2 * LANES), 1) == back, 1.0, 0.0).astype(BF)
    guide_out[...] = spread_guide(guide[...]) * 0.5
    block_of = LINE_PARTS - 1 - (iota(spread.shape, 1) >> 4)
    here = (iota(spread.shape, 0) & (LINE_PARTS - 1)) == block_of
    spread[...] = jnp.where(here, 1.0, 0.0).astype(BF)


def lines_kernel(
    offsets, order, flip, guide, spread, *rest
):
    pieces, (out, blocks, valid, gate_rows, cost_rows, vol, done, wts) = rest[:-8], rest[-8:]
    near, pieces = pieces[0], pieces[1:]
    tiles = len(pieces)
    width = tiles * LANES
    me = 2 * lax.axis_index("cols") + lax.axis_index("view")
    rows = PAIR * CHANNELS
    for key, piece in enumerate(pieces):
        blocks[me ^ key] = piece[:rows, :]
        if piece.shape[0] > rows:
            masks = piece[rows:, :].astype(F32)
            valid[(me ^ key) // 2] = jnp.concatenate([masks[0:1], masks[MASKS // 2 : MASKS // 2 + 1]], axis=0)
    valid[me // 2] = near[...]
    at = PAIR * me
    offs = [offsets[at + i] for i in range(PAIR)]
    ch_lane = iota((CHANNELS, LANES), 1)
    reached = iota((8, LANES), 1) + LINE_RUN * iota((8, LANES), 0)
    low_half = iota((LANES, LANES), 1) < CHANNELS
    scale = 1.0 / math.sqrt(CHANNELS)
    empty = jnp.zeros((CHANNELS, LANES), F32)

    def mask_of(view, w):
        lo = (w % 2) * LANES
        return valid[w // 2, view : view + 1, lo : lo + LANES]

    def tile_of(view, i, w):
        lo = (w % 2) * LANES
        return blocks[2 * (w // 2) + view, i * CHANNELS : (i + 1) * CHANNELS, lo : lo + LANES]

    def place_of(i, quad, two):
        return i * LINE_PARTS + 8 * (tiles - 2 - 4 * quad - 2 * two)

    quads = [(i, quad) for i in range(PAIR) for quad in range(tiles // 4)]
    for i, quad in quads:
        refs = [tile_of(0, i, 4 * quad + q) for q in range(4)]
        cols = dot_t(order[...], jnp.concatenate(refs, axis=0))
        for two in range(2):
            pair = cols[:, two * LANES : (two + 1) * LANES]
            gates = [jnp.where(low_half, pair, 0.0), jnp.where(low_half, 0.0, pair)]
            place = place_of(i, quad, two)
            for t in range(LINE_RUN):
                row = t * LANES + place
                r = 8 * t
                gate_rows[row : row + 16, :] = jnp.concatenate(
                    [gates[1][r : r + 8], gates[0][r : r + 8]], axis=0
                ).astype(BF)

    x_base = width - 1 - LINE_RUN * (iota((KEYS, LANES), 1) & (LINE_PARTS - 1))
    row = iota((KEYS, LANES), 0)
    reach = jnp.where(row >= 2 * GROUPS, 9, jnp.where(row >= GROUPS, 3, 1))
    room_left = x_base - reach
    room_right = x_base + reach - width
    unit = jnp.where(row >= 2 * GROUPS, SHARPNESS / math.log(2.0), 1.0)

    def weigh(two):
        lo = 2 * two * LANES
        logits = dot_t(guide[...], gate_rows[lo : lo + 2 * LANES, :])
        for i in range(2):
            t = 2 * two + i
            z = jnp.tanh(logits[:, i * LANES : (i + 1) * LANES]) + GATE_FLOOR
            taps = [z[m * KEYS : (m + 1) * KEYS] for m in range(3)]
            factor = unit / (taps[0] + taps[1] + taps[2])
            taps = [tap * factor for tap in taps]
            if t >= LINE_RUN - 9:
                taps[0] = jnp.where(room_left >= t, taps[0], 0.0)
            if t < 9:
                taps[2] = jnp.where(room_right < t, taps[2], 0.0)
            for m in range(3):
                wts[t, m * KEYS : (m + 1) * KEYS, :] = taps[m]

    shifted = []
    for i in range(PAIR):
        off = offs[i]
        rolled = [pltpu.roll(tile_of(1, i, w).astype(F32) * mask_of(1, w), off, 1) for w in range(tiles)]
        line = [empty.astype(BF)] * 2
        for w in range(tiles):
            line.append(jnp.where(ch_lane < off, rolled[w - 1] if w else empty, rolled[w]).astype(BF))
        shifted.append(line)

    step = 0
    for i, quad in quads:
        masked = [
            tile_of(0, i, 4 * quad + q) * (mask_of(0, 4 * quad + q) * scale).astype(BF) for q in range(4)
        ]
        masked = dot_t(order[...], jnp.concatenate(masked, axis=0))
        for two in range(2):
            products = []
            lhs = masked[:, two * LANES : (two + 1) * LANES].astype(BF)
            for side in range(2):
                w = 4 * quad + 2 * two + side
                window = jnp.concatenate(shifted[i][w : w + 3], axis=1)
                rhs = [jnp.zeros_like(window)] * 2
                rhs[side] = window
                rhs = jnp.concatenate(rhs, axis=0)
                products.append(jnp.dot(lhs, rhs, preferred_element_type=F32))
            place = place_of(i, quad, two)
            for t in range(LINE_RUN):
                row = t * LANES + place
                r = 8 * t
                within = reached < LANES - t
                both = []
                for side in (1, 0):
                    part = [products[side][r : r + 8, m * LANES : (m + 1) * LANES] for m in range(3)]
                    both.append(
                        jnp.concatenate(
                            [
                                pltpu.roll(
                                    jnp.where(within, part[m + 1], part[m]),
                                    t, 1, stride=LINE_RUN, stride_axis=0,
                                )
                                for m in range(2)
                            ],
                            axis=1,
                        )
                    )
                cost_rows[row : row + 16, :] = jnp.concatenate(both, axis=0).astype(BF)
            weigh(step)
            step += 1

    for two in range(LINE_RUN // 2):
        lo = 2 * two * LANES
        costs = dot_t(flip[...], cost_rows[lo : lo + 2 * LANES, :])
        for i in range(2):
            vol[2 * two + i] = costs[:, i * LANES : (i + 1) * LANES]

    for group in range(GROUPS):
        starts = [group * DGROUP + 8 * half for half in range(2)]
        v = [[vol[t, at : at + 8, :] for t in range(LINE_RUN)] for at in starts]
        for layer in range(LAYERS):
            s = 3**layer
            fresh = [[], []]
            for t in range(LINE_RUN):
                rows = [k * KEYS + layer * GROUPS + group for k in range(3)]
                w = [jnp.broadcast_to(wts[t, r : r + 1, :], (8, LANES)) for r in rows]
                for half in range(2):
                    blk, r = divmod(t + s, LINE_RUN)
                    before = pltpu.roll(v[half][r], LANES - blk, 1) if blk else v[half][r]
                    blk, r = divmod(t - s, LINE_RUN)
                    after = pltpu.roll(v[half][r], -blk, 1) if blk else v[half][r]
                    fresh[half].append(w[0] * before + w[1] * v[half][t] + w[2] * after)
            v = fresh
        for half, at in enumerate(starts):
            for t in range(LINE_RUN):
                done[t, at : at + 8, :] = v[half][t]

    sub = iota((8, LANES), 0)
    results = []
    for block in range(LINE_RUN // 8):
        totals = jnp.zeros((8, LANES), F32)
        moments = totals
        for s in range(8):
            t = LINE_RUN - 1 - (8 * block + s)
            v = [done[t, 8 * i : 8 * i + 8, :] for i in range(DISP // 8)]
            top = v
            while len(top) > 1:
                top = [jnp.maximum(a, b) for a, b in zip(top[::2], top[1::2])] + top[len(top) & ~1 :]
            top = jnp.max(top[0], axis=0, keepdims=True)
            total = jnp.exp2(v[-1] - top)
            moment = total
            for i in range(DISP // 8 - 2, -1, -1):
                total = total + jnp.exp2(v[i] - top)
                if i:
                    moment = moment + total
            moment = 8.0 * moment + sub.astype(F32) * total
            totals = jnp.where(sub == s, jnp.sum(total, axis=0, keepdims=True), totals)
            moments = jnp.where(sub == s, jnp.sum(moment, axis=0, keepdims=True), moments)
        lane_line = iota((8, LANES), 1) >> 6
        shift = jnp.zeros((8, LANES), F32)
        for i in range(PAIR):
            shift = jnp.where(lane_line == i, offs[i].astype(F32), shift)
        results.append((moments / totals + shift) * (1.0 / DISP))
    vals = jnp.concatenate(results, axis=0)
    lane_line = iota((LINE_RUN, LANES), 1) >> 6
    both = jnp.concatenate([jnp.where(lane_line == i, vals, 0.0) for i in range(PAIR)], axis=0)
    high = both.astype(BF)
    rest = both - high.astype(F32)
    middle = rest.astype(BF)
    low = (rest - middle.astype(F32)).astype(BF)
    pieces = jnp.dot(
        jnp.concatenate([high, middle, low], axis=0), spread[...], preferred_element_type=F32
    )
    size = PAIR * LINE_RUN
    pieces = pieces[:size] + pieces[size : 2 * size] + pieces[2 * size :]
    wanted = iota((LINE_RUN, width), 0) == (iota((LINE_RUN, width), 1) & (LINE_RUN - 1))
    for i in range(PAIR):
        piece = jnp.where(wanted, pieces[i * LINE_RUN : (i + 1) * LINE_RUN], 0.0)
        out[i : i + 1, :] = jnp.sum(piece, axis=0, keepdims=True)


def lines_plan(features, valid_cols, offsets, guide_weight):
    n = lax.axis_size("cols")
    devices = 2 * n
    width = n * BLOCK
    rows = PAIR * CHANNELS
    own = features.reshape(devices, rows, BLOCK)
    pieces = [None] * devices
    gone = ()
    me = 2 * lax.axis_index("cols") + lax.axis_index("view")
    heads = [lax.dynamic_index_in_dim(own, me ^ key, 0, False) for key in (6, 4)]
    for key in (1, 2, 6, 4, 7, 5, 3, 0):
        masked = key % 2 and key > 1
        if key in (4, 6):
            piece = heads[0 if key == 6 else 1]
            pieces[key] = lax.ppermute(piece, ("cols", "view"), [(i, i ^ key) for i in range(devices)])
            continue
        (piece,) = call(
            functools.partial(pack_kernel, key),
            [((rows + (MASKS if masked else 0), BLOCK), BF)],
            [], 0,
            (own,) + ((valid_cols,) if masked else ()) + gone + tuple(heads),
            1_000_000,
        )
        gone = (piece,)
        moves = [(i, i ^ key) for i in range(devices)]
        pieces[key] = lax.ppermute(piece, ("cols", "view"), moves) if key else piece
    consts = call(
        constants_kernel,
        [
            ((LANES, LANES), BF), ((DISP, 2 * LANES), BF), ((3 * KEYS, LANES), BF), ((LANES, width), BF),
            (valid_cols.shape, F32),
        ],
        [], 1, (offsets, guide_weight, valid_cols), 1_000_000,
    )
    (rows,) = call(
        lines_kernel,
        [((PAIR, width), F32)],
        [
            pltpu.VMEM((devices, rows, BLOCK), BF),
            pltpu.VMEM((n,) + valid_cols.shape, F32),
            pltpu.VMEM((LINE_RUN * LANES, LANES), BF),
            pltpu.VMEM((LINE_RUN * LANES, 2 * LANES), BF),
            pltpu.VMEM((LINE_RUN, DISP, LANES), F32),
            pltpu.VMEM((LINE_RUN, DISP, LANES), F32),
            pltpu.VMEM((LINE_RUN, 3 * KEYS, LANES), F32),
        ],
        1, (offsets, *consts, *pieces), 1_000_000_000,
    )
    others = lax.ppermute(rows, "view", [(0, 1), (1, 0)])
    first = lax.axis_index("view") == 0
    return jnp.where(first, jnp.concatenate([rows, others]), jnp.concatenate([others, rows]))[None]


def on_device(features, valid_cols, offsets, guide_weight):
    n = lax.axis_size("cols")
    lines = features.shape[1]
    if lines == 2 * PAIR * n and n * BLOCK == LINE_RUN * LINE_PARTS:
        return lines_plan(features, valid_cols, offsets, guide_weight)
    return halo_plan(features, valid_cols, offsets, guide_weight)


def solution(mesh):
    return jax.shard_map(
        on_device,
        mesh=mesh,
        in_specs=(
            P("view", ("tiles", "lines"), None, "cols"),
            P(None, ("tiles", "cols")),
            P(("tiles", "lines")),
            P(),
        ),
        out_specs=P(("tiles", "lines"), "cols", None),
        check_vma=False,
    )
```

```python
import functools
import math

import jax
import jax.numpy as jnp
from jax import lax
from jax.experimental import pallas as pl
from jax.experimental.pallas import tpu as pltpu
from jax.sharding import PartitionSpec as P

DISP = 192
DGROUP = 16
GROUPS = DISP // DGROUP
LAYERS = 3
SHARPNESS = 2.0
HALO = 32
LANES = 128
LINES = 8
CHANNELS = 64
BLOCK = 256
SPAN = BLOCK + HALO
PARTS = LANES // LINES
RUN = SPAN // PARTS
KEYS = 40
WIDE = BLOCK + LANES
SEC_ROWS = LINES * CHANNELS
QUAD_ROWS = SEC_ROWS // 2
MASK_AT = QUAD_ROWS + CHANNELS
PAYLOAD = MASK_AT + 16
QUAD = LINES // 2
QUAD_LANES = LANES // 2
PACK = LANES // HALO
CUT = 16

BF = jnp.bfloat16
F32 = jnp.float32


def iota(shape, dim):
    return lax.broadcasted_iota(jnp.int32, shape, dim)


def dot_t(a, b):
    return lax.dot_general(a, b, (((1,), (1,)), ((), ())), preferred_element_type=F32)


def call(kernel, outs, scratch, smem, args, flops=0, space=pltpu.VMEM, limit=24, to=None):
    specs = [pl.BlockSpec(memory_space=pltpu.SMEM)] * smem
    specs += [pl.BlockSpec(memory_space=space)] * (len(args) - smem)
    return pl.pallas_call(
        kernel,
        out_shape=[jax.ShapeDtypeStruct(shape, dtype) for shape, dtype in outs],
        in_specs=specs,
        out_specs=[pl.BlockSpec(memory_space=to or space)] * len(outs),
        scratch_shapes=scratch,
        compiler_params=pltpu.CompilerParams(vmem_limit_bytes=limit * 1024 * 1024),
        cost_estimate=pl.CostEstimate(flops=flops, bytes_accessed=1_000_000, transcendentals=0),
    )(*args)


def spread_guide(guide):
    keys = LAYERS * 3 * GROUPS
    row = iota((3 * KEYS, keys), 0)
    tap = jnp.where(row >= KEYS, 1, 0) + jnp.where(row >= 2 * KEYS, 1, 0)
    row = row - KEYS * tap
    layer = jnp.where(row >= GROUPS, 1, 0) + jnp.where(row >= 2 * GROUPS, 1, 0)
    key = 2 * GROUPS * layer + GROUPS * tap + row
    chosen = jnp.where((iota((3 * KEYS, keys), 1) == key) & (row < 3 * GROUPS), 1.0, 0.0).astype(BF)
    guide_t = dot_t(chosen, guide).astype(BF)
    return jnp.concatenate([guide_t, guide_t], axis=1)


def normalise(z, wts, t, room_left, room_right):
    z = (0.55 + 0.45 * jnp.tanh(0.5 * z)).astype(BF).astype(F32)
    taps = [z[k * KEYS : (k + 1) * KEYS] for k in range(3)]
    scale = 1.0 / (taps[0] + taps[1] + taps[2])
    wts[t, 0:KEYS, :] = jnp.where(room_left >= t, taps[0] * scale, 0.0)
    wts[t, KEYS : 2 * KEYS, :] = taps[1] * scale
    wts[t, 2 * KEYS : 3 * KEYS, :] = jnp.where(room_right < t, taps[2] * scale, 0.0)


def prefetch_kernel(own, valid, guide, own_out, masks, perm, flip, guide_out, valid_in, guide_in, sems):
    copies = [
        pltpu.make_async_copy(src, dst, sems.at[i])
        for i, (src, dst) in enumerate([(own, own_out), (guide, guide_in), (valid, valid_in)])
    ]
    for copy in copies:
        copy.start()
    perm[...] = jnp.where(
        iota((SPAN, WIDE), 1) == WIDE - 1 - iota((SPAN, WIDE), 0), 1.0, 0.0
    ).astype(BF)
    back = 2 * LANES - 1 - iota((DISP, 2 * LANES), 0)
    flip[...] = jnp.where(iota((DISP, 2 * LANES), 1) == back, 1.0, 0.0).astype(BF)

    copies[1].wait()
    guide_out[...] = spread_guide(guide_in[...])
    copies[2].wait()
    masks[...] = valid_in[...].astype(F32)
    copies[0].wait()


def payload_kernel(own, other, masks, first, second, ref_own):
    view = lax.axis_index("view")
    first_view = view == 0
    sec_mask = masks[1:2, :].astype(BF)
    lane = iota((CHANNELS, LANES), 1)
    tails = []
    for line in range(LINES):
        at = view * LINES + line
        mine, theirs = own[at], other[at]
        lo = line * CHANNELS
        dest, start = (first, lo) if line < QUAD else (second, lo - QUAD_ROWS)
        dest[start : start + CHANNELS, :] = jnp.where(first_view, theirs, mine) * sec_mask
        ref = jnp.where(first_view, mine, theirs)
        ref_own[lo : lo + CHANNELS, :] = ref
        tail = ref[:, BLOCK - LANES :].astype(F32)
        slot = line % PACK
        turn = (HALO * (slot + 1)) % LANES
        if turn:
            tail = pltpu.roll(tail, turn, 1)
        if slot:
            tails[-1] = jnp.where(lane >= HALO * slot, tail, tails[-1])
        else:
            tails.append(tail)
    for i, tail in enumerate(tails):
        first[QUAD_ROWS:MASK_AT, i * LANES : (i + 1) * LANES] = tail.astype(BF)
    first[MASK_AT:, :] = jnp.broadcast_to(masks[0:1, :], (16, BLOCK)).astype(BF)


def shifted(left, mine, lo, off):
    ch_lane = iota((CHANNELS, LANES), 1)
    tiles = [
        src[lo : lo + CHANNELS, i * LANES : (i + 1) * LANES].astype(F32)
        for src in (left, mine)
        for i in range(2)
    ]
    tiles = [pltpu.roll(tile, off, 1) for tile in tiles]
    tiles = [jnp.where(ch_lane < off, tiles[max(i - 1, 0)], tiles[i]).astype(BF) for i in range(4)]
    return jnp.concatenate(tiles, axis=1)


def line_costs(lhs, rhs, slot, skew, cost_rows):
    diagonal = iota((8, LANES), 1) - iota((8, LANES), 0)
    for chunk in range(3):
        rows = min(LANES, SPAN - chunk * LANES)
        first = max(1 - chunk, 0)
        last = 3 - chunk
        products = jnp.dot(
            lhs[chunk * LANES : chunk * LANES + rows],
            rhs[:, first * LANES : (last + 1) * LANES],
            preferred_element_type=F32,
        )
        for j in range(rows // 8):
            tiles = [
                pltpu.roll(
                    products[8 * j : 8 * j + 8, i * LANES : (i + 1) * LANES],
                    8 * j, 1, stride=1, stride_axis=0,
                )
                for i in range(last + 1 - first)
            ]
            if len(tiles) < 3:
                tiles = [tiles[0]] + tiles
            beyond = diagonal >= 8 * j
            at = chunk * LANES + 8 * j
            skew[slot, 0, at : at + 8, :] = jnp.where(beyond, tiles[1], tiles[0])
            skew[slot, 1, at : at + 8, :] = jnp.where(beyond, tiles[2], tiles[1])
    for t in range(RUN):
        at = t * QUAD_LANES + slot * PARTS
        for v in range(2):
            cost_rows[at : at + PARTS, v * LANES : (v + 1) * LANES] = skew[
                slot, v, pl.ds(t, PARTS, stride=RUN), :
            ].astype(BF)


def early_kernel(
    offsets, ref_own, mine, left, masks, perm, guide, wts, cost_rows, lhs_out,
    ref_rows, ref_cols, gate_rows, skew
):
    base = lax.axis_index("view") * LINES
    low = jnp.where(lax.axis_index("cols") == 0, HALO, 0)
    for line in range(LINES):
        lo = line * CHANNELS
        ref_rows[lo : lo + CHANNELS, LANES:] = ref_own[lo : lo + CHANNELS, :]
        half = line // PACK
        packed = left[QUAD_ROWS:MASK_AT, half * LANES : (half + 1) * LANES].astype(F32)
        turn = (LANES - HALO) - HALO * (line % PACK)
        if turn:
            packed = pltpu.roll(packed, turn, 1)
        ref_rows[lo : lo + CHANNELS, :LANES] = packed.astype(BF)

    mask_left = left[MASK_AT : MASK_AT + 1, BLOCK - LANES :].astype(F32)
    ref_mask = jnp.concatenate([mask_left, masks[0:1, :]], axis=1)
    ref_mask = jnp.broadcast_to(ref_mask * (1.0 / math.sqrt(CHANNELS)), (LANES, WIDE))
    mask_cols = dot_t(perm[...], ref_mask.astype(BF))
    half_lane = iota((PARTS, LANES), 1) < CHANNELS
    span_lane = iota((SPAN, LANES), 1) < CHANNELS

    for quad in range(LINES // QUAD):
        ref_t = dot_t(perm[...], ref_rows[quad * QUAD_ROWS : (quad + 1) * QUAD_ROWS, :])
        for pair in range(QUAD // 2):
            cols = ref_t[:, pair * LANES : (pair + 1) * LANES]
            slot = quad * 2 + pair
            ref_cols[slot] = cols
            masked = cols * mask_cols
            if quad == 0:
                rhs = jnp.concatenate(
                    [
                        shifted(left, mine, line * CHANNELS, offsets[base + line])
                        for line in (2 * slot, 2 * slot + 1)
                    ],
                    axis=0,
                )
            for side in range(2):
                line = 2 * slot + side
                for t in range(RUN):
                    picked = ref_cols[slot, pl.ds(t, PARTS, stride=RUN), :]
                    picked = jnp.where(half_lane if side == 0 else ~half_lane, picked, 0.0)
                    at = t * LANES + line * PARTS
                    gate_rows[at : at + PARTS, :] = picked.astype(BF)
                lhs = jnp.where(span_lane if side == 0 else ~span_lane, masked, 0.0).astype(BF)
                if quad == 0:
                    line_costs(lhs, rhs, line, skew, cost_rows)
                else:
                    lhs_out[line - QUAD] = lhs

    place = iota((KEYS, LANES), 1)
    x_base = SPAN - 1 - RUN * (place & (PARTS - 1))
    row = iota((KEYS, LANES), 0)
    reach = jnp.where(row >= 2 * GROUPS, 9, jnp.where(row >= GROUPS, 3, 1))
    room_left = x_base - reach - low
    room_right = x_base + reach - SPAN
    for two in range(RUN // 2):
        at = 2 * two * LANES
        logits = dot_t(guide[...], gate_rows[at : at + 2 * LANES, :])
        for i in range(2):
            t = 2 * two + i
            normalise(logits[:, i * LANES : (i + 1) * LANES], wts, t, room_left, room_right)


def late_kernel(
    offsets, mine, left, lhs, early_rows, wts, flip, out, skew, cost_rows, vol, vals, turned
):
    base = lax.axis_index("view") * LINES
    for pair in range(QUAD // 2):
        rhs = jnp.concatenate(
            [
                shifted(left, mine, line * CHANNELS, offsets[base + QUAD + line])
                for line in (2 * pair, 2 * pair + 1)
            ],
            axis=0,
        )
        for line in (2 * pair, 2 * pair + 1):
            line_costs(lhs[line], rhs, line, skew, cost_rows)

    for two in range(RUN // 2):
        rows = []
        for t in (2 * two, 2 * two + 1):
            for part in (early_rows, cost_rows):
                rows.append(part[t * QUAD_LANES : (t + 1) * QUAD_LANES, :])
        costs = dot_t(flip[...], jnp.concatenate(rows, axis=0))
        vol[2 * two] = costs[:, :LANES]
        vol[2 * two + 1] = costs[:, LANES:]

    def aggregate(group, carry):
        for half in range(2):
            at = pl.multiple_of(group * DGROUP + half * 8, 8)
            v = [vol[t, pl.ds(at, 8), :] for t in range(RUN)]
            for layer in range(LAYERS):
                s = 3**layer
                before = [v[t + s] if t + s < RUN else pltpu.roll(v[t + s - RUN], LANES - 1, 1) for t in range(RUN)]
                after = [v[t - s] if t >= s else pltpu.roll(v[t - s + RUN], 1, 1) for t in range(RUN)]
                fresh = []
                for t in range(RUN):
                    w = [wts[t, pl.ds(k * KEYS + layer * GROUPS + group, 1), :] for k in range(3)]
                    fresh.append(w[0] * before[t] + w[1] * v[t] + w[2] * after[t])
                v = fresh
            for t in range(RUN):
                vol[t, pl.ds(at, 8), :] = v[t]
        return carry

    lax.fori_loop(0, GROUPS, aggregate, 0)

    vals[...] = jnp.zeros((LANES, LANES), F32)
    sub = iota((8, LANES), 0).astype(F32)
    line_of = iota((1, LANES), 1) >> 4
    offs = jnp.zeros((1, LANES), F32)
    for line in range(LINES):
        offs = jnp.where(line_of == line, offsets[base + line].astype(F32), offs)

    def softmax(t, carry):
        v = [vol[t, 8 * i : 8 * i + 8, :] for i in range(DISP // 8)]
        top = v
        while len(top) > 1:
            top = [jnp.maximum(a, b) for a, b in zip(top[::2], top[1::2])] + top[len(top) & ~1 :]
        top = jnp.max(top[0], axis=0, keepdims=True)
        e = [jnp.exp(SHARPNESS * (a - top)) for a in v]
        total = e[0]
        moment = jnp.zeros((8, LANES), F32)
        for i in range(1, DISP // 8):
            total = total + e[i]
            moment = moment + float(8 * i) * e[i]
        moment = jnp.sum(moment + sub * total, axis=0, keepdims=True)
        total = jnp.sum(total, axis=0, keepdims=True)
        vals[pl.ds(RUN - 1 - t, 1), :] = (moment / total + offs) * (1.0 / DISP)
        return carry

    lax.fori_loop(0, RUN, softmax, 0)

    turned[...] = jnp.transpose(vals[...])
    lane = iota((8, LANES), 1)
    result = [jnp.zeros((8, LANES), F32) for _ in range(WIDE // LANES)]
    for part in range(PARTS):
        piece = turned[pl.ds(part, LINES, stride=PARTS), :]
        start = (RUN * (PARTS - 1 - part) - HALO) % WIDE
        tile, turn = divmod(start, LANES)
        if turn:
            piece = pltpu.roll(piece, turn, 1)
        if turn + RUN > LANES:
            after = (tile + 1) % len(result)
            result[after] = result[after] + jnp.where(lane < turn, piece, 0.0)
            piece = jnp.where(lane >= turn, piece, 0.0)
        result[tile] = result[tile] + piece
    for tile, value in enumerate(result):
        out[:, tile * LANES : (tile + 1) * LANES] = value


def join(pieces, sub, n):
    block = lax.axis_index("cols")
    pieces = pieces.reshape(n, 2, LINES, WIDE)
    start = (0, block // (n // 2), (block % (n // 2)) * sub, 0)
    pieces = lax.dynamic_slice(pieces, start, (n, 1, sub, WIDE))[:, 0]
    main = pieces[:, :, :BLOCK]
    tail = jnp.pad(pieces[1:, :, BLOCK:], ((0, 1), (0, 0), (LANES, 0)))
    place = (n, sub, BLOCK)
    keep = (iota(place, 2) < BLOCK - CUT) | (iota(place, 0) == n - 1)
    joined = jnp.where(keep, main, tail)
    return jnp.transpose(joined, (1, 0, 2)).reshape(1, sub, n * BLOCK)


def halo_plan(features, valid_cols, offsets, guide_weight):
    own = features[0]
    n = lax.axis_size("cols")
    right = [(c, c + 1) for c in range(n - 1)]
    other = lax.ppermute(own, "view", [(0, 1), (1, 0)])
    near, masks, perm, flip, guide = call(
        prefetch_kernel,
        [(own.shape, BF), (valid_cols.shape, F32), ((SPAN, WIDE), BF), ((DISP, 2 * LANES), BF), ((3 * KEYS, LANES), BF)],
        [pltpu.VMEM(valid_cols.shape, jnp.int32), pltpu.VMEM(guide_weight.shape, BF), pltpu.SemaphoreType.DMA((3,))],
        0, (own, valid_cols, guide_weight), 100_000_000, pl.ANY, 24, pltpu.VMEM,
    )
    first, second, ref_own = call(
        payload_kernel,
        [((PAYLOAD, BLOCK), BF), ((QUAD_ROWS, BLOCK), BF), ((SEC_ROWS, BLOCK), BF)],
        [], 0, (near, other, masks),
    )
    left_first = lax.ppermute(first, "cols", right)
    left_second = lax.ppermute(second, "cols", right)
    quad_rows = (RUN * QUAD_LANES, 2 * LANES)
    skew = pltpu.VMEM((QUAD, 2, SPAN, LANES), F32)
    square = pltpu.VMEM((LANES, LANES), F32)
    wts, early_rows, lhs = call(
        early_kernel,
        [((RUN, 3 * KEYS, LANES), F32), (quad_rows, BF), ((QUAD, SPAN, LANES), BF)],
        [pltpu.VMEM((SEC_ROWS, WIDE), BF), pltpu.VMEM((QUAD, SPAN, LANES), F32), pltpu.VMEM((RUN * LANES, LANES), BF), skew],
        1, (offsets, ref_own, first, left_first, masks, perm, guide), 1_000_000_000,
    )
    (result,) = call(
        late_kernel,
        [((LINES, WIDE), F32)],
        [skew, pltpu.VMEM(quad_rows, BF), pltpu.VMEM((RUN, DISP, LANES), F32), square, square],
        1, (offsets, second, left_second, lhs, early_rows, wts, flip), 1_000_000_000,
    )
    copies = jnp.broadcast_to(result[None], (2 * n, LINES, WIDE))
    pieces = lax.all_to_all(copies, ("cols", "view"), split_axis=0, concat_axis=0, tiled=True)
    return join(pieces, own.shape[0] // n, n)


LINE_RUN = 16
PAIR = 2
LINE_PARTS = LANES // PAIR


MASKS = 8
GATE_FLOOR = 11.0 / 9.0


def pack_kernel(key, own, *rest):
    out = rest[-1]
    me = 2 * lax.axis_index("cols") + lax.axis_index("view")
    rows = PAIR * CHANNELS
    out[:rows, :] = own[me ^ key]
    if out.shape[0] > rows:
        masks = rest[0][...].astype(F32)
        out[rows:, :] = jnp.where(
            iota((MASKS, BLOCK), 0) < MASKS // 2, masks[0:1, :], masks[1:2, :]
        ).astype(BF)


def constants_kernel(offsets, guide, valid, order, order_band, flip, guide_out, spread, masks):
    masks[...] = valid[...].astype(F32)
    row = iota((LANES, LANES), 0)
    from_lane = LANES - 1 - LINE_RUN * (row & 7) - (row >> 3)
    order[...] = jnp.where(iota((LANES, LANES), 1) == from_lane, 1.0, 0.0).astype(BF)
    from_lane = LANES - 1 - (row & 64) - 8 * (row & 7) - ((row >> 3) & 7)
    order_band[...] = jnp.where(iota((LANES, LANES), 1) == from_lane, 1.0, 0.0).astype(BF)
    back = 2 * LANES - 1 - iota((DISP, 2 * LANES), 0)
    flip[...] = jnp.where(iota((DISP, 2 * LANES), 1) == back, 1.0, 0.0).astype(BF)
    guide_out[...] = spread_guide(guide[...]) * 0.5
    block_of = LINE_PARTS - 1 - (iota(spread.shape, 1) >> 4)
    here = (iota(spread.shape, 0) & (LINE_PARTS - 1)) == block_of
    spread[...] = jnp.where(here, 1.0, 0.0).astype(BF)


def lines_kernel(
    offsets, order, order_band, flip, guide, spread, *rest
):
    pieces, (out, blocks, valid, gate_rows, cost_rows, vol, done, wts, band) = rest[:-9], rest[-9:]
    near, pieces = pieces[0], pieces[1:]
    tiles = len(pieces)
    width = tiles * LANES
    me = 2 * lax.axis_index("cols") + lax.axis_index("view")
    rows = PAIR * CHANNELS
    for key, piece in enumerate(pieces):
        blocks[me ^ key] = piece[:rows, :]
        if piece.shape[0] > rows:
            masks = piece[rows:, :].astype(F32)
            valid[(me ^ key) // 2] = jnp.concatenate([masks[0:1], masks[MASKS // 2 : MASKS // 2 + 1]], axis=0)
    valid[me // 2] = near[...]
    at = PAIR * me
    offs = [offsets[at + i] for i in range(PAIR)]
    ch_lane = iota((CHANNELS, LANES), 1)
    reached = iota((8, LANES), 1) + LINE_RUN * iota((8, LANES), 0)
    low_half = iota((LANES, LANES), 1) < CHANNELS
    scale = 1.0 / math.sqrt(CHANNELS)
    empty = jnp.zeros((CHANNELS, LANES), F32)

    def mask_of(view, w):
        lo = (w % 2) * LANES
        return valid[w // 2, view : view + 1, lo : lo + LANES]

    def tile_of(view, i, w):
        lo = (w % 2) * LANES
        return blocks[2 * (w // 2) + view, i * CHANNELS : (i + 1) * CHANNELS, lo : lo + LANES]

    def place_of(i, quad, two):
        return i * LINE_PARTS + 8 * (tiles - 2 - 4 * quad - 2 * two)

    quads = [(i, quad) for i in range(PAIR) for quad in range(tiles // 4)]
    for i, quad in quads:
        refs = [tile_of(0, i, 4 * quad + q) for q in range(4)]
        cols = dot_t(order[...], jnp.concatenate(refs, axis=0))
        for two in range(2):
            pair = cols[:, two * LANES : (two + 1) * LANES]
            gates = [jnp.where(low_half, pair, 0.0), jnp.where(low_half, 0.0, pair)]
            place = place_of(i, quad, two)
            for t in range(LINE_RUN):
                row = t * LANES + place
                r = 8 * t
                gate_rows[row : row + 16, :] = jnp.concatenate(
                    [gates[1][r : r + 8], gates[0][r : r + 8]], axis=0
                ).astype(BF)

    x_base = width - 1 - LINE_RUN * (iota((KEYS, LANES), 1) & (LINE_PARTS - 1))
    row = iota((KEYS, LANES), 0)
    reach = jnp.where(row >= 2 * GROUPS, 9, jnp.where(row >= GROUPS, 3, 1))
    room_left = x_base - reach
    room_right = x_base + reach - width
    unit = jnp.where(row >= 2 * GROUPS, SHARPNESS / math.log(2.0), 1.0)

    def weigh(two):
        lo = 2 * two * LANES
        logits = dot_t(guide[...], gate_rows[lo : lo + 2 * LANES, :])
        for i in range(2):
            t = 2 * two + i
            z = jnp.tanh(logits[:, i * LANES : (i + 1) * LANES]) + GATE_FLOOR
            taps = [z[m * KEYS : (m + 1) * KEYS] for m in range(3)]
            factor = unit / (taps[0] + taps[1] + taps[2])
            taps = [tap * factor for tap in taps]
            if t >= LINE_RUN - 9:
                taps[0] = jnp.where(room_left >= t, taps[0], 0.0)
            if t < 9:
                taps[2] = jnp.where(room_right < t, taps[2], 0.0)
            for m in range(3):
                wts[t, m * KEYS : (m + 1) * KEYS, :] = taps[m]

    shifted, halfway = [], []
    low_lane = ch_lane < LANES // 2
    for i in range(PAIR):
        off = offs[i]
        rolled = [pltpu.roll(tile_of(1, i, w).astype(F32) * mask_of(1, w), off, 1) for w in range(tiles)]
        line = [empty, empty]
        for w in range(tiles):
            line.append(jnp.where(ch_lane < off, rolled[w - 1] if w else empty, rolled[w]))
        turned = [empty] + [pltpu.roll(tile, LANES // 2, 1) if w else tile for w, tile in enumerate(line[1:])]
        shifted.append([tile.astype(BF) for tile in line])
        halfway.append([jnp.where(low_lane, a, b).astype(BF) for a, b in zip(turned, turned[1:])])

    reached = iota((8, LANES), 1) + 8 * iota((8, LANES), 0)
    step = 0
    for i, quad in quads:
        masked = [
            tile_of(0, i, 4 * quad + q) * (mask_of(0, 4 * quad + q) * scale).astype(BF) for q in range(4)
        ]
        masked = dot_t(order_band[...], jnp.concatenate(masked, axis=0))
        for two in range(2):
            w = 4 * quad + 2 * two
            pair = masked[:, two * LANES : (two + 1) * LANES]
            sides = [jnp.where(low_half, pair, 0.0).astype(BF), jnp.where(low_half, 0.0, pair).astype(BF)]
            for half, source, first in ((0, shifted[i], w + 1), (1, halfway[i], w)):
                lo = half * LANES // 2
                lhs = jnp.concatenate([side[lo : lo + LANES // 2] for side in sides], axis=0)
                rhs = jnp.concatenate(
                    [jnp.concatenate(source[first + side : first + side + 2], axis=1) for side in range(2)], axis=0
                )
                products = jnp.dot(lhs, rhs, preferred_element_type=F32)
                for side in range(2):
                    for t in range(8):
                        r = side * LANES // 2 + 8 * t
                        near, far = products[r : r + 8, :LANES], products[r : r + 8, LANES:]
                        joined = jnp.where(reached < LANES - t, far, near)
                        for v, value in enumerate((near, joined)):
                            band[i, w + side, t, v, 8 * half : 8 * half + 8, :] = pltpu.roll(
                                value, t, 1, stride=8, stride_axis=0
                            )
            place = place_of(i, quad, two)
            for t in range(LINE_RUN):
                row = t * LANES + place
                for v in range(2):
                    both = [
                        band[i, w + side, t % 8, v, pl.ds(t // 8, 8, stride=2), :] for side in (1, 0)
                    ]
                    cost_rows[row : row + 16, v * LANES : (v + 1) * LANES] = jnp.concatenate(both, axis=0).astype(BF)
            weigh(step)
            step += 1

    for two in range(LINE_RUN // 2):
        lo = 2 * two * LANES
        costs = dot_t(flip[...], cost_rows[lo : lo + 2 * LANES, :])
        for i in range(2):
            vol[2 * two + i] = costs[:, i * LANES : (i + 1) * LANES]

    for group in range(GROUPS):
        starts = [group * DGROUP + 8 * half for half in range(2)]
        v = [[vol[t, at : at + 8, :] for t in range(LINE_RUN)] for at in starts]
        for layer in range(LAYERS):
            s = 3**layer
            fresh = [[], []]
            for t in range(LINE_RUN):
                rows = [k * KEYS + layer * GROUPS + group for k in range(3)]
                w = [jnp.broadcast_to(wts[t, r : r + 1, :], (8, LANES)) for r in rows]
                for half in range(2):
                    blk, r = divmod(t + s, LINE_RUN)
                    before = pltpu.roll(v[half][r], LANES - blk, 1) if blk else v[half][r]
                    blk, r = divmod(t - s, LINE_RUN)
                    after = pltpu.roll(v[half][r], -blk, 1) if blk else v[half][r]
                    fresh[half].append(w[0] * before + w[1] * v[half][t] + w[2] * after)
            v = fresh
        for half, at in enumerate(starts):
            for t in range(LINE_RUN):
                done[t, at : at + 8, :] = v[half][t]

    sub = iota((8, LANES), 0)
    results = []
    for block in range(LINE_RUN // 8):
        totals = jnp.zeros((8, LANES), F32)
        moments = totals
        for s in range(8):
            t = LINE_RUN - 1 - (8 * block + s)
            v = [done[t, 8 * i : 8 * i + 8, :] for i in range(DISP // 8)]
            top = v
            while len(top) > 1:
                top = [jnp.maximum(a, b) for a, b in zip(top[::2], top[1::2])] + top[len(top) & ~1 :]
            top = jnp.max(top[0], axis=0, keepdims=True)
            total = jnp.exp2(v[-1] - top)
            moment = total
            for i in range(DISP // 8 - 2, -1, -1):
                total = total + jnp.exp2(v[i] - top)
                if i:
                    moment = moment + total
            moment = 8.0 * moment + sub.astype(F32) * total
            totals = jnp.where(sub == s, jnp.sum(total, axis=0, keepdims=True), totals)
            moments = jnp.where(sub == s, jnp.sum(moment, axis=0, keepdims=True), moments)
        lane_line = iota((8, LANES), 1) >> 6
        shift = jnp.zeros((8, LANES), F32)
        for i in range(PAIR):
            shift = jnp.where(lane_line == i, offs[i].astype(F32), shift)
        results.append((moments / totals + shift) * (1.0 / DISP))
    vals = jnp.concatenate(results, axis=0)
    lane_line = iota((LINE_RUN, LANES), 1) >> 6
    both = jnp.concatenate([jnp.where(lane_line == i, vals, 0.0) for i in range(PAIR)], axis=0)
    high = both.astype(BF)
    rest = both - high.astype(F32)
    middle = rest.astype(BF)
    low = (rest - middle.astype(F32)).astype(BF)
    pieces = jnp.dot(
        jnp.concatenate([high, middle, low], axis=0), spread[...], preferred_element_type=F32
    )
    size = PAIR * LINE_RUN
    pieces = pieces[:size] + pieces[size : 2 * size] + pieces[2 * size :]
    wanted = iota((LINE_RUN, width), 0) == (iota((LINE_RUN, width), 1) & (LINE_RUN - 1))
    for i in range(PAIR):
        piece = jnp.where(wanted, pieces[i * LINE_RUN : (i + 1) * LINE_RUN], 0.0)
        out[i : i + 1, :] = jnp.sum(piece, axis=0, keepdims=True)


def lines_plan(features, valid_cols, offsets, guide_weight):
    n = lax.axis_size("cols")
    devices = 2 * n
    width = n * BLOCK
    rows = PAIR * CHANNELS
    own = features.reshape(devices, rows, BLOCK)
    pieces = [None] * devices
    gone = ()
    for key in (1, 2, 6, 4, 7, 5, 3, 0):
        masked = key % 2 and key > 1
        (piece,) = call(
            functools.partial(pack_kernel, key),
            [((rows + (MASKS if masked else 0), BLOCK), BF)],
            [], 0,
            (own,) + ((valid_cols,) if masked else ()) + gone,
            1_000_000,
        )
        gone = (piece,)
        moves = [(i, i ^ key) for i in range(devices)]
        pieces[key] = lax.ppermute(piece, ("cols", "view"), moves) if key else piece
    consts = call(
        constants_kernel,
        [
            ((LANES, LANES), BF), ((LANES, LANES), BF), ((DISP, 2 * LANES), BF), ((3 * KEYS, LANES), BF),
            ((LANES, width), BF), (valid_cols.shape, F32),
        ],
        [], 1, (offsets, guide_weight, valid_cols), 1_000_000,
    )
    (rows,) = call(
        lines_kernel,
        [((PAIR, width), F32)],
        [
            pltpu.VMEM((devices, rows, BLOCK), BF),
            pltpu.VMEM((n,) + valid_cols.shape, F32),
            pltpu.VMEM((LINE_RUN * LANES, LANES), BF),
            pltpu.VMEM((LINE_RUN * LANES, 2 * LANES), BF),
            pltpu.VMEM((LINE_RUN, DISP, LANES), F32),
            pltpu.VMEM((LINE_RUN, DISP, LANES), F32),
            pltpu.VMEM((LINE_RUN, 3 * KEYS, LANES), F32),
            pltpu.VMEM((PAIR, devices, 8, 2, 16, LANES), F32),
        ],
        1, (offsets, *consts, *pieces), 1_000_000_000,
    )
    others = lax.ppermute(rows, "view", [(0, 1), (1, 0)])
    first = lax.axis_index("view") == 0
    return jnp.where(first, jnp.concatenate([rows, others]), jnp.concatenate([others, rows]))[None]


def on_device(features, valid_cols, offsets, guide_weight):
    n = lax.axis_size("cols")
    lines = features.shape[1]
    if lines == 2 * PAIR * n and n * BLOCK == LINE_RUN * LINE_PARTS:
        return lines_plan(features, valid_cols, offsets, guide_weight)
    return halo_plan(features, valid_cols, offsets, guide_weight)


def solution(mesh):
    return jax.shard_map(
        on_device,
        mesh=mesh,
        in_specs=(
            P("view", ("tiles", "lines"), None, "cols"),
            P(None, ("tiles", "cols")),
            P(("tiles", "lines")),
            P(),
        ),
        out_specs=P(("tiles", "lines"), "cols", None),
        check_vma=False,
    )
```

```python
import functools
import math

import jax
import jax.numpy as jnp
from jax import lax
from jax.experimental import pallas as pl
from jax.experimental.pallas import tpu as pltpu
from jax.sharding import PartitionSpec as P

DISP = 192
DGROUP = 16
GROUPS = DISP // DGROUP
LAYERS = 3
SHARPNESS = 2.0
HALO = 32
LANES = 128
LINES = 8
CHANNELS = 64
BLOCK = 256
SPAN = BLOCK + HALO
PARTS = LANES // LINES
RUN = SPAN // PARTS
KEYS = 40
WIDE = BLOCK + LANES
SEC_ROWS = LINES * CHANNELS
QUAD_ROWS = SEC_ROWS // 2
MASK_AT = QUAD_ROWS + CHANNELS
PAYLOAD = MASK_AT + 16
QUAD = LINES // 2
QUAD_LANES = LANES // 2
PACK = LANES // HALO
CUT = 16

BF = jnp.bfloat16
F32 = jnp.float32


def iota(shape, dim):
    return lax.broadcasted_iota(jnp.int32, shape, dim)


def dot_t(a, b):
    return lax.dot_general(a, b, (((1,), (1,)), ((), ())), preferred_element_type=F32)


def call(kernel, outs, scratch, smem, args, flops=0, space=pltpu.VMEM, limit=24, to=None):
    specs = [pl.BlockSpec(memory_space=pltpu.SMEM)] * smem
    specs += [pl.BlockSpec(memory_space=space)] * (len(args) - smem)
    return pl.pallas_call(
        kernel,
        out_shape=[jax.ShapeDtypeStruct(shape, dtype) for shape, dtype in outs],
        in_specs=specs,
        out_specs=[pl.BlockSpec(memory_space=to or space)] * len(outs),
        scratch_shapes=scratch,
        compiler_params=pltpu.CompilerParams(vmem_limit_bytes=limit * 1024 * 1024),
        cost_estimate=pl.CostEstimate(flops=flops, bytes_accessed=1_000_000, transcendentals=0),
    )(*args)


def spread_guide(guide):
    keys = LAYERS * 3 * GROUPS
    row = iota((3 * KEYS, keys), 0)
    tap = jnp.where(row >= KEYS, 1, 0) + jnp.where(row >= 2 * KEYS, 1, 0)
    row = row - KEYS * tap
    layer = jnp.where(row >= GROUPS, 1, 0) + jnp.where(row >= 2 * GROUPS, 1, 0)
    key = 2 * GROUPS * layer + GROUPS * tap + row
    chosen = jnp.where((iota((3 * KEYS, keys), 1) == key) & (row < 3 * GROUPS), 1.0, 0.0).astype(BF)
    guide_t = dot_t(chosen, guide).astype(BF)
    return jnp.concatenate([guide_t, guide_t], axis=1)


def normalise(z, wts, t, room_left, room_right):
    z = (0.55 + 0.45 * jnp.tanh(0.5 * z)).astype(BF).astype(F32)
    taps = [z[k * KEYS : (k + 1) * KEYS] for k in range(3)]
    scale = 1.0 / (taps[0] + taps[1] + taps[2])
    wts[t, 0:KEYS, :] = jnp.where(room_left >= t, taps[0] * scale, 0.0)
    wts[t, KEYS : 2 * KEYS, :] = taps[1] * scale
    wts[t, 2 * KEYS : 3 * KEYS, :] = jnp.where(room_right < t, taps[2] * scale, 0.0)


def prefetch_kernel(own, valid, guide, own_out, masks, perm, flip, guide_out, valid_in, guide_in, sems):
    copies = [
        pltpu.make_async_copy(src, dst, sems.at[i])
        for i, (src, dst) in enumerate([(own, own_out), (guide, guide_in), (valid, valid_in)])
    ]
    for copy in copies:
        copy.start()
    perm[...] = jnp.where(
        iota((SPAN, WIDE), 1) == WIDE - 1 - iota((SPAN, WIDE), 0), 1.0, 0.0
    ).astype(BF)
    back = 2 * LANES - 1 - iota((DISP, 2 * LANES), 0)
    flip[...] = jnp.where(iota((DISP, 2 * LANES), 1) == back, 1.0, 0.0).astype(BF)

    copies[1].wait()
    guide_out[...] = spread_guide(guide_in[...])
    copies[2].wait()
    masks[...] = valid_in[...].astype(F32)
    copies[0].wait()


def payload_kernel(own, other, masks, first, second, ref_own):
    view = lax.axis_index("view")
    first_view = view == 0
    sec_mask = masks[1:2, :].astype(BF)
    lane = iota((CHANNELS, LANES), 1)
    tails = []
    for line in range(LINES):
        at = view * LINES + line
        mine, theirs = own[at], other[at]
        lo = line * CHANNELS
        dest, start = (first, lo) if line < QUAD else (second, lo - QUAD_ROWS)
        dest[start : start + CHANNELS, :] = jnp.where(first_view, theirs, mine) * sec_mask
        ref = jnp.where(first_view, mine, theirs)
        ref_own[lo : lo + CHANNELS, :] = ref
        tail = ref[:, BLOCK - LANES :].astype(F32)
        slot = line % PACK
        turn = (HALO * (slot + 1)) % LANES
        if turn:
            tail = pltpu.roll(tail, turn, 1)
        if slot:
            tails[-1] = jnp.where(lane >= HALO * slot, tail, tails[-1])
        else:
            tails.append(tail)
    for i, tail in enumerate(tails):
        first[QUAD_ROWS:MASK_AT, i * LANES : (i + 1) * LANES] = tail.astype(BF)
    first[MASK_AT:, :] = jnp.broadcast_to(masks[0:1, :], (16, BLOCK)).astype(BF)


def shifted(left, mine, lo, off):
    ch_lane = iota((CHANNELS, LANES), 1)
    tiles = [
        src[lo : lo + CHANNELS, i * LANES : (i + 1) * LANES].astype(F32)
        for src in (left, mine)
        for i in range(2)
    ]
    tiles = [pltpu.roll(tile, off, 1) for tile in tiles]
    tiles = [jnp.where(ch_lane < off, tiles[max(i - 1, 0)], tiles[i]).astype(BF) for i in range(4)]
    return jnp.concatenate(tiles, axis=1)


def line_costs(lhs, rhs, slot, skew, cost_rows):
    diagonal = iota((8, LANES), 1) - iota((8, LANES), 0)
    for chunk in range(3):
        rows = min(LANES, SPAN - chunk * LANES)
        first = max(1 - chunk, 0)
        last = 3 - chunk
        products = jnp.dot(
            lhs[chunk * LANES : chunk * LANES + rows],
            rhs[:, first * LANES : (last + 1) * LANES],
            preferred_element_type=F32,
        )
        for j in range(rows // 8):
            tiles = [
                pltpu.roll(
                    products[8 * j : 8 * j + 8, i * LANES : (i + 1) * LANES],
                    8 * j, 1, stride=1, stride_axis=0,
                )
                for i in range(last + 1 - first)
            ]
            if len(tiles) < 3:
                tiles = [tiles[0]] + tiles
            beyond = diagonal >= 8 * j
            at = chunk * LANES + 8 * j
            skew[slot, 0, at : at + 8, :] = jnp.where(beyond, tiles[1], tiles[0])
            skew[slot, 1, at : at + 8, :] = jnp.where(beyond, tiles[2], tiles[1])
    for t in range(RUN):
        at = t * QUAD_LANES + slot * PARTS
        for v in range(2):
            cost_rows[at : at + PARTS, v * LANES : (v + 1) * LANES] = skew[
                slot, v, pl.ds(t, PARTS, stride=RUN), :
            ].astype(BF)


def early_kernel(
    offsets, ref_own, mine, left, masks, perm, guide, wts, cost_rows, lhs_out,
    ref_rows, ref_cols, gate_rows, skew
):
    base = lax.axis_index("view") * LINES
    low = jnp.where(lax.axis_index("cols") == 0, HALO, 0)
    for line in range(LINES):
        lo = line * CHANNELS
        ref_rows[lo : lo + CHANNELS, LANES:] = ref_own[lo : lo + CHANNELS, :]
        half = line // PACK
        packed = left[QUAD_ROWS:MASK_AT, half * LANES : (half + 1) * LANES].astype(F32)
        turn = (LANES - HALO) - HALO * (line % PACK)
        if turn:
            packed = pltpu.roll(packed, turn, 1)
        ref_rows[lo : lo + CHANNELS, :LANES] = packed.astype(BF)

    mask_left = left[MASK_AT : MASK_AT + 1, BLOCK - LANES :].astype(F32)
    ref_mask = jnp.concatenate([mask_left, masks[0:1, :]], axis=1)
    ref_mask = jnp.broadcast_to(ref_mask * (1.0 / math.sqrt(CHANNELS)), (LANES, WIDE))
    mask_cols = dot_t(perm[...], ref_mask.astype(BF))
    half_lane = iota((PARTS, LANES), 1) < CHANNELS
    span_lane = iota((SPAN, LANES), 1) < CHANNELS

    for quad in range(LINES // QUAD):
        ref_t = dot_t(perm[...], ref_rows[quad * QUAD_ROWS : (quad + 1) * QUAD_ROWS, :])
        for pair in range(QUAD // 2):
            cols = ref_t[:, pair * LANES : (pair + 1) * LANES]
            slot = quad * 2 + pair
            ref_cols[slot] = cols
            masked = cols * mask_cols
            if quad == 0:
                rhs = jnp.concatenate(
                    [
                        shifted(left, mine, line * CHANNELS, offsets[base + line])
                        for line in (2 * slot, 2 * slot + 1)
                    ],
                    axis=0,
                )
            for side in range(2):
                line = 2 * slot + side
                for t in range(RUN):
                    picked = ref_cols[slot, pl.ds(t, PARTS, stride=RUN), :]
                    picked = jnp.where(half_lane if side == 0 else ~half_lane, picked, 0.0)
                    at = t * LANES + line * PARTS
                    gate_rows[at : at + PARTS, :] = picked.astype(BF)
                lhs = jnp.where(span_lane if side == 0 else ~span_lane, masked, 0.0).astype(BF)
                if quad == 0:
                    line_costs(lhs, rhs, line, skew, cost_rows)
                else:
                    lhs_out[line - QUAD] = lhs

    place = iota((KEYS, LANES), 1)
    x_base = SPAN - 1 - RUN * (place & (PARTS - 1))
    row = iota((KEYS, LANES), 0)
    reach = jnp.where(row >= 2 * GROUPS, 9, jnp.where(row >= GROUPS, 3, 1))
    room_left = x_base - reach - low
    room_right = x_base + reach - SPAN
    for two in range(RUN // 2):
        at = 2 * two * LANES
        logits = dot_t(guide[...], gate_rows[at : at + 2 * LANES, :])
        for i in range(2):
            t = 2 * two + i
            normalise(logits[:, i * LANES : (i + 1) * LANES], wts, t, room_left, room_right)


def late_kernel(
    offsets, mine, left, lhs, early_rows, wts, flip, out, skew, cost_rows, vol, vals, turned
):
    base = lax.axis_index("view") * LINES
    for pair in range(QUAD // 2):
        rhs = jnp.concatenate(
            [
                shifted(left, mine, line * CHANNELS, offsets[base + QUAD + line])
                for line in (2 * pair, 2 * pair + 1)
            ],
            axis=0,
        )
        for line in (2 * pair, 2 * pair + 1):
            line_costs(lhs[line], rhs, line, skew, cost_rows)

    for two in range(RUN // 2):
        rows = []
        for t in (2 * two, 2 * two + 1):
            for part in (early_rows, cost_rows):
                rows.append(part[t * QUAD_LANES : (t + 1) * QUAD_LANES, :])
        costs = dot_t(flip[...], jnp.concatenate(rows, axis=0))
        vol[2 * two] = costs[:, :LANES]
        vol[2 * two + 1] = costs[:, LANES:]

    def aggregate(group, carry):
        for half in range(2):
            at = pl.multiple_of(group * DGROUP + half * 8, 8)
            v = [vol[t, pl.ds(at, 8), :] for t in range(RUN)]
            for layer in range(LAYERS):
                s = 3**layer
                before = [v[t + s] if t + s < RUN else pltpu.roll(v[t + s - RUN], LANES - 1, 1) for t in range(RUN)]
                after = [v[t - s] if t >= s else pltpu.roll(v[t - s + RUN], 1, 1) for t in range(RUN)]
                fresh = []
                for t in range(RUN):
                    w = [wts[t, pl.ds(k * KEYS + layer * GROUPS + group, 1), :] for k in range(3)]
                    fresh.append(w[0] * before[t] + w[1] * v[t] + w[2] * after[t])
                v = fresh
            for t in range(RUN):
                vol[t, pl.ds(at, 8), :] = v[t]
        return carry

    lax.fori_loop(0, GROUPS, aggregate, 0)

    vals[...] = jnp.zeros((LANES, LANES), F32)
    sub = iota((8, LANES), 0).astype(F32)
    line_of = iota((1, LANES), 1) >> 4
    offs = jnp.zeros((1, LANES), F32)
    for line in range(LINES):
        offs = jnp.where(line_of == line, offsets[base + line].astype(F32), offs)

    def softmax(t, carry):
        v = [vol[t, 8 * i : 8 * i + 8, :] for i in range(DISP // 8)]
        top = v
        while len(top) > 1:
            top = [jnp.maximum(a, b) for a, b in zip(top[::2], top[1::2])] + top[len(top) & ~1 :]
        top = jnp.max(top[0], axis=0, keepdims=True)
        e = [jnp.exp(SHARPNESS * (a - top)) for a in v]
        total = e[0]
        moment = jnp.zeros((8, LANES), F32)
        for i in range(1, DISP // 8):
            total = total + e[i]
            moment = moment + float(8 * i) * e[i]
        moment = jnp.sum(moment + sub * total, axis=0, keepdims=True)
        total = jnp.sum(total, axis=0, keepdims=True)
        vals[pl.ds(RUN - 1 - t, 1), :] = (moment / total + offs) * (1.0 / DISP)
        return carry

    lax.fori_loop(0, RUN, softmax, 0)

    turned[...] = jnp.transpose(vals[...])
    lane = iota((8, LANES), 1)
    result = [jnp.zeros((8, LANES), F32) for _ in range(WIDE // LANES)]
    for part in range(PARTS):
        piece = turned[pl.ds(part, LINES, stride=PARTS), :]
        start = (RUN * (PARTS - 1 - part) - HALO) % WIDE
        tile, turn = divmod(start, LANES)
        if turn:
            piece = pltpu.roll(piece, turn, 1)
        if turn + RUN > LANES:
            after = (tile + 1) % len(result)
            result[after] = result[after] + jnp.where(lane < turn, piece, 0.0)
            piece = jnp.where(lane >= turn, piece, 0.0)
        result[tile] = result[tile] + piece
    for tile, value in enumerate(result):
        out[:, tile * LANES : (tile + 1) * LANES] = value


def join(pieces, sub, n):
    block = lax.axis_index("cols")
    pieces = pieces.reshape(n, 2, LINES, WIDE)
    start = (0, block // (n // 2), (block % (n // 2)) * sub, 0)
    pieces = lax.dynamic_slice(pieces, start, (n, 1, sub, WIDE))[:, 0]
    main = pieces[:, :, :BLOCK]
    tail = jnp.pad(pieces[1:, :, BLOCK:], ((0, 1), (0, 0), (LANES, 0)))
    place = (n, sub, BLOCK)
    keep = (iota(place, 2) < BLOCK - CUT) | (iota(place, 0) == n - 1)
    joined = jnp.where(keep, main, tail)
    return jnp.transpose(joined, (1, 0, 2)).reshape(1, sub, n * BLOCK)


def halo_plan(features, valid_cols, offsets, guide_weight):
    own = features[0]
    n = lax.axis_size("cols")
    right = [(c, c + 1) for c in range(n - 1)]
    other = lax.ppermute(own, "view", [(0, 1), (1, 0)])
    near, masks, perm, flip, guide = call(
        prefetch_kernel,
        [(own.shape, BF), (valid_cols.shape, F32), ((SPAN, WIDE), BF), ((DISP, 2 * LANES), BF), ((3 * KEYS, LANES), BF)],
        [pltpu.VMEM(valid_cols.shape, jnp.int32), pltpu.VMEM(guide_weight.shape, BF), pltpu.SemaphoreType.DMA((3,))],
        0, (own, valid_cols, guide_weight), 100_000_000, pl.ANY, 24, pltpu.VMEM,
    )
    first, second, ref_own = call(
        payload_kernel,
        [((PAYLOAD, BLOCK), BF), ((QUAD_ROWS, BLOCK), BF), ((SEC_ROWS, BLOCK), BF)],
        [], 0, (near, other, masks),
    )
    left_first = lax.ppermute(first, "cols", right)
    left_second = lax.ppermute(second, "cols", right)
    quad_rows = (RUN * QUAD_LANES, 2 * LANES)
    skew = pltpu.VMEM((QUAD, 2, SPAN, LANES), F32)
    square = pltpu.VMEM((LANES, LANES), F32)
    wts, early_rows, lhs = call(
        early_kernel,
        [((RUN, 3 * KEYS, LANES), F32), (quad_rows, BF), ((QUAD, SPAN, LANES), BF)],
        [pltpu.VMEM((SEC_ROWS, WIDE), BF), pltpu.VMEM((QUAD, SPAN, LANES), F32), pltpu.VMEM((RUN * LANES, LANES), BF), skew],
        1, (offsets, ref_own, first, left_first, masks, perm, guide), 1_000_000_000,
    )
    (result,) = call(
        late_kernel,
        [((LINES, WIDE), F32)],
        [skew, pltpu.VMEM(quad_rows, BF), pltpu.VMEM((RUN, DISP, LANES), F32), square, square],
        1, (offsets, second, left_second, lhs, early_rows, wts, flip), 1_000_000_000,
    )
    copies = jnp.broadcast_to(result[None], (2 * n, LINES, WIDE))
    pieces = lax.all_to_all(copies, ("cols", "view"), split_axis=0, concat_axis=0, tiled=True)
    return join(pieces, own.shape[0] // n, n)


LINE_RUN = 16
PAIR = 2
LINE_PARTS = LANES // PAIR


MASKS = 8
GATE_FLOOR = 11.0 / 9.0


def pack_kernel(key, own, *rest):
    out = rest[-1]
    me = 2 * lax.axis_index("cols") + lax.axis_index("view")
    rows = PAIR * CHANNELS
    out[:rows, :] = own[me ^ key]
    if out.shape[0] > rows:
        masks = rest[0][...].astype(F32)
        out[rows:, :] = jnp.where(
            iota((MASKS, BLOCK), 0) < MASKS // 2, masks[0:1, :], masks[1:2, :]
        ).astype(BF)


def constants_kernel(offsets, guide, valid, order, flip, guide_out, spread, masks):
    masks[...] = valid[...].astype(F32)
    row = iota((LANES, LANES), 0)
    from_lane = LANES - 1 - LINE_RUN * (row & 7) - (row >> 3)
    order[...] = jnp.where(iota((LANES, LANES), 1) == from_lane, 1.0, 0.0).astype(BF)
    back = 2 * LANES - 1 - iota((DISP, 2 * LANES), 0)
    flip[...] = jnp.where(iota((DISP, 2 * LANES), 1) == back, 1.0, 0.0).astype(BF)
    guide_out[...] = spread_guide(guide[...]) * 0.5
    block_of = LINE_PARTS - 1 - (iota(spread.shape, 1) >> 4)
    here = (iota(spread.shape, 0) & (LINE_PARTS - 1)) == block_of
    spread[...] = jnp.where(here, 1.0, 0.0).astype(BF)


def lines_kernel(
    offsets, order, flip, guide, spread, *rest
):
    pieces, (out, blocks, valid, wts) = rest[:-4], rest[-4:]
    near, pieces = pieces[0], pieces[1:]
    tiles = len(pieces)
    width = tiles * LANES
    me = 2 * lax.axis_index("cols") + lax.axis_index("view")
    rows = PAIR * CHANNELS
    for key, piece in enumerate(pieces):
        blocks[me ^ key] = piece[:rows, :]
        if piece.shape[0] > rows:
            masks = piece[rows:, :].astype(F32)
            valid[(me ^ key) // 2] = jnp.concatenate([masks[0:1], masks[MASKS // 2 : MASKS // 2 + 1]], axis=0)
    valid[me // 2] = near[...]
    at = PAIR * me
    offs = [offsets[at + i] for i in range(PAIR)]
    ch_lane = iota((CHANNELS, LANES), 1)
    reached = iota((8, LANES), 1) + LINE_RUN * iota((8, LANES), 0)
    low_half = iota((LANES, LANES), 1) < CHANNELS
    scale = 1.0 / math.sqrt(CHANNELS)
    empty = jnp.zeros((CHANNELS, LANES), F32)

    def mask_of(view, w):
        lo = (w % 2) * LANES
        return valid[w // 2, view : view + 1, lo : lo + LANES]

    def tile_of(view, i, w):
        lo = (w % 2) * LANES
        return blocks[2 * (w // 2) + view, i * CHANNELS : (i + 1) * CHANNELS, lo : lo + LANES]

    def place_of(i, quad, two):
        return i * LINE_PARTS + 8 * (tiles - 2 - 4 * quad - 2 * two)

    gate_parts, cost_parts = {}, {}

    def joined(parts, two):
        rows = [
            parts[t, place]
            for t in (2 * two, 2 * two + 1)
            for place in range(0, LANES, 16)
        ]
        return jnp.concatenate(rows, axis=0)

    quads = [(i, quad) for i in range(PAIR) for quad in range(tiles // 4)]
    for i, quad in quads:
        refs = [tile_of(0, i, 4 * quad + q) for q in range(4)]
        cols = dot_t(order[...], jnp.concatenate(refs, axis=0))
        for two in range(2):
            pair = cols[:, two * LANES : (two + 1) * LANES]
            gates = [jnp.where(low_half, pair, 0.0), jnp.where(low_half, 0.0, pair)]
            place = place_of(i, quad, two)
            for t in range(LINE_RUN):
                r = 8 * t
                gate_parts[t, place] = jnp.concatenate(
                    [gates[1][r : r + 8], gates[0][r : r + 8]], axis=0
                ).astype(BF)

    x_base = width - 1 - LINE_RUN * (iota((KEYS, LANES), 1) & (LINE_PARTS - 1))
    row = iota((KEYS, LANES), 0)
    reach = jnp.where(row >= 2 * GROUPS, 9, jnp.where(row >= GROUPS, 3, 1))
    room_left = x_base - reach
    room_right = x_base + reach - width
    unit = jnp.where(row >= 2 * GROUPS, SHARPNESS / math.log(2.0), 1.0)

    def weigh(two):
        logits = dot_t(guide[...], joined(gate_parts, two))
        for i in range(2):
            t = 2 * two + i
            z = jnp.tanh(logits[:, i * LANES : (i + 1) * LANES]) + GATE_FLOOR
            taps = [z[m * KEYS : (m + 1) * KEYS] for m in range(3)]
            factor = unit / (taps[0] + taps[1] + taps[2])
            taps = [tap * factor for tap in taps]
            if t >= LINE_RUN - 9:
                taps[0] = jnp.where(room_left >= t, taps[0], 0.0)
            if t < 9:
                taps[2] = jnp.where(room_right < t, taps[2], 0.0)
            for m in range(3):
                wts[t, m * KEYS : (m + 1) * KEYS, :] = taps[m]

    shifted = []
    for i in range(PAIR):
        off = offs[i]
        rolled = [pltpu.roll(tile_of(1, i, w).astype(F32) * mask_of(1, w), off, 1) for w in range(tiles)]
        line = [empty.astype(BF)] * 2
        for w in range(tiles):
            line.append(jnp.where(ch_lane < off, rolled[w - 1] if w else empty, rolled[w]).astype(BF))
        shifted.append(line)

    step = 0
    for i, quad in quads:
        masked = [
            tile_of(0, i, 4 * quad + q) * (mask_of(0, 4 * quad + q) * scale).astype(BF) for q in range(4)
        ]
        masked = dot_t(order[...], jnp.concatenate(masked, axis=0))
        for two in range(2):
            products = []
            lhs = masked[:, two * LANES : (two + 1) * LANES].astype(BF)
            for side in range(2):
                w = 4 * quad + 2 * two + side
                window = jnp.concatenate(shifted[i][w : w + 3], axis=1)
                rhs = [jnp.zeros_like(window)] * 2
                rhs[side] = window
                rhs = jnp.concatenate(rhs, axis=0)
                products.append(jnp.dot(lhs, rhs, preferred_element_type=F32))
            place = place_of(i, quad, two)
            for t in range(LINE_RUN):
                r = 8 * t
                within = reached < LANES - t
                both = []
                for side in (1, 0):
                    part = [products[side][r : r + 8, m * LANES : (m + 1) * LANES] for m in range(3)]
                    both.append(
                        jnp.concatenate(
                            [
                                pltpu.roll(
                                    jnp.where(within, part[m + 1], part[m]),
                                    t, 1, stride=LINE_RUN, stride_axis=0,
                                )
                                for m in range(2)
                            ],
                            axis=1,
                        )
                    )
                cost_parts[t, place] = jnp.concatenate(both, axis=0).astype(BF)
            weigh(step)
            step += 1

    vol = []
    for two in range(LINE_RUN // 2):
        costs = dot_t(flip[...], joined(cost_parts, two))
        vol += [costs[:, :LANES], costs[:, LANES:]]
    done = {}

    for group in range(GROUPS):
        starts = [group * DGROUP + 8 * half for half in range(2)]
        v = [[vol[t][at : at + 8] for t in range(LINE_RUN)] for at in starts]
        for layer in range(LAYERS):
            s = 3**layer
            fresh = [[], []]
            for t in range(LINE_RUN):
                rows = [k * KEYS + layer * GROUPS + group for k in range(3)]
                w = [jnp.broadcast_to(wts[t, r : r + 1, :], (8, LANES)) for r in rows]
                for half in range(2):
                    blk, r = divmod(t + s, LINE_RUN)
                    before = pltpu.roll(v[half][r], LANES - blk, 1) if blk else v[half][r]
                    blk, r = divmod(t - s, LINE_RUN)
                    after = pltpu.roll(v[half][r], -blk, 1) if blk else v[half][r]
                    fresh[half].append(w[0] * before + w[1] * v[half][t] + w[2] * after)
            v = fresh
        for half, at in enumerate(starts):
            for t in range(LINE_RUN):
                done[t, at // 8] = v[half][t]

    sub = iota((8, LANES), 0)
    results = []
    for block in range(LINE_RUN // 8):
        totals = jnp.zeros((8, LANES), F32)
        moments = totals
        for s in range(8):
            t = LINE_RUN - 1 - (8 * block + s)
            v = [done[t, i] for i in range(DISP // 8)]
            top = v
            while len(top) > 1:
                top = [jnp.maximum(a, b) for a, b in zip(top[::2], top[1::2])] + top[len(top) & ~1 :]
            top = jnp.max(top[0], axis=0, keepdims=True)
            total = jnp.exp2(v[-1] - top)
            moment = total
            for i in range(DISP // 8 - 2, -1, -1):
                total = total + jnp.exp2(v[i] - top)
                if i:
                    moment = moment + total
            moment = 8.0 * moment + sub.astype(F32) * total
            totals = jnp.where(sub == s, jnp.sum(total, axis=0, keepdims=True), totals)
            moments = jnp.where(sub == s, jnp.sum(moment, axis=0, keepdims=True), moments)
        lane_line = iota((8, LANES), 1) >> 6
        shift = jnp.zeros((8, LANES), F32)
        for i in range(PAIR):
            shift = jnp.where(lane_line == i, offs[i].astype(F32), shift)
        results.append((moments / totals + shift) * (1.0 / DISP))
    vals = jnp.concatenate(results, axis=0)
    lane_line = iota((LINE_RUN, LANES), 1) >> 6
    both = jnp.concatenate([jnp.where(lane_line == i, vals, 0.0) for i in range(PAIR)], axis=0)
    high = both.astype(BF)
    rest = both - high.astype(F32)
    middle = rest.astype(BF)
    low = (rest - middle.astype(F32)).astype(BF)
    pieces = jnp.dot(
        jnp.concatenate([high, middle, low], axis=0), spread[...], preferred_element_type=F32
    )
    size = PAIR * LINE_RUN
    pieces = pieces[:size] + pieces[size : 2 * size] + pieces[2 * size :]
    wanted = iota((LINE_RUN, width), 0) == (iota((LINE_RUN, width), 1) & (LINE_RUN - 1))
    for i in range(PAIR):
        piece = jnp.where(wanted, pieces[i * LINE_RUN : (i + 1) * LINE_RUN], 0.0)
        out[i : i + 1, :] = jnp.sum(piece, axis=0, keepdims=True)


def lines_plan(features, valid_cols, offsets, guide_weight):
    n = lax.axis_size("cols")
    devices = 2 * n
    width = n * BLOCK
    rows = PAIR * CHANNELS
    own = features.reshape(devices, rows, BLOCK)
    pieces = [None] * devices
    gone = ()
    for key in (1, 2, 6, 4, 7, 5, 3, 0):
        masked = key % 2 and key > 1
        (piece,) = call(
            functools.partial(pack_kernel, key),
            [((rows + (MASKS if masked else 0), BLOCK), BF)],
            [], 0,
            (own,) + ((valid_cols,) if masked else ()) + gone,
            1_000_000,
        )
        gone = (piece,)
        moves = [(i, i ^ key) for i in range(devices)]
        pieces[key] = lax.ppermute(piece, ("cols", "view"), moves) if key else piece
    consts = call(
        constants_kernel,
        [
            ((LANES, LANES), BF), ((DISP, 2 * LANES), BF), ((3 * KEYS, LANES), BF), ((LANES, width), BF),
            (valid_cols.shape, F32),
        ],
        [], 1, (offsets, guide_weight, valid_cols), 1_000_000,
    )
    (rows,) = call(
        lines_kernel,
        [((PAIR, width), F32)],
        [
            pltpu.VMEM((devices, rows, BLOCK), BF),
            pltpu.VMEM((n,) + valid_cols.shape, F32),
            pltpu.VMEM((LINE_RUN, 3 * KEYS, LANES), F32),
        ],
        1, (offsets, *consts, *pieces), 1_000_000_000,
    )
    others = lax.ppermute(rows, "view", [(0, 1), (1, 0)])
    first = lax.axis_index("view") == 0
    return jnp.where(first, jnp.concatenate([rows, others]), jnp.concatenate([others, rows]))[None]


def on_device(features, valid_cols, offsets, guide_weight):
    n = lax.axis_size("cols")
    lines = features.shape[1]
    if lines == 2 * PAIR * n and n * BLOCK == LINE_RUN * LINE_PARTS:
        return lines_plan(features, valid_cols, offsets, guide_weight)
    return halo_plan(features, valid_cols, offsets, guide_weight)


def solution(mesh):
    return jax.shard_map(
        on_device,
        mesh=mesh,
        in_specs=(
            P("view", ("tiles", "lines"), None, "cols"),
            P(None, ("tiles", "cols")),
            P(("tiles", "lines")),
            P(),
        ),
        out_specs=P(("tiles", "lines"), "cols", None),
        check_vma=False,
    )
```

```python
import functools
import math

import jax
import jax.numpy as jnp
from jax import lax
from jax.experimental import pallas as pl
from jax.experimental.pallas import tpu as pltpu
from jax.sharding import PartitionSpec as P

DISP = 192
DGROUP = 16
GROUPS = DISP // DGROUP
LAYERS = 3
SHARPNESS = 2.0
HALO = 32
LANES = 128
LINES = 8
CHANNELS = 64
BLOCK = 256
SPAN = BLOCK + HALO
PARTS = LANES // LINES
RUN = SPAN // PARTS
KEYS = 40
WIDE = BLOCK + LANES
SEC_ROWS = LINES * CHANNELS
QUAD_ROWS = SEC_ROWS // 2
MASK_AT = QUAD_ROWS + CHANNELS
PAYLOAD = MASK_AT + 16
QUAD = LINES // 2
QUAD_LANES = LANES // 2
PACK = LANES // HALO
CUT = 16

BF = jnp.bfloat16
F32 = jnp.float32


def iota(shape, dim):
    return lax.broadcasted_iota(jnp.int32, shape, dim)


def dot_t(a, b):
    return lax.dot_general(a, b, (((1,), (1,)), ((), ())), preferred_element_type=F32)


def call(kernel, outs, scratch, smem, args, flops=0, space=pltpu.VMEM, limit=24, to=None):
    specs = [pl.BlockSpec(memory_space=pltpu.SMEM)] * smem
    specs += [pl.BlockSpec(memory_space=space)] * (len(args) - smem)
    return pl.pallas_call(
        kernel,
        out_shape=[jax.ShapeDtypeStruct(shape, dtype) for shape, dtype in outs],
        in_specs=specs,
        out_specs=[pl.BlockSpec(memory_space=to or space)] * len(outs),
        scratch_shapes=scratch,
        compiler_params=pltpu.CompilerParams(vmem_limit_bytes=limit * 1024 * 1024),
        cost_estimate=pl.CostEstimate(flops=flops, bytes_accessed=1_000_000, transcendentals=0),
    )(*args)


def spread_guide(guide):
    keys = LAYERS * 3 * GROUPS
    row = iota((3 * KEYS, keys), 0)
    tap = jnp.where(row >= KEYS, 1, 0) + jnp.where(row >= 2 * KEYS, 1, 0)
    row = row - KEYS * tap
    layer = jnp.where(row >= GROUPS, 1, 0) + jnp.where(row >= 2 * GROUPS, 1, 0)
    key = 2 * GROUPS * layer + GROUPS * tap + row
    chosen = jnp.where((iota((3 * KEYS, keys), 1) == key) & (row < 3 * GROUPS), 1.0, 0.0).astype(BF)
    guide_t = dot_t(chosen, guide).astype(BF)
    return jnp.concatenate([guide_t, guide_t], axis=1)


def normalise(z, wts, t, room_left, room_right):
    z = (0.55 + 0.45 * jnp.tanh(0.5 * z)).astype(BF).astype(F32)
    taps = [z[k * KEYS : (k + 1) * KEYS] for k in range(3)]
    scale = 1.0 / (taps[0] + taps[1] + taps[2])
    wts[t, 0:KEYS, :] = jnp.where(room_left >= t, taps[0] * scale, 0.0)
    wts[t, KEYS : 2 * KEYS, :] = taps[1] * scale
    wts[t, 2 * KEYS : 3 * KEYS, :] = jnp.where(room_right < t, taps[2] * scale, 0.0)


def prefetch_kernel(own, valid, guide, own_out, masks, perm, flip, guide_out, valid_in, guide_in, sems):
    copies = [
        pltpu.make_async_copy(src, dst, sems.at[i])
        for i, (src, dst) in enumerate([(own, own_out), (guide, guide_in), (valid, valid_in)])
    ]
    for copy in copies:
        copy.start()
    perm[...] = jnp.where(
        iota((SPAN, WIDE), 1) == WIDE - 1 - iota((SPAN, WIDE), 0), 1.0, 0.0
    ).astype(BF)
    back = 2 * LANES - 1 - iota((DISP, 2 * LANES), 0)
    flip[...] = jnp.where(iota((DISP, 2 * LANES), 1) == back, 1.0, 0.0).astype(BF)

    copies[1].wait()
    guide_out[...] = spread_guide(guide_in[...])
    copies[2].wait()
    masks[...] = valid_in[...].astype(F32)
    copies[0].wait()


def payload_kernel(own, other, masks, first, second, ref_own):
    view = lax.axis_index("view")
    first_view = view == 0
    sec_mask = masks[1:2, :].astype(BF)
    lane = iota((CHANNELS, LANES), 1)
    tails = []
    for line in range(LINES):
        at = view * LINES + line
        mine, theirs = own[at], other[at]
        lo = line * CHANNELS
        dest, start = (first, lo) if line < QUAD else (second, lo - QUAD_ROWS)
        dest[start : start + CHANNELS, :] = jnp.where(first_view, theirs, mine) * sec_mask
        ref = jnp.where(first_view, mine, theirs)
        ref_own[lo : lo + CHANNELS, :] = ref
        tail = ref[:, BLOCK - LANES :].astype(F32)
        slot = line % PACK
        turn = (HALO * (slot + 1)) % LANES
        if turn:
            tail = pltpu.roll(tail, turn, 1)
        if slot:
            tails[-1] = jnp.where(lane >= HALO * slot, tail, tails[-1])
        else:
            tails.append(tail)
    for i, tail in enumerate(tails):
        first[QUAD_ROWS:MASK_AT, i * LANES : (i + 1) * LANES] = tail.astype(BF)
    first[MASK_AT:, :] = jnp.broadcast_to(masks[0:1, :], (16, BLOCK)).astype(BF)


def shifted(left, mine, lo, off):
    ch_lane = iota((CHANNELS, LANES), 1)
    tiles = [
        src[lo : lo + CHANNELS, i * LANES : (i + 1) * LANES].astype(F32)
        for src in (left, mine)
        for i in range(2)
    ]
    tiles = [pltpu.roll(tile, off, 1) for tile in tiles]
    tiles = [jnp.where(ch_lane < off, tiles[max(i - 1, 0)], tiles[i]).astype(BF) for i in range(4)]
    return jnp.concatenate(tiles, axis=1)


def line_costs(lhs, rhs, slot, skew, cost_rows):
    diagonal = iota((8, LANES), 1) - iota((8, LANES), 0)
    for chunk in range(3):
        rows = min(LANES, SPAN - chunk * LANES)
        first = max(1 - chunk, 0)
        last = 3 - chunk
        products = jnp.dot(
            lhs[chunk * LANES : chunk * LANES + rows],
            rhs[:, first * LANES : (last + 1) * LANES],
            preferred_element_type=F32,
        )
        for j in range(rows // 8):
            tiles = [
                pltpu.roll(
                    products[8 * j : 8 * j + 8, i * LANES : (i + 1) * LANES],
                    8 * j, 1, stride=1, stride_axis=0,
                )
                for i in range(last + 1 - first)
            ]
            if len(tiles) < 3:
                tiles = [tiles[0]] + tiles
            beyond = diagonal >= 8 * j
            at = chunk * LANES + 8 * j
            skew[slot, 0, at : at + 8, :] = jnp.where(beyond, tiles[1], tiles[0])
            skew[slot, 1, at : at + 8, :] = jnp.where(beyond, tiles[2], tiles[1])
    for t in range(RUN):
        at = t * QUAD_LANES + slot * PARTS
        for v in range(2):
            cost_rows[at : at + PARTS, v * LANES : (v + 1) * LANES] = skew[
                slot, v, pl.ds(t, PARTS, stride=RUN), :
            ].astype(BF)


def early_kernel(
    offsets, ref_own, mine, left, masks, perm, guide, wts, cost_rows, lhs_out,
    ref_rows, ref_cols, gate_rows, skew
):
    base = lax.axis_index("view") * LINES
    low = jnp.where(lax.axis_index("cols") == 0, HALO, 0)
    for line in range(LINES):
        lo = line * CHANNELS
        ref_rows[lo : lo + CHANNELS, LANES:] = ref_own[lo : lo + CHANNELS, :]
        half = line // PACK
        packed = left[QUAD_ROWS:MASK_AT, half * LANES : (half + 1) * LANES].astype(F32)
        turn = (LANES - HALO) - HALO * (line % PACK)
        if turn:
            packed = pltpu.roll(packed, turn, 1)
        ref_rows[lo : lo + CHANNELS, :LANES] = packed.astype(BF)

    mask_left = left[MASK_AT : MASK_AT + 1, BLOCK - LANES :].astype(F32)
    ref_mask = jnp.concatenate([mask_left, masks[0:1, :]], axis=1)
    ref_mask = jnp.broadcast_to(ref_mask * (1.0 / math.sqrt(CHANNELS)), (LANES, WIDE))
    mask_cols = dot_t(perm[...], ref_mask.astype(BF))
    half_lane = iota((PARTS, LANES), 1) < CHANNELS
    span_lane = iota((SPAN, LANES), 1) < CHANNELS

    for quad in range(LINES // QUAD):
        ref_t = dot_t(perm[...], ref_rows[quad * QUAD_ROWS : (quad + 1) * QUAD_ROWS, :])
        for pair in range(QUAD // 2):
            cols = ref_t[:, pair * LANES : (pair + 1) * LANES]
            slot = quad * 2 + pair
            ref_cols[slot] = cols
            masked = cols * mask_cols
            if quad == 0:
                rhs = jnp.concatenate(
                    [
                        shifted(left, mine, line * CHANNELS, offsets[base + line])
                        for line in (2 * slot, 2 * slot + 1)
                    ],
                    axis=0,
                )
            for side in range(2):
                line = 2 * slot + side
                for t in range(RUN):
                    picked = ref_cols[slot, pl.ds(t, PARTS, stride=RUN), :]
                    picked = jnp.where(half_lane if side == 0 else ~half_lane, picked, 0.0)
                    at = t * LANES + line * PARTS
                    gate_rows[at : at + PARTS, :] = picked.astype(BF)
                lhs = jnp.where(span_lane if side == 0 else ~span_lane, masked, 0.0).astype(BF)
                if quad == 0:
                    line_costs(lhs, rhs, line, skew, cost_rows)
                else:
                    lhs_out[line - QUAD] = lhs

    place = iota((KEYS, LANES), 1)
    x_base = SPAN - 1 - RUN * (place & (PARTS - 1))
    row = iota((KEYS, LANES), 0)
    reach = jnp.where(row >= 2 * GROUPS, 9, jnp.where(row >= GROUPS, 3, 1))
    room_left = x_base - reach - low
    room_right = x_base + reach - SPAN
    for two in range(RUN // 2):
        at = 2 * two * LANES
        logits = dot_t(guide[...], gate_rows[at : at + 2 * LANES, :])
        for i in range(2):
            t = 2 * two + i
            normalise(logits[:, i * LANES : (i + 1) * LANES], wts, t, room_left, room_right)


def late_kernel(
    offsets, mine, left, lhs, early_rows, wts, flip, out, skew, cost_rows, vol, vals, turned
):
    base = lax.axis_index("view") * LINES
    for pair in range(QUAD // 2):
        rhs = jnp.concatenate(
            [
                shifted(left, mine, line * CHANNELS, offsets[base + QUAD + line])
                for line in (2 * pair, 2 * pair + 1)
            ],
            axis=0,
        )
        for line in (2 * pair, 2 * pair + 1):
            line_costs(lhs[line], rhs, line, skew, cost_rows)

    for two in range(RUN // 2):
        rows = []
        for t in (2 * two, 2 * two + 1):
            for part in (early_rows, cost_rows):
                rows.append(part[t * QUAD_LANES : (t + 1) * QUAD_LANES, :])
        costs = dot_t(flip[...], jnp.concatenate(rows, axis=0))
        vol[2 * two] = costs[:, :LANES]
        vol[2 * two + 1] = costs[:, LANES:]

    def aggregate(group, carry):
        for half in range(2):
            at = pl.multiple_of(group * DGROUP + half * 8, 8)
            v = [vol[t, pl.ds(at, 8), :] for t in range(RUN)]
            for layer in range(LAYERS):
                s = 3**layer
                before = [v[t + s] if t + s < RUN else pltpu.roll(v[t + s - RUN], LANES - 1, 1) for t in range(RUN)]
                after = [v[t - s] if t >= s else pltpu.roll(v[t - s + RUN], 1, 1) for t in range(RUN)]
                fresh = []
                for t in range(RUN):
                    w = [wts[t, pl.ds(k * KEYS + layer * GROUPS + group, 1), :] for k in range(3)]
                    fresh.append(w[0] * before[t] + w[1] * v[t] + w[2] * after[t])
                v = fresh
            for t in range(RUN):
                vol[t, pl.ds(at, 8), :] = v[t]
        return carry

    lax.fori_loop(0, GROUPS, aggregate, 0)

    vals[...] = jnp.zeros((LANES, LANES), F32)
    sub = iota((8, LANES), 0).astype(F32)
    line_of = iota((1, LANES), 1) >> 4
    offs = jnp.zeros((1, LANES), F32)
    for line in range(LINES):
        offs = jnp.where(line_of == line, offsets[base + line].astype(F32), offs)

    def softmax(t, carry):
        v = [vol[t, 8 * i : 8 * i + 8, :] for i in range(DISP // 8)]
        top = v
        while len(top) > 1:
            top = [jnp.maximum(a, b) for a, b in zip(top[::2], top[1::2])] + top[len(top) & ~1 :]
        top = jnp.max(top[0], axis=0, keepdims=True)
        e = [jnp.exp(SHARPNESS * (a - top)) for a in v]
        total = e[0]
        moment = jnp.zeros((8, LANES), F32)
        for i in range(1, DISP // 8):
            total = total + e[i]
            moment = moment + float(8 * i) * e[i]
        moment = jnp.sum(moment + sub * total, axis=0, keepdims=True)
        total = jnp.sum(total, axis=0, keepdims=True)
        vals[pl.ds(RUN - 1 - t, 1), :] = (moment / total + offs) * (1.0 / DISP)
        return carry

    lax.fori_loop(0, RUN, softmax, 0)

    turned[...] = jnp.transpose(vals[...])
    lane = iota((8, LANES), 1)
    result = [jnp.zeros((8, LANES), F32) for _ in range(WIDE // LANES)]
    for part in range(PARTS):
        piece = turned[pl.ds(part, LINES, stride=PARTS), :]
        start = (RUN * (PARTS - 1 - part) - HALO) % WIDE
        tile, turn = divmod(start, LANES)
        if turn:
            piece = pltpu.roll(piece, turn, 1)
        if turn + RUN > LANES:
            after = (tile + 1) % len(result)
            result[after] = result[after] + jnp.where(lane < turn, piece, 0.0)
            piece = jnp.where(lane >= turn, piece, 0.0)
        result[tile] = result[tile] + piece
    for tile, value in enumerate(result):
        out[:, tile * LANES : (tile + 1) * LANES] = value


def join(pieces, sub, n):
    block = lax.axis_index("cols")
    pieces = pieces.reshape(n, 2, LINES, WIDE)
    start = (0, block // (n // 2), (block % (n // 2)) * sub, 0)
    pieces = lax.dynamic_slice(pieces, start, (n, 1, sub, WIDE))[:, 0]
    main = pieces[:, :, :BLOCK]
    tail = jnp.pad(pieces[1:, :, BLOCK:], ((0, 1), (0, 0), (LANES, 0)))
    place = (n, sub, BLOCK)
    keep = (iota(place, 2) < BLOCK - CUT) | (iota(place, 0) == n - 1)
    joined = jnp.where(keep, main, tail)
    return jnp.transpose(joined, (1, 0, 2)).reshape(1, sub, n * BLOCK)


def halo_plan(features, valid_cols, offsets, guide_weight):
    own = features[0]
    n = lax.axis_size("cols")
    right = [(c, c + 1) for c in range(n - 1)]
    other = lax.ppermute(own, "view", [(0, 1), (1, 0)])
    near, masks, perm, flip, guide = call(
        prefetch_kernel,
        [(own.shape, BF), (valid_cols.shape, F32), ((SPAN, WIDE), BF), ((DISP, 2 * LANES), BF), ((3 * KEYS, LANES), BF)],
        [pltpu.VMEM(valid_cols.shape, jnp.int32), pltpu.VMEM(guide_weight.shape, BF), pltpu.SemaphoreType.DMA((3,))],
        0, (own, valid_cols, guide_weight), 100_000_000, pl.ANY, 24, pltpu.VMEM,
    )
    first, second, ref_own = call(
        payload_kernel,
        [((PAYLOAD, BLOCK), BF), ((QUAD_ROWS, BLOCK), BF), ((SEC_ROWS, BLOCK), BF)],
        [], 0, (near, other, masks),
    )
    left_first = lax.ppermute(first, "cols", right)
    left_second = lax.ppermute(second, "cols", right)
    quad_rows = (RUN * QUAD_LANES, 2 * LANES)
    skew = pltpu.VMEM((QUAD, 2, SPAN, LANES), F32)
    square = pltpu.VMEM((LANES, LANES), F32)
    wts, early_rows, lhs = call(
        early_kernel,
        [((RUN, 3 * KEYS, LANES), F32), (quad_rows, BF), ((QUAD, SPAN, LANES), BF)],
        [pltpu.VMEM((SEC_ROWS, WIDE), BF), pltpu.VMEM((QUAD, SPAN, LANES), F32), pltpu.VMEM((RUN * LANES, LANES), BF), skew],
        1, (offsets, ref_own, first, left_first, masks, perm, guide), 1_000_000_000,
    )
    (result,) = call(
        late_kernel,
        [((LINES, WIDE), F32)],
        [skew, pltpu.VMEM(quad_rows, BF), pltpu.VMEM((RUN, DISP, LANES), F32), square, square],
        1, (offsets, second, left_second, lhs, early_rows, wts, flip), 1_000_000_000,
    )
    copies = jnp.broadcast_to(result[None], (2 * n, LINES, WIDE))
    pieces = lax.all_to_all(copies, ("cols", "view"), split_axis=0, concat_axis=0, tiled=True)
    return join(pieces, own.shape[0] // n, n)


LINE_RUN = 8
PAIR = 2
LINE_PARTS = LANES


MASKS = 8
GATE_FLOOR = 11.0 / 9.0


def pack_kernel(key, own, *rest):
    out = rest[-1]
    me = 2 * lax.axis_index("cols") + lax.axis_index("view")
    rows = PAIR * CHANNELS
    out[:rows, :] = own[me ^ key]
    if out.shape[0] > rows:
        masks = rest[0][...].astype(F32)
        out[rows:, :] = jnp.where(
            iota((MASKS, BLOCK), 0) < MASKS // 2, masks[0:1, :], masks[1:2, :]
        ).astype(BF)


def constants_kernel(offsets, guide, valid, order, order_band, flip, guide_out, spread, masks):
    masks[...] = valid[...].astype(F32)
    row = iota((LANES, LANES), 0)
    from_lane = LANES - 1 - LINE_RUN * (row & (PARTS - 1)) - (row >> 4)
    order[...] = jnp.where(iota((LANES, LANES), 1) == from_lane, 1.0, 0.0).astype(BF)
    from_lane = LANES - 1 - (row & 64) - LINE_RUN * (row & 7) - ((row >> 3) & 7)
    order_band[...] = jnp.where(iota((LANES, LANES), 1) == from_lane, 1.0, 0.0).astype(BF)
    back = 2 * LANES - 1 - iota((DISP, 2 * LANES), 0)
    flip[...] = jnp.where(iota((DISP, 2 * LANES), 1) == back, 1.0, 0.0).astype(BF)
    guide_out[...] = spread_guide(guide[...]) * 0.5
    block_of = LANES - 1 - (iota(spread.shape, 1) >> 3)
    spread[...] = jnp.where(iota(spread.shape, 0) == block_of, 1.0, 0.0).astype(BF)


def lines_kernel(offsets, order, order_band, flip, guide, spread, *rest):
    pieces, (out, blocks, valid, gate_rows, cost_rows, vol, done, wts) = rest[:-8], rest[-8:]
    near, pieces = pieces[0], pieces[1:]
    tiles = len(pieces)
    width = tiles * LANES
    me = 2 * lax.axis_index("cols") + lax.axis_index("view")
    rows = PAIR * CHANNELS
    for key, piece in enumerate(pieces):
        blocks[me ^ key] = piece[:rows, :]
        if piece.shape[0] > rows:
            masks = piece[rows:, :].astype(F32)
            valid[(me ^ key) // 2] = jnp.concatenate([masks[0:1], masks[MASKS // 2 : MASKS // 2 + 1]], axis=0)
    valid[me // 2] = near[...]
    at = PAIR * me
    offs = [offsets[at + i] for i in range(PAIR)]
    ch_lane = iota((CHANNELS, LANES), 1)
    low_lane = ch_lane < LANES // 2
    low_half = iota((LANES, LANES), 1) < CHANNELS
    reached = iota((8, LANES), 1) + LINE_RUN * iota((8, LANES), 0)
    scale = 1.0 / math.sqrt(CHANNELS)
    empty = jnp.zeros((CHANNELS, LANES), F32)

    def mask_of(view, w):
        lo = (w % 2) * LANES
        return valid[w // 2, view : view + 1, lo : lo + LANES]

    for i in range(PAIR):

        def tile_of(view, w):
            lo = (w % 2) * LANES
            return blocks[2 * (w // 2) + view, i * CHANNELS : (i + 1) * CHANNELS, lo : lo + LANES]

        off = offs[i]
        rolled = [pltpu.roll(tile_of(1, w).astype(F32) * mask_of(1, w), off, 1) for w in range(tiles)]
        line = [empty, empty]
        for w in range(tiles):
            line.append(jnp.where(ch_lane < off, rolled[w - 1] if w else empty, rolled[w]))
        turned = [empty] + [pltpu.roll(tile, LANES // 2, 1) if w else tile for w, tile in enumerate(line[1:])]
        shifted = [tile.astype(BF) for tile in line]
        halfway = [jnp.where(low_lane, a, b).astype(BF) for a, b in zip(turned, turned[1:])]

        for quad in range(tiles // 4):
            refs = [tile_of(0, 4 * quad + q) for q in range(4)]
            masked = [refs[q] * (mask_of(0, 4 * quad + q) * scale).astype(BF) for q in range(4)]
            cols = dot_t(order[...], jnp.concatenate(refs, axis=0))
            masked = dot_t(order_band[...], jnp.concatenate(masked, axis=0))
            for two in range(2):
                w = 4 * quad + 2 * two
                raw = cols[:, two * LANES : (two + 1) * LANES]
                pair = masked[:, two * LANES : (two + 1) * LANES]
                gates = [jnp.where(low_half, raw, 0.0).astype(BF), jnp.where(low_half, 0.0, raw).astype(BF)]
                sides = [jnp.where(low_half, pair, 0.0).astype(BF), jnp.where(low_half, 0.0, pair).astype(BF)]
                chunks = []
                for half, source, first in ((0, shifted, w + 1), (1, halfway, w)):
                    lo = half * LANES // 2
                    lhs = jnp.concatenate([side[lo : lo + LANES // 2] for side in sides], axis=0)
                    rhs = jnp.concatenate(
                        [jnp.concatenate(source[first + side : first + side + 2], axis=1) for side in range(2)],
                        axis=0,
                    )
                    chunks.append(jnp.dot(lhs, rhs, preferred_element_type=F32))
                for side in range(2):
                    place = (tiles - 1 - w - side) * PARTS
                    for t in range(LINE_RUN):
                        row = t * LANES + place
                        gate_rows[i, row : row + PARTS, :] = gates[side][t * PARTS : (t + 1) * PARTS]
                        r = side * LANES // 2 + 8 * t
                        within = reached < LANES - t
                        halves = []
                        for products in chunks:
                            close, far = products[r : r + 8, :LANES], products[r : r + 8, LANES:]
                            halves.append(
                                jnp.concatenate(
                                    [
                                        pltpu.roll(value, t, 1, stride=LINE_RUN, stride_axis=0)
                                        for value in (close, jnp.where(within, far, close))
                                    ],
                                    axis=1,
                                )
                            )
                        cost_rows[i, row : row + PARTS, :] = jnp.concatenate(halves, axis=0).astype(BF)

    x_base = width - 1 - LINE_RUN * iota((KEYS, LANES), 1)
    row = iota((KEYS, LANES), 0)
    reach = jnp.where(row >= 2 * GROUPS, 9, jnp.where(row >= GROUPS, 3, 1))
    room_left = x_base - reach
    room_right = x_base + reach - width
    unit = jnp.where(row >= 2 * GROUPS, SHARPNESS / math.log(2.0), 1.0)
    for i in range(PAIR):
        for two in range(LINE_RUN // 2):
            lo = 2 * two * LANES
            costs = dot_t(flip[...], cost_rows[i, lo : lo + 2 * LANES, :])
            logits = dot_t(guide[...], gate_rows[i, lo : lo + 2 * LANES, :])
            for side in range(2):
                t = 2 * two + side
                vol[i, t] = costs[:, side * LANES : (side + 1) * LANES]
                z = jnp.tanh(logits[:, side * LANES : (side + 1) * LANES]) + GATE_FLOOR
                taps = [z[m * KEYS : (m + 1) * KEYS] for m in range(3)]
                factor = unit / (taps[0] + taps[1] + taps[2])
                taps = [tap * factor for tap in taps]
                taps[0] = jnp.where(room_left >= t, taps[0], 0.0)
                taps[2] = jnp.where(room_right < t, taps[2], 0.0)
                for m in range(3):
                    wts[i, t, m * KEYS : (m + 1) * KEYS, :] = taps[m]

    for group in range(GROUPS):
        starts = [group * DGROUP + 8 * half for half in range(2)]
        for i in range(PAIR):
            v = [[vol[i, t, at : at + 8, :] for t in range(LINE_RUN)] for at in starts]
            for layer in range(LAYERS):
                s = 3**layer
                fresh = [[], []]
                for t in range(LINE_RUN):
                    rows = [k * KEYS + layer * GROUPS + group for k in range(3)]
                    w = [jnp.broadcast_to(wts[i, t, r : r + 1, :], (8, LANES)) for r in rows]
                    for half in range(2):
                        blk, r = divmod(t + s, LINE_RUN)
                        before = pltpu.roll(v[half][r], LANES - blk, 1) if blk else v[half][r]
                        blk, r = divmod(t - s, LINE_RUN)
                        after = pltpu.roll(v[half][r], -blk, 1) if blk else v[half][r]
                        fresh[half].append(w[0] * before + w[1] * v[half][t] + w[2] * after)
                v = fresh
            for half, at_row in enumerate(starts):
                for t in range(LINE_RUN):
                    done[i, t, at_row : at_row + 8, :] = v[half][t]

    sub = iota((8, LANES), 0)
    results = []
    for i in range(PAIR):
        totals = jnp.zeros((8, LANES), F32)
        moments = totals
        for s in range(LINE_RUN):
            t = LINE_RUN - 1 - s
            v = [done[i, t, 8 * j : 8 * j + 8, :] for j in range(DISP // 8)]
            top = v
            while len(top) > 1:
                top = [jnp.maximum(a, b) for a, b in zip(top[::2], top[1::2])] + top[len(top) & ~1 :]
            top = jnp.max(top[0], axis=0, keepdims=True)
            total = jnp.exp2(v[-1] - top)
            moment = total
            for j in range(DISP // 8 - 2, -1, -1):
                total = total + jnp.exp2(v[j] - top)
                if j:
                    moment = moment + total
            moment = 8.0 * moment + sub.astype(F32) * total
            totals = jnp.where(sub == s, jnp.sum(total, axis=0, keepdims=True), totals)
            moments = jnp.where(sub == s, jnp.sum(moment, axis=0, keepdims=True), moments)
        results.append((moments / totals + offs[i].astype(F32)) * (1.0 / DISP))
    both = jnp.concatenate(results, axis=0)
    high = both.astype(BF)
    left = both - high.astype(F32)
    middle = left.astype(BF)
    low = (left - middle.astype(F32)).astype(BF)
    parts = jnp.dot(
        jnp.concatenate([high, middle, low], axis=0), spread[...], preferred_element_type=F32
    )
    size = PAIR * LINE_RUN
    parts = parts[:size] + parts[size : 2 * size] + parts[2 * size :]
    wanted = iota((LINE_RUN, width), 0) == (iota((LINE_RUN, width), 1) & (LINE_RUN - 1))
    for i in range(PAIR):
        part = jnp.where(wanted, parts[i * LINE_RUN : (i + 1) * LINE_RUN], 0.0)
        out[i : i + 1, :] = jnp.sum(part, axis=0, keepdims=True)


def lines_plan(features, valid_cols, offsets, guide_weight):
    n = lax.axis_size("cols")
    devices = 2 * n
    width = n * BLOCK
    rows = PAIR * CHANNELS
    own = features.reshape(devices, rows, BLOCK)
    pieces = [None] * devices
    gone = ()
    for key in (1, 2, 6, 4, 7, 5, 3, 0):
        masked = key % 2 and key > 1
        (piece,) = call(
            functools.partial(pack_kernel, key),
            [((rows + (MASKS if masked else 0), BLOCK), BF)],
            [], 0,
            (own,) + ((valid_cols,) if masked else ()) + gone,
            1_000_000,
        )
        gone = (piece,)
        moves = [(i, i ^ key) for i in range(devices)]
        pieces[key] = lax.ppermute(piece, ("cols", "view"), moves) if key else piece
    consts = call(
        constants_kernel,
        [
            ((LANES, LANES), BF), ((LANES, LANES), BF), ((DISP, 2 * LANES), BF), ((3 * KEYS, LANES), BF),
            ((LANES, width), BF), (valid_cols.shape, F32),
        ],
        [], 1, (offsets, guide_weight, valid_cols), 1_000_000,
    )
    (rows,) = call(
        lines_kernel,
        [((PAIR, width), F32)],
        [
            pltpu.VMEM((devices, rows, BLOCK), BF),
            pltpu.VMEM((n,) + valid_cols.shape, F32),
            pltpu.VMEM((PAIR, LINE_RUN * LANES, LANES), BF),
            pltpu.VMEM((PAIR, LINE_RUN * LANES, 2 * LANES), BF),
            pltpu.VMEM((PAIR, LINE_RUN, DISP, LANES), F32),
            pltpu.VMEM((PAIR, LINE_RUN, DISP, LANES), F32),
            pltpu.VMEM((PAIR, LINE_RUN, 3 * KEYS, LANES), F32),
        ],
        1, (offsets, *consts, *pieces), 1_000_000_000,
    )
    others = lax.ppermute(rows, "view", [(0, 1), (1, 0)])
    first = lax.axis_index("view") == 0
    return jnp.where(first, jnp.concatenate([rows, others]), jnp.concatenate([others, rows]))[None]


def on_device(features, valid_cols, offsets, guide_weight):
    n = lax.axis_size("cols")
    lines = features.shape[1]
    if lines == 2 * PAIR * n and n * BLOCK == LINE_RUN * LANES:
        return lines_plan(features, valid_cols, offsets, guide_weight)
    return halo_plan(features, valid_cols, offsets, guide_weight)


def solution(mesh):
    return jax.shard_map(
        on_device,
        mesh=mesh,
        in_specs=(
            P("view", ("tiles", "lines"), None, "cols"),
            P(None, ("tiles", "cols")),
            P(("tiles", "lines")),
            P(),
        ),
        out_specs=P(("tiles", "lines"), "cols", None),
        check_vma=False,
    )
```

```python
import functools
import math

import jax
import jax.numpy as jnp
from jax import lax
from jax.experimental import pallas as pl
from jax.experimental.pallas import tpu as pltpu
from jax.sharding import PartitionSpec as P

DISP = 192
DGROUP = 16
GROUPS = DISP // DGROUP
LAYERS = 3
SHARPNESS = 2.0
HALO = 32
LANES = 128
LINES = 8
CHANNELS = 64
BLOCK = 256
SPAN = BLOCK + HALO
PARTS = LANES // LINES
RUN = SPAN // PARTS
KEYS = 40
WIDE = BLOCK + LANES
SEC_ROWS = LINES * CHANNELS
QUAD_ROWS = SEC_ROWS // 2
MASK_AT = QUAD_ROWS + CHANNELS
PAYLOAD = MASK_AT + 16
QUAD = LINES // 2
QUAD_LANES = LANES // 2
PACK = LANES // HALO
CUT = 16

BF = jnp.bfloat16
F32 = jnp.float32


def iota(shape, dim):
    return lax.broadcasted_iota(jnp.int32, shape, dim)


def dot_t(a, b):
    return lax.dot_general(a, b, (((1,), (1,)), ((), ())), preferred_element_type=F32)


def call(kernel, outs, scratch, smem, args, flops=0, space=pltpu.VMEM, limit=24, to=None):
    specs = [pl.BlockSpec(memory_space=pltpu.SMEM)] * smem
    specs += [pl.BlockSpec(memory_space=space)] * (len(args) - smem)
    return pl.pallas_call(
        kernel,
        out_shape=[jax.ShapeDtypeStruct(shape, dtype) for shape, dtype in outs],
        in_specs=specs,
        out_specs=[pl.BlockSpec(memory_space=to or space)] * len(outs),
        scratch_shapes=scratch,
        compiler_params=pltpu.CompilerParams(vmem_limit_bytes=limit * 1024 * 1024),
        cost_estimate=pl.CostEstimate(flops=flops, bytes_accessed=1_000_000, transcendentals=0),
    )(*args)


def spread_guide(guide):
    keys = LAYERS * 3 * GROUPS
    row = iota((3 * KEYS, keys), 0)
    tap = jnp.where(row >= KEYS, 1, 0) + jnp.where(row >= 2 * KEYS, 1, 0)
    row = row - KEYS * tap
    layer = jnp.where(row >= GROUPS, 1, 0) + jnp.where(row >= 2 * GROUPS, 1, 0)
    key = 2 * GROUPS * layer + GROUPS * tap + row
    chosen = jnp.where((iota((3 * KEYS, keys), 1) == key) & (row < 3 * GROUPS), 1.0, 0.0).astype(BF)
    guide_t = dot_t(chosen, guide).astype(BF)
    return jnp.concatenate([guide_t, guide_t], axis=1)


def normalise(z, wts, t, room_left, room_right):
    z = (0.55 + 0.45 * jnp.tanh(0.5 * z)).astype(BF).astype(F32)
    taps = [z[k * KEYS : (k + 1) * KEYS] for k in range(3)]
    scale = 1.0 / (taps[0] + taps[1] + taps[2])
    wts[t, 0:KEYS, :] = jnp.where(room_left >= t, taps[0] * scale, 0.0)
    wts[t, KEYS : 2 * KEYS, :] = taps[1] * scale
    wts[t, 2 * KEYS : 3 * KEYS, :] = jnp.where(room_right < t, taps[2] * scale, 0.0)


def prefetch_kernel(own, valid, guide, own_out, masks, perm, flip, guide_out, valid_in, guide_in, sems):
    copies = [
        pltpu.make_async_copy(src, dst, sems.at[i])
        for i, (src, dst) in enumerate([(own, own_out), (guide, guide_in), (valid, valid_in)])
    ]
    for copy in copies:
        copy.start()
    perm[...] = jnp.where(
        iota((SPAN, WIDE), 1) == WIDE - 1 - iota((SPAN, WIDE), 0), 1.0, 0.0
    ).astype(BF)
    back = 2 * LANES - 1 - iota((DISP, 2 * LANES), 0)
    flip[...] = jnp.where(iota((DISP, 2 * LANES), 1) == back, 1.0, 0.0).astype(BF)

    copies[1].wait()
    guide_out[...] = spread_guide(guide_in[...])
    copies[2].wait()
    masks[...] = valid_in[...].astype(F32)
    copies[0].wait()


def payload_kernel(own, other, masks, first, second, ref_own):
    view = lax.axis_index("view")
    first_view = view == 0
    sec_mask = masks[1:2, :].astype(BF)
    lane = iota((CHANNELS, LANES), 1)
    tails = []
    for line in range(LINES):
        at = view * LINES + line
        mine, theirs = own[at], other[at]
        lo = line * CHANNELS
        dest, start = (first, lo) if line < QUAD else (second, lo - QUAD_ROWS)
        dest[start : start + CHANNELS, :] = jnp.where(first_view, theirs, mine) * sec_mask
        ref = jnp.where(first_view, mine, theirs)
        ref_own[lo : lo + CHANNELS, :] = ref
        tail = ref[:, BLOCK - LANES :].astype(F32)
        slot = line % PACK
        turn = (HALO * (slot + 1)) % LANES
        if turn:
            tail = pltpu.roll(tail, turn, 1)
        if slot:
            tails[-1] = jnp.where(lane >= HALO * slot, tail, tails[-1])
        else:
            tails.append(tail)
    for i, tail in enumerate(tails):
        first[QUAD_ROWS:MASK_AT, i * LANES : (i + 1) * LANES] = tail.astype(BF)
    first[MASK_AT:, :] = jnp.broadcast_to(masks[0:1, :], (16, BLOCK)).astype(BF)


def shifted(left, mine, lo, off):
    ch_lane = iota((CHANNELS, LANES), 1)
    tiles = [
        src[lo : lo + CHANNELS, i * LANES : (i + 1) * LANES].astype(F32)
        for src in (left, mine)
        for i in range(2)
    ]
    tiles = [pltpu.roll(tile, off, 1) for tile in tiles]
    tiles = [jnp.where(ch_lane < off, tiles[max(i - 1, 0)], tiles[i]).astype(BF) for i in range(4)]
    return jnp.concatenate(tiles, axis=1)


def line_costs(lhs, rhs, slot, skew, cost_rows):
    diagonal = iota((8, LANES), 1) - iota((8, LANES), 0)
    for chunk in range(3):
        rows = min(LANES, SPAN - chunk * LANES)
        first = max(1 - chunk, 0)
        last = 3 - chunk
        products = jnp.dot(
            lhs[chunk * LANES : chunk * LANES + rows],
            rhs[:, first * LANES : (last + 1) * LANES],
            preferred_element_type=F32,
        )
        for j in range(rows // 8):
            tiles = [
                pltpu.roll(
                    products[8 * j : 8 * j + 8, i * LANES : (i + 1) * LANES],
                    8 * j, 1, stride=1, stride_axis=0,
                )
                for i in range(last + 1 - first)
            ]
            if len(tiles) < 3:
                tiles = [tiles[0]] + tiles
            beyond = diagonal >= 8 * j
            at = chunk * LANES + 8 * j
            skew[slot, 0, at : at + 8, :] = jnp.where(beyond, tiles[1], tiles[0])
            skew[slot, 1, at : at + 8, :] = jnp.where(beyond, tiles[2], tiles[1])
    for t in range(RUN):
        at = t * QUAD_LANES + slot * PARTS
        for v in range(2):
            cost_rows[at : at + PARTS, v * LANES : (v + 1) * LANES] = skew[
                slot, v, pl.ds(t, PARTS, stride=RUN), :
            ].astype(BF)


def early_kernel(
    offsets, ref_own, mine, left, masks, perm, guide, wts, cost_rows, lhs_out,
    ref_rows, ref_cols, gate_rows, skew
):
    base = lax.axis_index("view") * LINES
    low = jnp.where(lax.axis_index("cols") == 0, HALO, 0)
    for line in range(LINES):
        lo = line * CHANNELS
        ref_rows[lo : lo + CHANNELS, LANES:] = ref_own[lo : lo + CHANNELS, :]
        half = line // PACK
        packed = left[QUAD_ROWS:MASK_AT, half * LANES : (half + 1) * LANES].astype(F32)
        turn = (LANES - HALO) - HALO * (line % PACK)
        if turn:
            packed = pltpu.roll(packed, turn, 1)
        ref_rows[lo : lo + CHANNELS, :LANES] = packed.astype(BF)

    mask_left = left[MASK_AT : MASK_AT + 1, BLOCK - LANES :].astype(F32)
    ref_mask = jnp.concatenate([mask_left, masks[0:1, :]], axis=1)
    ref_mask = jnp.broadcast_to(ref_mask * (1.0 / math.sqrt(CHANNELS)), (LANES, WIDE))
    mask_cols = dot_t(perm[...], ref_mask.astype(BF))
    half_lane = iota((PARTS, LANES), 1) < CHANNELS
    span_lane = iota((SPAN, LANES), 1) < CHANNELS

    for quad in range(LINES // QUAD):
        ref_t = dot_t(perm[...], ref_rows[quad * QUAD_ROWS : (quad + 1) * QUAD_ROWS, :])
        for pair in range(QUAD // 2):
            cols = ref_t[:, pair * LANES : (pair + 1) * LANES]
            slot = quad * 2 + pair
            ref_cols[slot] = cols
            masked = cols * mask_cols
            if quad == 0:
                rhs = jnp.concatenate(
                    [
                        shifted(left, mine, line * CHANNELS, offsets[base + line])
                        for line in (2 * slot, 2 * slot + 1)
                    ],
                    axis=0,
                )
            for side in range(2):
                line = 2 * slot + side
                for t in range(RUN):
                    picked = ref_cols[slot, pl.ds(t, PARTS, stride=RUN), :]
                    picked = jnp.where(half_lane if side == 0 else ~half_lane, picked, 0.0)
                    at = t * LANES + line * PARTS
                    gate_rows[at : at + PARTS, :] = picked.astype(BF)
                lhs = jnp.where(span_lane if side == 0 else ~span_lane, masked, 0.0).astype(BF)
                if quad == 0:
                    line_costs(lhs, rhs, line, skew, cost_rows)
                else:
                    lhs_out[line - QUAD] = lhs

    place = iota((KEYS, LANES), 1)
    x_base = SPAN - 1 - RUN * (place & (PARTS - 1))
    row = iota((KEYS, LANES), 0)
    reach = jnp.where(row >= 2 * GROUPS, 9, jnp.where(row >= GROUPS, 3, 1))
    room_left = x_base - reach - low
    room_right = x_base + reach - SPAN
    for two in range(RUN // 2):
        at = 2 * two * LANES
        logits = dot_t(guide[...], gate_rows[at : at + 2 * LANES, :])
        for i in range(2):
            t = 2 * two + i
            normalise(logits[:, i * LANES : (i + 1) * LANES], wts, t, room_left, room_right)


def late_kernel(
    offsets, mine, left, lhs, early_rows, wts, flip, out, skew, cost_rows, vol, vals, turned
):
    base = lax.axis_index("view") * LINES
    for pair in range(QUAD // 2):
        rhs = jnp.concatenate(
            [
                shifted(left, mine, line * CHANNELS, offsets[base + QUAD + line])
                for line in (2 * pair, 2 * pair + 1)
            ],
            axis=0,
        )
        for line in (2 * pair, 2 * pair + 1):
            line_costs(lhs[line], rhs, line, skew, cost_rows)

    for two in range(RUN // 2):
        rows = []
        for t in (2 * two, 2 * two + 1):
            for part in (early_rows, cost_rows):
                rows.append(part[t * QUAD_LANES : (t + 1) * QUAD_LANES, :])
        costs = dot_t(flip[...], jnp.concatenate(rows, axis=0))
        vol[2 * two] = costs[:, :LANES]
        vol[2 * two + 1] = costs[:, LANES:]

    def aggregate(group, carry):
        for half in range(2):
            at = pl.multiple_of(group * DGROUP + half * 8, 8)
            v = [vol[t, pl.ds(at, 8), :] for t in range(RUN)]
            for layer in range(LAYERS):
                s = 3**layer
                before = [v[t + s] if t + s < RUN else pltpu.roll(v[t + s - RUN], LANES - 1, 1) for t in range(RUN)]
                after = [v[t - s] if t >= s else pltpu.roll(v[t - s + RUN], 1, 1) for t in range(RUN)]
                fresh = []
                for t in range(RUN):
                    w = [wts[t, pl.ds(k * KEYS + layer * GROUPS + group, 1), :] for k in range(3)]
                    fresh.append(w[0] * before[t] + w[1] * v[t] + w[2] * after[t])
                v = fresh
            for t in range(RUN):
                vol[t, pl.ds(at, 8), :] = v[t]
        return carry

    lax.fori_loop(0, GROUPS, aggregate, 0)

    vals[...] = jnp.zeros((LANES, LANES), F32)
    sub = iota((8, LANES), 0).astype(F32)
    line_of = iota((1, LANES), 1) >> 4
    offs = jnp.zeros((1, LANES), F32)
    for line in range(LINES):
        offs = jnp.where(line_of == line, offsets[base + line].astype(F32), offs)

    def softmax(t, carry):
        v = [vol[t, 8 * i : 8 * i + 8, :] for i in range(DISP // 8)]
        top = v
        while len(top) > 1:
            top = [jnp.maximum(a, b) for a, b in zip(top[::2], top[1::2])] + top[len(top) & ~1 :]
        top = jnp.max(top[0], axis=0, keepdims=True)
        e = [jnp.exp(SHARPNESS * (a - top)) for a in v]
        total = e[0]
        moment = jnp.zeros((8, LANES), F32)
        for i in range(1, DISP // 8):
            total = total + e[i]
            moment = moment + float(8 * i) * e[i]
        moment = jnp.sum(moment + sub * total, axis=0, keepdims=True)
        total = jnp.sum(total, axis=0, keepdims=True)
        vals[pl.ds(RUN - 1 - t, 1), :] = (moment / total + offs) * (1.0 / DISP)
        return carry

    lax.fori_loop(0, RUN, softmax, 0)

    turned[...] = jnp.transpose(vals[...])
    lane = iota((8, LANES), 1)
    result = [jnp.zeros((8, LANES), F32) for _ in range(WIDE // LANES)]
    for part in range(PARTS):
        piece = turned[pl.ds(part, LINES, stride=PARTS), :]
        start = (RUN * (PARTS - 1 - part) - HALO) % WIDE
        tile, turn = divmod(start, LANES)
        if turn:
            piece = pltpu.roll(piece, turn, 1)
        if turn + RUN > LANES:
            after = (tile + 1) % len(result)
            result[after] = result[after] + jnp.where(lane < turn, piece, 0.0)
            piece = jnp.where(lane >= turn, piece, 0.0)
        result[tile] = result[tile] + piece
    for tile, value in enumerate(result):
        out[:, tile * LANES : (tile + 1) * LANES] = value


def join(pieces, sub, n):
    block = lax.axis_index("cols")
    pieces = pieces.reshape(n, 2, LINES, WIDE)
    start = (0, block // (n // 2), (block % (n // 2)) * sub, 0)
    pieces = lax.dynamic_slice(pieces, start, (n, 1, sub, WIDE))[:, 0]
    main = pieces[:, :, :BLOCK]
    tail = jnp.pad(pieces[1:, :, BLOCK:], ((0, 1), (0, 0), (LANES, 0)))
    place = (n, sub, BLOCK)
    keep = (iota(place, 2) < BLOCK - CUT) | (iota(place, 0) == n - 1)
    joined = jnp.where(keep, main, tail)
    return jnp.transpose(joined, (1, 0, 2)).reshape(1, sub, n * BLOCK)


def halo_plan(features, valid_cols, offsets, guide_weight):
    own = features[0]
    n = lax.axis_size("cols")
    right = [(c, c + 1) for c in range(n - 1)]
    other = lax.ppermute(own, "view", [(0, 1), (1, 0)])
    near, masks, perm, flip, guide = call(
        prefetch_kernel,
        [(own.shape, BF), (valid_cols.shape, F32), ((SPAN, WIDE), BF), ((DISP, 2 * LANES), BF), ((3 * KEYS, LANES), BF)],
        [pltpu.VMEM(valid_cols.shape, jnp.int32), pltpu.VMEM(guide_weight.shape, BF), pltpu.SemaphoreType.DMA((3,))],
        0, (own, valid_cols, guide_weight), 100_000_000, pl.ANY, 24, pltpu.VMEM,
    )
    first, second, ref_own = call(
        payload_kernel,
        [((PAYLOAD, BLOCK), BF), ((QUAD_ROWS, BLOCK), BF), ((SEC_ROWS, BLOCK), BF)],
        [], 0, (near, other, masks),
    )
    left_first = lax.ppermute(first, "cols", right)
    left_second = lax.ppermute(second, "cols", right)
    quad_rows = (RUN * QUAD_LANES, 2 * LANES)
    skew = pltpu.VMEM((QUAD, 2, SPAN, LANES), F32)
    square = pltpu.VMEM((LANES, LANES), F32)
    wts, early_rows, lhs = call(
        early_kernel,
        [((RUN, 3 * KEYS, LANES), F32), (quad_rows, BF), ((QUAD, SPAN, LANES), BF)],
        [pltpu.VMEM((SEC_ROWS, WIDE), BF), pltpu.VMEM((QUAD, SPAN, LANES), F32), pltpu.VMEM((RUN * LANES, LANES), BF), skew],
        1, (offsets, ref_own, first, left_first, masks, perm, guide), 1_000_000_000,
    )
    (result,) = call(
        late_kernel,
        [((LINES, WIDE), F32)],
        [skew, pltpu.VMEM(quad_rows, BF), pltpu.VMEM((RUN, DISP, LANES), F32), square, square],
        1, (offsets, second, left_second, lhs, early_rows, wts, flip), 1_000_000_000,
    )
    copies = jnp.broadcast_to(result[None], (2 * n, LINES, WIDE))
    pieces = lax.all_to_all(copies, ("cols", "view"), split_axis=0, concat_axis=0, tiled=True)
    return join(pieces, own.shape[0] // n, n)


LINE_RUN = 8
PAIR = 2
LINE_PARTS = LANES


MASKS = 8
GATE_FLOOR = 11.0 / 9.0


def pack_kernel(key, own, *rest):
    out = rest[-1]
    me = 2 * lax.axis_index("cols") + lax.axis_index("view")
    rows = PAIR * CHANNELS
    out[:rows, :] = own[me ^ key]
    if out.shape[0] > rows:
        masks = rest[0][...].astype(F32)
        out[rows:, :] = jnp.where(
            iota((MASKS, BLOCK), 0) < MASKS // 2, masks[0:1, :], masks[1:2, :]
        ).astype(BF)


def constants_kernel(offsets, guide, valid, order, order_band, flip, guide_out, spread, masks):
    masks[...] = valid[...].astype(F32)
    row = iota((LANES, LANES), 0)
    from_lane = LANES - 1 - LINE_RUN * (row & (PARTS - 1)) - (row >> 4)
    order[...] = jnp.where(iota((LANES, LANES), 1) == from_lane, 1.0, 0.0).astype(BF)
    from_lane = LANES - 1 - (row & 64) - LINE_RUN * (row & 7) - ((row >> 3) & 7)
    order_band[...] = jnp.where(iota((LANES, LANES), 1) == from_lane, 1.0, 0.0).astype(BF)
    back = 2 * LANES - 1 - iota((DISP, 2 * LANES), 0)
    flip[...] = jnp.where(iota((DISP, 2 * LANES), 1) == back, 1.0, 0.0).astype(BF)
    guide_out[...] = spread_guide(guide[...]) * 0.5
    block_of = LANES - 1 - (iota(spread.shape, 1) >> 3)
    spread[...] = jnp.where(iota(spread.shape, 0) == block_of, 1.0, 0.0).astype(BF)


def lines_kernel(offsets, order, order_band, flip, guide, spread, *rest):
    pieces, (out, blocks, valid, gate_rows, cost_rows, vol, done, wts) = rest[:-8], rest[-8:]
    near, pieces = pieces[0], pieces[1:]
    tiles = len(pieces)
    width = tiles * LANES
    me = 2 * lax.axis_index("cols") + lax.axis_index("view")
    rows = PAIR * CHANNELS
    for key, piece in enumerate(pieces):
        blocks[me ^ key] = piece[:rows, :]
        if piece.shape[0] > rows:
            masks = piece[rows:, :].astype(F32)
            valid[(me ^ key) // 2] = jnp.concatenate([masks[0:1], masks[MASKS // 2 : MASKS // 2 + 1]], axis=0)
    valid[me // 2] = near[...]
    at = PAIR * me
    offs = [offsets[at + i] for i in range(PAIR)]
    ch_lane = iota((CHANNELS, LANES), 1)
    low_lane = ch_lane < LANES // 2
    low_half = iota((LANES, LANES), 1) < CHANNELS
    reached = iota((8, LANES), 1) + LINE_RUN * iota((8, LANES), 0)
    scale = 1.0 / math.sqrt(CHANNELS)
    empty = jnp.zeros((CHANNELS, LANES), F32)

    def mask_of(view, w):
        lo = (w % 2) * LANES
        return valid[w // 2, view : view + 1, lo : lo + LANES]

    for i in range(PAIR):

        def tile_of(view, w):
            lo = (w % 2) * LANES
            return blocks[2 * (w // 2) + view, i * CHANNELS : (i + 1) * CHANNELS, lo : lo + LANES]

        off = offs[i]
        rolled = [pltpu.roll(tile_of(1, w).astype(F32) * mask_of(1, w), off, 1) for w in range(tiles)]
        line = [empty, empty]
        for w in range(tiles):
            line.append(jnp.where(ch_lane < off, rolled[w - 1] if w else empty, rolled[w]))
        turned = [empty] + [pltpu.roll(tile, LANES // 2, 1) if w else tile for w, tile in enumerate(line[1:])]
        shifted = [tile.astype(BF) for tile in line]
        halfway = [jnp.where(low_lane, a, b).astype(BF) for a, b in zip(turned, turned[1:])]

        for quad in range(tiles // 4):
            refs = [tile_of(0, 4 * quad + q) for q in range(4)]
            masked = [refs[q] * (mask_of(0, 4 * quad + q) * scale).astype(BF) for q in range(4)]
            cols = dot_t(order[...], jnp.concatenate(refs, axis=0))
            masked = dot_t(order_band[...], jnp.concatenate(masked, axis=0))
            for two in range(2):
                w = 4 * quad + 2 * two
                raw = cols[:, two * LANES : (two + 1) * LANES]
                pair = masked[:, two * LANES : (two + 1) * LANES]
                gates = [jnp.where(low_half, raw, 0.0).astype(BF), jnp.where(low_half, 0.0, raw).astype(BF)]
                sides = [jnp.where(low_half, pair, 0.0).astype(BF), jnp.where(low_half, 0.0, pair).astype(BF)]
                chunks = []
                for half, source, first in ((0, shifted, w + 1), (1, halfway, w)):
                    lo = half * LANES // 2
                    lhs = jnp.concatenate([side[lo : lo + LANES // 2] for side in sides], axis=0)
                    rhs = jnp.concatenate(
                        [jnp.concatenate(source[first + side : first + side + 2], axis=1) for side in range(2)],
                        axis=0,
                    )
                    chunks.append(jnp.dot(lhs, rhs, preferred_element_type=F32))
                for side in range(2):
                    place = (tiles - 1 - w - side) * PARTS
                    for t in range(LINE_RUN):
                        row = t * LANES + place
                        gate_rows[i, row : row + PARTS, :] = gates[side][t * PARTS : (t + 1) * PARTS]
                        r = side * LANES // 2 + 8 * t
                        within = reached < LANES - t
                        halves = []
                        for products in chunks:
                            close, far = products[r : r + 8, :LANES], products[r : r + 8, LANES:]
                            halves.append(
                                jnp.concatenate(
                                    [
                                        pltpu.roll(value, t, 1, stride=LINE_RUN, stride_axis=0)
                                        for value in (close, jnp.where(within, far, close))
                                    ],
                                    axis=1,
                                )
                            )
                        cost_rows[i, row : row + PARTS, :] = jnp.concatenate(halves, axis=0).astype(BF)

    x_base = width - 1 - LINE_RUN * iota((KEYS, LANES), 1)
    row = iota((KEYS, LANES), 0)
    reach = jnp.where(row >= 2 * GROUPS, 9, jnp.where(row >= GROUPS, 3, 1))
    room_left = x_base - reach
    room_right = x_base + reach - width
    unit = jnp.where(row >= 2 * GROUPS, SHARPNESS / math.log(2.0), 1.0)
    for i in range(PAIR):
        for two in range(LINE_RUN // 2):
            lo = 2 * two * LANES
            costs = dot_t(flip[...], cost_rows[i, lo : lo + 2 * LANES, :])
            logits = dot_t(guide[...], gate_rows[i, lo : lo + 2 * LANES, :])
            for side in range(2):
                t = 2 * two + side
                vol[i, t] = costs[:, side * LANES : (side + 1) * LANES]
                z = jnp.tanh(logits[:, side * LANES : (side + 1) * LANES]) + GATE_FLOOR
                taps = [z[m * KEYS : (m + 1) * KEYS] for m in range(3)]
                factor = unit / (taps[0] + taps[1] + taps[2])
                taps = [tap * factor for tap in taps]
                taps[0] = jnp.where(room_left >= t, taps[0], 0.0)
                taps[2] = jnp.where(room_right < t, taps[2], 0.0)
                for m in range(3):
                    wts[i, t, m * KEYS : (m + 1) * KEYS, :] = taps[m]

    for group in range(GROUPS):
        starts = [group * DGROUP + 8 * half for half in range(2)]
        for i in range(PAIR):
            v = [[vol[i, t, at : at + 8, :] for t in range(LINE_RUN)] for at in starts]
            for layer in range(LAYERS):
                s = 3**layer
                fresh = [[], []]
                for t in range(LINE_RUN):
                    rows = [k * KEYS + layer * GROUPS + group for k in range(3)]
                    w = [jnp.broadcast_to(wts[i, t, r : r + 1, :], (8, LANES)) for r in rows]
                    for half in range(2):
                        blk, r = divmod(t + s, LINE_RUN)
                        before = pltpu.roll(v[half][r], LANES - blk, 1) if blk else v[half][r]
                        blk, r = divmod(t - s, LINE_RUN)
                        after = pltpu.roll(v[half][r], -blk, 1) if blk else v[half][r]
                        fresh[half].append(w[0] * before + w[1] * v[half][t] + w[2] * after)
                v = fresh
            for half, at_row in enumerate(starts):
                for t in range(LINE_RUN):
                    done[i, t, at_row : at_row + 8, :] = v[half][t]

    sub = iota((8, LANES), 0)
    results = []
    for i in range(PAIR):
        totals = jnp.zeros((8, LANES), F32)
        moments = totals
        for s in range(LINE_RUN):
            t = LINE_RUN - 1 - s
            v = [done[i, t, 8 * j : 8 * j + 8, :] for j in range(DISP // 8)]
            top = v
            while len(top) > 1:
                top = [jnp.maximum(a, b) for a, b in zip(top[::2], top[1::2])] + top[len(top) & ~1 :]
            top = jnp.max(top[0], axis=0, keepdims=True)
            total = jnp.exp2(v[-1] - top)
            moment = total
            for j in range(DISP // 8 - 2, -1, -1):
                total = total + jnp.exp2(v[j] - top)
                if j:
                    moment = moment + total
            moment = 8.0 * moment + sub.astype(F32) * total
            totals = jnp.where(sub == s, jnp.sum(total, axis=0, keepdims=True), totals)
            moments = jnp.where(sub == s, jnp.sum(moment, axis=0, keepdims=True), moments)
        results.append((moments / totals + offs[i].astype(F32)) * (1.0 / DISP))
    both = jnp.concatenate(results, axis=0)
    high = both.astype(BF)
    left = both - high.astype(F32)
    middle = left.astype(BF)
    low = (left - middle.astype(F32)).astype(BF)
    parts = jnp.dot(
        jnp.concatenate([high, middle, low], axis=0), spread[...], preferred_element_type=F32
    )
    size = PAIR * LINE_RUN
    parts = parts[:size] + parts[size : 2 * size] + parts[2 * size :]
    wanted = iota((LINE_RUN, width), 0) == (iota((LINE_RUN, width), 1) & (LINE_RUN - 1))
    for i in range(PAIR):
        part = jnp.where(wanted, parts[i * LINE_RUN : (i + 1) * LINE_RUN], 0.0)
        out[i : i + 1, :] = jnp.sum(part, axis=0, keepdims=True)


def lines_plan(features, valid_cols, offsets, guide_weight):
    n = lax.axis_size("cols")
    devices = 2 * n
    width = n * BLOCK
    rows = PAIR * CHANNELS
    own = features.reshape(devices, rows, BLOCK)
    pieces = [None] * devices
    gone = ()
    for key in (1, 2, 6, 4, 3, 5, 7, 0):
        masked = key % 2 and key > 1
        (piece,) = call(
            functools.partial(pack_kernel, key),
            [((rows + (MASKS if masked else 0), BLOCK), BF)],
            [], 0,
            (own,) + ((valid_cols,) if masked else ()) + gone,
            1_000_000,
        )
        gone = (piece,)
        moves = [(i, i ^ key) for i in range(devices)]
        pieces[key] = lax.ppermute(piece, ("cols", "view"), moves) if key else piece
    consts = call(
        constants_kernel,
        [
            ((LANES, LANES), BF), ((LANES, LANES), BF), ((DISP, 2 * LANES), BF), ((3 * KEYS, LANES), BF),
            ((LANES, width), BF), (valid_cols.shape, F32),
        ],
        [], 1, (offsets, guide_weight, valid_cols), 1_000_000,
    )
    (rows,) = call(
        lines_kernel,
        [((PAIR, width), F32)],
        [
            pltpu.VMEM((devices, rows, BLOCK), BF),
            pltpu.VMEM((n,) + valid_cols.shape, F32),
            pltpu.VMEM((PAIR, LINE_RUN * LANES, LANES), BF),
            pltpu.VMEM((PAIR, LINE_RUN * LANES, 2 * LANES), BF),
            pltpu.VMEM((PAIR, LINE_RUN, DISP, LANES), F32),
            pltpu.VMEM((PAIR, LINE_RUN, DISP, LANES), F32),
            pltpu.VMEM((PAIR, LINE_RUN, 3 * KEYS, LANES), F32),
        ],
        1, (offsets, *consts, *pieces), 1_000_000_000,
    )
    others = lax.ppermute(rows, "view", [(0, 1), (1, 0)])
    first = lax.axis_index("view") == 0
    return jnp.where(first, jnp.concatenate([rows, others]), jnp.concatenate([others, rows]))[None]


def on_device(features, valid_cols, offsets, guide_weight):
    n = lax.axis_size("cols")
    lines = features.shape[1]
    if lines == 2 * PAIR * n and n * BLOCK == LINE_RUN * LANES:
        return lines_plan(features, valid_cols, offsets, guide_weight)
    return halo_plan(features, valid_cols, offsets, guide_weight)


def solution(mesh):
    return jax.shard_map(
        on_device,
        mesh=mesh,
        in_specs=(
            P("view", ("tiles", "lines"), None, "cols"),
            P(None, ("tiles", "cols")),
            P(("tiles", "lines")),
            P(),
        ),
        out_specs=P(("tiles", "lines"), "cols", None),
        check_vma=False,
    )
```

```python
import functools
import math

import jax
import jax.numpy as jnp
from jax import lax
from jax.experimental import pallas as pl
from jax.experimental.pallas import tpu as pltpu
from jax.sharding import PartitionSpec as P

DISP = 192
DGROUP = 16
GROUPS = DISP // DGROUP
LAYERS = 3
SHARPNESS = 2.0
HALO = 32
LANES = 128
LINES = 8
CHANNELS = 64
BLOCK = 256
SPAN = BLOCK + HALO
PARTS = LANES // LINES
RUN = SPAN // PARTS
KEYS = 40
WIDE = BLOCK + LANES
SEC_ROWS = LINES * CHANNELS
QUAD_ROWS = SEC_ROWS // 2
MASK_AT = QUAD_ROWS + CHANNELS
PAYLOAD = MASK_AT + 16
QUAD = LINES // 2
QUAD_LANES = LANES // 2
PACK = LANES // HALO
CUT = 16

BF = jnp.bfloat16
F32 = jnp.float32


def iota(shape, dim):
    return lax.broadcasted_iota(jnp.int32, shape, dim)


def dot_t(a, b):
    return lax.dot_general(a, b, (((1,), (1,)), ((), ())), preferred_element_type=F32)


def call(kernel, outs, scratch, smem, args, flops=0, space=pltpu.VMEM, limit=24, to=None):
    specs = [pl.BlockSpec(memory_space=pltpu.SMEM)] * smem
    specs += [pl.BlockSpec(memory_space=space)] * (len(args) - smem)
    return pl.pallas_call(
        kernel,
        out_shape=[jax.ShapeDtypeStruct(shape, dtype) for shape, dtype in outs],
        in_specs=specs,
        out_specs=[pl.BlockSpec(memory_space=to or space)] * len(outs),
        scratch_shapes=scratch,
        compiler_params=pltpu.CompilerParams(vmem_limit_bytes=limit * 1024 * 1024),
        cost_estimate=pl.CostEstimate(flops=flops, bytes_accessed=1_000_000, transcendentals=0),
    )(*args)


def spread_guide(guide):
    keys = LAYERS * 3 * GROUPS
    row = iota((3 * KEYS, keys), 0)
    tap = jnp.where(row >= KEYS, 1, 0) + jnp.where(row >= 2 * KEYS, 1, 0)
    row = row - KEYS * tap
    layer = jnp.where(row >= GROUPS, 1, 0) + jnp.where(row >= 2 * GROUPS, 1, 0)
    key = 2 * GROUPS * layer + GROUPS * tap + row
    chosen = jnp.where((iota((3 * KEYS, keys), 1) == key) & (row < 3 * GROUPS), 1.0, 0.0).astype(BF)
    guide_t = dot_t(chosen, guide).astype(BF)
    return jnp.concatenate([guide_t, guide_t], axis=1)


def normalise(z, wts, t, room_left, room_right):
    z = (0.55 + 0.45 * jnp.tanh(0.5 * z)).astype(BF).astype(F32)
    taps = [z[k * KEYS : (k + 1) * KEYS] for k in range(3)]
    scale = 1.0 / (taps[0] + taps[1] + taps[2])
    wts[t, 0:KEYS, :] = jnp.where(room_left >= t, taps[0] * scale, 0.0)
    wts[t, KEYS : 2 * KEYS, :] = taps[1] * scale
    wts[t, 2 * KEYS : 3 * KEYS, :] = jnp.where(room_right < t, taps[2] * scale, 0.0)


def prefetch_kernel(own, valid, guide, own_out, masks, perm, flip, guide_out, valid_in, guide_in, sems):
    copies = [
        pltpu.make_async_copy(src, dst, sems.at[i])
        for i, (src, dst) in enumerate([(own, own_out), (guide, guide_in), (valid, valid_in)])
    ]
    for copy in copies:
        copy.start()
    perm[...] = jnp.where(
        iota((SPAN, WIDE), 1) == WIDE - 1 - iota((SPAN, WIDE), 0), 1.0, 0.0
    ).astype(BF)
    back = 2 * LANES - 1 - iota((DISP, 2 * LANES), 0)
    flip[...] = jnp.where(iota((DISP, 2 * LANES), 1) == back, 1.0, 0.0).astype(BF)

    copies[1].wait()
    guide_out[...] = spread_guide(guide_in[...])
    copies[2].wait()
    masks[...] = valid_in[...].astype(F32)
    copies[0].wait()


def payload_kernel(own, other, masks, first, second, ref_own):
    view = lax.axis_index("view")
    first_view = view == 0
    sec_mask = masks[1:2, :].astype(BF)
    lane = iota((CHANNELS, LANES), 1)
    tails = []
    for line in range(LINES):
        at = view * LINES + line
        mine, theirs = own[at], other[at]
        lo = line * CHANNELS
        dest, start = (first, lo) if line < QUAD else (second, lo - QUAD_ROWS)
        dest[start : start + CHANNELS, :] = jnp.where(first_view, theirs, mine) * sec_mask
        ref = jnp.where(first_view, mine, theirs)
        ref_own[lo : lo + CHANNELS, :] = ref
        tail = ref[:, BLOCK - LANES :].astype(F32)
        slot = line % PACK
        turn = (HALO * (slot + 1)) % LANES
        if turn:
            tail = pltpu.roll(tail, turn, 1)
        if slot:
            tails[-1] = jnp.where(lane >= HALO * slot, tail, tails[-1])
        else:
            tails.append(tail)
    for i, tail in enumerate(tails):
        first[QUAD_ROWS:MASK_AT, i * LANES : (i + 1) * LANES] = tail.astype(BF)
    first[MASK_AT:, :] = jnp.broadcast_to(masks[0:1, :], (16, BLOCK)).astype(BF)


def shifted(left, mine, lo, off):
    ch_lane = iota((CHANNELS, LANES), 1)
    tiles = [
        src[lo : lo + CHANNELS, i * LANES : (i + 1) * LANES].astype(F32)
        for src in (left, mine)
        for i in range(2)
    ]
    tiles = [pltpu.roll(tile, off, 1) for tile in tiles]
    tiles = [jnp.where(ch_lane < off, tiles[max(i - 1, 0)], tiles[i]).astype(BF) for i in range(4)]
    return jnp.concatenate(tiles, axis=1)


def line_costs(lhs, rhs, slot, skew, cost_rows):
    diagonal = iota((8, LANES), 1) - iota((8, LANES), 0)
    for chunk in range(3):
        rows = min(LANES, SPAN - chunk * LANES)
        first = max(1 - chunk, 0)
        last = 3 - chunk
        products = jnp.dot(
            lhs[chunk * LANES : chunk * LANES + rows],
            rhs[:, first * LANES : (last + 1) * LANES],
            preferred_element_type=F32,
        )
        for j in range(rows // 8):
            tiles = [
                pltpu.roll(
                    products[8 * j : 8 * j + 8, i * LANES : (i + 1) * LANES],
                    8 * j, 1, stride=1, stride_axis=0,
                )
                for i in range(last + 1 - first)
            ]
            if len(tiles) < 3:
                tiles = [tiles[0]] + tiles
            beyond = diagonal >= 8 * j
            at = chunk * LANES + 8 * j
            skew[slot, 0, at : at + 8, :] = jnp.where(beyond, tiles[1], tiles[0])
            skew[slot, 1, at : at + 8, :] = jnp.where(beyond, tiles[2], tiles[1])
    for t in range(RUN):
        at = t * QUAD_LANES + slot * PARTS
        for v in range(2):
            cost_rows[at : at + PARTS, v * LANES : (v + 1) * LANES] = skew[
                slot, v, pl.ds(t, PARTS, stride=RUN), :
            ].astype(BF)


def early_kernel(
    offsets, ref_own, mine, left, masks, perm, guide, wts, cost_rows, lhs_out,
    ref_rows, ref_cols, gate_rows, skew
):
    base = lax.axis_index("view") * LINES
    low = jnp.where(lax.axis_index("cols") == 0, HALO, 0)
    for line in range(LINES):
        lo = line * CHANNELS
        ref_rows[lo : lo + CHANNELS, LANES:] = ref_own[lo : lo + CHANNELS, :]
        half = line // PACK
        packed = left[QUAD_ROWS:MASK_AT, half * LANES : (half + 1) * LANES].astype(F32)
        turn = (LANES - HALO) - HALO * (line % PACK)
        if turn:
            packed = pltpu.roll(packed, turn, 1)
        ref_rows[lo : lo + CHANNELS, :LANES] = packed.astype(BF)

    mask_left = left[MASK_AT : MASK_AT + 1, BLOCK - LANES :].astype(F32)
    ref_mask = jnp.concatenate([mask_left, masks[0:1, :]], axis=1)
    ref_mask = jnp.broadcast_to(ref_mask * (1.0 / math.sqrt(CHANNELS)), (LANES, WIDE))
    mask_cols = dot_t(perm[...], ref_mask.astype(BF))
    half_lane = iota((PARTS, LANES), 1) < CHANNELS
    span_lane = iota((SPAN, LANES), 1) < CHANNELS

    for quad in range(LINES // QUAD):
        ref_t = dot_t(perm[...], ref_rows[quad * QUAD_ROWS : (quad + 1) * QUAD_ROWS, :])
        for pair in range(QUAD // 2):
            cols = ref_t[:, pair * LANES : (pair + 1) * LANES]
            slot = quad * 2 + pair
            ref_cols[slot] = cols
            masked = cols * mask_cols
            if quad == 0:
                rhs = jnp.concatenate(
                    [
                        shifted(left, mine, line * CHANNELS, offsets[base + line])
                        for line in (2 * slot, 2 * slot + 1)
                    ],
                    axis=0,
                )
            for side in range(2):
                line = 2 * slot + side
                for t in range(RUN):
                    picked = ref_cols[slot, pl.ds(t, PARTS, stride=RUN), :]
                    picked = jnp.where(half_lane if side == 0 else ~half_lane, picked, 0.0)
                    at = t * LANES + line * PARTS
                    gate_rows[at : at + PARTS, :] = picked.astype(BF)
                lhs = jnp.where(span_lane if side == 0 else ~span_lane, masked, 0.0).astype(BF)
                if quad == 0:
                    line_costs(lhs, rhs, line, skew, cost_rows)
                else:
                    lhs_out[line - QUAD] = lhs

    place = iota((KEYS, LANES), 1)
    x_base = SPAN - 1 - RUN * (place & (PARTS - 1))
    row = iota((KEYS, LANES), 0)
    reach = jnp.where(row >= 2 * GROUPS, 9, jnp.where(row >= GROUPS, 3, 1))
    room_left = x_base - reach - low
    room_right = x_base + reach - SPAN
    for two in range(RUN // 2):
        at = 2 * two * LANES
        logits = dot_t(guide[...], gate_rows[at : at + 2 * LANES, :])
        for i in range(2):
            t = 2 * two + i
            normalise(logits[:, i * LANES : (i + 1) * LANES], wts, t, room_left, room_right)


def late_kernel(
    offsets, mine, left, lhs, early_rows, wts, flip, out, skew, cost_rows, vol, vals, turned
):
    base = lax.axis_index("view") * LINES
    for pair in range(QUAD // 2):
        rhs = jnp.concatenate(
            [
                shifted(left, mine, line * CHANNELS, offsets[base + QUAD + line])
                for line in (2 * pair, 2 * pair + 1)
            ],
            axis=0,
        )
        for line in (2 * pair, 2 * pair + 1):
            line_costs(lhs[line], rhs, line, skew, cost_rows)

    for two in range(RUN // 2):
        rows = []
        for t in (2 * two, 2 * two + 1):
            for part in (early_rows, cost_rows):
                rows.append(part[t * QUAD_LANES : (t + 1) * QUAD_LANES, :])
        costs = dot_t(flip[...], jnp.concatenate(rows, axis=0))
        vol[2 * two] = costs[:, :LANES]
        vol[2 * two + 1] = costs[:, LANES:]

    def aggregate(group, carry):
        for half in range(2):
            at = pl.multiple_of(group * DGROUP + half * 8, 8)
            v = [vol[t, pl.ds(at, 8), :] for t in range(RUN)]
            for layer in range(LAYERS):
                s = 3**layer
                before = [v[t + s] if t + s < RUN else pltpu.roll(v[t + s - RUN], LANES - 1, 1) for t in range(RUN)]
                after = [v[t - s] if t >= s else pltpu.roll(v[t - s + RUN], 1, 1) for t in range(RUN)]
                fresh = []
                for t in range(RUN):
                    w = [wts[t, pl.ds(k * KEYS + layer * GROUPS + group, 1), :] for k in range(3)]
                    fresh.append(w[0] * before[t] + w[1] * v[t] + w[2] * after[t])
                v = fresh
            for t in range(RUN):
                vol[t, pl.ds(at, 8), :] = v[t]
        return carry

    lax.fori_loop(0, GROUPS, aggregate, 0)

    vals[...] = jnp.zeros((LANES, LANES), F32)
    sub = iota((8, LANES), 0).astype(F32)
    line_of = iota((1, LANES), 1) >> 4
    offs = jnp.zeros((1, LANES), F32)
    for line in range(LINES):
        offs = jnp.where(line_of == line, offsets[base + line].astype(F32), offs)

    def softmax(t, carry):
        v = [vol[t, 8 * i : 8 * i + 8, :] for i in range(DISP // 8)]
        top = v
        while len(top) > 1:
            top = [jnp.maximum(a, b) for a, b in zip(top[::2], top[1::2])] + top[len(top) & ~1 :]
        top = jnp.max(top[0], axis=0, keepdims=True)
        e = [jnp.exp(SHARPNESS * (a - top)) for a in v]
        total = e[0]
        moment = jnp.zeros((8, LANES), F32)
        for i in range(1, DISP // 8):
            total = total + e[i]
            moment = moment + float(8 * i) * e[i]
        moment = jnp.sum(moment + sub * total, axis=0, keepdims=True)
        total = jnp.sum(total, axis=0, keepdims=True)
        vals[pl.ds(RUN - 1 - t, 1), :] = (moment / total + offs) * (1.0 / DISP)
        return carry

    lax.fori_loop(0, RUN, softmax, 0)

    turned[...] = jnp.transpose(vals[...])
    lane = iota((8, LANES), 1)
    result = [jnp.zeros((8, LANES), F32) for _ in range(WIDE // LANES)]
    for part in range(PARTS):
        piece = turned[pl.ds(part, LINES, stride=PARTS), :]
        start = (RUN * (PARTS - 1 - part) - HALO) % WIDE
        tile, turn = divmod(start, LANES)
        if turn:
            piece = pltpu.roll(piece, turn, 1)
        if turn + RUN > LANES:
            after = (tile + 1) % len(result)
            result[after] = result[after] + jnp.where(lane < turn, piece, 0.0)
            piece = jnp.where(lane >= turn, piece, 0.0)
        result[tile] = result[tile] + piece
    for tile, value in enumerate(result):
        out[:, tile * LANES : (tile + 1) * LANES] = value


def join(pieces, sub, n):
    block = lax.axis_index("cols")
    pieces = pieces.reshape(n, 2, LINES, WIDE)
    start = (0, block // (n // 2), (block % (n // 2)) * sub, 0)
    pieces = lax.dynamic_slice(pieces, start, (n, 1, sub, WIDE))[:, 0]
    main = pieces[:, :, :BLOCK]
    tail = jnp.pad(pieces[1:, :, BLOCK:], ((0, 1), (0, 0), (LANES, 0)))
    place = (n, sub, BLOCK)
    keep = (iota(place, 2) < BLOCK - CUT) | (iota(place, 0) == n - 1)
    joined = jnp.where(keep, main, tail)
    return jnp.transpose(joined, (1, 0, 2)).reshape(1, sub, n * BLOCK)


def halo_plan(features, valid_cols, offsets, guide_weight):
    own = features[0]
    n = lax.axis_size("cols")
    right = [(c, c + 1) for c in range(n - 1)]
    other = lax.ppermute(own, "view", [(0, 1), (1, 0)])
    near, masks, perm, flip, guide = call(
        prefetch_kernel,
        [(own.shape, BF), (valid_cols.shape, F32), ((SPAN, WIDE), BF), ((DISP, 2 * LANES), BF), ((3 * KEYS, LANES), BF)],
        [pltpu.VMEM(valid_cols.shape, jnp.int32), pltpu.VMEM(guide_weight.shape, BF), pltpu.SemaphoreType.DMA((3,))],
        0, (own, valid_cols, guide_weight), 100_000_000, pl.ANY, 24, pltpu.VMEM,
    )
    first, second, ref_own = call(
        payload_kernel,
        [((PAYLOAD, BLOCK), BF), ((QUAD_ROWS, BLOCK), BF), ((SEC_ROWS, BLOCK), BF)],
        [], 0, (near, other, masks),
    )
    left_first = lax.ppermute(first, "cols", right)
    left_second = lax.ppermute(second, "cols", right)
    quad_rows = (RUN * QUAD_LANES, 2 * LANES)
    skew = pltpu.VMEM((QUAD, 2, SPAN, LANES), F32)
    square = pltpu.VMEM((LANES, LANES), F32)
    wts, early_rows, lhs = call(
        early_kernel,
        [((RUN, 3 * KEYS, LANES), F32), (quad_rows, BF), ((QUAD, SPAN, LANES), BF)],
        [pltpu.VMEM((SEC_ROWS, WIDE), BF), pltpu.VMEM((QUAD, SPAN, LANES), F32), pltpu.VMEM((RUN * LANES, LANES), BF), skew],
        1, (offsets, ref_own, first, left_first, masks, perm, guide), 1_000_000_000,
    )
    (result,) = call(
        late_kernel,
        [((LINES, WIDE), F32)],
        [skew, pltpu.VMEM(quad_rows, BF), pltpu.VMEM((RUN, DISP, LANES), F32), square, square],
        1, (offsets, second, left_second, lhs, early_rows, wts, flip), 1_000_000_000,
    )
    copies = jnp.broadcast_to(result[None], (2 * n, LINES, WIDE))
    pieces = lax.all_to_all(copies, ("cols", "view"), split_axis=0, concat_axis=0, tiled=True)
    return join(pieces, own.shape[0] // n, n)


LINE_RUN = 8
PAIR = 2
LINE_PARTS = LANES


MASKS = 8
GATE_FLOOR = 11.0 / 9.0


def pack_kernel(key, own, *rest):
    out = rest[-1]
    me = 2 * lax.axis_index("cols") + lax.axis_index("view")
    rows = PAIR * CHANNELS
    out[:rows, :] = own[me ^ key]
    if out.shape[0] > rows:
        masks = rest[0][...].astype(F32)
        out[rows:, :] = jnp.where(
            iota((MASKS, BLOCK), 0) < MASKS // 2, masks[0:1, :], masks[1:2, :]
        ).astype(BF)


def constants_kernel(offsets, guide, valid, order, order_band, flip, guide_out, spread, masks):
    masks[...] = valid[...].astype(F32)
    row = iota((LANES, LANES), 0)
    from_lane = LANES - 1 - LINE_RUN * (row & (PARTS - 1)) - (row >> 4)
    order[...] = jnp.where(iota((LANES, LANES), 1) == from_lane, 1.0, 0.0).astype(BF)
    from_lane = LANES - 1 - (row & 64) - LINE_RUN * (row & 7) - ((row >> 3) & 7)
    order_band[...] = jnp.where(iota((LANES, LANES), 1) == from_lane, 1.0, 0.0).astype(BF)
    back = 2 * LANES - 1 - iota((DISP, 2 * LANES), 0)
    flip[...] = jnp.where(iota((DISP, 2 * LANES), 1) == back, 1.0, 0.0).astype(BF)
    guide_out[...] = spread_guide(guide[...]) * 0.5
    block_of = LANES - 1 - (iota(spread.shape, 1) >> 3)
    spread[...] = jnp.where(iota(spread.shape, 0) == block_of, 1.0, 0.0).astype(BF)


def lines_kernel(offsets, order, order_band, flip, guide, spread, *rest):
    pieces, (out, blocks, valid, gate_rows, cost_rows, vol, done, wts) = rest[:-8], rest[-8:]
    near, pieces = pieces[0], pieces[1:]
    tiles = len(pieces)
    width = tiles * LANES
    me = 2 * lax.axis_index("cols") + lax.axis_index("view")
    rows = PAIR * CHANNELS
    for key, piece in enumerate(pieces):
        blocks[me ^ key] = piece[:rows, :]
        if piece.shape[0] > rows:
            masks = piece[rows:, :].astype(F32)
            valid[(me ^ key) // 2] = jnp.concatenate([masks[0:1], masks[MASKS // 2 : MASKS // 2 + 1]], axis=0)
    valid[me // 2] = near[...]
    at = PAIR * me
    offs = [offsets[at + i] for i in range(PAIR)]
    ch_lane = iota((CHANNELS, LANES), 1)
    low_lane = ch_lane < LANES // 2
    low_half = iota((LANES, LANES), 1) < CHANNELS
    reached = iota((8, LANES), 1) + LINE_RUN * iota((8, LANES), 0)
    scale = 1.0 / math.sqrt(CHANNELS)
    empty = jnp.zeros((CHANNELS, LANES), F32)

    def mask_of(view, w):
        lo = (w % 2) * LANES
        return valid[w // 2, view : view + 1, lo : lo + LANES]

    for i in range(PAIR):

        def tile_of(view, w):
            lo = (w % 2) * LANES
            return blocks[2 * (w // 2) + view, i * CHANNELS : (i + 1) * CHANNELS, lo : lo + LANES]

        off = offs[i]
        rolled = [pltpu.roll(tile_of(1, w).astype(F32) * mask_of(1, w), off, 1) for w in range(tiles)]
        line = [empty, empty]
        for w in range(tiles):
            line.append(jnp.where(ch_lane < off, rolled[w - 1] if w else empty, rolled[w]))
        turned = [empty] + [pltpu.roll(tile, LANES // 2, 1) if w else tile for w, tile in enumerate(line[1:])]
        shifted = [tile.astype(BF) for tile in line]
        halfway = [jnp.where(low_lane, a, b).astype(BF) for a, b in zip(turned, turned[1:])]

        for quad in range(tiles // 4):
            refs = [tile_of(0, 4 * quad + q) for q in range(4)]
            masked = [refs[q] * (mask_of(0, 4 * quad + q) * scale).astype(BF) for q in range(4)]
            cols = dot_t(order[...], jnp.concatenate(refs, axis=0))
            masked = dot_t(order_band[...], jnp.concatenate(masked, axis=0))
            for two in range(2):
                w = 4 * quad + 2 * two
                raw = cols[:, two * LANES : (two + 1) * LANES]
                pair = masked[:, two * LANES : (two + 1) * LANES]
                gates = [jnp.where(low_half, raw, 0.0).astype(BF), jnp.where(low_half, 0.0, raw).astype(BF)]
                sides = [jnp.where(low_half, pair, 0.0).astype(BF), jnp.where(low_half, 0.0, pair).astype(BF)]
                chunks = []
                for half, source, first in ((0, shifted, w + 1), (1, halfway, w)):
                    lo = half * LANES // 2
                    lhs = jnp.concatenate([side[lo : lo + LANES // 2] for side in sides], axis=0)
                    rhs = jnp.concatenate(
                        [jnp.concatenate(source[first + side : first + side + 2], axis=1) for side in range(2)],
                        axis=0,
                    )
                    chunks.append(jnp.dot(lhs, rhs, preferred_element_type=F32))
                for side in range(2):
                    place = (tiles - 1 - w - side) * PARTS
                    for t in range(LINE_RUN):
                        row = t * LANES + place
                        gate_rows[i, row : row + PARTS, :] = gates[side][t * PARTS : (t + 1) * PARTS]
                        r = side * LANES // 2 + 8 * t
                        within = reached < LANES - t
                        halves = []
                        for products in chunks:
                            close, far = products[r : r + 8, :LANES], products[r : r + 8, LANES:]
                            halves.append(
                                jnp.concatenate(
                                    [
                                        pltpu.roll(value, t, 1, stride=LINE_RUN, stride_axis=0)
                                        for value in (close, jnp.where(within, far, close))
                                    ],
                                    axis=1,
                                )
                            )
                        cost_rows[i, row : row + PARTS, :] = jnp.concatenate(halves, axis=0).astype(BF)

    x_base = width - 1 - LINE_RUN * iota((KEYS, LANES), 1)
    row = iota((KEYS, LANES), 0)
    reach = jnp.where(row >= 2 * GROUPS, 9, jnp.where(row >= GROUPS, 3, 1))
    room_left = x_base - reach
    room_right = x_base + reach - width
    unit = jnp.where(row >= 2 * GROUPS, SHARPNESS / math.log(2.0), 1.0)
    for i in range(PAIR):
        for two in range(LINE_RUN // 2):
            lo = 2 * two * LANES
            costs = dot_t(flip[...], cost_rows[i, lo : lo + 2 * LANES, :])
            logits = dot_t(guide[...], gate_rows[i, lo : lo + 2 * LANES, :])
            for side in range(2):
                t = 2 * two + side
                vol[i, t] = costs[:, side * LANES : (side + 1) * LANES]
                z = jnp.tanh(logits[:, side * LANES : (side + 1) * LANES]) + GATE_FLOOR
                taps = [z[m * KEYS : (m + 1) * KEYS] for m in range(3)]
                factor = unit / (taps[0] + taps[1] + taps[2])
                taps = [tap * factor for tap in taps]
                taps[0] = jnp.where(room_left >= t, taps[0], 0.0)
                taps[2] = jnp.where(room_right < t, taps[2], 0.0)
                for m in range(3):
                    wts[i, t, m * KEYS : (m + 1) * KEYS, :] = taps[m]

    for group in range(GROUPS):
        starts = [group * DGROUP + 8 * half for half in range(2)]
        for i in range(PAIR):
            v = [[vol[i, t, at : at + 8, :] for t in range(LINE_RUN)] for at in starts]
            for layer in range(LAYERS):
                s = 3**layer
                fresh = [[], []]
                for t in range(LINE_RUN):
                    rows = [k * KEYS + layer * GROUPS + group for k in range(3)]
                    w = [jnp.broadcast_to(wts[i, t, r : r + 1, :], (8, LANES)) for r in rows]
                    for half in range(2):
                        blk, r = divmod(t + s, LINE_RUN)
                        before = pltpu.roll(v[half][r], LANES - blk, 1) if blk else v[half][r]
                        blk, r = divmod(t - s, LINE_RUN)
                        after = pltpu.roll(v[half][r], -blk, 1) if blk else v[half][r]
                        fresh[half].append(w[0] * before + w[1] * v[half][t] + w[2] * after)
                v = fresh
            for half, at_row in enumerate(starts):
                for t in range(LINE_RUN):
                    done[i, t, at_row : at_row + 8, :] = v[half][t]

    sub = iota((8, LANES), 0)
    results = []
    for i in range(PAIR):
        totals = jnp.zeros((8, LANES), F32)
        moments = totals
        for s in range(LINE_RUN):
            t = LINE_RUN - 1 - s
            v = [done[i, t, 8 * j : 8 * j + 8, :] for j in range(DISP // 8)]
            top = v
            while len(top) > 1:
                top = [jnp.maximum(a, b) for a, b in zip(top[::2], top[1::2])] + top[len(top) & ~1 :]
            top = jnp.max(top[0], axis=0, keepdims=True)
            total = jnp.exp2(v[-1] - top)
            moment = total
            for j in range(DISP // 8 - 2, -1, -1):
                total = total + jnp.exp2(v[j] - top)
                if j:
                    moment = moment + total
            moment = 8.0 * moment + sub.astype(F32) * total
            totals = jnp.where(sub == s, jnp.sum(total, axis=0, keepdims=True), totals)
            moments = jnp.where(sub == s, jnp.sum(moment, axis=0, keepdims=True), moments)
        results.append((moments / totals + offs[i].astype(F32)) * (1.0 / DISP))
    both = jnp.concatenate(results, axis=0)
    high = both.astype(BF)
    left = both - high.astype(F32)
    middle = left.astype(BF)
    low = (left - middle.astype(F32)).astype(BF)
    parts = jnp.dot(
        jnp.concatenate([high, middle, low], axis=0), spread[...], preferred_element_type=F32
    )
    size = PAIR * LINE_RUN
    parts = parts[:size] + parts[size : 2 * size] + parts[2 * size :]
    wanted = iota((LINE_RUN, width), 0) == (iota((LINE_RUN, width), 1) & (LINE_RUN - 1))
    for i in range(PAIR):
        part = jnp.where(wanted, parts[i * LINE_RUN : (i + 1) * LINE_RUN], 0.0)
        out[i : i + 1, :] = jnp.sum(part, axis=0, keepdims=True)


def lines_plan(features, valid_cols, offsets, guide_weight):
    n = lax.axis_size("cols")
    devices = 2 * n
    width = n * BLOCK
    rows = PAIR * CHANNELS
    own = features.reshape(devices, rows, BLOCK)
    pieces = [None] * devices
    plain, gone = (), ()
    for key in (1, 7, 6, 4, 2, 5, 3, 0):
        masked = key % 2 and key > 1
        (piece,) = call(
            functools.partial(pack_kernel, key),
            [((rows + (MASKS if masked else 0), BLOCK), BF)],
            [], 0,
            (own,) + ((valid_cols,) + gone if masked else plain),
            1_000_000,
        )
        gone = (piece,)
        if not masked:
            plain = gone
        moves = [(i, i ^ key) for i in range(devices)]
        pieces[key] = lax.ppermute(piece, ("cols", "view"), moves) if key else piece
    consts = call(
        constants_kernel,
        [
            ((LANES, LANES), BF), ((LANES, LANES), BF), ((DISP, 2 * LANES), BF), ((3 * KEYS, LANES), BF),
            ((LANES, width), BF), (valid_cols.shape, F32),
        ],
        [], 1, (offsets, guide_weight, valid_cols), 1_000_000,
    )
    (rows,) = call(
        lines_kernel,
        [((PAIR, width), F32)],
        [
            pltpu.VMEM((devices, rows, BLOCK), BF),
            pltpu.VMEM((n,) + valid_cols.shape, F32),
            pltpu.VMEM((PAIR, LINE_RUN * LANES, LANES), BF),
            pltpu.VMEM((PAIR, LINE_RUN * LANES, 2 * LANES), BF),
            pltpu.VMEM((PAIR, LINE_RUN, DISP, LANES), F32),
            pltpu.VMEM((PAIR, LINE_RUN, DISP, LANES), F32),
            pltpu.VMEM((PAIR, LINE_RUN, 3 * KEYS, LANES), F32),
        ],
        1, (offsets, *consts, *pieces), 1_000_000_000,
    )
    others = lax.ppermute(rows, "view", [(0, 1), (1, 0)])
    first = lax.axis_index("view") == 0
    return jnp.where(first, jnp.concatenate([rows, others]), jnp.concatenate([others, rows]))[None]


def on_device(features, valid_cols, offsets, guide_weight):
    n = lax.axis_size("cols")
    lines = features.shape[1]
    if lines == 2 * PAIR * n and n * BLOCK == LINE_RUN * LANES:
        return lines_plan(features, valid_cols, offsets, guide_weight)
    return halo_plan(features, valid_cols, offsets, guide_weight)


def solution(mesh):
    return jax.shard_map(
        on_device,
        mesh=mesh,
        in_specs=(
            P("view", ("tiles", "lines"), None, "cols"),
            P(None, ("tiles", "cols")),
            P(("tiles", "lines")),
            P(),
        ),
        out_specs=P(("tiles", "lines"), "cols", None),
        check_vma=False,
    )
```

```python
import functools
import math

import jax
import jax.numpy as jnp
from jax import lax
from jax.experimental import pallas as pl
from jax.experimental.pallas import tpu as pltpu
from jax.sharding import PartitionSpec as P

DISP = 192
DGROUP = 16
GROUPS = DISP // DGROUP
LAYERS = 3
SHARPNESS = 2.0
HALO = 32
LANES = 128
LINES = 8
CHANNELS = 64
BLOCK = 256
SPAN = BLOCK + HALO
PARTS = LANES // LINES
RUN = SPAN // PARTS
KEYS = 40
WIDE = BLOCK + LANES
SEC_ROWS = LINES * CHANNELS
QUAD_ROWS = SEC_ROWS // 2
MASK_AT = QUAD_ROWS + CHANNELS
PAYLOAD = MASK_AT + 16
QUAD = LINES // 2
QUAD_LANES = LANES // 2
PACK = LANES // HALO
CUT = 16

BF = jnp.bfloat16
F32 = jnp.float32


def iota(shape, dim):
    return lax.broadcasted_iota(jnp.int32, shape, dim)


def dot_t(a, b):
    return lax.dot_general(a, b, (((1,), (1,)), ((), ())), preferred_element_type=F32)


def call(kernel, outs, scratch, smem, args, flops=0, space=pltpu.VMEM, limit=24, to=None):
    specs = [pl.BlockSpec(memory_space=pltpu.SMEM)] * smem
    specs += [pl.BlockSpec(memory_space=space)] * (len(args) - smem)
    return pl.pallas_call(
        kernel,
        out_shape=[jax.ShapeDtypeStruct(shape, dtype) for shape, dtype in outs],
        in_specs=specs,
        out_specs=[pl.BlockSpec(memory_space=to or space)] * len(outs),
        scratch_shapes=scratch,
        compiler_params=pltpu.CompilerParams(vmem_limit_bytes=limit * 1024 * 1024),
        cost_estimate=pl.CostEstimate(flops=flops, bytes_accessed=1_000_000, transcendentals=0),
    )(*args)


def spread_guide(guide):
    keys = LAYERS * 3 * GROUPS
    row = iota((3 * KEYS, keys), 0)
    tap = jnp.where(row >= KEYS, 1, 0) + jnp.where(row >= 2 * KEYS, 1, 0)
    row = row - KEYS * tap
    layer = jnp.where(row >= GROUPS, 1, 0) + jnp.where(row >= 2 * GROUPS, 1, 0)
    key = 2 * GROUPS * layer + GROUPS * tap + row
    chosen = jnp.where((iota((3 * KEYS, keys), 1) == key) & (row < 3 * GROUPS), 1.0, 0.0).astype(BF)
    guide_t = dot_t(chosen, guide).astype(BF)
    return jnp.concatenate([guide_t, guide_t], axis=1)


def normalise(z, wts, t, room_left, room_right):
    z = (0.55 + 0.45 * jnp.tanh(0.5 * z)).astype(BF).astype(F32)
    taps = [z[k * KEYS : (k + 1) * KEYS] for k in range(3)]
    scale = 1.0 / (taps[0] + taps[1] + taps[2])
    wts[t, 0:KEYS, :] = jnp.where(room_left >= t, taps[0] * scale, 0.0)
    wts[t, KEYS : 2 * KEYS, :] = taps[1] * scale
    wts[t, 2 * KEYS : 3 * KEYS, :] = jnp.where(room_right < t, taps[2] * scale, 0.0)


def prefetch_kernel(own, valid, guide, own_out, masks, perm, flip, guide_out, valid_in, guide_in, sems):
    copies = [
        pltpu.make_async_copy(src, dst, sems.at[i])
        for i, (src, dst) in enumerate([(own, own_out), (guide, guide_in), (valid, valid_in)])
    ]
    for copy in copies:
        copy.start()
    perm[...] = jnp.where(
        iota((SPAN, WIDE), 1) == WIDE - 1 - iota((SPAN, WIDE), 0), 1.0, 0.0
    ).astype(BF)
    back = 2 * LANES - 1 - iota((DISP, 2 * LANES), 0)
    flip[...] = jnp.where(iota((DISP, 2 * LANES), 1) == back, 1.0, 0.0).astype(BF)

    copies[1].wait()
    guide_out[...] = spread_guide(guide_in[...])
    copies[2].wait()
    masks[...] = valid_in[...].astype(F32)
    copies[0].wait()


def payload_kernel(own, other, masks, first, second, ref_own):
    view = lax.axis_index("view")
    first_view = view == 0
    sec_mask = masks[1:2, :].astype(BF)
    lane = iota((CHANNELS, LANES), 1)
    tails = []
    for line in range(LINES):
        at = view * LINES + line
        mine, theirs = own[at], other[at]
        lo = line * CHANNELS
        dest, start = (first, lo) if line < QUAD else (second, lo - QUAD_ROWS)
        dest[start : start + CHANNELS, :] = jnp.where(first_view, theirs, mine) * sec_mask
        ref = jnp.where(first_view, mine, theirs)
        ref_own[lo : lo + CHANNELS, :] = ref
        tail = ref[:, BLOCK - LANES :].astype(F32)
        slot = line % PACK
        turn = (HALO * (slot + 1)) % LANES
        if turn:
            tail = pltpu.roll(tail, turn, 1)
        if slot:
            tails[-1] = jnp.where(lane >= HALO * slot, tail, tails[-1])
        else:
            tails.append(tail)
    for i, tail in enumerate(tails):
        first[QUAD_ROWS:MASK_AT, i * LANES : (i + 1) * LANES] = tail.astype(BF)
    first[MASK_AT:, :] = jnp.broadcast_to(masks[0:1, :], (16, BLOCK)).astype(BF)


def shifted(left, mine, lo, off):
    ch_lane = iota((CHANNELS, LANES), 1)
    tiles = [
        src[lo : lo + CHANNELS, i * LANES : (i + 1) * LANES].astype(F32)
        for src in (left, mine)
        for i in range(2)
    ]
    tiles = [pltpu.roll(tile, off, 1) for tile in tiles]
    tiles = [jnp.where(ch_lane < off, tiles[max(i - 1, 0)], tiles[i]).astype(BF) for i in range(4)]
    return jnp.concatenate(tiles, axis=1)


def line_costs(lhs, rhs, slot, skew, cost_rows):
    diagonal = iota((8, LANES), 1) - iota((8, LANES), 0)
    for chunk in range(3):
        rows = min(LANES, SPAN - chunk * LANES)
        first = max(1 - chunk, 0)
        last = 3 - chunk
        products = jnp.dot(
            lhs[chunk * LANES : chunk * LANES + rows],
            rhs[:, first * LANES : (last + 1) * LANES],
            preferred_element_type=F32,
        )
        for j in range(rows // 8):
            tiles = [
                pltpu.roll(
                    products[8 * j : 8 * j + 8, i * LANES : (i + 1) * LANES],
                    8 * j, 1, stride=1, stride_axis=0,
                )
                for i in range(last + 1 - first)
            ]
            if len(tiles) < 3:
                tiles = [tiles[0]] + tiles
            beyond = diagonal >= 8 * j
            at = chunk * LANES + 8 * j
            skew[slot, 0, at : at + 8, :] = jnp.where(beyond, tiles[1], tiles[0])
            skew[slot, 1, at : at + 8, :] = jnp.where(beyond, tiles[2], tiles[1])
    for t in range(RUN):
        at = t * QUAD_LANES + slot * PARTS
        for v in range(2):
            cost_rows[at : at + PARTS, v * LANES : (v + 1) * LANES] = skew[
                slot, v, pl.ds(t, PARTS, stride=RUN), :
            ].astype(BF)


def early_kernel(
    offsets, ref_own, mine, left, masks, perm, guide, wts, cost_rows, lhs_out,
    ref_rows, ref_cols, gate_rows, skew
):
    base = lax.axis_index("view") * LINES
    low = jnp.where(lax.axis_index("cols") == 0, HALO, 0)
    for line in range(LINES):
        lo = line * CHANNELS
        ref_rows[lo : lo + CHANNELS, LANES:] = ref_own[lo : lo + CHANNELS, :]
        half = line // PACK
        packed = left[QUAD_ROWS:MASK_AT, half * LANES : (half + 1) * LANES].astype(F32)
        turn = (LANES - HALO) - HALO * (line % PACK)
        if turn:
            packed = pltpu.roll(packed, turn, 1)
        ref_rows[lo : lo + CHANNELS, :LANES] = packed.astype(BF)

    mask_left = left[MASK_AT : MASK_AT + 1, BLOCK - LANES :].astype(F32)
    ref_mask = jnp.concatenate([mask_left, masks[0:1, :]], axis=1)
    ref_mask = jnp.broadcast_to(ref_mask * (1.0 / math.sqrt(CHANNELS)), (LANES, WIDE))
    mask_cols = dot_t(perm[...], ref_mask.astype(BF))
    half_lane = iota((PARTS, LANES), 1) < CHANNELS
    span_lane = iota((SPAN, LANES), 1) < CHANNELS

    for quad in range(LINES // QUAD):
        ref_t = dot_t(perm[...], ref_rows[quad * QUAD_ROWS : (quad + 1) * QUAD_ROWS, :])
        for pair in range(QUAD // 2):
            cols = ref_t[:, pair * LANES : (pair + 1) * LANES]
            slot = quad * 2 + pair
            ref_cols[slot] = cols
            masked = cols * mask_cols
            if quad == 0:
                rhs = jnp.concatenate(
                    [
                        shifted(left, mine, line * CHANNELS, offsets[base + line])
                        for line in (2 * slot, 2 * slot + 1)
                    ],
                    axis=0,
                )
            for side in range(2):
                line = 2 * slot + side
                for t in range(RUN):
                    picked = ref_cols[slot, pl.ds(t, PARTS, stride=RUN), :]
                    picked = jnp.where(half_lane if side == 0 else ~half_lane, picked, 0.0)
                    at = t * LANES + line * PARTS
                    gate_rows[at : at + PARTS, :] = picked.astype(BF)
                lhs = jnp.where(span_lane if side == 0 else ~span_lane, masked, 0.0).astype(BF)
                if quad == 0:
                    line_costs(lhs, rhs, line, skew, cost_rows)
                else:
                    lhs_out[line - QUAD] = lhs

    place = iota((KEYS, LANES), 1)
    x_base = SPAN - 1 - RUN * (place & (PARTS - 1))
    row = iota((KEYS, LANES), 0)
    reach = jnp.where(row >= 2 * GROUPS, 9, jnp.where(row >= GROUPS, 3, 1))
    room_left = x_base - reach - low
    room_right = x_base + reach - SPAN
    for two in range(RUN // 2):
        at = 2 * two * LANES
        logits = dot_t(guide[...], gate_rows[at : at + 2 * LANES, :])
        for i in range(2):
            t = 2 * two + i
            normalise(logits[:, i * LANES : (i + 1) * LANES], wts, t, room_left, room_right)


def late_kernel(
    offsets, mine, left, lhs, early_rows, wts, flip, out, skew, cost_rows, vol, vals, turned
):
    base = lax.axis_index("view") * LINES
    for pair in range(QUAD // 2):
        rhs = jnp.concatenate(
            [
                shifted(left, mine, line * CHANNELS, offsets[base + QUAD + line])
                for line in (2 * pair, 2 * pair + 1)
            ],
            axis=0,
        )
        for line in (2 * pair, 2 * pair + 1):
            line_costs(lhs[line], rhs, line, skew, cost_rows)

    for two in range(RUN // 2):
        rows = []
        for t in (2 * two, 2 * two + 1):
            for part in (early_rows, cost_rows):
                rows.append(part[t * QUAD_LANES : (t + 1) * QUAD_LANES, :])
        costs = dot_t(flip[...], jnp.concatenate(rows, axis=0))
        vol[2 * two] = costs[:, :LANES]
        vol[2 * two + 1] = costs[:, LANES:]

    def aggregate(group, carry):
        for half in range(2):
            at = pl.multiple_of(group * DGROUP + half * 8, 8)
            v = [vol[t, pl.ds(at, 8), :] for t in range(RUN)]
            for layer in range(LAYERS):
                s = 3**layer
                before = [v[t + s] if t + s < RUN else pltpu.roll(v[t + s - RUN], LANES - 1, 1) for t in range(RUN)]
                after = [v[t - s] if t >= s else pltpu.roll(v[t - s + RUN], 1, 1) for t in range(RUN)]
                fresh = []
                for t in range(RUN):
                    w = [wts[t, pl.ds(k * KEYS + layer * GROUPS + group, 1), :] for k in range(3)]
                    fresh.append(w[0] * before[t] + w[1] * v[t] + w[2] * after[t])
                v = fresh
            for t in range(RUN):
                vol[t, pl.ds(at, 8), :] = v[t]
        return carry

    lax.fori_loop(0, GROUPS, aggregate, 0)

    vals[...] = jnp.zeros((LANES, LANES), F32)
    sub = iota((8, LANES), 0).astype(F32)
    line_of = iota((1, LANES), 1) >> 4
    offs = jnp.zeros((1, LANES), F32)
    for line in range(LINES):
        offs = jnp.where(line_of == line, offsets[base + line].astype(F32), offs)

    def softmax(t, carry):
        v = [vol[t, 8 * i : 8 * i + 8, :] for i in range(DISP // 8)]
        top = v
        while len(top) > 1:
            top = [jnp.maximum(a, b) for a, b in zip(top[::2], top[1::2])] + top[len(top) & ~1 :]
        top = jnp.max(top[0], axis=0, keepdims=True)
        e = [jnp.exp(SHARPNESS * (a - top)) for a in v]
        total = e[0]
        moment = jnp.zeros((8, LANES), F32)
        for i in range(1, DISP // 8):
            total = total + e[i]
            moment = moment + float(8 * i) * e[i]
        moment = jnp.sum(moment + sub * total, axis=0, keepdims=True)
        total = jnp.sum(total, axis=0, keepdims=True)
        vals[pl.ds(RUN - 1 - t, 1), :] = (moment / total + offs) * (1.0 / DISP)
        return carry

    lax.fori_loop(0, RUN, softmax, 0)

    turned[...] = jnp.transpose(vals[...])
    lane = iota((8, LANES), 1)
    result = [jnp.zeros((8, LANES), F32) for _ in range(WIDE // LANES)]
    for part in range(PARTS):
        piece = turned[pl.ds(part, LINES, stride=PARTS), :]
        start = (RUN * (PARTS - 1 - part) - HALO) % WIDE
        tile, turn = divmod(start, LANES)
        if turn:
            piece = pltpu.roll(piece, turn, 1)
        if turn + RUN > LANES:
            after = (tile + 1) % len(result)
            result[after] = result[after] + jnp.where(lane < turn, piece, 0.0)
            piece = jnp.where(lane >= turn, piece, 0.0)
        result[tile] = result[tile] + piece
    for tile, value in enumerate(result):
        out[:, tile * LANES : (tile + 1) * LANES] = value


def join(pieces, sub, n):
    block = lax.axis_index("cols")
    pieces = pieces.reshape(n, 2, LINES, WIDE)
    start = (0, block // (n // 2), (block % (n // 2)) * sub, 0)
    pieces = lax.dynamic_slice(pieces, start, (n, 1, sub, WIDE))[:, 0]
    main = pieces[:, :, :BLOCK]
    tail = jnp.pad(pieces[1:, :, BLOCK:], ((0, 1), (0, 0), (LANES, 0)))
    place = (n, sub, BLOCK)
    keep = (iota(place, 2) < BLOCK - CUT) | (iota(place, 0) == n - 1)
    joined = jnp.where(keep, main, tail)
    return jnp.transpose(joined, (1, 0, 2)).reshape(1, sub, n * BLOCK)


def halo_plan(features, valid_cols, offsets, guide_weight):
    own = features[0]
    n = lax.axis_size("cols")
    right = [(c, c + 1) for c in range(n - 1)]
    other = lax.ppermute(own, "view", [(0, 1), (1, 0)])
    near, masks, perm, flip, guide = call(
        prefetch_kernel,
        [(own.shape, BF), (valid_cols.shape, F32), ((SPAN, WIDE), BF), ((DISP, 2 * LANES), BF), ((3 * KEYS, LANES), BF)],
        [pltpu.VMEM(valid_cols.shape, jnp.int32), pltpu.VMEM(guide_weight.shape, BF), pltpu.SemaphoreType.DMA((3,))],
        0, (own, valid_cols, guide_weight), 100_000_000, pl.ANY, 24, pltpu.VMEM,
    )
    first, second, ref_own = call(
        payload_kernel,
        [((PAYLOAD, BLOCK), BF), ((QUAD_ROWS, BLOCK), BF), ((SEC_ROWS, BLOCK), BF)],
        [], 0, (near, other, masks),
    )
    left_first = lax.ppermute(first, "cols", right)
    left_second = lax.ppermute(second, "cols", right)
    quad_rows = (RUN * QUAD_LANES, 2 * LANES)
    skew = pltpu.VMEM((QUAD, 2, SPAN, LANES), F32)
    square = pltpu.VMEM((LANES, LANES), F32)
    wts, early_rows, lhs = call(
        early_kernel,
        [((RUN, 3 * KEYS, LANES), F32), (quad_rows, BF), ((QUAD, SPAN, LANES), BF)],
        [pltpu.VMEM((SEC_ROWS, WIDE), BF), pltpu.VMEM((QUAD, SPAN, LANES), F32), pltpu.VMEM((RUN * LANES, LANES), BF), skew],
        1, (offsets, ref_own, first, left_first, masks, perm, guide), 1_000_000_000,
    )
    (result,) = call(
        late_kernel,
        [((LINES, WIDE), F32)],
        [skew, pltpu.VMEM(quad_rows, BF), pltpu.VMEM((RUN, DISP, LANES), F32), square, square],
        1, (offsets, second, left_second, lhs, early_rows, wts, flip), 1_000_000_000,
    )
    copies = jnp.broadcast_to(result[None], (2 * n, LINES, WIDE))
    pieces = lax.all_to_all(copies, ("cols", "view"), split_axis=0, concat_axis=0, tiled=True)
    return join(pieces, own.shape[0] // n, n)


LINE_RUN = 8
PAIR = 2
LINE_PARTS = LANES


MASKS = 8
GATE_FLOOR = 11.0 / 9.0


def pack_kernel(key, own, *rest):
    out = rest[-1]
    me = 2 * lax.axis_index("cols") + lax.axis_index("view")
    rows = PAIR * CHANNELS
    out[:rows, :] = own[me ^ key]
    if out.shape[0] > rows:
        masks = rest[0][...].astype(F32)
        out[rows:, :] = jnp.where(
            iota((MASKS, BLOCK), 0) < MASKS // 2, masks[0:1, :], masks[1:2, :]
        ).astype(BF)


def constants_kernel(offsets, guide, valid, order, order_band, flip, guide_out, spread, masks):
    masks[...] = valid[...].astype(F32)
    row = iota((LANES, LANES), 0)
    from_lane = LANES - 1 - LINE_RUN * (row & (PARTS - 1)) - (row >> 4)
    order[...] = jnp.where(iota((LANES, LANES), 1) == from_lane, 1.0, 0.0).astype(BF)
    from_lane = LANES - 1 - (row & 64) - LINE_RUN * (row & 7) - ((row >> 3) & 7)
    order_band[...] = jnp.where(iota((LANES, LANES), 1) == from_lane, 1.0, 0.0).astype(BF)
    back = 2 * LANES - 1 - iota((DISP, 2 * LANES), 0)
    flip[...] = jnp.where(iota((DISP, 2 * LANES), 1) == back, 1.0, 0.0).astype(BF)
    guide_out[...] = spread_guide(guide[...]) * 0.5
    block_of = LANES - 1 - (iota(spread.shape, 1) >> 3)
    spread[...] = jnp.where(iota(spread.shape, 0) == block_of, 1.0, 0.0).astype(BF)


def lines_kernel(offsets, order, order_band, flip, guide, spread, *rest):
    pieces, (out, blocks, valid, gate_rows, cost_rows, vol, done, wts) = rest[:-8], rest[-8:]
    near, pieces = pieces[0], pieces[1:]
    tiles = len(pieces)
    width = tiles * LANES
    me = 2 * lax.axis_index("cols") + lax.axis_index("view")
    rows = PAIR * CHANNELS
    for key, piece in enumerate(pieces):
        blocks[me ^ key] = piece[:rows, :]
        if piece.shape[0] > rows:
            masks = piece[rows:, :].astype(F32)
            valid[(me ^ key) // 2] = jnp.concatenate([masks[0:1], masks[MASKS // 2 : MASKS // 2 + 1]], axis=0)
    valid[me // 2] = near[...]
    at = PAIR * me
    offs = [offsets[at + i] for i in range(PAIR)]
    ch_lane = iota((CHANNELS, LANES), 1)
    low_lane = ch_lane < LANES // 2
    low_half = iota((LANES, LANES), 1) < CHANNELS
    reached = iota((8, LANES), 1) + LINE_RUN * iota((8, LANES), 0)
    scale = 1.0 / math.sqrt(CHANNELS)
    empty = jnp.zeros((CHANNELS, LANES), F32)

    def mask_of(view, w):
        lo = (w % 2) * LANES
        return valid[w // 2, view : view + 1, lo : lo + LANES]

    def correlate(i):
        def tile_of(view, w):
            lo = (w % 2) * LANES
            return blocks[2 * (w // 2) + view, i * CHANNELS : (i + 1) * CHANNELS, lo : lo + LANES]

        off = offs[i]
        rolled = [pltpu.roll(tile_of(1, w).astype(F32) * mask_of(1, w), off, 1) for w in range(tiles)]
        line = [empty, empty]
        for w in range(tiles):
            line.append(jnp.where(ch_lane < off, rolled[w - 1] if w else empty, rolled[w]))
        turned = [empty] + [pltpu.roll(tile, LANES // 2, 1) if w else tile for w, tile in enumerate(line[1:])]
        shifted = [tile.astype(BF) for tile in line]
        halfway = [jnp.where(low_lane, a, b).astype(BF) for a, b in zip(turned, turned[1:])]

        for quad in range(tiles // 4):
            refs = [tile_of(0, 4 * quad + q) for q in range(4)]
            masked = [refs[q] * (mask_of(0, 4 * quad + q) * scale).astype(BF) for q in range(4)]
            cols = dot_t(order[...], jnp.concatenate(refs, axis=0))
            masked = dot_t(order_band[...], jnp.concatenate(masked, axis=0))
            for two in range(2):
                w = 4 * quad + 2 * two
                raw = cols[:, two * LANES : (two + 1) * LANES]
                pair = masked[:, two * LANES : (two + 1) * LANES]
                gates = [jnp.where(low_half, raw, 0.0).astype(BF), jnp.where(low_half, 0.0, raw).astype(BF)]
                sides = [jnp.where(low_half, pair, 0.0).astype(BF), jnp.where(low_half, 0.0, pair).astype(BF)]
                chunks = []
                for half, source, first in ((0, shifted, w + 1), (1, halfway, w)):
                    lo = half * LANES // 2
                    lhs = jnp.concatenate([side[lo : lo + LANES // 2] for side in sides], axis=0)
                    rhs = jnp.concatenate(
                        [jnp.concatenate(source[first + side : first + side + 2], axis=1) for side in range(2)],
                        axis=0,
                    )
                    chunks.append(jnp.dot(lhs, rhs, preferred_element_type=F32))
                for side in range(2):
                    place = (tiles - 1 - w - side) * PARTS
                    for t in range(LINE_RUN):
                        row = t * LANES + place
                        gate_rows[i, row : row + PARTS, :] = gates[side][t * PARTS : (t + 1) * PARTS]
                        r = side * LANES // 2 + 8 * t
                        within = reached < LANES - t
                        halves = []
                        for products in chunks:
                            close, far = products[r : r + 8, :LANES], products[r : r + 8, LANES:]
                            halves.append(
                                jnp.concatenate(
                                    [
                                        pltpu.roll(value, t, 1, stride=LINE_RUN, stride_axis=0)
                                        for value in (close, jnp.where(within, far, close))
                                    ],
                                    axis=1,
                                )
                            )
                        cost_rows[i, row : row + PARTS, :] = jnp.concatenate(halves, axis=0).astype(BF)
                yield

    x_base = width - 1 - LINE_RUN * iota((KEYS, LANES), 1)
    row = iota((KEYS, LANES), 0)
    reach = jnp.where(row >= 2 * GROUPS, 9, jnp.where(row >= GROUPS, 3, 1))
    room_left = x_base - reach
    room_right = x_base + reach - width
    unit = jnp.where(row >= 2 * GROUPS, SHARPNESS / math.log(2.0), 1.0)
    def prepare(i):
        for two in range(LINE_RUN // 2):
            lo = 2 * two * LANES
            costs = dot_t(flip[...], cost_rows[i, lo : lo + 2 * LANES, :])
            logits = dot_t(guide[...], gate_rows[i, lo : lo + 2 * LANES, :])
            for side in range(2):
                t = 2 * two + side
                vol[i, t] = costs[:, side * LANES : (side + 1) * LANES]
                z = jnp.tanh(logits[:, side * LANES : (side + 1) * LANES]) + GATE_FLOOR
                taps = [z[m * KEYS : (m + 1) * KEYS] for m in range(3)]
                factor = unit / (taps[0] + taps[1] + taps[2])
                taps = [tap * factor for tap in taps]
                taps[0] = jnp.where(room_left >= t, taps[0], 0.0)
                taps[2] = jnp.where(room_right < t, taps[2], 0.0)
                for m in range(3):
                    wts[i, t, m * KEYS : (m + 1) * KEYS, :] = taps[m]
            yield

    def aggregate(i):
        for group in range(GROUPS):
            starts = [group * DGROUP + 8 * half for half in range(2)]
            v = [[vol[i, t, at : at + 8, :] for t in range(LINE_RUN)] for at in starts]
            for layer in range(LAYERS):
                s = 3**layer
                fresh = [[], []]
                for t in range(LINE_RUN):
                    rows = [k * KEYS + layer * GROUPS + group for k in range(3)]
                    w = [jnp.broadcast_to(wts[i, t, r : r + 1, :], (8, LANES)) for r in rows]
                    for half in range(2):
                        blk, r = divmod(t + s, LINE_RUN)
                        before = pltpu.roll(v[half][r], LANES - blk, 1) if blk else v[half][r]
                        blk, r = divmod(t - s, LINE_RUN)
                        after = pltpu.roll(v[half][r], -blk, 1) if blk else v[half][r]
                        fresh[half].append(w[0] * before + w[1] * v[half][t] + w[2] * after)
                v = fresh
            for half, at_row in enumerate(starts):
                for t in range(LINE_RUN):
                    done[i, t, at_row : at_row + 8, :] = v[half][t]
            yield

    sub = iota((8, LANES), 0)
    results = []

    def softmax(i):
        totals = jnp.zeros((8, LANES), F32)
        moments = totals
        for s in range(LINE_RUN):
            t = LINE_RUN - 1 - s
            v = [done[i, t, 8 * j : 8 * j + 8, :] for j in range(DISP // 8)]
            top = v
            while len(top) > 1:
                top = [jnp.maximum(a, b) for a, b in zip(top[::2], top[1::2])] + top[len(top) & ~1 :]
            top = jnp.max(top[0], axis=0, keepdims=True)
            total = jnp.exp2(v[-1] - top)
            moment = total
            for j in range(DISP // 8 - 2, -1, -1):
                total = total + jnp.exp2(v[j] - top)
                if j:
                    moment = moment + total
            moment = 8.0 * moment + sub.astype(F32) * total
            totals = jnp.where(sub == s, jnp.sum(total, axis=0, keepdims=True), totals)
            moments = jnp.where(sub == s, jnp.sum(moment, axis=0, keepdims=True), moments)
            yield
        results.append((moments / totals + offs[i].astype(F32)) * (1.0 / DISP))
    def beside(first, second, count):
        for _ in first:
            for _ in range(count):
                next(second, None)
        for _ in second:
            pass

    beside(correlate(0), iter(()), 0)
    beside(prepare(0), iter(()), 0)
    beside(correlate(1), aggregate(0), 3)
    beside(prepare(1), softmax(0), 2)
    beside(aggregate(1), iter(()), 0)
    beside(softmax(1), iter(()), 0)
    both = jnp.concatenate(results, axis=0)
    high = both.astype(BF)
    left = both - high.astype(F32)
    middle = left.astype(BF)
    low = (left - middle.astype(F32)).astype(BF)
    parts = jnp.dot(
        jnp.concatenate([high, middle, low], axis=0), spread[...], preferred_element_type=F32
    )
    size = PAIR * LINE_RUN
    parts = parts[:size] + parts[size : 2 * size] + parts[2 * size :]
    wanted = iota((LINE_RUN, width), 0) == (iota((LINE_RUN, width), 1) & (LINE_RUN - 1))
    for i in range(PAIR):
        part = jnp.where(wanted, parts[i * LINE_RUN : (i + 1) * LINE_RUN], 0.0)
        out[i : i + 1, :] = jnp.sum(part, axis=0, keepdims=True)


def lines_plan(features, valid_cols, offsets, guide_weight):
    n = lax.axis_size("cols")
    devices = 2 * n
    width = n * BLOCK
    rows = PAIR * CHANNELS
    own = features.reshape(devices, rows, BLOCK)
    pieces = [None] * devices
    gone = ()
    for key in (1, 2, 6, 4, 7, 5, 3, 0):
        masked = key % 2 and key > 1
        (piece,) = call(
            functools.partial(pack_kernel, key),
            [((rows + (MASKS if masked else 0), BLOCK), BF)],
            [], 0,
            (own,) + ((valid_cols,) if masked else ()) + gone,
            1_000_000,
        )
        gone = (piece,)
        moves = [(i, i ^ key) for i in range(devices)]
        pieces[key] = lax.ppermute(piece, ("cols", "view"), moves) if key else piece
    consts = call(
        constants_kernel,
        [
            ((LANES, LANES), BF), ((LANES, LANES), BF), ((DISP, 2 * LANES), BF), ((3 * KEYS, LANES), BF),
            ((LANES, width), BF), (valid_cols.shape, F32),
        ],
        [], 1, (offsets, guide_weight, valid_cols), 1_000_000,
    )
    (rows,) = call(
        lines_kernel,
        [((PAIR, width), F32)],
        [
            pltpu.VMEM((devices, rows, BLOCK), BF),
            pltpu.VMEM((n,) + valid_cols.shape, F32),
            pltpu.VMEM((PAIR, LINE_RUN * LANES, LANES), BF),
            pltpu.VMEM((PAIR, LINE_RUN * LANES, 2 * LANES), BF),
            pltpu.VMEM((PAIR, LINE_RUN, DISP, LANES), F32),
            pltpu.VMEM((PAIR, LINE_RUN, DISP, LANES), F32),
            pltpu.VMEM((PAIR, LINE_RUN, 3 * KEYS, LANES), F32),
        ],
        1, (offsets, *consts, *pieces), 1_000_000_000,
    )
    others = lax.ppermute(rows, "view", [(0, 1), (1, 0)])
    first = lax.axis_index("view") == 0
    return jnp.where(first, jnp.concatenate([rows, others]), jnp.concatenate([others, rows]))[None]


def on_device(features, valid_cols, offsets, guide_weight):
    n = lax.axis_size("cols")
    lines = features.shape[1]
    if lines == 2 * PAIR * n and n * BLOCK == LINE_RUN * LANES:
        return lines_plan(features, valid_cols, offsets, guide_weight)
    return halo_plan(features, valid_cols, offsets, guide_weight)


def solution(mesh):
    return jax.shard_map(
        on_device,
        mesh=mesh,
        in_specs=(
            P("view", ("tiles", "lines"), None, "cols"),
            P(None, ("tiles", "cols")),
            P(("tiles", "lines")),
            P(),
        ),
        out_specs=P(("tiles", "lines"), "cols", None),
        check_vma=False,
    )
```

```python
import functools
import math

import jax
import jax.numpy as jnp
from jax import lax
from jax.experimental import pallas as pl
from jax.experimental.pallas import tpu as pltpu
from jax.sharding import PartitionSpec as P

DISP = 192
DGROUP = 16
GROUPS = DISP // DGROUP
LAYERS = 3
SHARPNESS = 2.0
HALO = 32
LANES = 128
LINES = 8
CHANNELS = 64
BLOCK = 256
SPAN = BLOCK + HALO
PARTS = LANES // LINES
RUN = SPAN // PARTS
KEYS = 40
WIDE = BLOCK + LANES
SEC_ROWS = LINES * CHANNELS
QUAD_ROWS = SEC_ROWS // 2
MASK_AT = QUAD_ROWS + CHANNELS
PAYLOAD = MASK_AT + 16
QUAD = LINES // 2
QUAD_LANES = LANES // 2
PACK = LANES // HALO
CUT = 16

BF = jnp.bfloat16
F32 = jnp.float32


def iota(shape, dim):
    return lax.broadcasted_iota(jnp.int32, shape, dim)


def dot_t(a, b):
    return lax.dot_general(a, b, (((1,), (1,)), ((), ())), preferred_element_type=F32)


def call(kernel, outs, scratch, smem, args, flops=0, space=pltpu.VMEM, limit=24, to=None):
    specs = [pl.BlockSpec(memory_space=pltpu.SMEM)] * smem
    specs += [pl.BlockSpec(memory_space=space)] * (len(args) - smem)
    return pl.pallas_call(
        kernel,
        out_shape=[jax.ShapeDtypeStruct(shape, dtype) for shape, dtype in outs],
        in_specs=specs,
        out_specs=[pl.BlockSpec(memory_space=to or space)] * len(outs),
        scratch_shapes=scratch,
        compiler_params=pltpu.CompilerParams(vmem_limit_bytes=limit * 1024 * 1024),
        cost_estimate=pl.CostEstimate(flops=flops, bytes_accessed=1_000_000, transcendentals=0),
    )(*args)


def spread_guide(guide):
    keys = LAYERS * 3 * GROUPS
    row = iota((3 * KEYS, keys), 0)
    tap = jnp.where(row >= KEYS, 1, 0) + jnp.where(row >= 2 * KEYS, 1, 0)
    row = row - KEYS * tap
    layer = jnp.where(row >= GROUPS, 1, 0) + jnp.where(row >= 2 * GROUPS, 1, 0)
    key = 2 * GROUPS * layer + GROUPS * tap + row
    chosen = jnp.where((iota((3 * KEYS, keys), 1) == key) & (row < 3 * GROUPS), 1.0, 0.0).astype(BF)
    guide_t = dot_t(chosen, guide).astype(BF)
    return jnp.concatenate([guide_t, guide_t], axis=1)


def normalise(z, wts, t, room_left, room_right):
    z = (0.55 + 0.45 * jnp.tanh(0.5 * z)).astype(BF).astype(F32)
    taps = [z[k * KEYS : (k + 1) * KEYS] for k in range(3)]
    scale = 1.0 / (taps[0] + taps[1] + taps[2])
    wts[t, 0:KEYS, :] = jnp.where(room_left >= t, taps[0] * scale, 0.0)
    wts[t, KEYS : 2 * KEYS, :] = taps[1] * scale
    wts[t, 2 * KEYS : 3 * KEYS, :] = jnp.where(room_right < t, taps[2] * scale, 0.0)


def prefetch_kernel(own, valid, guide, own_out, masks, perm, flip, guide_out, valid_in, guide_in, sems):
    copies = [
        pltpu.make_async_copy(src, dst, sems.at[i])
        for i, (src, dst) in enumerate([(own, own_out), (guide, guide_in), (valid, valid_in)])
    ]
    for copy in copies:
        copy.start()
    perm[...] = jnp.where(
        iota((SPAN, WIDE), 1) == WIDE - 1 - iota((SPAN, WIDE), 0), 1.0, 0.0
    ).astype(BF)
    back = 2 * LANES - 1 - iota((DISP, 2 * LANES), 0)
    flip[...] = jnp.where(iota((DISP, 2 * LANES), 1) == back, 1.0, 0.0).astype(BF)

    copies[1].wait()
    guide_out[...] = spread_guide(guide_in[...])
    copies[2].wait()
    masks[...] = valid_in[...].astype(F32)
    copies[0].wait()


def payload_kernel(own, other, masks, first, second, ref_own):
    view = lax.axis_index("view")
    first_view = view == 0
    sec_mask = masks[1:2, :].astype(BF)
    lane = iota((CHANNELS, LANES), 1)
    tails = []
    for line in range(LINES):
        at = view * LINES + line
        mine, theirs = own[at], other[at]
        lo = line * CHANNELS
        dest, start = (first, lo) if line < QUAD else (second, lo - QUAD_ROWS)
        dest[start : start + CHANNELS, :] = jnp.where(first_view, theirs, mine) * sec_mask
        ref = jnp.where(first_view, mine, theirs)
        ref_own[lo : lo + CHANNELS, :] = ref
        tail = ref[:, BLOCK - LANES :].astype(F32)
        slot = line % PACK
        turn = (HALO * (slot + 1)) % LANES
        if turn:
            tail = pltpu.roll(tail, turn, 1)
        if slot:
            tails[-1] = jnp.where(lane >= HALO * slot, tail, tails[-1])
        else:
            tails.append(tail)
    for i, tail in enumerate(tails):
        first[QUAD_ROWS:MASK_AT, i * LANES : (i + 1) * LANES] = tail.astype(BF)
    first[MASK_AT:, :] = jnp.broadcast_to(masks[0:1, :], (16, BLOCK)).astype(BF)


def shifted(left, mine, lo, off):
    ch_lane = iota((CHANNELS, LANES), 1)
    tiles = [
        src[lo : lo + CHANNELS, i * LANES : (i + 1) * LANES].astype(F32)
        for src in (left, mine)
        for i in range(2)
    ]
    tiles = [pltpu.roll(tile, off, 1) for tile in tiles]
    tiles = [jnp.where(ch_lane < off, tiles[max(i - 1, 0)], tiles[i]).astype(BF) for i in range(4)]
    return jnp.concatenate(tiles, axis=1)


def line_costs(lhs, rhs, slot, skew, cost_rows):
    diagonal = iota((8, LANES), 1) - iota((8, LANES), 0)
    for chunk in range(3):
        rows = min(LANES, SPAN - chunk * LANES)
        first = max(1 - chunk, 0)
        last = 3 - chunk
        products = jnp.dot(
            lhs[chunk * LANES : chunk * LANES + rows],
            rhs[:, first * LANES : (last + 1) * LANES],
            preferred_element_type=F32,
        )
        for j in range(rows // 8):
            tiles = [
                pltpu.roll(
                    products[8 * j : 8 * j + 8, i * LANES : (i + 1) * LANES],
                    8 * j, 1, stride=1, stride_axis=0,
                )
                for i in range(last + 1 - first)
            ]
            if len(tiles) < 3:
                tiles = [tiles[0]] + tiles
            beyond = diagonal >= 8 * j
            at = chunk * LANES + 8 * j
            skew[slot, 0, at : at + 8, :] = jnp.where(beyond, tiles[1], tiles[0])
            skew[slot, 1, at : at + 8, :] = jnp.where(beyond, tiles[2], tiles[1])
    for t in range(RUN):
        at = t * QUAD_LANES + slot * PARTS
        for v in range(2):
            cost_rows[at : at + PARTS, v * LANES : (v + 1) * LANES] = skew[
                slot, v, pl.ds(t, PARTS, stride=RUN), :
            ].astype(BF)


def early_kernel(
    offsets, ref_own, mine, left, masks, perm, guide, wts, cost_rows, lhs_out,
    ref_rows, ref_cols, gate_rows, skew
):
    base = lax.axis_index("view") * LINES
    low = jnp.where(lax.axis_index("cols") == 0, HALO, 0)
    for line in range(LINES):
        lo = line * CHANNELS
        ref_rows[lo : lo + CHANNELS, LANES:] = ref_own[lo : lo + CHANNELS, :]
        half = line // PACK
        packed = left[QUAD_ROWS:MASK_AT, half * LANES : (half + 1) * LANES].astype(F32)
        turn = (LANES - HALO) - HALO * (line % PACK)
        if turn:
            packed = pltpu.roll(packed, turn, 1)
        ref_rows[lo : lo + CHANNELS, :LANES] = packed.astype(BF)

    mask_left = left[MASK_AT : MASK_AT + 1, BLOCK - LANES :].astype(F32)
    ref_mask = jnp.concatenate([mask_left, masks[0:1, :]], axis=1)
    ref_mask = jnp.broadcast_to(ref_mask * (1.0 / math.sqrt(CHANNELS)), (LANES, WIDE))
    mask_cols = dot_t(perm[...], ref_mask.astype(BF))
    half_lane = iota((PARTS, LANES), 1) < CHANNELS
    span_lane = iota((SPAN, LANES), 1) < CHANNELS

    for quad in range(LINES // QUAD):
        ref_t = dot_t(perm[...], ref_rows[quad * QUAD_ROWS : (quad + 1) * QUAD_ROWS, :])
        for pair in range(QUAD // 2):
            cols = ref_t[:, pair * LANES : (pair + 1) * LANES]
            slot = quad * 2 + pair
            ref_cols[slot] = cols
            masked = cols * mask_cols
            if quad == 0:
                rhs = jnp.concatenate(
                    [
                        shifted(left, mine, line * CHANNELS, offsets[base + line])
                        for line in (2 * slot, 2 * slot + 1)
                    ],
                    axis=0,
                )
            for side in range(2):
                line = 2 * slot + side
                for t in range(RUN):
                    picked = ref_cols[slot, pl.ds(t, PARTS, stride=RUN), :]
                    picked = jnp.where(half_lane if side == 0 else ~half_lane, picked, 0.0)
                    at = t * LANES + line * PARTS
                    gate_rows[at : at + PARTS, :] = picked.astype(BF)
                lhs = jnp.where(span_lane if side == 0 else ~span_lane, masked, 0.0).astype(BF)
                if quad == 0:
                    line_costs(lhs, rhs, line, skew, cost_rows)
                else:
                    lhs_out[line - QUAD] = lhs

    place = iota((KEYS, LANES), 1)
    x_base = SPAN - 1 - RUN * (place & (PARTS - 1))
    row = iota((KEYS, LANES), 0)
    reach = jnp.where(row >= 2 * GROUPS, 9, jnp.where(row >= GROUPS, 3, 1))
    room_left = x_base - reach - low
    room_right = x_base + reach - SPAN
    for two in range(RUN // 2):
        at = 2 * two * LANES
        logits = dot_t(guide[...], gate_rows[at : at + 2 * LANES, :])
        for i in range(2):
            t = 2 * two + i
            normalise(logits[:, i * LANES : (i + 1) * LANES], wts, t, room_left, room_right)


def late_kernel(
    offsets, mine, left, lhs, early_rows, wts, flip, out, skew, cost_rows, vol, vals, turned
):
    base = lax.axis_index("view") * LINES
    for pair in range(QUAD // 2):
        rhs = jnp.concatenate(
            [
                shifted(left, mine, line * CHANNELS, offsets[base + QUAD + line])
                for line in (2 * pair, 2 * pair + 1)
            ],
            axis=0,
        )
        for line in (2 * pair, 2 * pair + 1):
            line_costs(lhs[line], rhs, line, skew, cost_rows)

    for two in range(RUN // 2):
        rows = []
        for t in (2 * two, 2 * two + 1):
            for part in (early_rows, cost_rows):
                rows.append(part[t * QUAD_LANES : (t + 1) * QUAD_LANES, :])
        costs = dot_t(flip[...], jnp.concatenate(rows, axis=0))
        vol[2 * two] = costs[:, :LANES]
        vol[2 * two + 1] = costs[:, LANES:]

    def aggregate(group, carry):
        for half in range(2):
            at = pl.multiple_of(group * DGROUP + half * 8, 8)
            v = [vol[t, pl.ds(at, 8), :] for t in range(RUN)]
            for layer in range(LAYERS):
                s = 3**layer
                before = [v[t + s] if t + s < RUN else pltpu.roll(v[t + s - RUN], LANES - 1, 1) for t in range(RUN)]
                after = [v[t - s] if t >= s else pltpu.roll(v[t - s + RUN], 1, 1) for t in range(RUN)]
                fresh = []
                for t in range(RUN):
                    w = [wts[t, pl.ds(k * KEYS + layer * GROUPS + group, 1), :] for k in range(3)]
                    fresh.append(w[0] * before[t] + w[1] * v[t] + w[2] * after[t])
                v = fresh
            for t in range(RUN):
                vol[t, pl.ds(at, 8), :] = v[t]
        return carry

    lax.fori_loop(0, GROUPS, aggregate, 0)

    vals[...] = jnp.zeros((LANES, LANES), F32)
    sub = iota((8, LANES), 0).astype(F32)
    line_of = iota((1, LANES), 1) >> 4
    offs = jnp.zeros((1, LANES), F32)
    for line in range(LINES):
        offs = jnp.where(line_of == line, offsets[base + line].astype(F32), offs)

    def softmax(t, carry):
        v = [vol[t, 8 * i : 8 * i + 8, :] for i in range(DISP // 8)]
        top = v
        while len(top) > 1:
            top = [jnp.maximum(a, b) for a, b in zip(top[::2], top[1::2])] + top[len(top) & ~1 :]
        top = jnp.max(top[0], axis=0, keepdims=True)
        e = [jnp.exp(SHARPNESS * (a - top)) for a in v]
        total = e[0]
        moment = jnp.zeros((8, LANES), F32)
        for i in range(1, DISP // 8):
            total = total + e[i]
            moment = moment + float(8 * i) * e[i]
        moment = jnp.sum(moment + sub * total, axis=0, keepdims=True)
        total = jnp.sum(total, axis=0, keepdims=True)
        vals[pl.ds(RUN - 1 - t, 1), :] = (moment / total + offs) * (1.0 / DISP)
        return carry

    lax.fori_loop(0, RUN, softmax, 0)

    turned[...] = jnp.transpose(vals[...])
    lane = iota((8, LANES), 1)
    result = [jnp.zeros((8, LANES), F32) for _ in range(WIDE // LANES)]
    for part in range(PARTS):
        piece = turned[pl.ds(part, LINES, stride=PARTS), :]
        start = (RUN * (PARTS - 1 - part) - HALO) % WIDE
        tile, turn = divmod(start, LANES)
        if turn:
            piece = pltpu.roll(piece, turn, 1)
        if turn + RUN > LANES:
            after = (tile + 1) % len(result)
            result[after] = result[after] + jnp.where(lane < turn, piece, 0.0)
            piece = jnp.where(lane >= turn, piece, 0.0)
        result[tile] = result[tile] + piece
    for tile, value in enumerate(result):
        out[:, tile * LANES : (tile + 1) * LANES] = value


def join(pieces, sub, n):
    block = lax.axis_index("cols")
    pieces = pieces.reshape(n, 2, LINES, WIDE)
    start = (0, block // (n // 2), (block % (n // 2)) * sub, 0)
    pieces = lax.dynamic_slice(pieces, start, (n, 1, sub, WIDE))[:, 0]
    main = pieces[:, :, :BLOCK]
    tail = jnp.pad(pieces[1:, :, BLOCK:], ((0, 1), (0, 0), (LANES, 0)))
    place = (n, sub, BLOCK)
    keep = (iota(place, 2) < BLOCK - CUT) | (iota(place, 0) == n - 1)
    joined = jnp.where(keep, main, tail)
    return jnp.transpose(joined, (1, 0, 2)).reshape(1, sub, n * BLOCK)


def halo_plan(features, valid_cols, offsets, guide_weight):
    own = features[0]
    n = lax.axis_size("cols")
    right = [(c, c + 1) for c in range(n - 1)]
    other = lax.ppermute(own, "view", [(0, 1), (1, 0)])
    near, masks, perm, flip, guide = call(
        prefetch_kernel,
        [(own.shape, BF), (valid_cols.shape, F32), ((SPAN, WIDE), BF), ((DISP, 2 * LANES), BF), ((3 * KEYS, LANES), BF)],
        [pltpu.VMEM(valid_cols.shape, jnp.int32), pltpu.VMEM(guide_weight.shape, BF), pltpu.SemaphoreType.DMA((3,))],
        0, (own, valid_cols, guide_weight), 100_000_000, pl.ANY, 24, pltpu.VMEM,
    )
    first, second, ref_own = call(
        payload_kernel,
        [((PAYLOAD, BLOCK), BF), ((QUAD_ROWS, BLOCK), BF), ((SEC_ROWS, BLOCK), BF)],
        [], 0, (near, other, masks),
    )
    left_first = lax.ppermute(first, "cols", right)
    left_second = lax.ppermute(second, "cols", right)
    quad_rows = (RUN * QUAD_LANES, 2 * LANES)
    skew = pltpu.VMEM((QUAD, 2, SPAN, LANES), F32)
    square = pltpu.VMEM((LANES, LANES), F32)
    wts, early_rows, lhs = call(
        early_kernel,
        [((RUN, 3 * KEYS, LANES), F32), (quad_rows, BF), ((QUAD, SPAN, LANES), BF)],
        [pltpu.VMEM((SEC_ROWS, WIDE), BF), pltpu.VMEM((QUAD, SPAN, LANES), F32), pltpu.VMEM((RUN * LANES, LANES), BF), skew],
        1, (offsets, ref_own, first, left_first, masks, perm, guide), 1_000_000_000,
    )
    (result,) = call(
        late_kernel,
        [((LINES, WIDE), F32)],
        [skew, pltpu.VMEM(quad_rows, BF), pltpu.VMEM((RUN, DISP, LANES), F32), square, square],
        1, (offsets, second, left_second, lhs, early_rows, wts, flip), 1_000_000_000,
    )
    copies = jnp.broadcast_to(result[None], (2 * n, LINES, WIDE))
    pieces = lax.all_to_all(copies, ("cols", "view"), split_axis=0, concat_axis=0, tiled=True)
    return join(pieces, own.shape[0] // n, n)


LINE_RUN = 8
PAIR = 2
LINE_PARTS = LANES


MASKS = 8
GATE_FLOOR = 11.0 / 9.0


def pack_kernel(key, own, *rest):
    out = rest[-1]
    me = 2 * lax.axis_index("cols") + lax.axis_index("view")
    rows = PAIR * CHANNELS
    out[:rows, :] = own[me ^ key]
    if out.shape[0] > rows:
        masks = rest[0][...].astype(F32)
        out[rows:, :] = jnp.where(
            iota((MASKS, BLOCK), 0) < MASKS // 2, masks[0:1, :], masks[1:2, :]
        ).astype(BF)


def constants_kernel(offsets, guide, valid, order, order_band, flip, guide_out, spread, masks):
    masks[...] = valid[...].astype(F32)
    row = iota((LANES, LANES), 0)
    from_lane = LANES - 1 - LINE_RUN * (row & (PARTS - 1)) - (row >> 4)
    order[...] = jnp.where(iota((LANES, LANES), 1) == from_lane, 1.0, 0.0).astype(BF)
    from_lane = LANES - 1 - (row & 64) - LINE_RUN * (row & 7) - ((row >> 3) & 7)
    order_band[...] = jnp.where(iota((LANES, LANES), 1) == from_lane, 1.0, 0.0).astype(BF)
    back = 2 * LANES - 1 - iota((DISP, 2 * LANES), 0)
    flip[...] = jnp.where(iota((DISP, 2 * LANES), 1) == back, 1.0, 0.0).astype(BF)
    guide_out[...] = spread_guide(guide[...]) * 0.5
    block_of = LANES - 1 - (iota(spread.shape, 1) >> 3)
    spread[...] = jnp.where(iota(spread.shape, 0) == block_of, 1.0, 0.0).astype(BF)


def lines_kernel(offsets, order, order_band, flip, guide, spread, *rest):
    pieces, (out, blocks, valid, gate_rows, cost_rows, vol, done, wts) = rest[:-8], rest[-8:]
    near, pieces = pieces[0], pieces[1:]
    tiles = len(pieces)
    width = tiles * LANES
    me = 2 * lax.axis_index("cols") + lax.axis_index("view")
    rows = PAIR * CHANNELS
    for key, piece in enumerate(pieces):
        blocks[me ^ key] = piece[:rows, :]
        if piece.shape[0] > rows:
            masks = piece[rows:, :].astype(F32)
            valid[(me ^ key) // 2] = jnp.concatenate([masks[0:1], masks[MASKS // 2 : MASKS // 2 + 1]], axis=0)
    valid[me // 2] = near[...]
    at = PAIR * me
    offs = [offsets[at + i] for i in range(PAIR)]
    ch_lane = iota((CHANNELS, LANES), 1)
    low_lane = ch_lane < LANES // 2
    low_half = iota((LANES, LANES), 1) < CHANNELS
    reached = iota((8, LANES), 1) + LINE_RUN * iota((8, LANES), 0)
    scale = 1.0 / math.sqrt(CHANNELS)
    empty = jnp.zeros((CHANNELS, LANES), F32)

    def mask_of(view, w):
        lo = (w % 2) * LANES
        return valid[w // 2, view : view + 1, lo : lo + LANES]

    for i in range(PAIR):

        def tile_of(view, w):
            lo = (w % 2) * LANES
            return blocks[2 * (w // 2) + view, i * CHANNELS : (i + 1) * CHANNELS, lo : lo + LANES]

        off = offs[i]
        rolled = [pltpu.roll(tile_of(1, w).astype(F32) * mask_of(1, w), off, 1) for w in range(tiles)]
        line = [empty, empty]
        for w in range(tiles):
            line.append(jnp.where(ch_lane < off, rolled[w - 1] if w else empty, rolled[w]))
        turned = [empty] + [pltpu.roll(tile, LANES // 2, 1) if w else tile for w, tile in enumerate(line[1:])]
        shifted = [tile.astype(BF) for tile in line]
        halfway = [jnp.where(low_lane, a, b).astype(BF) for a, b in zip(turned, turned[1:])]

        for quad in range(tiles // 4):
            refs = [tile_of(0, 4 * quad + q) for q in range(4)]
            masked = [refs[q] * (mask_of(0, 4 * quad + q) * scale).astype(BF) for q in range(4)]
            cols = dot_t(order[...], jnp.concatenate(refs, axis=0))
            masked = dot_t(order_band[...], jnp.concatenate(masked, axis=0))
            for two in range(2):
                w = 4 * quad + 2 * two
                raw = cols[:, two * LANES : (two + 1) * LANES]
                pair = masked[:, two * LANES : (two + 1) * LANES]
                gates = [jnp.where(low_half, raw, 0.0).astype(BF), jnp.where(low_half, 0.0, raw).astype(BF)]
                sides = [jnp.where(low_half, pair, 0.0).astype(BF), jnp.where(low_half, 0.0, pair).astype(BF)]
                chunks = []
                for half, source, first in ((0, shifted, w + 1), (1, halfway, w)):
                    lo = half * LANES // 2
                    lhs = jnp.concatenate([side[lo : lo + LANES // 2] for side in sides], axis=0)
                    rhs = jnp.concatenate(
                        [jnp.concatenate(source[first + side : first + side + 2], axis=1) for side in range(2)],
                        axis=0,
                    )
                    chunks.append(jnp.dot(lhs, rhs, preferred_element_type=F32))
                for side in range(2):
                    place = (tiles - 1 - w - side) * PARTS
                    for t in range(LINE_RUN):
                        row = t * LANES + place
                        gate_rows[i, row : row + PARTS, :] = gates[side][t * PARTS : (t + 1) * PARTS]
                        r = side * LANES // 2 + 8 * t
                        within = reached < LANES - t
                        halves = []
                        for products in chunks:
                            close, far = products[r : r + 8, :LANES], products[r : r + 8, LANES:]
                            halves.append(
                                jnp.concatenate(
                                    [
                                        pltpu.roll(value, t, 1, stride=LINE_RUN, stride_axis=0)
                                        for value in (close, jnp.where(within, far, close))
                                    ],
                                    axis=1,
                                )
                            )
                        cost_rows[i, row : row + PARTS, :] = jnp.concatenate(halves, axis=0).astype(BF)

    x_base = width - 1 - LINE_RUN * iota((KEYS, LANES), 1)
    row = iota((KEYS, LANES), 0)
    reach = jnp.where(row >= 2 * GROUPS, 9, jnp.where(row >= GROUPS, 3, 1))
    room_left = x_base - reach
    room_right = x_base + reach - width
    unit = jnp.where(row >= 2 * GROUPS, SHARPNESS / math.log(2.0), 1.0)
    for i in range(PAIR):
        for two in range(LINE_RUN // 2):
            lo = 2 * two * LANES
            costs = dot_t(flip[...], cost_rows[i, lo : lo + 2 * LANES, :])
            logits = dot_t(guide[...], gate_rows[i, lo : lo + 2 * LANES, :])
            for side in range(2):
                t = 2 * two + side
                vol[i, t] = costs[:, side * LANES : (side + 1) * LANES]
                z = jnp.tanh(logits[:, side * LANES : (side + 1) * LANES]) + GATE_FLOOR
                taps = [z[m * KEYS : (m + 1) * KEYS] for m in range(3)]
                factor = unit / (taps[0] + taps[1] + taps[2])
                taps = [tap * factor for tap in taps]
                taps[0] = jnp.where(room_left >= t, taps[0], 0.0)
                taps[2] = jnp.where(room_right < t, taps[2], 0.0)
                for m in range(3):
                    wts[i, t, m * KEYS : (m + 1) * KEYS, :] = taps[m]

    peaks = [[None] * LINE_RUN for _ in range(PAIR)]
    for group in range(GROUPS):
        starts = [group * DGROUP + 8 * half for half in range(2)]
        for i in range(PAIR):
            v = [[vol[i, t, at : at + 8, :] for t in range(LINE_RUN)] for at in starts]
            for layer in range(LAYERS):
                s = 3**layer
                fresh = [[], []]
                for t in range(LINE_RUN):
                    rows = [k * KEYS + layer * GROUPS + group for k in range(3)]
                    w = [jnp.broadcast_to(wts[i, t, r : r + 1, :], (8, LANES)) for r in rows]
                    for half in range(2):
                        blk, r = divmod(t + s, LINE_RUN)
                        before = pltpu.roll(v[half][r], LANES - blk, 1) if blk else v[half][r]
                        blk, r = divmod(t - s, LINE_RUN)
                        after = pltpu.roll(v[half][r], -blk, 1) if blk else v[half][r]
                        fresh[half].append(w[0] * before + w[1] * v[half][t] + w[2] * after)
                v = fresh
            for half, at_row in enumerate(starts):
                for t in range(LINE_RUN):
                    done[i, t, at_row : at_row + 8, :] = v[half][t]
            for t in range(LINE_RUN):
                peak = jnp.maximum(v[0][t], v[1][t])
                peaks[i][t] = peak if group == 0 else jnp.maximum(peaks[i][t], peak)

    sub = iota((8, LANES), 0)
    results = []
    for i in range(PAIR):
        totals = jnp.zeros((8, LANES), F32)
        moments = totals
        for s in range(LINE_RUN):
            t = LINE_RUN - 1 - s
            v = [done[i, t, 8 * j : 8 * j + 8, :] for j in range(DISP // 8)]
            top = jnp.max(peaks[i][t], axis=0, keepdims=True)
            total = jnp.exp2(v[-1] - top)
            moment = total
            for j in range(DISP // 8 - 2, -1, -1):
                total = total + jnp.exp2(v[j] - top)
                if j:
                    moment = moment + total
            moment = 8.0 * moment + sub.astype(F32) * total
            totals = jnp.where(sub == s, jnp.sum(total, axis=0, keepdims=True), totals)
            moments = jnp.where(sub == s, jnp.sum(moment, axis=0, keepdims=True), moments)
        results.append((moments / totals + offs[i].astype(F32)) * (1.0 / DISP))
    both = jnp.concatenate(results, axis=0)
    high = both.astype(BF)
    left = both - high.astype(F32)
    middle = left.astype(BF)
    low = (left - middle.astype(F32)).astype(BF)
    parts = jnp.dot(
        jnp.concatenate([high, middle, low], axis=0), spread[...], preferred_element_type=F32
    )
    size = PAIR * LINE_RUN
    parts = parts[:size] + parts[size : 2 * size] + parts[2 * size :]
    wanted = iota((LINE_RUN, width), 0) == (iota((LINE_RUN, width), 1) & (LINE_RUN - 1))
    for i in range(PAIR):
        part = jnp.where(wanted, parts[i * LINE_RUN : (i + 1) * LINE_RUN], 0.0)
        out[i : i + 1, :] = jnp.sum(part, axis=0, keepdims=True)


def lines_plan(features, valid_cols, offsets, guide_weight):
    n = lax.axis_size("cols")
    devices = 2 * n
    width = n * BLOCK
    rows = PAIR * CHANNELS
    own = features.reshape(devices, rows, BLOCK)
    pieces = [None] * devices
    gone = ()
    for key in (1, 2, 6, 4, 7, 5, 3, 0):
        masked = key % 2 and key > 1
        (piece,) = call(
            functools.partial(pack_kernel, key),
            [((rows + (MASKS if masked else 0), BLOCK), BF)],
            [], 0,
            (own,) + ((valid_cols,) if masked else ()) + gone,
            1_000_000,
        )
        gone = (piece,)
        moves = [(i, i ^ key) for i in range(devices)]
        pieces[key] = lax.ppermute(piece, ("cols", "view"), moves) if key else piece
    consts = call(
        constants_kernel,
        [
            ((LANES, LANES), BF), ((LANES, LANES), BF), ((DISP, 2 * LANES), BF), ((3 * KEYS, LANES), BF),
            ((LANES, width), BF), (valid_cols.shape, F32),
        ],
        [], 1, (offsets, guide_weight, valid_cols), 1_000_000,
    )
    (rows,) = call(
        lines_kernel,
        [((PAIR, width), F32)],
        [
            pltpu.VMEM((devices, rows, BLOCK), BF),
            pltpu.VMEM((n,) + valid_cols.shape, F32),
            pltpu.VMEM((PAIR, LINE_RUN * LANES, LANES), BF),
            pltpu.VMEM((PAIR, LINE_RUN * LANES, 2 * LANES), BF),
            pltpu.VMEM((PAIR, LINE_RUN, DISP, LANES), F32),
            pltpu.VMEM((PAIR, LINE_RUN, DISP, LANES), F32),
            pltpu.VMEM((PAIR, LINE_RUN, 3 * KEYS, LANES), F32),
        ],
        1, (offsets, *consts, *pieces), 1_000_000_000,
    )
    others = lax.ppermute(rows, "view", [(0, 1), (1, 0)])
    first = lax.axis_index("view") == 0
    return jnp.where(first, jnp.concatenate([rows, others]), jnp.concatenate([others, rows]))[None]


def on_device(features, valid_cols, offsets, guide_weight):
    n = lax.axis_size("cols")
    lines = features.shape[1]
    if lines == 2 * PAIR * n and n * BLOCK == LINE_RUN * LANES:
        return lines_plan(features, valid_cols, offsets, guide_weight)
    return halo_plan(features, valid_cols, offsets, guide_weight)


def solution(mesh):
    return jax.shard_map(
        on_device,
        mesh=mesh,
        in_specs=(
            P("view", ("tiles", "lines"), None, "cols"),
            P(None, ("tiles", "cols")),
            P(("tiles", "lines")),
            P(),
        ),
        out_specs=P(("tiles", "lines"), "cols", None),
        check_vma=False,
    )
```

```python
import functools
import math

import jax
import jax.numpy as jnp
from jax import lax
from jax.experimental import pallas as pl
from jax.experimental.pallas import tpu as pltpu
from jax.sharding import PartitionSpec as P

DISP = 192
DGROUP = 16
GROUPS = DISP // DGROUP
LAYERS = 3
SHARPNESS = 2.0
HALO = 32
LANES = 128
LINES = 8
CHANNELS = 64
BLOCK = 256
SPAN = BLOCK + HALO
PARTS = LANES // LINES
RUN = SPAN // PARTS
KEYS = 40
WIDE = BLOCK + LANES
SEC_ROWS = LINES * CHANNELS
QUAD_ROWS = SEC_ROWS // 2
MASK_AT = QUAD_ROWS + CHANNELS
PAYLOAD = MASK_AT + 16
QUAD = LINES // 2
QUAD_LANES = LANES // 2
PACK = LANES // HALO
CUT = 16

BF = jnp.bfloat16
F32 = jnp.float32


def iota(shape, dim):
    return lax.broadcasted_iota(jnp.int32, shape, dim)


def dot_t(a, b):
    return lax.dot_general(a, b, (((1,), (1,)), ((), ())), preferred_element_type=F32)


def call(kernel, outs, scratch, smem, args, flops=0, space=pltpu.VMEM, limit=24, to=None):
    specs = [pl.BlockSpec(memory_space=pltpu.SMEM)] * smem
    specs += [pl.BlockSpec(memory_space=space)] * (len(args) - smem)
    return pl.pallas_call(
        kernel,
        out_shape=[jax.ShapeDtypeStruct(shape, dtype) for shape, dtype in outs],
        in_specs=specs,
        out_specs=[pl.BlockSpec(memory_space=to or space)] * len(outs),
        scratch_shapes=scratch,
        compiler_params=pltpu.CompilerParams(vmem_limit_bytes=limit * 1024 * 1024),
        cost_estimate=pl.CostEstimate(flops=flops, bytes_accessed=1_000_000, transcendentals=0),
    )(*args)


def spread_guide(guide):
    keys = LAYERS * 3 * GROUPS
    row = iota((3 * KEYS, keys), 0)
    tap = jnp.where(row >= KEYS, 1, 0) + jnp.where(row >= 2 * KEYS, 1, 0)
    row = row - KEYS * tap
    layer = jnp.where(row >= GROUPS, 1, 0) + jnp.where(row >= 2 * GROUPS, 1, 0)
    key = 2 * GROUPS * layer + GROUPS * tap + row
    chosen = jnp.where((iota((3 * KEYS, keys), 1) == key) & (row < 3 * GROUPS), 1.0, 0.0).astype(BF)
    guide_t = dot_t(chosen, guide).astype(BF)
    return jnp.concatenate([guide_t, guide_t], axis=1)


def normalise(z, wts, t, room_left, room_right):
    z = (0.55 + 0.45 * jnp.tanh(0.5 * z)).astype(BF).astype(F32)
    taps = [z[k * KEYS : (k + 1) * KEYS] for k in range(3)]
    scale = 1.0 / (taps[0] + taps[1] + taps[2])
    wts[t, 0:KEYS, :] = jnp.where(room_left >= t, taps[0] * scale, 0.0)
    wts[t, KEYS : 2 * KEYS, :] = taps[1] * scale
    wts[t, 2 * KEYS : 3 * KEYS, :] = jnp.where(room_right < t, taps[2] * scale, 0.0)


def prefetch_kernel(own, valid, guide, own_out, masks, perm, flip, guide_out, valid_in, guide_in, sems):
    copies = [
        pltpu.make_async_copy(src, dst, sems.at[i])
        for i, (src, dst) in enumerate([(own, own_out), (guide, guide_in), (valid, valid_in)])
    ]
    for copy in copies:
        copy.start()
    perm[...] = jnp.where(
        iota((SPAN, WIDE), 1) == WIDE - 1 - iota((SPAN, WIDE), 0), 1.0, 0.0
    ).astype(BF)
    back = 2 * LANES - 1 - iota((DISP, 2 * LANES), 0)
    flip[...] = jnp.where(iota((DISP, 2 * LANES), 1) == back, 1.0, 0.0).astype(BF)

    copies[1].wait()
    guide_out[...] = spread_guide(guide_in[...])
    copies[2].wait()
    masks[...] = valid_in[...].astype(F32)
    copies[0].wait()


def payload_kernel(own, other, masks, first, second, ref_own):
    view = lax.axis_index("view")
    first_view = view == 0
    sec_mask = masks[1:2, :].astype(BF)
    lane = iota((CHANNELS, LANES), 1)
    tails = []
    for line in range(LINES):
        at = view * LINES + line
        mine, theirs = own[at], other[at]
        lo = line * CHANNELS
        dest, start = (first, lo) if line < QUAD else (second, lo - QUAD_ROWS)
        dest[start : start + CHANNELS, :] = jnp.where(first_view, theirs, mine) * sec_mask
        ref = jnp.where(first_view, mine, theirs)
        ref_own[lo : lo + CHANNELS, :] = ref
        tail = ref[:, BLOCK - LANES :].astype(F32)
        slot = line % PACK
        turn = (HALO * (slot + 1)) % LANES
        if turn:
            tail = pltpu.roll(tail, turn, 1)
        if slot:
            tails[-1] = jnp.where(lane >= HALO * slot, tail, tails[-1])
        else:
            tails.append(tail)
    for i, tail in enumerate(tails):
        first[QUAD_ROWS:MASK_AT, i * LANES : (i + 1) * LANES] = tail.astype(BF)
    first[MASK_AT:, :] = jnp.broadcast_to(masks[0:1, :], (16, BLOCK)).astype(BF)


def shifted(left, mine, lo, off):
    ch_lane = iota((CHANNELS, LANES), 1)
    tiles = [
        src[lo : lo + CHANNELS, i * LANES : (i + 1) * LANES].astype(F32)
        for src in (left, mine)
        for i in range(2)
    ]
    tiles = [pltpu.roll(tile, off, 1) for tile in tiles]
    tiles = [jnp.where(ch_lane < off, tiles[max(i - 1, 0)], tiles[i]).astype(BF) for i in range(4)]
    return jnp.concatenate(tiles, axis=1)


def line_costs(lhs, rhs, slot, skew, cost_rows):
    diagonal = iota((8, LANES), 1) - iota((8, LANES), 0)
    for chunk in range(3):
        rows = min(LANES, SPAN - chunk * LANES)
        first = max(1 - chunk, 0)
        last = 3 - chunk
        products = jnp.dot(
            lhs[chunk * LANES : chunk * LANES + rows],
            rhs[:, first * LANES : (last + 1) * LANES],
            preferred_element_type=F32,
        )
        for j in range(rows // 8):
            tiles = [
                pltpu.roll(
                    products[8 * j : 8 * j + 8, i * LANES : (i + 1) * LANES],
                    8 * j, 1, stride=1, stride_axis=0,
                )
                for i in range(last + 1 - first)
            ]
            if len(tiles) < 3:
                tiles = [tiles[0]] + tiles
            beyond = diagonal >= 8 * j
            at = chunk * LANES + 8 * j
            skew[slot, 0, at : at + 8, :] = jnp.where(beyond, tiles[1], tiles[0])
            skew[slot, 1, at : at + 8, :] = jnp.where(beyond, tiles[2], tiles[1])
    for t in range(RUN):
        at = t * QUAD_LANES + slot * PARTS
        for v in range(2):
            cost_rows[at : at + PARTS, v * LANES : (v + 1) * LANES] = skew[
                slot, v, pl.ds(t, PARTS, stride=RUN), :
            ].astype(BF)


def early_kernel(
    offsets, ref_own, mine, left, masks, perm, guide, wts, cost_rows, lhs_out,
    ref_rows, ref_cols, gate_rows, skew
):
    base = lax.axis_index("view") * LINES
    low = jnp.where(lax.axis_index("cols") == 0, HALO, 0)
    for line in range(LINES):
        lo = line * CHANNELS
        ref_rows[lo : lo + CHANNELS, LANES:] = ref_own[lo : lo + CHANNELS, :]
        half = line // PACK
        packed = left[QUAD_ROWS:MASK_AT, half * LANES : (half + 1) * LANES].astype(F32)
        turn = (LANES - HALO) - HALO * (line % PACK)
        if turn:
            packed = pltpu.roll(packed, turn, 1)
        ref_rows[lo : lo + CHANNELS, :LANES] = packed.astype(BF)

    mask_left = left[MASK_AT : MASK_AT + 1, BLOCK - LANES :].astype(F32)
    ref_mask = jnp.concatenate([mask_left, masks[0:1, :]], axis=1)
    ref_mask = jnp.broadcast_to(ref_mask * (1.0 / math.sqrt(CHANNELS)), (LANES, WIDE))
    mask_cols = dot_t(perm[...], ref_mask.astype(BF))
    half_lane = iota((PARTS, LANES), 1) < CHANNELS
    span_lane = iota((SPAN, LANES), 1) < CHANNELS

    for quad in range(LINES // QUAD):
        ref_t = dot_t(perm[...], ref_rows[quad * QUAD_ROWS : (quad + 1) * QUAD_ROWS, :])
        for pair in range(QUAD // 2):
            cols = ref_t[:, pair * LANES : (pair + 1) * LANES]
            slot = quad * 2 + pair
            ref_cols[slot] = cols
            masked = cols * mask_cols
            if quad == 0:
                rhs = jnp.concatenate(
                    [
                        shifted(left, mine, line * CHANNELS, offsets[base + line])
                        for line in (2 * slot, 2 * slot + 1)
                    ],
                    axis=0,
                )
            for side in range(2):
                line = 2 * slot + side
                for t in range(RUN):
                    picked = ref_cols[slot, pl.ds(t, PARTS, stride=RUN), :]
                    picked = jnp.where(half_lane if side == 0 else ~half_lane, picked, 0.0)
                    at = t * LANES + line * PARTS
                    gate_rows[at : at + PARTS, :] = picked.astype(BF)
                lhs = jnp.where(span_lane if side == 0 else ~span_lane, masked, 0.0).astype(BF)
                if quad == 0:
                    line_costs(lhs, rhs, line, skew, cost_rows)
                else:
                    lhs_out[line - QUAD] = lhs

    place = iota((KEYS, LANES), 1)
    x_base = SPAN - 1 - RUN * (place & (PARTS - 1))
    row = iota((KEYS, LANES), 0)
    reach = jnp.where(row >= 2 * GROUPS, 9, jnp.where(row >= GROUPS, 3, 1))
    room_left = x_base - reach - low
    room_right = x_base + reach - SPAN
    for two in range(RUN // 2):
        at = 2 * two * LANES
        logits = dot_t(guide[...], gate_rows[at : at + 2 * LANES, :])
        for i in range(2):
            t = 2 * two + i
            normalise(logits[:, i * LANES : (i + 1) * LANES], wts, t, room_left, room_right)


def late_kernel(
    offsets, mine, left, lhs, early_rows, wts, flip, out, skew, cost_rows, vol, vals, turned
):
    base = lax.axis_index("view") * LINES
    for pair in range(QUAD // 2):
        rhs = jnp.concatenate(
            [
                shifted(left, mine, line * CHANNELS, offsets[base + QUAD + line])
                for line in (2 * pair, 2 * pair + 1)
            ],
            axis=0,
        )
        for line in (2 * pair, 2 * pair + 1):
            line_costs(lhs[line], rhs, line, skew, cost_rows)

    for two in range(RUN // 2):
        rows = []
        for t in (2 * two, 2 * two + 1):
            for part in (early_rows, cost_rows):
                rows.append(part[t * QUAD_LANES : (t + 1) * QUAD_LANES, :])
        costs = dot_t(flip[...], jnp.concatenate(rows, axis=0))
        vol[2 * two] = costs[:, :LANES]
        vol[2 * two + 1] = costs[:, LANES:]

    def aggregate(group, carry):
        for half in range(2):
            at = pl.multiple_of(group * DGROUP + half * 8, 8)
            v = [vol[t, pl.ds(at, 8), :] for t in range(RUN)]
            for layer in range(LAYERS):
                s = 3**layer
                before = [v[t + s] if t + s < RUN else pltpu.roll(v[t + s - RUN], LANES - 1, 1) for t in range(RUN)]
                after = [v[t - s] if t >= s else pltpu.roll(v[t - s + RUN], 1, 1) for t in range(RUN)]
                fresh = []
                for t in range(RUN):
                    w = [wts[t, pl.ds(k * KEYS + layer * GROUPS + group, 1), :] for k in range(3)]
                    fresh.append(w[0] * before[t] + w[1] * v[t] + w[2] * after[t])
                v = fresh
            for t in range(RUN):
                vol[t, pl.ds(at, 8), :] = v[t]
        return carry

    lax.fori_loop(0, GROUPS, aggregate, 0)

    vals[...] = jnp.zeros((LANES, LANES), F32)
    sub = iota((8, LANES), 0).astype(F32)
    line_of = iota((1, LANES), 1) >> 4
    offs = jnp.zeros((1, LANES), F32)
    for line in range(LINES):
        offs = jnp.where(line_of == line, offsets[base + line].astype(F32), offs)

    def softmax(t, carry):
        v = [vol[t, 8 * i : 8 * i + 8, :] for i in range(DISP // 8)]
        top = v
        while len(top) > 1:
            top = [jnp.maximum(a, b) for a, b in zip(top[::2], top[1::2])] + top[len(top) & ~1 :]
        top = jnp.max(top[0], axis=0, keepdims=True)
        e = [jnp.exp(SHARPNESS * (a - top)) for a in v]
        total = e[0]
        moment = jnp.zeros((8, LANES), F32)
        for i in range(1, DISP // 8):
            total = total + e[i]
            moment = moment + float(8 * i) * e[i]
        moment = jnp.sum(moment + sub * total, axis=0, keepdims=True)
        total = jnp.sum(total, axis=0, keepdims=True)
        vals[pl.ds(RUN - 1 - t, 1), :] = (moment / total + offs) * (1.0 / DISP)
        return carry

    lax.fori_loop(0, RUN, softmax, 0)

    turned[...] = jnp.transpose(vals[...])
    lane = iota((8, LANES), 1)
    result = [jnp.zeros((8, LANES), F32) for _ in range(WIDE // LANES)]
    for part in range(PARTS):
        piece = turned[pl.ds(part, LINES, stride=PARTS), :]
        start = (RUN * (PARTS - 1 - part) - HALO) % WIDE
        tile, turn = divmod(start, LANES)
        if turn:
            piece = pltpu.roll(piece, turn, 1)
        if turn + RUN > LANES:
            after = (tile + 1) % len(result)
            result[after] = result[after] + jnp.where(lane < turn, piece, 0.0)
            piece = jnp.where(lane >= turn, piece, 0.0)
        result[tile] = result[tile] + piece
    for tile, value in enumerate(result):
        out[:, tile * LANES : (tile + 1) * LANES] = value


def join(pieces, sub, n):
    block = lax.axis_index("cols")
    pieces = pieces.reshape(n, 2, LINES, WIDE)
    start = (0, block // (n // 2), (block % (n // 2)) * sub, 0)
    pieces = lax.dynamic_slice(pieces, start, (n, 1, sub, WIDE))[:, 0]
    main = pieces[:, :, :BLOCK]
    tail = jnp.pad(pieces[1:, :, BLOCK:], ((0, 1), (0, 0), (LANES, 0)))
    place = (n, sub, BLOCK)
    keep = (iota(place, 2) < BLOCK - CUT) | (iota(place, 0) == n - 1)
    joined = jnp.where(keep, main, tail)
    return jnp.transpose(joined, (1, 0, 2)).reshape(1, sub, n * BLOCK)


def halo_plan(features, valid_cols, offsets, guide_weight):
    own = features[0]
    n = lax.axis_size("cols")
    right = [(c, c + 1) for c in range(n - 1)]
    other = lax.ppermute(own, "view", [(0, 1), (1, 0)])
    near, masks, perm, flip, guide = call(
        prefetch_kernel,
        [(own.shape, BF), (valid_cols.shape, F32), ((SPAN, WIDE), BF), ((DISP, 2 * LANES), BF), ((3 * KEYS, LANES), BF)],
        [pltpu.VMEM(valid_cols.shape, jnp.int32), pltpu.VMEM(guide_weight.shape, BF), pltpu.SemaphoreType.DMA((3,))],
        0, (own, valid_cols, guide_weight), 100_000_000, pl.ANY, 24, pltpu.VMEM,
    )
    first, second, ref_own = call(
        payload_kernel,
        [((PAYLOAD, BLOCK), BF), ((QUAD_ROWS, BLOCK), BF), ((SEC_ROWS, BLOCK), BF)],
        [], 0, (near, other, masks),
    )
    left_first = lax.ppermute(first, "cols", right)
    left_second = lax.ppermute(second, "cols", right)
    quad_rows = (RUN * QUAD_LANES, 2 * LANES)
    skew = pltpu.VMEM((QUAD, 2, SPAN, LANES), F32)
    square = pltpu.VMEM((LANES, LANES), F32)
    wts, early_rows, lhs = call(
        early_kernel,
        [((RUN, 3 * KEYS, LANES), F32), (quad_rows, BF), ((QUAD, SPAN, LANES), BF)],
        [pltpu.VMEM((SEC_ROWS, WIDE), BF), pltpu.VMEM((QUAD, SPAN, LANES), F32), pltpu.VMEM((RUN * LANES, LANES), BF), skew],
        1, (offsets, ref_own, first, left_first, masks, perm, guide), 1_000_000_000,
    )
    (result,) = call(
        late_kernel,
        [((LINES, WIDE), F32)],
        [skew, pltpu.VMEM(quad_rows, BF), pltpu.VMEM((RUN, DISP, LANES), F32), square, square],
        1, (offsets, second, left_second, lhs, early_rows, wts, flip), 1_000_000_000,
    )
    copies = jnp.broadcast_to(result[None], (2 * n, LINES, WIDE))
    pieces = lax.all_to_all(copies, ("cols", "view"), split_axis=0, concat_axis=0, tiled=True)
    return join(pieces, own.shape[0] // n, n)


LINE_RUN = 8
PAIR = 2
LINE_PARTS = LANES


MASKS = 8
GATE_FLOOR = 11.0 / 9.0


def pack_kernel(key, own, *rest):
    out = rest[-1]
    me = 2 * lax.axis_index("cols") + lax.axis_index("view")
    rows = PAIR * CHANNELS
    out[:rows, :] = own[me ^ key]
    if out.shape[0] > rows:
        masks = rest[0][...].astype(F32)
        out[rows:, :] = jnp.where(
            iota((MASKS, BLOCK), 0) < MASKS // 2, masks[0:1, :], masks[1:2, :]
        ).astype(BF)


def constants_kernel(offsets, guide, valid, order, order_band, flip, guide_out, spread, masks):
    masks[...] = valid[...].astype(F32)
    row = iota((LANES, LANES), 0)
    from_lane = LANES - 1 - LINE_RUN * (row & (PARTS - 1)) - (row >> 4)
    order[...] = jnp.where(iota((LANES, LANES), 1) == from_lane, 1.0, 0.0).astype(BF)
    from_lane = LANES - 1 - (row & 64) - LINE_RUN * (row & 7) - ((row >> 3) & 7)
    order_band[...] = jnp.where(iota((LANES, LANES), 1) == from_lane, 1.0, 0.0).astype(BF)
    back = 2 * LANES - 1 - iota((DISP, 2 * LANES), 0)
    flip[...] = jnp.where(iota((DISP, 2 * LANES), 1) == back, 1.0, 0.0).astype(BF)
    guide_out[...] = spread_guide(guide[...]) * 0.5
    block_of = LANES - 1 - (iota(spread.shape, 1) >> 3)
    spread[...] = jnp.where(iota(spread.shape, 0) == block_of, 1.0, 0.0).astype(BF)


def lines_kernel(offsets, order, order_band, flip, guide, spread, *rest):
    pieces, (out, blocks, valid, gate_rows, cost_rows, vol, done, wts) = rest[:-8], rest[-8:]
    near, pieces = pieces[0], pieces[1:]
    tiles = len(pieces)
    width = tiles * LANES
    me = 2 * lax.axis_index("cols") + lax.axis_index("view")
    rows = PAIR * CHANNELS
    for key, piece in enumerate(pieces):
        blocks[me ^ key] = piece[:rows, :]
        if piece.shape[0] > rows:
            masks = piece[rows:, :].astype(F32)
            valid[(me ^ key) // 2] = jnp.concatenate([masks[0:1], masks[MASKS // 2 : MASKS // 2 + 1]], axis=0)
    valid[me // 2] = near[...]
    at = PAIR * me
    offs = [offsets[at + i] for i in range(PAIR)]
    ch_lane = iota((CHANNELS, LANES), 1)
    low_lane = ch_lane < LANES // 2
    low_half = iota((LANES, LANES), 1) < CHANNELS
    reached = iota((8, LANES), 1) + LINE_RUN * iota((8, LANES), 0)
    scale = 1.0 / math.sqrt(CHANNELS)
    empty = jnp.zeros((CHANNELS, LANES), F32)

    def mask_of(view, w):
        lo = (w % 2) * LANES
        return valid[w // 2, view : view + 1, lo : lo + LANES]

    for i in range(PAIR):

        def tile_of(view, w):
            lo = (w % 2) * LANES
            return blocks[2 * (w // 2) + view, i * CHANNELS : (i + 1) * CHANNELS, lo : lo + LANES]

        off = offs[i]
        rolled = [pltpu.roll(tile_of(1, w).astype(F32) * mask_of(1, w), off, 1) for w in range(tiles)]
        line = [empty, empty]
        for w in range(tiles):
            line.append(jnp.where(ch_lane < off, rolled[w - 1] if w else empty, rolled[w]))
        turned = [empty] + [pltpu.roll(tile, LANES // 2, 1) if w else tile for w, tile in enumerate(line[1:])]
        shifted = [tile.astype(BF) for tile in line]
        halfway = [jnp.where(low_lane, a, b).astype(BF) for a, b in zip(turned, turned[1:])]

        for quad in range(tiles // 4):
            refs = [tile_of(0, 4 * quad + q) for q in range(4)]
            masked = [refs[q] * (mask_of(0, 4 * quad + q) * scale).astype(BF) for q in range(4)]
            cols = dot_t(order[...], jnp.concatenate(refs, axis=0))
            masked = dot_t(order_band[...], jnp.concatenate(masked, axis=0))
            for two in range(2):
                w = 4 * quad + 2 * two
                raw = cols[:, two * LANES : (two + 1) * LANES]
                pair = masked[:, two * LANES : (two + 1) * LANES]
                gates = [jnp.where(low_half, raw, 0.0).astype(BF), jnp.where(low_half, 0.0, raw).astype(BF)]
                sides = [jnp.where(low_half, pair, 0.0).astype(BF), jnp.where(low_half, 0.0, pair).astype(BF)]
                chunks = []
                for half, source, first in ((0, shifted, w + 1), (1, halfway, w)):
                    lo = half * LANES // 2
                    lhs = jnp.concatenate([side[lo : lo + LANES // 2] for side in sides], axis=0)
                    rhs = jnp.concatenate(
                        [jnp.concatenate(source[first + side : first + side + 2], axis=1) for side in range(2)],
                        axis=0,
                    )
                    chunks.append(jnp.dot(lhs, rhs, preferred_element_type=F32))
                for side in range(2):
                    place = (tiles - 1 - w - side) * PARTS
                    for t in range(LINE_RUN):
                        row = t * LANES + place
                        gate_rows[i, row : row + PARTS, :] = gates[side][t * PARTS : (t + 1) * PARTS]
                        r = side * LANES // 2 + 8 * t
                        within = reached < LANES - t
                        halves = []
                        for products in chunks:
                            close, far = products[r : r + 8, :LANES], products[r : r + 8, LANES:]
                            halves.append(
                                jnp.concatenate(
                                    [
                                        pltpu.roll(value, t, 1, stride=LINE_RUN, stride_axis=0)
                                        for value in (close, jnp.where(within, far, close))
                                    ],
                                    axis=1,
                                )
                            )
                        cost_rows[i, row : row + PARTS, :] = jnp.concatenate(halves, axis=0).astype(BF)

    x_base = width - 1 - LINE_RUN * iota((KEYS, LANES), 1)
    row = iota((KEYS, LANES), 0)
    reach = jnp.where(row >= 2 * GROUPS, 9, jnp.where(row >= GROUPS, 3, 1))
    room_left = x_base - reach
    room_right = x_base + reach - width
    unit = jnp.where(row >= 2 * GROUPS, SHARPNESS / math.log(2.0), 1.0)
    for i in range(PAIR):
        for two in range(LINE_RUN // 2):
            lo = 2 * two * LANES
            costs = dot_t(flip[...], cost_rows[i, lo : lo + 2 * LANES, :])
            logits = dot_t(guide[...], gate_rows[i, lo : lo + 2 * LANES, :])
            for side in range(2):
                t = 2 * two + side
                vol[i, t] = costs[:, side * LANES : (side + 1) * LANES]
                z = jnp.tanh(logits[:, side * LANES : (side + 1) * LANES]) + GATE_FLOOR
                taps = [z[m * KEYS : (m + 1) * KEYS] for m in range(3)]
                factor = unit / (taps[0] + taps[1] + taps[2])
                taps = [tap * factor for tap in taps]
                taps[0] = jnp.where(room_left >= t, taps[0], 0.0)
                taps[2] = jnp.where(room_right < t, taps[2], 0.0)
                for m in range(3):
                    wts[i, t, m * KEYS : (m + 1) * KEYS, :] = taps[m]

    for i in range(PAIR):
        for group in range(GROUPS):
            starts = [group * DGROUP + 8 * half for half in range(2)]
            v = [[vol[i, t, at : at + 8, :] for t in range(LINE_RUN)] for at in starts]
            for layer in range(LAYERS):
                s = 3**layer
                fresh = [[], []]
                for t in range(LINE_RUN):
                    rows = [k * KEYS + layer * GROUPS + group for k in range(3)]
                    w = [jnp.broadcast_to(wts[i, t, r : r + 1, :], (8, LANES)) for r in rows]
                    for half in range(2):
                        blk, r = divmod(t + s, LINE_RUN)
                        before = pltpu.roll(v[half][r], LANES - blk, 1) if blk else v[half][r]
                        blk, r = divmod(t - s, LINE_RUN)
                        after = pltpu.roll(v[half][r], -blk, 1) if blk else v[half][r]
                        fresh[half].append(w[0] * before + w[1] * v[half][t] + w[2] * after)
                v = fresh
            for half, at_row in enumerate(starts):
                for t in range(LINE_RUN):
                    done[i, t, at_row : at_row + 8, :] = v[half][t]

    sub = iota((8, LANES), 0)
    results = []
    for i in range(PAIR):
        totals = jnp.zeros((8, LANES), F32)
        moments = totals
        for s in range(LINE_RUN):
            t = LINE_RUN - 1 - s
            v = [done[i, t, 8 * j : 8 * j + 8, :] for j in range(DISP // 8)]
            top = v
            while len(top) > 1:
                top = [jnp.maximum(a, b) for a, b in zip(top[::2], top[1::2])] + top[len(top) & ~1 :]
            top = jnp.max(top[0], axis=0, keepdims=True)
            total = jnp.exp2(v[-1] - top)
            moment = total
            for j in range(DISP // 8 - 2, -1, -1):
                total = total + jnp.exp2(v[j] - top)
                if j:
                    moment = moment + total
            moment = 8.0 * moment + sub.astype(F32) * total
            totals = jnp.where(sub == s, jnp.sum(total, axis=0, keepdims=True), totals)
            moments = jnp.where(sub == s, jnp.sum(moment, axis=0, keepdims=True), moments)
        results.append((moments / totals + offs[i].astype(F32)) * (1.0 / DISP))
    both = jnp.concatenate(results, axis=0)
    high = both.astype(BF)
    left = both - high.astype(F32)
    middle = left.astype(BF)
    low = (left - middle.astype(F32)).astype(BF)
    parts = jnp.dot(
        jnp.concatenate([high, middle, low], axis=0), spread[...], preferred_element_type=F32
    )
    size = PAIR * LINE_RUN
    parts = parts[:size] + parts[size : 2 * size] + parts[2 * size :]
    wanted = iota((LINE_RUN, width), 0) == (iota((LINE_RUN, width), 1) & (LINE_RUN - 1))
    for i in range(PAIR):
        part = jnp.where(wanted, parts[i * LINE_RUN : (i + 1) * LINE_RUN], 0.0)
        out[i : i + 1, :] = jnp.sum(part, axis=0, keepdims=True)


def lines_plan(features, valid_cols, offsets, guide_weight):
    n = lax.axis_size("cols")
    devices = 2 * n
    width = n * BLOCK
    rows = PAIR * CHANNELS
    own = features.reshape(devices, rows, BLOCK)
    pieces = [None] * devices
    gone = ()
    for key in (1, 2, 6, 4, 7, 5, 3, 0):
        masked = key % 2 and key > 1
        (piece,) = call(
            functools.partial(pack_kernel, key),
            [((rows + (MASKS if masked else 0), BLOCK), BF)],
            [], 0,
            (own,) + ((valid_cols,) if masked else ()) + gone,
            1_000_000,
        )
        gone = (piece,)
        moves = [(i, i ^ key) for i in range(devices)]
        pieces[key] = lax.ppermute(piece, ("cols", "view"), moves) if key else piece
    consts = call(
        constants_kernel,
        [
            ((LANES, LANES), BF), ((LANES, LANES), BF), ((DISP, 2 * LANES), BF), ((3 * KEYS, LANES), BF),
            ((LANES, width), BF), (valid_cols.shape, F32),
        ],
        [], 1, (offsets, guide_weight, valid_cols), 1_000_000,
    )
    (rows,) = call(
        lines_kernel,
        [((PAIR, width), F32)],
        [
            pltpu.VMEM((devices, rows, BLOCK), BF),
            pltpu.VMEM((n,) + valid_cols.shape, F32),
            pltpu.VMEM((PAIR, LINE_RUN * LANES, LANES), BF),
            pltpu.VMEM((PAIR, LINE_RUN * LANES, 2 * LANES), BF),
            pltpu.VMEM((PAIR, LINE_RUN, DISP, LANES), F32),
            pltpu.VMEM((PAIR, LINE_RUN, DISP, LANES), F32),
            pltpu.VMEM((PAIR, LINE_RUN, 3 * KEYS, LANES), F32),
        ],
        1, (offsets, *consts, *pieces), 1_000_000_000,
    )
    others = lax.ppermute(rows, "view", [(0, 1), (1, 0)])
    first = lax.axis_index("view") == 0
    return jnp.where(first, jnp.concatenate([rows, others]), jnp.concatenate([others, rows]))[None]


def on_device(features, valid_cols, offsets, guide_weight):
    n = lax.axis_size("cols")
    lines = features.shape[1]
    if lines == 2 * PAIR * n and n * BLOCK == LINE_RUN * LANES:
        return lines_plan(features, valid_cols, offsets, guide_weight)
    return halo_plan(features, valid_cols, offsets, guide_weight)


def solution(mesh):
    return jax.shard_map(
        on_device,
        mesh=mesh,
        in_specs=(
            P("view", ("tiles", "lines"), None, "cols"),
            P(None, ("tiles", "cols")),
            P(("tiles", "lines")),
            P(),
        ),
        out_specs=P(("tiles", "lines"), "cols", None),
        check_vma=False,
    )
```
